32 devices in a mesh: shard: 2 (over core), context: 4 (over z), tensor: 4 (over y, x).
Axes of the slice: x: 2, y: 2, z: 4, core: 2. Of those that a mesh axis runs over, the one named last changes fastest.
Arguments:
- tokens: bfloat16 [2, 8192, 1536], P('shard', 'context'), may hold values from -6 to 6
- cotangent: bfloat16 [2, 8192, 1536], P('shard', 'context'), may hold values from -6 to 6
- doc_lengths: int32 [2, 8], P('shard'), may hold values from 1 to 5120, as said below
- zx_weight: float32 [1536, 2, 3072], P(('shard', 'context'), None, 'tensor'), may hold values from -0.15625 to 0.15625
- bcdt_weight: float32 [1536, 304], P(('shard', 'context'), 'tensor'), may hold values from -0.15625 to 0.15625
- out_weight: float32 [3072, 1536], P('tensor', ('shard', 'context')), may hold values from -0.109375 to 0.109375
- input_gain: float32 [1536], replicated, may hold values from 0.5 to 1.5
- chan_params: float32 [6, 3072], replicated, may hold values from -0.5 to 1.4, as said below
- bc_params: float32 [5, 256], replicated, may hold values from -0.5 to 0.5
- head_params: float32 [3, 48], replicated, as said below
- zx_first: float32 [1536, 2, 3072], P(('shard', 'context'), None, 'tensor'), may hold values from -48 to 48
- bcdt_first: float32 [1536, 304], P(('shard', 'context'), 'tensor'), may hold values from -48 to 48
- out_first: float32 [3072, 1536], P('tensor', ('shard', 'context')), may hold values from -80 to 80
- gain_first: float32 [1536], replicated, may hold values from -48 to 48
- chan_first: float32 [6, 3072], replicated, may hold values from -48 to 48
- bc_first: float32 [5, 256], replicated, may hold values from -160 to 160
- head_first: float32 [3, 48], replicated, may hold values from -320 to 320
- zx_second: float32 [1536, 2, 3072], P(('shard', 'context'), None, 'tensor'), may hold values from 4.096 to 16.384
- bcdt_second: float32 [1536, 304], P(('shard', 'context'), 'tensor'), may hold values from 4.096 to 16.384
- out_second: float32 [3072, 1536], P('tensor', ('shard', 'context')), may hold values from 16.384 to 65.536
- gain_second: float32 [1536], replicated, may hold values from 4.096 to 16.384
- chan_second: float32 [6, 3072], replicated, may hold values from 4.096 to 16.384
- bc_second: float32 [5, 256], replicated, may hold values from 65.536 to 262.144
- head_second: float32 [3, 48], replicated, may hold values from 262.144 to 1048.576
Outputs:
- block_out: bfloat16 [2, 8192, 1536], P('shard', 'context', 'tensor')
- tokens_grad: bfloat16 [2, 8192, 1536], P('shard', 'context', 'tensor')
- zx_weight_new: float32 [1536, 2, 3072], P(('shard', 'context'), None, 'tensor')
- zx_first_new: float32 [1536, 2, 3072], P(('shard', 'context'), None, 'tensor')
- zx_second_new: float32 [1536, 2, 3072], P(('shard', 'context'), None, 'tensor')
- bcdt_weight_new: float32 [1536, 304], P(('shard', 'context'), 'tensor')
- bcdt_first_new: float32 [1536, 304], P(('shard', 'context'), 'tensor')
- bcdt_second_new: float32 [1536, 304], P(('shard', 'context'), 'tensor')
- out_weight_new: float32 [3072, 1536], P('tensor', ('shard', 'context'))
- out_first_new: float32 [3072, 1536], P('tensor', ('shard', 'context'))
- out_second_new: float32 [3072, 1536], P('tensor', ('shard', 'context'))
- input_gain_new: float32 [1536], replicated
- gain_first_new: float32 [1536], replicated
- gain_second_new: float32 [1536], replicated
- chan_params_new: float32 [6, 3072], replicated
- chan_first_new: float32 [6, 3072], replicated
- chan_second_new: float32 [6, 3072], replicated
- bc_params_new: float32 [5, 256], replicated
- bc_first_new: float32 [5, 256], replicated
- bc_second_new: float32 [5, 256], replicated
- head_params_new: float32 [3, 48], replicated
- head_first_new: float32 [3, 48], replicated
- head_second_new: float32 [3, 48], replicated
The draws below stay inside these ranges and needn't reach their ends.
Inputs may be any that keep to these rules, and one draw needn't show every extreme that they name: `doc_lengths`: in each pack the 8 lengths sum to 8192. The first (7) // 2 documents together hold 1025 or 1026 positions; the next document is the longest, of length exactly 5120; the remaining documents hold the rest of the pack, each shorter than 2048. `chan_params`: rows 0 to 4 lie in -0.5 to 0.5, row 5 in 0.6 to 1.4. `head_params`: row 0 lies in -5.5 to -3.5, row 1 below log(4), row 2 in 0.5 to 1.5.
All inputs are finite; a program needn't handle non-finite values.
Results may differ from the reference program's by a relative error of at most 0.003.
The reference program's roundings to bfloat16 on the way count: a program that leaves them out, or rounds other values in their place, can miss the bound.
Values may be sent and summed in bfloat16 or wider, within the bound.
A program may use at most 320 MiB of HBM per device.

```python
import math
import jax
import jax.numpy as jnp
from jax import lax

D = 1536
INNER = 3072
H = 48
P_SIZE = 64
N = 128
KERNEL = 4
SPAN = 256
TOK_DEV = 2048
NDOCS = 8
STEP = 10
SEQ = 8192
PACKS = 2
TOKENS = 16384
BCDT = 304


def split_total(key, total, parts):
    chosen = jax.random.permutation(key, total - 1)[:parts - 1] + 1
    cut_points = jnp.sort(chosen.astype(jnp.int32))
    fences = jnp.concatenate([jnp.zeros((1,), jnp.int32), cut_points, jnp.full((1,), total, jnp.int32)])
    return (fences[1:] - fences[:-1]).astype(jnp.int32)


def pack_lengths(key):
    before_count = (NDOCS - 1) // 2
    after_count = NDOCS - 1 - before_count
    over_key, before_key, after_key, pick_before, pick_after = jax.random.split(key, 5)
    overhang = jax.random.randint(over_key, (), 1, 3).astype(jnp.int32)
    before = split_total(before_key, TOK_DEV // 2, before_count)
    chosen_before = jax.random.randint(pick_before, (), 0, before_count)
    before = before + (jnp.arange(before_count) == chosen_before).astype(jnp.int32) * overhang
    after = split_total(after_key, TOK_DEV - 2, after_count)
    chosen_after = jax.random.randint(pick_after, (), 0, after_count)
    after = after + (jnp.arange(after_count) == chosen_after).astype(jnp.int32) * (2 - overhang)
    longest = jnp.full((1,), SEQ - TOK_DEV - TOK_DEV // 2, jnp.int32)
    return jnp.concatenate([before, longest, after]).astype(jnp.int32)


def draw_doc_lengths(key, part):
    key = jax.random.fold_in(key, 7)
    keys = jax.random.split(key, PACKS)
    return jax.vmap(pack_lengths)(keys).astype(jnp.int32)


def draw_chan_params(key, part):
    key = jax.random.fold_in(key, 13)
    tap_key, gain_key = jax.random.split(key)
    taps = jax.random.uniform(tap_key, (KERNEL + 1, INNER), jnp.float32, -0.5, 0.5)
    gains = jax.random.uniform(gain_key, (1, INNER), jnp.float32, 0.6, 1.4)
    return jnp.concatenate([taps, gains], axis=0)


def draw_head_params(key, part):
    key = jax.random.fold_in(key, 17)
    keys = jax.random.split(key, 5)
    slow_share = 0.5
    bias = jax.random.uniform(keys[0], (1, H), jnp.float32, -5.5, -3.5)
    slow = jax.random.bernoulli(keys[1], slow_share, (1, H))
    slow_rate = jax.random.uniform(keys[2], (1, H), jnp.float32, jnp.log(20.0 / SEQ), jnp.log(120.0 / SEQ))
    fast_rate = jax.random.uniform(keys[3], (1, H), jnp.float32, jnp.log(0.5), jnp.log(4.0))
    rates = jnp.where(slow, slow_rate, fast_rate)
    skip = jax.random.uniform(keys[4], (1, H), jnp.float32, 0.5, 1.5)
    return jnp.concatenate([bias, rates, skip], axis=0)


def block_levels(stream_key, extent, cuts, least, top_value):
    level = 1.0
    for position, shards_of in cuts:
        heights = jax.random.uniform(jax.random.fold_in(jax.random.fold_in(stream_key, 6), position), (shards_of,), jnp.float32, least / len(cuts), top_value / len(cuts))
        level = level * jnp.repeat(jnp.exp(heights), extent[position] // shards_of).reshape((-1,) + (1,) * (len(extent) - 1 - position))
    return level


def scatter_about(stream_key, dims, scale, reach, pieces=(), kind=jnp.bfloat16):
    entries = scale * jax.random.normal(stream_key, dims, jnp.float32)
    if pieces:
        entries = entries * block_levels(stream_key, dims, pieces, -0.22, 0.18)
    return jnp.clip(entries, -reach, reach).astype(kind)


def setup_inputs(seed: int = 0) -> dict:
    key_list = jax.random.split(jax.random.key(seed), 25)
    return {
        "tokens": scatter_about(key_list[0], (PACKS, SEQ, D), 1.0, 6.0, ((0, 2), (1, 4))),
        "cotangent": scatter_about(key_list[1], (PACKS, SEQ, D), 1.0, 6.0, ((0, 2), (1, 4))),
        "doc_lengths": draw_doc_lengths(jax.random.fold_in(key_list[24], 71), 0),
        "zx_weight": scatter_about(key_list[3], (D, 2, INNER), D ** -0.5, 0.15625, ((0, 8), (2, 4)), jnp.float32),
        "bcdt_weight": scatter_about(key_list[4], (D, BCDT), D ** -0.5, 0.15625, ((0, 8), (1, 4)), jnp.float32),
        "out_weight": scatter_about(key_list[5], (INNER, D), INNER ** -0.5, 0.109375, ((0, 4), (1, 8)), jnp.float32),
        "input_gain": jnp.clip(1.0 + 0.1 * jax.random.normal(key_list[6], (D,), jnp.float32), 0.5, 1.5),
        "chan_params": draw_chan_params(jax.random.fold_in(key_list[24], 71), 0),
        "bc_params": jnp.clip(jax.random.uniform(key_list[8], (KERNEL + 1, 2 * N), jnp.float32, -0.5, 0.5), -0.5, 0.5),
        "head_params": draw_head_params(jax.random.fold_in(key_list[24], 71), 0),
        "zx_first": scatter_about(key_list[10], (D, 2, INNER), (0.06 * TOKENS ** 0.5), 48.0, ((0, 8), (2, 4)), jnp.float32),
        "bcdt_first": scatter_about(key_list[11], (D, BCDT), (0.06 * TOKENS ** 0.5), 48.0, ((0, 8), (1, 4)), jnp.float32),
        "out_first": scatter_about(key_list[12], (INNER, D), (0.11 * TOKENS ** 0.5), 80.0, ((0, 4), (1, 8)), jnp.float32),
        "gain_first": scatter_about(key_list[13], (D,), (0.06 * TOKENS ** 0.5), 48.0, (), jnp.float32),
        "chan_first": scatter_about(key_list[14], (KERNEL + 2, INNER), (0.06 * TOKENS ** 0.5), 48.0, (), jnp.float32),
        "bc_first": scatter_about(key_list[15], (KERNEL + 1, 2 * N), (0.22 * TOKENS ** 0.5), 160.0, (), jnp.float32),
        "head_first": scatter_about(key_list[16], (3, H), (0.44 * TOKENS ** 0.5), 320.0, (), jnp.float32),
        "zx_second": jnp.clip(jnp.exp(math.log(16.384) - 1.3862944 * jax.random.uniform(key_list[17], (D, 2, INNER), jnp.float32) ** block_levels(key_list[17], (D, 2, INNER), ((0, 8), (2, 4)), -0.2, 0.2)), 4.096, 16.384),
        "bcdt_second": jnp.clip(jnp.exp(math.log(16.384) - 1.3862944 * jax.random.uniform(key_list[18], (D, BCDT), jnp.float32) ** block_levels(key_list[18], (D, BCDT), ((0, 8), (1, 4)), -0.2, 0.2)), 4.096, 16.384),
        "out_second": jnp.clip(jnp.exp(math.log(65.536) - 1.3862944 * jax.random.uniform(key_list[19], (INNER, D), jnp.float32) ** block_levels(key_list[19], (INNER, D), ((0, 4), (1, 8)), -0.2, 0.2)), 16.384, 65.536),
        "gain_second": jnp.clip(jnp.exp(jax.random.uniform(key_list[20], (D,), jnp.float32, math.log(4.096), math.log(16.384))), 4.096, 16.384),
        "chan_second": jnp.clip(jnp.exp(jax.random.uniform(key_list[21], (KERNEL + 2, INNER), jnp.float32, math.log(4.096), math.log(16.384))), 4.096, 16.384),
        "bc_second": jnp.clip(jnp.exp(jax.random.uniform(key_list[22], (KERNEL + 1, 2 * N), jnp.float32, math.log(65.536), math.log(262.144))), 65.536, 262.144),
        "head_second": jnp.clip(jnp.exp(jax.random.uniform(key_list[23], (3, H), jnp.float32, math.log(262.144), math.log(1048.576))), 262.144, 1048.576),
    }


EPS = 1e-05
BETA_ONE = 0.9
BETA_TWO = 0.999
ADAM_EPS = 1e-08
DECAY = 0.1
RATE_MATRIX = 0.05
RATE_SMALL = 0.2
HIGH = lax.Precision.HIGHEST

@jax.custom_vjp
def low(v):
    return lax.optimization_barrier(v.astype(jnp.bfloat16)).astype(jnp.float32)

@jax.custom_vjp
def low_back(v):
    return v

def low_keep(v):
    return (low(v), None)

def low_pass(kept, grad):
    return (grad,)

def back_keep(v):
    return (v, None)

def back_low(kept, grad):
    return (low(grad),)
low.defvjp(low_keep, low_pass)
low_back.defvjp(back_keep, back_low)

def product(left, right):
    return jnp.dot(left, right, precision=HIGH)

def doc_index(lengths, positions):
    bounds = jnp.cumsum(lengths)[:-1]
    found = lax.optimization_barrier(jnp.sum((positions[:, None] >= bounds[None, :]).astype(jnp.int32), axis=1))
    return jnp.where(positions < 0, -1, found).astype(jnp.int32)

def ssd_span(state, xs, bmat, cmat, delta, dlog, marks, before):
    size = xs.shape[0]
    order = jnp.arange(size)
    lower = order[:, None] >= order[None, :]
    cum = jnp.dot(lower.astype(jnp.float32), dlog, precision=HIGH)
    keep = jnp.logical_and(lower, marks[:, None] == marks[None, :])[:, :, None]
    spread = jnp.where(keep, cum[:, None, :] - cum[None, :, :], 0.0)
    decay = jnp.where(keep, jnp.exp(spread), 0.0)
    scores = jnp.dot(cmat, bmat.T, precision=HIGH)
    mixing = scores[:, :, None] * decay * delta[None, :, :]
    inside = jnp.einsum('ijh,jhp->ihp', mixing, xs, precision=HIGH)
    carried = (marks == before).astype(jnp.float32)[:, None] * jnp.exp(cum)
    entering = jnp.einsum('hpn,in->ihp', state, cmat, precision=HIGH) * carried[:, :, None]
    last = marks[size - 1]
    tail_weight = (marks == last).astype(jnp.float32)[:, None] * jnp.exp(cum[size - 1][None, :] - cum) * delta
    through = jnp.exp(cum[size - 1]) * (last == before).astype(jnp.float32)
    fresh = jnp.einsum('jh,jhp,jn->hpn', tail_weight, xs, bmat, precision=HIGH)
    return (state * through[:, None, None] + fresh, inside + entering)

def forward(tokens, docs, zx_weight, bcdt_weight, out_weight, input_gain, chan_params, bc_params, head_params):
    w_gate = low(zx_weight[:, 0, :])
    w_value = low(zx_weight[:, 1, :])
    w_cols = low(bcdt_weight)
    w_down = low(out_weight)
    taps = jnp.concatenate([chan_params[:KERNEL + 1], bc_params], axis=1)

    def step(carry, inputs):
        state, tail_vals, tail_docs = carry
        resid, marks = inputs
        size = resid.shape[0]
        normed = low(resid * lax.rsqrt(lax.optimization_barrier(jnp.mean(resid * resid, axis=1, keepdims=True)) + EPS) * input_gain)
        projected = low_back(jnp.concatenate([product(normed, w_gate), product(normed, w_value), product(normed, w_cols)], axis=1))
        gate = projected[:, :INNER]
        conv_in = projected[:, INNER:2 * INNER + 2 * N]
        raw_delta = projected[:, 2 * INNER + 2 * N:]
        ext = jnp.concatenate([tail_vals, conv_in], axis=0)
        ext_docs = jnp.concatenate([tail_docs, marks])
        total = jnp.broadcast_to(taps[KERNEL], conv_in.shape)
        for shift in range(KERNEL):
            same = (ext_docs[shift:shift + size] == marks).astype(jnp.float32)[:, None]
            total = total + taps[shift] * ext[shift:shift + size] * same
        active = jax.nn.silu(total)
        xs = active[:, :INNER].reshape(size, H, P_SIZE)
        bmat = active[:, INNER:INNER + N]
        cmat = active[:, INNER + N:]
        delta = jax.nn.softplus(raw_delta + head_params[0])
        dlog = -delta * jnp.exp(head_params[1])
        new_state, mixed = ssd_span(state, xs, bmat, cmat, delta, dlog, marks, ext_docs[KERNEL - 2])
        ssd_out = (mixed + head_params[2][None, :, None] * xs).reshape(size, INNER)
        gated = ssd_out * jax.nn.silu(gate)
        scaled = low(gated * lax.rsqrt(lax.optimization_barrier(jnp.mean(gated * gated, axis=1, keepdims=True)) + EPS) * chan_params[KERNEL + 1])
        result = resid + product(scaled, w_down)
        return ((new_state, ext[size:], ext_docs[size:]), result)

    def one_pack(resid, marks):
        start = (jnp.zeros((H, P_SIZE, N), jnp.float32), jnp.zeros((KERNEL - 1, INNER + 2 * N), jnp.float32), jnp.full((KERNEL - 1,), -1, jnp.int32))
        count = resid.shape[0] // SPAN
        _, outs = lax.scan(jax.checkpoint(step), start, (resid.reshape(count, SPAN, D), marks.reshape(count, SPAN)))
        return outs.reshape(resid.shape[0], D)
    return jax.vmap(one_pack)(tokens, docs)

def adamw(weight, grad, first, second, rate, decay):
    first_new = BETA_ONE * first + (1.0 - BETA_ONE) * grad
    second_new = BETA_TWO * second + (1.0 - BETA_TWO) * grad * grad
    scale_one = 1.0 - BETA_ONE ** STEP
    scale_two = 1.0 - BETA_TWO ** STEP
    update = first_new / scale_one / (jnp.sqrt(second_new / scale_two) + ADAM_EPS)
    return (weight - rate * (update + decay * weight), first_new, second_new)

def reference(tokens, cotangent, doc_lengths, zx_weight, bcdt_weight, out_weight, input_gain, chan_params, bc_params, head_params, zx_first, bcdt_first, out_first, gain_first, chan_first, bc_first, head_first, zx_second, bcdt_second, out_second, gain_second, chan_second, bc_second, head_second):
    positions = jnp.arange(SEQ).astype(jnp.int32)

    def pack_docs(lengths):
        return doc_index(lengths, positions)
    docs = jax.vmap(pack_docs)(doc_lengths)

    def run(inputs, w_zx, w_bcdt, w_out, g_in, chans, bcs, heads):
        return forward(inputs, docs, w_zx, w_bcdt, w_out, g_in, chans, bcs, heads)
    block, pull = jax.vjp(run, tokens.astype(jnp.float32), zx_weight, bcdt_weight, out_weight, input_gain, chan_params, bc_params, head_params)
    grads = pull(cotangent.astype(jnp.float32))
    zx_new = adamw(zx_weight, grads[1], zx_first, zx_second, RATE_MATRIX, DECAY)
    bcdt_new = adamw(bcdt_weight, grads[2], bcdt_first, bcdt_second, RATE_MATRIX, DECAY)
    out_new = adamw(out_weight, grads[3], out_first, out_second, RATE_MATRIX, DECAY)
    gain_new = adamw(input_gain, grads[4], gain_first, gain_second, RATE_SMALL, 0.0)
    chan_new = adamw(chan_params, grads[5], chan_first, chan_second, RATE_SMALL, 0.0)
    bc_new = adamw(bc_params, grads[6], bc_first, bc_second, RATE_SMALL, 0.0)
    head_new = adamw(head_params, grads[7], head_first, head_second, RATE_SMALL, 0.0)
    return (block.astype(jnp.bfloat16), grads[0].astype(jnp.bfloat16), zx_new[0], zx_new[1], zx_new[2], bcdt_new[0], bcdt_new[1], bcdt_new[2], out_new[0], out_new[1], out_new[2], gain_new[0], gain_new[1], gain_new[2], chan_new[0], chan_new[1], chan_new[2], bc_new[0], bc_new[1], bc_new[2], head_new[0], head_new[1], head_new[2])
```

```python
import functools

import jax
import jax.numpy as jnp
from jax import lax
from jax.experimental import pallas as pl
from jax.experimental.pallas import tpu as pltpu
from jax.sharding import PartitionSpec as P

D = 1536
INNER = 3072
H = 48
P_SIZE = 64
N = 128
KERNEL = 4
STEP = 10

EPS = 1e-05
BETA_ONE = 0.9
BETA_TWO = 0.999
ADAM_EPS = 1e-08
DECAY = 0.1
RATE_MATRIX = 0.05
RATE_SMALL = 0.2

L = 128
LANE = 128
LOG2E = 1.4426950408889634
F32 = jnp.float32
BF16 = jnp.bfloat16
VMEM_LIMIT = 48 * 1024 * 1024


def from_behind(block, axis, distance):
    devices = range(lax.axis_size(axis))
    route = [(i - distance, i) for i in devices if i - distance in devices]
    return lax.ppermute(block, axis, route)


def adamw(weight, grad, first, second, rate, decay):
    first_new = BETA_ONE * first + (1.0 - BETA_ONE) * grad
    second_new = BETA_TWO * second + (1.0 - BETA_TWO) * grad * grad
    scale_one = 1.0 - BETA_ONE**STEP
    scale_two = 1.0 - BETA_TWO**STEP
    update = first_new / scale_one / (jnp.sqrt(second_new / scale_two) + ADAM_EPS)
    return (weight - rate * (update + decay * weight), first_new, second_new)


def two(x):
    hi = x.astype(BF16)
    return hi, (x - hi.astype(F32)).astype(BF16)


def dot(a, b, ca=1, cb=0):
    return lax.dot_general(a, b, (((ca,), (cb,)), ((), ())), preferred_element_type=F32)


def dot3(a, b, ca=1, cb=0):
    ah, al = two(a)
    bh, bl = two(b)
    return dot(
        jnp.concatenate([ah, al, ah], axis=ca), jnp.concatenate([bh, bh, bl], axis=cb), ca, cb
    )


def tri_sum(tri, x):
    hi = x.astype(BF16)
    rest = x - hi.astype(F32)
    mid = rest.astype(BF16)
    low = (rest - mid.astype(F32)).astype(BF16)
    out = dot(tri, jnp.concatenate([hi, mid, low], axis=1))
    w = x.shape[1]
    return out[:, :w] + out[:, w : 2 * w] + out[:, 2 * w :]


def spread(x, e_ref):
    hi, lo = two(x)
    return dot(jnp.concatenate([hi, lo], axis=1), e_ref[...])


def per_head(x, e_ref):
    hi, lo = two(x)
    e = e_ref[:LANE, :]
    return dot(hi, e, 1, 1) + dot(lo, e, 1, 1)


def sigmoid(x):
    return 1.0 / (1.0 + jnp.exp(-x))


def softplus(x):
    return jnp.maximum(x, 0.0) + jnp.log1p(jnp.exp(-jnp.abs(x)))


def tiles(width):
    return [slice(k, k + LANE) for k in range(0, width, LANE)]


def fold(x):
    return jnp.sum(x.reshape(x.shape[0] // 8, 8, x.shape[1]), axis=0)


def lower_mask():
    row = lax.broadcasted_iota(jnp.int32, (L, L), 0)
    col = lax.broadcasted_iota(jnp.int32, (L, L), 1)
    return row >= col


def keep_mask(info, marks_row):
    return jnp.logical_and(lower_mask(), info[:, 5:6] == marks_row[0:1, :])


def decay_of(keep, cum, cum_t, h):
    return jnp.exp2(jnp.where(keep, cum[:, h : h + 1] - cum_t[h : h + 1, :], -1e30))


def load_ext(ext_ref, prev_ref, halo_ref, cur_ref, first):
    @pl.when(first)
    def _():
        ext_ref[0:8, :] = halo_ref[...]

    @pl.when(jnp.logical_not(first))
    def _():
        ext_ref[0:8, :] = prev_ref[...]

    ext_ref[8 : 8 + L, :] = cur_ref[...]


def conv_tile(ext_ref, info, taps, sl):
    shifted = []
    total = jnp.broadcast_to(taps[KERNEL : KERNEL + 1, :], (L, LANE))
    for k in range(KERNEL):
        val = ext_ref[pl.ds(8 - KERNEL + 1 + k, L), sl]
        if k < KERNEL - 1:
            val = val * info[:, k : k + 1]
        shifted.append(val)
        total = total + taps[k : k + 1, :] * val
    return shifted, total


def prep_kernel(
    heads, val, valp, bc, bcp, halo_v, halo_b, info_ref, chan, bcpar, head, e_ref,
    act, delta_ref, cum_ref, sloc, pfx, fin, thr, ext_v, ext_b, state, prod,
):
    i = pl.program_id(0)
    first = i == 0

    @pl.when(first)
    def _():
        state[...] = jnp.zeros_like(state)
        prod[...] = jnp.ones_like(prod)

    load_ext(ext_v, valp, halo_v, val, first)
    load_ext(ext_b, bcp, halo_b, bc, first)
    info = info_ref[...]
    width = val.shape[1]
    for sl in tiles(width):
        _, total = conv_tile(ext_v, info, chan[:, sl], sl)
        act[:, sl] = total * sigmoid(total)
    for sl in tiles(2 * N):
        _, total = conv_tile(ext_b, info, bcpar[:, sl], sl)
        act[:, slice(width + sl.start, width + sl.stop)] = total * sigmoid(total)
    raw = bc[:, 2 * N : 3 * N]
    delta = softplus(raw + head[0:1, :])
    dlog = -delta * (jnp.exp(head[1:2, :]) * LOG2E)
    tri = jnp.where(lower_mask(), 1.0, 0.0).astype(BF16)
    cum = tri_sum(tri, dlog)
    delta_ref[...] = delta
    cum_ref[...] = cum
    sloc[0] = state[...]
    pfx[0] = prod[...]
    last = cum[L - 1 : L, :]
    tail = info[:, 4:5] * jnp.exp2(last - cum) * delta
    through = spread(
        jnp.broadcast_to(info[L - 1 : L, 3:4] * jnp.exp2(last), (8, LANE)), e_ref
    )
    weights = spread(tail, e_ref)
    tail_u = act[:, :width] * weights
    fresh = dot3(act[:, width : width + N], tail_u, 0, 0)
    state[...] = state[...] * through[0:1, :] + fresh
    prod[...] = prod[...] * through

    @pl.when(i == pl.num_programs(0) - 1)
    def _():
        fin[...] = state[...]
        thr[...] = prod[...]


def row_block(width, col=0):
    return pl.BlockSpec((L, width), lambda i: (i, col))


def prev_block(width, col=0):
    return pl.BlockSpec((8, width), lambda i: (jnp.maximum(i * (L // 8) - 1, 0), col))


def whole(*shape):
    return pl.BlockSpec(shape, lambda i: (0,) * len(shape))


def params(**kw):
    return pltpu.CompilerParams(
        dimension_semantics=("arbitrary",), vmem_limit_bytes=VMEM_LIMIT, **kw
    )


def shape(*dims, dtype=F32):
    return jax.ShapeDtypeStruct(dims, dtype)


def run_prep(projected, cols, halo_v, halo_b, info, chan, bcpar, head, expand, heads):
    steps, width = projected.shape[0], projected.shape[1] // 2
    count = steps // L
    return pl.pallas_call(
        functools.partial(prep_kernel, heads),
        grid=(count,),
        in_specs=[
            row_block(width, 1), prev_block(width, 1), row_block(3 * N), prev_block(3 * N),
            whole(8, width), whole(8, 3 * N), row_block(LANE),
            whole(8, width), whole(8, 2 * N), whole(8, LANE), whole(2 * LANE, width),
        ],
        out_specs=[
            row_block(width + 2 * N), row_block(LANE), row_block(LANE),
            pl.BlockSpec((1, N, width), lambda i: (i, 0, 0)),
            pl.BlockSpec((1, 8, width), lambda i: (i, 0, 0)),
            whole(N, width), whole(8, width),
        ],
        out_shape=[
            shape(steps, width + 2 * N), shape(steps, LANE), shape(steps, LANE),
            shape(count, N, width), shape(count, 8, width), shape(N, width), shape(8, width),
        ],
        scratch_shapes=[
            pltpu.VMEM((8 + L, width), F32), pltpu.VMEM((8 + L, 3 * N), F32),
            pltpu.VMEM((N, width), F32), pltpu.VMEM((8, width), F32),
        ],
        compiler_params=params(),
        name="prep",
    )(projected, projected, cols, cols, halo_v, halo_b, info, chan, bcpar, head, expand)


def ahead_kernel(
    heads, act, delta_ref, cum_ref, info_ref, marks_ref, sloc, pfx, entry, gate, back, chan, head,
    e_ref, ssd, sums,
):
    width = act.shape[1] - 2 * N
    info = info_ref[...]
    cum = cum_ref[...]
    cum_t = cum.T
    keep = keep_mask(info, marks_ref[0])
    bmat = act[:, width : width + N]
    cmat = act[:, width + N :]
    scores = dot3(cmat, bmat, 1, 1)
    xs = act[:, :width]
    u_hi, u_lo = two(xs * spread(delta_ref[...], e_ref))
    state = sloc[0] + entry[...] * pfx[0, 0:1, :]
    entering = dot3(cmat, state)
    eexp = spread(info[:, 3:4] * jnp.exp2(cum), e_ref)
    skip = spread(jnp.broadcast_to(head[2:3, :], (8, LANE)), e_ref)
    lane = lax.broadcasted_iota(jnp.int32, (1, LANE), 1)
    left = jnp.where(lane < P_SIZE, 1.0, 0.0).astype(BF16)
    right = jnp.where(lane < P_SIZE, 0.0, 1.0).astype(BF16)
    square = jnp.zeros((L, LANE), F32)
    cross = jnp.zeros((L, LANE), F32)
    for q, sl in enumerate(tiles(width)):
        mix = jnp.concatenate(
            [(scores * decay_of(keep, cum, cum_t, 2 * q + r)).astype(BF16) for r in (0, 1)], axis=1
        )
        both = jnp.concatenate([u_hi[:, sl], u_lo[:, sl]], axis=1)
        rhs = jnp.concatenate(
            [both * jnp.concatenate([m, m], axis=1) for m in (left, right)], axis=0
        )
        out = dot(mix, rhs)
        y = out[:, :LANE] + out[:, LANE:] + entering[:, sl] * eexp[:, sl]
        y = y + skip[0:1, sl] * xs[:, sl]
        ssd[:, sl] = y
        g = gate[:, sl]
        gated = y * g * sigmoid(g)
        square = square + gated * gated
        cross = cross + gated * (back[:, sl] * chan[KERNEL + 1 : KERNEL + 2, sl])
    ones = jnp.ones((8, LANE), BF16)
    rows = []
    for part in (square, cross):
        hi, lo = two(part)
        rows.append(dot(ones, hi, 1, 1) + dot(ones, lo, 1, 1))
    pick = lax.broadcasted_iota(jnp.int32, (8, LANE), 0)
    sums[0] = jnp.where(pick == 0, rows[0], jnp.where(pick == 1, rows[1], 0.0))


def run_ahead(act, delta, cum, info, marks, sloc, pfx, entry, projected, back, chan, head, expand, heads):
    steps, width = projected.shape[0], projected.shape[1] // 2
    count = steps // L
    return pl.pallas_call(
        functools.partial(ahead_kernel, heads),
        grid=(count,),
        in_specs=[
            row_block(width + 2 * N), row_block(LANE), row_block(LANE), row_block(LANE),
            pl.BlockSpec((1, 8, L), lambda i: (i, 0, 0)),
            pl.BlockSpec((1, N, width), lambda i: (i, 0, 0)),
            pl.BlockSpec((1, 8, width), lambda i: (i, 0, 0)),
            whole(N, width), row_block(width, 0), row_block(width),
            whole(8, width), whole(8, LANE), whole(2 * LANE, width),
        ],
        out_specs=[row_block(width), pl.BlockSpec((1, 8, L), lambda i: (i, 0, 0))],
        out_shape=[shape(steps, width), shape(count, 8, L)],
        compiler_params=params(),
        name="ahead",
    )(act, delta, cum, info, marks, sloc, pfx, entry, projected, back, chan, head, expand)


def norm_kernel(
    heads, ssd, gate, back, sums, cmat_ref, cum_ref, info_ref, chan, e_ref,
    scaled, gate_grad, mixed_grad, aloc, sfx, fin, gain_grad, state, prod,
):
    i = pl.program_id(0)
    width = ssd.shape[1]

    @pl.when(i == 0)
    def _():
        state[...] = jnp.zeros_like(state)
        prod[...] = jnp.ones_like(prod)
        gain_grad[...] = jnp.zeros_like(gain_grad)

    rows = sums[0]
    inv_row = lax.rsqrt(rows[0:1, :] / INNER + EPS)
    cross_row = inv_row * inv_row * inv_row * (rows[1:2, :] / INNER)
    inv = jnp.broadcast_to(inv_row, (LANE, L)).T
    cross = jnp.broadcast_to(cross_row, (LANE, L)).T
    info = info_ref[...]
    cum = cum_ref[...]
    eexp = spread(info[:, 3:4] * jnp.exp2(cum), e_ref)
    e_mixed = []
    for sl in tiles(width):
        g = gate[:, sl]
        sig = sigmoid(g)
        soft = g * sig
        y = ssd[:, sl]
        gated = y * soft
        bs = back[:, sl]
        gain = chan[KERNEL + 1 : KERNEL + 2, sl]
        normed = gated * inv
        scaled[:, sl] = (normed * gain).astype(BF16)
        gain_grad[:, sl] += fold(bs * normed)
        gg = inv * (bs * gain) - gated * cross
        mg = gg * soft
        mixed_grad[:, sl] = mg
        gate_grad[:, sl] = (gg * y * sig * (1.0 + g * (1.0 - sig))).astype(BF16)
        e_mixed.append(mg * eexp[:, sl])
    aloc[0] = state[...]
    sfx[0] = prod[...]
    through = spread(
        jnp.broadcast_to(info[L - 1 : L, 3:4] * jnp.exp2(cum[L - 1 : L, :]), (8, LANE)), e_ref
    )
    fresh = dot3(cmat_ref[...], jnp.concatenate(e_mixed, axis=1), 0, 0)
    state[...] = state[...] * through[0:1, :] + fresh
    prod[...] = prod[...] * through

    @pl.when(i == pl.num_programs(0) - 1)
    def _():
        fin[...] = state[...]


def run_norm(ssd, projected, back, sums, act, cum, info, chan, expand, heads):
    steps, width = ssd.shape
    count = steps // L
    turn = lambda spec: pl.BlockSpec(
        spec.block_shape, lambda i, m=spec.index_map: m(count - 1 - i)
    )
    c_col = width // N + 1
    return pl.pallas_call(
        functools.partial(norm_kernel, heads),
        grid=(count,),
        in_specs=[
            turn(row_block(width)), turn(row_block(width, 0)), turn(row_block(width)),
            turn(pl.BlockSpec((1, 8, L), lambda i: (i, 0, 0))),
            turn(row_block(N, c_col)), turn(row_block(LANE)), turn(row_block(LANE)),
            whole(8, width), whole(2 * LANE, width),
        ],
        out_specs=[
            turn(row_block(width)), turn(row_block(width)), turn(row_block(width)),
            turn(pl.BlockSpec((1, N, width), lambda i: (i, 0, 0))),
            turn(pl.BlockSpec((1, 8, width), lambda i: (i, 0, 0))),
            whole(N, width), whole(8, width),
        ],
        out_shape=[
            shape(steps, width, dtype=BF16), shape(steps, width, dtype=BF16), shape(steps, width),
            shape(count, N, width), shape(count, 8, width), shape(N, width), shape(8, width),
        ],
        scratch_shapes=[pltpu.VMEM((N, width), F32), pltpu.VMEM((8, width), F32)],
        compiler_params=params(),
        name="norm_back",
    )(ssd, projected, back, sums, act, cum, info, chan, expand)


def behind_kernel(
    heads, val, valp, bc, bcp, halo_v, halo_b, info_ref, marks_ref, delta_ref, cum_ref, ssd, mixed_grad,
    sloc, pfx, entry, aloc, sfx, later, chan, bcpar, head, e_ref,
    grad_v, grad_b, raw_grad, tail_rows, head_rows, taps_grad, bias_grad, skip_grad, head_grad,
    ext_v, ext_b, slope, d_tot,
):
    i = pl.program_id(0)
    n_steps = pl.num_programs(0)
    first = i == n_steps - 1
    width = val.shape[1]
    total_width = width + 2 * N

    @pl.when(i == 0)
    def _():
        d_tot[L:, :] = jnp.zeros((8, total_width), F32)
        taps_grad[...] = jnp.zeros_like(taps_grad)
        bias_grad[...] = jnp.zeros_like(bias_grad)
        skip_grad[...] = jnp.zeros_like(skip_grad)
        head_grad[...] = jnp.zeros_like(head_grad)

    @pl.when(i > 0)
    def _():
        d_tot[L:, :] = d_tot[0:8, :]

    load_ext(ext_v, valp, halo_v, val, first)
    load_ext(ext_b, bcp, halo_b, bc, first)
    info = info_ref[...]

    def activate(ext_ref, taps, sl, at):
        _, total = conv_tile(ext_ref, info, taps[:, sl], sl)
        sig = sigmoid(total)
        slope[:, slice(at, at + LANE)] = sig * (1.0 + total * (1.0 - sig))
        return total * sig

    xs = jnp.concatenate([activate(ext_v, chan, sl, sl.start) for sl in tiles(width)], axis=1)
    bmat = activate(ext_b, bcpar, slice(0, N), width)
    cmat = activate(ext_b, bcpar, slice(N, 2 * N), width + N)

    delta = delta_ref[...]
    cum = cum_ref[...]
    cum_t = cum.T
    keep = keep_mask(info, marks_ref[0])
    last = cum[L - 1 : L, :]
    scores = dot3(cmat, bmat, 1, 1)
    dexp = spread(delta, e_ref)
    eexp = spread(info[:, 3:4] * jnp.exp2(cum), e_ref)
    texp = spread(info[:, 4:5] * jnp.exp2(last - cum), e_ref)
    u = xs * dexp
    u_hi, u_lo = two(u)
    dy = mixed_grad[...]
    dy_hi, dy_lo = two(dy)
    skip = spread(jnp.broadcast_to(head[2:3, :], (8, LANE)), e_ref)
    state = sloc[0] + entry[...] * pfx[0, 0:1, :]
    adj = aloc[0] + later[...] * sfx[0, 0:1, :]
    tail_du = dot3(bmat, adj) * texp
    lane = lax.broadcasted_iota(jnp.int32, (1, LANE), 1)
    left = jnp.where(lane < P_SIZE, 1.0, 0.0).astype(BF16)
    right = jnp.where(lane < P_SIZE, 0.0, 1.0).astype(BF16)
    two_left = jnp.concatenate([left, left], axis=1)
    two_right = jnp.concatenate([right, right], axis=1)
    d_scores = jnp.zeros((L, L), F32)
    inner_du = []
    for q, sl in enumerate(tiles(width)):
        decays = [decay_of(keep, cum, cum_t, 2 * q + r) for r in (0, 1)]
        mix = jnp.concatenate([(scores * d).astype(BF16) for d in decays], axis=0)
        dy_both = jnp.concatenate([dy_hi[:, sl], dy_lo[:, sl]], axis=1)
        rhs = jnp.concatenate([dy_both * two_left, dy_both * two_right], axis=0)
        out = dot(mix, rhs, 0, 0)
        inner_du.append(out[:, :LANE] + out[:, LANE:])
        u_twice = jnp.concatenate([u_hi[:, sl], u_hi[:, sl]], axis=1)
        u_rows = jnp.concatenate([u_twice * two_left, u_twice * two_right], axis=0)
        d_mix = dot(dy_both, u_rows, 1, 1)
        d_scores = d_scores + d_mix[:, :L] * decays[0] + d_mix[:, L:] * decays[1]
    du = jnp.concatenate(inner_du, axis=1) + tail_du
    d_xs = dexp * du + skip[0:1, :] * dy
    d_b = dot3(d_scores, cmat, 0, 0) + dot3(u * texp, adj, 1, 1)
    d_c = dot3(d_scores, bmat) + dot3(dy * eexp, state, 1, 1)
    skip_grad[...] += fold(dy * xs)

    direct = per_head(xs * du, e_ref)
    mixed = ssd[...] - skip[0:1, :] * xs
    d_cum = per_head(dy * mixed, e_ref) - delta * direct
    at_last = jnp.sum(per_head(u * tail_du, e_ref), axis=0, keepdims=True)
    through = info[L - 1 : L, 3:4] * jnp.exp2(last)
    pair = per_head(fold(adj * state), e_ref)
    at_last = at_last + through * jnp.sum(pair, axis=0, keepdims=True)
    upper = jnp.where(lower_mask(), 1.0, 0.0).astype(BF16).T
    d_log = tri_sum(upper, d_cum) + at_last
    rate = jnp.exp(head[1:2, :])
    raw = bc[:, 2 * N : 3 * N]
    valid = lane < heads
    d_raw = (direct - d_log * rate) * sigmoid(raw + head[0:1, :])
    d_raw = jnp.where(valid, d_raw, 0.0)
    raw_grad[...] = d_raw
    head_grad[0:8, :] += fold(d_raw)
    head_grad[8:16, :] += fold(jnp.where(valid, -d_log * delta * rate, 0.0))

    d_act = [d_xs[:, sl] for sl in tiles(width)] + [d_b, d_c]
    for q in range(total_width // LANE):
        sl = slice(q * LANE, (q + 1) * LANE)
        if q < width // LANE:
            ext_ref, taps, part = ext_v, chan[:, sl], sl
        else:
            part = slice(sl.start - width, sl.stop - width)
            ext_ref, taps = ext_b, bcpar[:, part]
        dt = d_act[q] * slope[:, sl]
        d_tot[0:L, sl] = dt
        bias_grad[:, sl] += fold(dt)
        for k in range(KERNEL):
            moved = ext_ref[pl.ds(8 - KERNEL + 1 + k, L), part]
            if k < KERNEL - 1:
                moved = moved * info[:, k : k + 1]
            taps_grad[8 * k : 8 * k + 8, sl] += fold(dt * moved)
        total = dt * taps[KERNEL - 1 : KERNEL, :]
        for s in range(1, KERNEL):
            total = total + taps[KERNEL - 1 - s : KERNEL - s, :] * (
                d_tot[pl.ds(s, L), sl] * info[:, 7 + s : 8 + s]
            )
        if q < width // LANE:
            grad_v[:, sl] = total.astype(BF16)
        else:
            grad_b[:, part] = total

        @pl.when(i == 0)
        def _():
            tail_rows[:, sl] = total[L - 8 :, :]

    @pl.when(first)
    def _():
        head_rows[...] = d_tot[0:8, :]


def run_behind(
    projected, cols, halo_v, halo_b, info, marks, delta, cum, ssd, mixed_grad, sloc, pfx, entry,
    aloc, sfx, later, chan, bcpar, head, expand, heads,
):
    steps, width = ssd.shape
    count = steps // L
    turn = lambda spec: pl.BlockSpec(
        spec.block_shape, lambda i, m=spec.index_map: m(count - 1 - i)
    )
    chunk = pl.BlockSpec((1, N, width), lambda i: (i, 0, 0))
    few = pl.BlockSpec((1, 8, width), lambda i: (i, 0, 0))
    total = width + 2 * N
    return pl.pallas_call(
        functools.partial(behind_kernel, heads),
        grid=(count,),
        in_specs=[
            turn(row_block(width, 1)), turn(prev_block(width, 1)),
            turn(row_block(3 * N)), turn(prev_block(3 * N)),
            whole(8, width), whole(8, 3 * N), turn(row_block(LANE)),
            turn(pl.BlockSpec((1, 8, L), lambda i: (i, 0, 0))),
            turn(row_block(LANE)), turn(row_block(LANE)), turn(row_block(width)), turn(row_block(width)),
            turn(chunk), turn(few), whole(N, width), turn(chunk), turn(few), whole(N, width),
            whole(8, width), whole(8, 2 * N), whole(8, LANE), whole(2 * LANE, width),
        ],
        out_specs=[
            turn(row_block(width)), turn(row_block(2 * N)), turn(row_block(LANE)),
            whole(8, total), whole(8, total), whole(8 * KERNEL, total), whole(8, total),
            whole(8, width), whole(16, LANE),
        ],
        out_shape=[
            shape(steps, width, dtype=BF16), shape(steps, 2 * N), shape(steps, LANE),
            shape(8, total), shape(8, total), shape(8 * KERNEL, total), shape(8, total),
            shape(8, width), shape(16, LANE),
        ],
        scratch_shapes=[
            pltpu.VMEM((8 + L, width), F32), pltpu.VMEM((8 + L, 3 * N), F32),
            pltpu.VMEM((L, total), F32), pltpu.VMEM((L + 8, total), F32),
        ],
        compiler_params=params(),
        name="behind",
    )(
        projected, projected, cols, cols, halo_v, halo_b, info, marks, delta, cum, ssd, mixed_grad,
        sloc, pfx, entry, aloc, sfx, later, chan, bcpar, head, expand,
    )


def carried_states(state, through, backward):
    count, mine = lax.axis_size("context"), lax.axis_index("context")
    states = lax.all_gather(state, "context")
    throughs = lax.all_gather(through, "context")
    so_far = jnp.zeros_like(state)
    for position in range(count - 1):
        at = count - 1 - position if backward else position
        longer = so_far * throughs[at][None, :] + states[at]
        use = mine < at if backward else at < mine
        so_far = jnp.where(use, longer, so_far)
    return so_far


def pad_rows(x, rows=8):
    return jnp.concatenate([x, jnp.zeros((rows - x.shape[0], x.shape[1]), x.dtype)], axis=0)


def pad_cols(x, cols=LANE):
    return jnp.concatenate([x, jnp.zeros((x.shape[0], cols - x.shape[1]), x.dtype)], axis=1)


def on_device(
    tokens, cotangent, doc_lengths, zx_weight, bcdt_weight, out_weight, input_gain, chan_params,
    bc_params, head_params, zx_first, bcdt_first, out_first, gain_first, chan_first, bc_first,
    head_first, zx_second, bcdt_second, out_second, gain_second, chan_second, bc_second, head_second,
):
    n_tensor = lax.axis_size("tensor")
    t_index = lax.axis_index("tensor")
    c_index = lax.axis_index("context")
    tok = tokens[0]
    resid = tok.astype(F32)
    back = cotangent[0]
    steps = resid.shape[0]
    inner_loc = INNER // n_tensor
    heads_loc = H // n_tensor
    share = D // n_tensor
    count = steps // L
    rows_loc = zx_weight.shape[0]
    cols_loc = bcdt_weight.shape[1]

    zx_flat = zx_weight.reshape(rows_loc, 2 * inner_loc)
    proj_w = lax.all_gather(zx_flat.astype(BF16), ("shard", "context"), axis=0, tiled=True)
    cols_all = lax.all_gather(bcdt_weight.astype(BF16), ("shard", "context", "tensor"))
    cols_w = cols_all.reshape(-1, n_tensor, rows_loc, cols_loc).transpose(0, 2, 1, 3)
    cols_w = cols_w.reshape(D, n_tensor * cols_loc)
    down_w = lax.all_gather(out_weight.astype(BF16), ("shard", "context"), axis=1, tiled=True)

    bounds = jnp.cumsum(doc_lengths[0])[:-1]
    positions = c_index * steps + jnp.arange(1 - KERNEL, steps + KERNEL - 1)
    found = jnp.sum((positions[:, None] >= bounds[None, :]).astype(jnp.int32), axis=1)
    all_docs = jnp.where(positions < 0, -1, found)
    marks = all_docs[KERNEL - 1 : KERNEL - 1 + steps]
    marks_c = marks.reshape(count, L)
    before_c = all_docs[KERNEL - 2 : KERNEL - 2 + steps].reshape(count, L)[:, :1]
    inside = jnp.arange(steps)

    def near(distance):
        return all_docs[KERNEL - 1 + distance : KERNEL - 1 + distance + steps] == marks

    info_cols = [near(k - KERNEL + 1) for k in range(KERNEL - 1)]
    info_cols += [
        (marks_c == before_c).reshape(steps),
        (marks_c == marks_c[:, L - 1 :]).reshape(steps),
        marks,
        jnp.zeros_like(marks),
        jnp.zeros_like(marks),
    ]
    info_cols += [jnp.logical_and(near(s), inside + s < steps) for s in range(1, KERNEL)]
    info = pad_cols(jnp.stack([c.astype(F32) for c in info_cols], axis=1))
    marks_rows = jnp.broadcast_to(marks_c.astype(F32)[:, None, :], (count, 8, L))

    chan_loc = lax.dynamic_slice_in_dim(chan_params, t_index * inner_loc, inner_loc, 1)
    head_loc = lax.dynamic_slice_in_dim(head_params, t_index * heads_loc, heads_loc, 1)
    chan8 = pad_rows(chan_loc)
    bc8 = pad_rows(bc_params)
    head8 = pad_rows(pad_cols(head_loc))
    spread_at = jnp.arange(2 * LANE)[:, None] % LANE
    expand = (spread_at == jnp.arange(inner_loc)[None, :] // P_SIZE).astype(BF16)

    inv_rms = lax.rsqrt(jnp.mean(resid * resid, axis=1, keepdims=True) + EPS)
    normed = (resid * inv_rms * input_gain).astype(BF16)
    delta_w = lax.dynamic_slice_in_dim(cols_w, 2 * N + t_index * heads_loc, heads_loc, 1)
    cols = jnp.dot(
        normed, jnp.concatenate([cols_w[:, : 2 * N], pad_cols(delta_w)], axis=1),
        preferred_element_type=F32,
    )
    projected = jnp.dot(normed, proj_w, preferred_element_type=F32)
    edge = jnp.concatenate(
        [projected[steps - 8 :, inner_loc:], cols[steps - 8 :]], axis=1
    )
    halo = from_behind(edge, "context", 1)
    halo_v, halo_b = halo[:, :inner_loc], halo[:, inner_loc:]

    act, delta, cum, sloc, pfx, final, through = run_prep(
        projected, cols, halo_v, halo_b, info, chan8, bc8, head8, expand, heads_loc
    )
    entry = carried_states(final, through[0], False)
    back_scaled = lax.dot_general(
        back, down_w, (((1,), (1,)), ((), ())), preferred_element_type=F32
    )
    ssd, sums = run_ahead(
        act, delta, cum, info, marks_rows, sloc, pfx, entry, projected, back_scaled, chan8, head8,
        expand, heads_loc,
    )
    sums = lax.psum(sums, "tensor")
    scaled, gate_grad, mixed_grad, aloc, sfx, first_adj, norm_gain_grad = run_norm(
        ssd, projected, back_scaled, sums, act, cum, info, chan8, expand, heads_loc
    )
    later = carried_states(first_adj, through[0], True)

    partial_out = jnp.dot(scaled, down_w, preferred_element_type=F32)
    out_share = lax.psum_scatter(partial_out, "tensor", scatter_dimension=1, tiled=True)
    resid_share = lax.dynamic_slice_in_dim(resid, t_index * share, share, 1)
    block_out = (resid_share + out_share).astype(BF16)[None]
    down_grad = lax.dot_general(
        scaled, back, (((0,), (0,)), ((), ())), preferred_element_type=F32
    )
    down_g = lax.psum_scatter(
        down_grad, ("shard", "context"), scatter_dimension=1, tiled=True
    )

    (
        grad_v, grad_b, raw_grad, tail_rows, head_rows, taps_grad, bias_grad, skip_grad, head_grad
    ) = run_behind(
        projected, cols, halo_v, halo_b, info, marks_rows, delta, cum, ssd, mixed_grad, sloc, pfx,
        entry, aloc, sfx, later, chan8, bc8, head8, expand, heads_loc,
    )
    next_rows = from_behind(head_rows, "context", -1)
    all_taps = jnp.concatenate([chan_loc[:KERNEL], bc_params[:KERNEL]], axis=1)
    edge_grad = jnp.zeros((8, inner_loc + 2 * N), F32)
    for s in range(1, KERNEL):
        same = (
            all_docs[KERNEL - 1 + steps : KERNEL - 1 + steps + s]
            == all_docs[KERNEL - 1 + steps - s : KERNEL - 1 + steps]
        ).astype(F32)[:, None]
        piece = all_taps[KERNEL - 1 - s] * next_rows[:s] * same
        edge_grad = edge_grad.at[8 - s :].add(piece)
    last_rows = tail_rows + edge_grad
    grad_v = lax.dynamic_update_slice(
        grad_v, last_rows[:, :inner_loc].astype(BF16), (steps - 8, 0)
    )
    grad_b = lax.dynamic_update_slice(grad_b, last_rows[:, inner_loc:], (steps - 8, 0))
    delta_full = lax.dynamic_update_slice_in_dim(
        jnp.zeros((steps, H), F32), raw_grad[:, :heads_loc], t_index * heads_loc, 1
    )
    cols_full = jnp.concatenate([grad_b, delta_full], axis=1)
    cols_grad = lax.psum_scatter(cols_full, "tensor", scatter_dimension=1, tiled=True).astype(BF16)
    cols_mine = lax.dynamic_slice_in_dim(cols_w, t_index * cols_loc, cols_loc, 1)
    proj_grad = jnp.concatenate([gate_grad, grad_v], axis=1)
    normed_grad = lax.dot_general(
        proj_grad, proj_w, (((1,), (1,)), ((), ())), preferred_element_type=F32
    ) + lax.dot_general(
        cols_grad, cols_mine, (((1,), (1,)), ((), ())), preferred_element_type=F32
    )
    proj_w_grad = lax.dot_general(
        normed, proj_grad, (((0,), (0,)), ((), ())), preferred_element_type=F32
    )
    cols_w_grad = lax.dot_general(
        normed, cols_grad, (((0,), (0,)), ((), ())), preferred_element_type=F32
    )
    full_share = lax.psum_scatter(normed_grad, "tensor", scatter_dimension=1, tiled=True)
    row_part = jnp.sum(normed_grad * input_gain * resid, axis=1, keepdims=True)
    row_dot = lax.psum(row_part, "tensor")
    gain_share = lax.dynamic_slice_in_dim(input_gain, t_index * share, share, 0)
    resid_grad = inv_rms * (full_share * gain_share) - resid_share * (
        inv_rms * inv_rms * inv_rms
    ) * (row_dot / D)
    back_share = lax.dynamic_slice_in_dim(back, t_index * share, share, 1).astype(F32)
    tokens_grad = (back_share + resid_grad).astype(BF16)[None]
    gain_piece = jnp.sum(normed_grad * resid * inv_rms, axis=0)

    proj_g = lax.psum_scatter(proj_w_grad, ("shard", "context"), scatter_dimension=0, tiled=True)
    cols_g = lax.psum_scatter(cols_w_grad, ("shard", "context"), scatter_dimension=0, tiled=True)

    taps_sum = jnp.sum(taps_grad.reshape(KERNEL, 8, -1), axis=1)
    conv_par = jnp.concatenate([taps_sum, jnp.sum(bias_grad, axis=0)[None]], axis=0)
    chan_piece = jnp.concatenate(
        [conv_par[:, :inner_loc], jnp.sum(norm_gain_grad, axis=0)[None]], axis=0
    )
    chan_full = lax.dynamic_update_slice_in_dim(
        jnp.zeros((KERNEL + 2, INNER), F32), chan_piece, t_index * inner_loc, 1
    )
    bc_grad = conv_par[:, inner_loc:]
    skip_piece = jnp.sum(jnp.sum(skip_grad, axis=0).reshape(heads_loc, P_SIZE), axis=1)
    head_sums = jnp.sum(head_grad.reshape(2, 8, LANE), axis=1)[:, :heads_loc]
    head_piece = jnp.concatenate([head_sums, skip_piece[None]], axis=0)
    head_full = lax.dynamic_update_slice_in_dim(
        jnp.zeros((3, H), F32), head_piece, t_index * heads_loc, 1
    )
    chan_g, bc_g, head_g, gain_g = lax.psum(
        (chan_full, bc_grad, head_full, gain_piece), ("shard", "context", "tensor")
    )
    zx_new = adamw(
        zx_weight, proj_g.reshape(zx_weight.shape), zx_first, zx_second, RATE_MATRIX, DECAY
    )
    bcdt_new = adamw(bcdt_weight, cols_g, bcdt_first, bcdt_second, RATE_MATRIX, DECAY)
    out_new = adamw(out_weight, down_g, out_first, out_second, RATE_MATRIX, DECAY)
    gain_new = adamw(input_gain, gain_g, gain_first, gain_second, RATE_SMALL, 0.0)
    chan_new = adamw(chan_params, chan_g, chan_first, chan_second, RATE_SMALL, 0.0)
    bc_new = adamw(bc_params, bc_g, bc_first, bc_second, RATE_SMALL, 0.0)
    head_new = adamw(head_params, head_g, head_first, head_second, RATE_SMALL, 0.0)
    return (
        block_out, tokens_grad, *zx_new, *bcdt_new, *out_new, *gain_new, *chan_new, *bc_new, *head_new
    )


def solution(mesh):
    big = P(("shard", "context"), None, "tensor")
    cols = P(("shard", "context"), "tensor")
    down = P("tensor", ("shard", "context"))
    rows = P("shard", "context", None)
    out_rows = P("shard", "context", "tensor")
    return jax.shard_map(
        on_device,
        mesh=mesh,
        in_specs=(
            rows, rows, P("shard", None), big, cols, down, P(), P(), P(), P(),
            big, cols, down, P(), P(), P(), P(),
            big, cols, down, P(), P(), P(), P(),
        ),
        out_specs=(
            out_rows, out_rows, big, big, big, cols, cols, cols, down, down, down,
            *([P()] * 12),
        ),
        check_vma=False,
    )
```

```python
import functools

import jax
import jax.numpy as jnp
from jax import lax
from jax.experimental import pallas as pl
from jax.experimental.pallas import tpu as pltpu
from jax.sharding import PartitionSpec as P

D = 1536
INNER = 3072
H = 48
P_SIZE = 64
N = 128
KERNEL = 4
STEP = 10

EPS = 1e-05
BETA_ONE = 0.9
BETA_TWO = 0.999
ADAM_EPS = 1e-08
DECAY = 0.1
RATE_MATRIX = 0.05
RATE_SMALL = 0.2

L = 128
LANE = 128
LOG2E = 1.4426950408889634
F32 = jnp.float32
BF16 = jnp.bfloat16
VMEM_LIMIT = 48 * 1024 * 1024


def from_behind(block, axis, distance):
    devices = range(lax.axis_size(axis))
    route = [(i - distance, i) for i in devices if i - distance in devices]
    return lax.ppermute(block, axis, route)


def adamw(weight, grad, first, second, rate, decay):
    first_new = BETA_ONE * first + (1.0 - BETA_ONE) * grad
    second_new = BETA_TWO * second + (1.0 - BETA_TWO) * grad * grad
    scale_one = 1.0 - BETA_ONE**STEP
    scale_two = 1.0 - BETA_TWO**STEP
    update = first_new / scale_one / (jnp.sqrt(second_new / scale_two) + ADAM_EPS)
    return (weight - rate * (update + decay * weight), first_new, second_new)


def two(x):
    hi = x.astype(BF16)
    return hi, (x - hi.astype(F32)).astype(BF16)


def dot(a, b, ca=1, cb=0):
    return lax.dot_general(a, b, (((ca,), (cb,)), ((), ())), preferred_element_type=F32)


def dot3(a, b, ca=1, cb=0):
    ah, al = two(a)
    bh, bl = two(b)
    return dot(
        jnp.concatenate([ah, al, ah], axis=ca), jnp.concatenate([bh, bh, bl], axis=cb), ca, cb
    )


def tri_sum(tri, x):
    hi = x.astype(BF16)
    rest = x - hi.astype(F32)
    mid = rest.astype(BF16)
    low = (rest - mid.astype(F32)).astype(BF16)
    out = dot(tri, jnp.concatenate([hi, mid, low], axis=1))
    w = x.shape[1]
    return out[:, :w] + out[:, w : 2 * w] + out[:, 2 * w :]


def spread(x, e_ref):
    hi, lo = two(x)
    return dot(jnp.concatenate([hi, lo], axis=1), e_ref[...])


def per_head(x, e_ref):
    hi, lo = two(x)
    e = e_ref[:LANE, :]
    return dot(hi, e, 1, 1) + dot(lo, e, 1, 1)


def sigmoid(x):
    return 1.0 / (1.0 + jnp.exp(-x))


def softplus(x):
    return jnp.maximum(x, 0.0) + jnp.log1p(jnp.exp(-jnp.abs(x)))


def tiles(width):
    return [slice(k, k + LANE) for k in range(0, width, LANE)]


def fold(x):
    return jnp.sum(x.reshape(x.shape[0] // 8, 8, x.shape[1]), axis=0)


def lower_mask():
    row = lax.broadcasted_iota(jnp.int32, (L, L), 0)
    col = lax.broadcasted_iota(jnp.int32, (L, L), 1)
    return row >= col


def keep_mask(info, marks_row):
    return jnp.logical_and(lower_mask(), info[:, 5:6] == marks_row[0:1, :])


def decay_of(keep, cum, cum_t, h):
    return jnp.exp2(jnp.where(keep, cum[:, h : h + 1] - cum_t[h : h + 1, :], -1e30))


def load_ext(ext_ref, prev_ref, halo_ref, cur_ref, first):
    @pl.when(first)
    def _():
        ext_ref[0:8, :] = halo_ref[...]

    @pl.when(jnp.logical_not(first))
    def _():
        ext_ref[0:8, :] = prev_ref[...]

    ext_ref[8 : 8 + L, :] = cur_ref[...]


def conv_tile(ext_ref, info, taps, sl):
    shifted = []
    total = jnp.broadcast_to(taps[KERNEL : KERNEL + 1, :], (L, LANE))
    for k in range(KERNEL):
        val = ext_ref[pl.ds(8 - KERNEL + 1 + k, L), sl]
        if k < KERNEL - 1:
            val = val * info[:, k : k + 1]
        shifted.append(val)
        total = total + taps[k : k + 1, :] * val
    return shifted, total


def prep_kernel(
    heads, val, valp, bc, bcp, halo_v, halo_b, info_ref, chan, bcpar, head, e_ref,
    act, delta_ref, cum_ref, sloc, pfx, fin, ext_v, ext_b, state, prod,
):
    i = pl.program_id(0)
    first = i == 0

    @pl.when(first)
    def _():
        state[...] = jnp.zeros_like(state)
        prod[...] = jnp.ones_like(prod)

    load_ext(ext_v, valp, halo_v, val, first)
    load_ext(ext_b, bcp, halo_b, bc, first)
    info = info_ref[...]
    width = val.shape[1]
    for sl in tiles(width):
        _, total = conv_tile(ext_v, info, chan[:, sl], sl)
        act[:, sl] = total * sigmoid(total)
    for sl in tiles(2 * N):
        _, total = conv_tile(ext_b, info, bcpar[:, sl], sl)
        act[:, slice(width + sl.start, width + sl.stop)] = total * sigmoid(total)
    raw = bc[:, 2 * N : 3 * N]
    delta = softplus(raw + head[0:1, :])
    dlog = -delta * (jnp.exp(head[1:2, :]) * LOG2E)
    tri = jnp.where(lower_mask(), 1.0, 0.0).astype(BF16)
    cum = tri_sum(tri, dlog)
    delta_ref[...] = delta
    cum_ref[...] = cum
    sloc[0] = state[...]
    pfx[0] = prod[...]
    last = cum[L - 1 : L, :]
    tail = info[:, 4:5] * jnp.exp2(last - cum) * delta
    through = spread(
        jnp.broadcast_to(info[L - 1 : L, 3:4] * jnp.exp2(last), (8, LANE)), e_ref
    )
    weights = spread(tail, e_ref)
    tail_u = act[:, :width] * weights
    fresh = dot3(act[:, width : width + N], tail_u, 0, 0)
    state[...] = state[...] * through[0:1, :] + fresh
    prod[...] = prod[...] * through

    @pl.when(i == pl.num_programs(0) - 1)
    def _():
        fin[:N, :] = state[...]
        fin[N:, :] = prod[...]


def row_block(width, col=0):
    return pl.BlockSpec((L, width), lambda i: (i, col))


def prev_block(width, col=0):
    return pl.BlockSpec((8, width), lambda i: (jnp.maximum(i * (L // 8) - 1, 0), col))


def whole(*shape):
    return pl.BlockSpec(shape, lambda i: (0,) * len(shape))


def estimate(us):
    return pl.CostEstimate(flops=int(us * 1.1e9), bytes_accessed=int(us * 1e6), transcendentals=0)


def params(**kw):
    return pltpu.CompilerParams(
        dimension_semantics=("arbitrary",), vmem_limit_bytes=VMEM_LIMIT, **kw
    )


def shape(*dims, dtype=F32):
    return jax.ShapeDtypeStruct(dims, dtype)


def run_prep(projected, cols, halo_v, halo_b, info, chan, bcpar, head, expand, heads):
    steps, width = projected.shape[0], projected.shape[1] // 2
    count = steps // L
    return pl.pallas_call(
        functools.partial(prep_kernel, heads),
        grid=(count,),
        in_specs=[
            row_block(width, 1), prev_block(width, 1), row_block(3 * N), prev_block(3 * N),
            whole(8, width), whole(8, 3 * N), row_block(LANE),
            whole(8, width), whole(8, 2 * N), whole(8, LANE), whole(2 * LANE, width),
        ],
        out_specs=[
            row_block(width + 2 * N), row_block(LANE), row_block(LANE),
            pl.BlockSpec((1, N, width), lambda i: (i, 0, 0)),
            pl.BlockSpec((1, 8, width), lambda i: (i, 0, 0)),
            whole(N + 8, width),
        ],
        out_shape=[
            shape(steps, width + 2 * N), shape(steps, LANE), shape(steps, LANE),
            shape(count, N, width), shape(count, 8, width), shape(N + 8, width),
        ],
        scratch_shapes=[
            pltpu.VMEM((8 + L, width), F32), pltpu.VMEM((8 + L, 3 * N), F32),
            pltpu.VMEM((N, width), F32), pltpu.VMEM((8, width), F32),
        ],
        compiler_params=params(),
        cost_estimate=estimate(23),
        name="prep",
    )(projected, projected, cols, cols, halo_v, halo_b, info, chan, bcpar, head, expand)


def ahead_kernel(
    heads, act, delta_ref, cum_ref, info_ref, marks_ref, sloc, pfx, entry, gate, back, chan, head,
    e_ref, ssd, sums,
):
    width = act.shape[1] - 2 * N
    info = info_ref[...]
    cum = cum_ref[...]
    cum_t = cum.T
    keep = keep_mask(info, marks_ref[0])
    bmat = act[:, width : width + N]
    cmat = act[:, width + N :]
    scores = dot3(cmat, bmat, 1, 1)
    xs = act[:, :width]
    u_hi, u_lo = two(xs * spread(delta_ref[...], e_ref))
    state = sloc[0] + entry[...] * pfx[0, 0:1, :]
    entering = dot3(cmat, state)
    eexp = spread(info[:, 3:4] * jnp.exp2(cum), e_ref)
    skip = spread(jnp.broadcast_to(head[2:3, :], (8, LANE)), e_ref)
    lane = lax.broadcasted_iota(jnp.int32, (1, LANE), 1)
    left = jnp.where(lane < P_SIZE, 1.0, 0.0).astype(BF16)
    right = jnp.where(lane < P_SIZE, 0.0, 1.0).astype(BF16)
    square = jnp.zeros((L, LANE), F32)
    cross = jnp.zeros((L, LANE), F32)
    for q, sl in enumerate(tiles(width)):
        mix = jnp.concatenate(
            [(scores * decay_of(keep, cum, cum_t, 2 * q + r)).astype(BF16) for r in (0, 1)], axis=1
        )
        both = jnp.concatenate([u_hi[:, sl], u_lo[:, sl]], axis=1)
        rhs = jnp.concatenate(
            [both * jnp.concatenate([m, m], axis=1) for m in (left, right)], axis=0
        )
        out = dot(mix, rhs)
        y = out[:, :LANE] + out[:, LANE:] + entering[:, sl] * eexp[:, sl]
        y = y + skip[0:1, sl] * xs[:, sl]
        ssd[:, sl] = y
        g = gate[:, sl]
        gated = y * g * sigmoid(g)
        square = square + gated * gated
        cross = cross + gated * (back[:, sl] * chan[KERNEL + 1 : KERNEL + 2, sl])
    ones = jnp.ones((8, LANE), BF16)
    rows = []
    for part in (square, cross):
        hi, lo = two(part)
        rows.append(dot(ones, hi, 1, 1) + dot(ones, lo, 1, 1))
    pick = lax.broadcasted_iota(jnp.int32, (8, LANE), 0)
    sums[0] = jnp.where(pick == 0, rows[0], jnp.where(pick == 1, rows[1], 0.0))


def run_ahead(act, delta, cum, info, marks, sloc, pfx, entry, projected, back, chan, head, expand, heads):
    steps, width = projected.shape[0], projected.shape[1] // 2
    count = steps // L
    return pl.pallas_call(
        functools.partial(ahead_kernel, heads),
        grid=(count,),
        in_specs=[
            row_block(width + 2 * N), row_block(LANE), row_block(LANE), row_block(LANE),
            pl.BlockSpec((1, 8, L), lambda i: (i, 0, 0)),
            pl.BlockSpec((1, N, width), lambda i: (i, 0, 0)),
            pl.BlockSpec((1, 8, width), lambda i: (i, 0, 0)),
            whole(N, width), row_block(width, 0), row_block(width),
            whole(8, width), whole(8, LANE), whole(2 * LANE, width),
        ],
        out_specs=[row_block(width), pl.BlockSpec((1, 8, L), lambda i: (i, 0, 0))],
        out_shape=[shape(steps, width), shape(count, 8, L)],
        compiler_params=params(),
        cost_estimate=estimate(20),
        name="ahead",
    )(act, delta, cum, info, marks, sloc, pfx, entry, projected, back, chan, head, expand)


def norm_kernel(
    heads, ssd, gate, back, sums, cmat_ref, cum_ref, info_ref, chan, e_ref,
    gate_grad, mixed_grad, aloc, sfx, fin, gain_grad, state, prod,
):
    i = pl.program_id(0)
    width = ssd.shape[1]

    @pl.when(i == 0)
    def _():
        state[...] = jnp.zeros_like(state)
        prod[...] = jnp.ones_like(prod)
        gain_grad[...] = jnp.zeros_like(gain_grad)

    rows = sums[0]
    inv_row = lax.rsqrt(rows[0:1, :] / INNER + EPS)
    cross_row = inv_row * inv_row * inv_row * (rows[1:2, :] / INNER)
    inv = jnp.broadcast_to(inv_row, (LANE, L)).T
    cross = jnp.broadcast_to(cross_row, (LANE, L)).T
    info = info_ref[...]
    cum = cum_ref[...]
    eexp = spread(info[:, 3:4] * jnp.exp2(cum), e_ref)
    e_mixed = []
    for sl in tiles(width):
        g = gate[:, sl]
        sig = sigmoid(g)
        soft = g * sig
        y = ssd[:, sl]
        gated = y * soft
        bs = back[:, sl]
        gain = chan[KERNEL + 1 : KERNEL + 2, sl]
        normed = gated * inv
        gain_grad[:, sl] += fold(bs * normed)
        gg = inv * (bs * gain) - gated * cross
        mg = gg * soft
        mixed_grad[:, sl] = mg
        gate_grad[:, sl] = (gg * y * sig * (1.0 + g * (1.0 - sig))).astype(BF16)
        e_mixed.append(mg * eexp[:, sl])
    aloc[0] = state[...]
    sfx[0] = prod[...]
    through = spread(
        jnp.broadcast_to(info[L - 1 : L, 3:4] * jnp.exp2(cum[L - 1 : L, :]), (8, LANE)), e_ref
    )
    fresh = dot3(cmat_ref[...], jnp.concatenate(e_mixed, axis=1), 0, 0)
    state[...] = state[...] * through[0:1, :] + fresh
    prod[...] = prod[...] * through

    @pl.when(i == pl.num_programs(0) - 1)
    def _():
        fin[:N, :] = state[...]
        fin[N:, :] = prod[...]


def run_norm(ssd, projected, back, sums, act, cum, info, chan, expand, heads):
    steps, width = ssd.shape
    count = steps // L
    turn = lambda spec: pl.BlockSpec(
        spec.block_shape, lambda i, m=spec.index_map: m(count - 1 - i)
    )
    c_col = width // N + 1
    return pl.pallas_call(
        functools.partial(norm_kernel, heads),
        grid=(count,),
        in_specs=[
            turn(row_block(width)), turn(row_block(width, 0)), turn(row_block(width)),
            turn(pl.BlockSpec((1, 8, L), lambda i: (i, 0, 0))),
            turn(row_block(N, c_col)), turn(row_block(LANE)), turn(row_block(LANE)),
            whole(8, width), whole(2 * LANE, width),
        ],
        out_specs=[
            turn(row_block(width)), turn(row_block(width)),
            turn(pl.BlockSpec((1, N, width), lambda i: (i, 0, 0))),
            turn(pl.BlockSpec((1, 8, width), lambda i: (i, 0, 0))),
            whole(N + 8, width), whole(8, width),
        ],
        out_shape=[
            shape(steps, width, dtype=BF16), shape(steps, width),
            shape(count, N, width), shape(count, 8, width), shape(N + 8, width), shape(8, width),
        ],
        scratch_shapes=[pltpu.VMEM((N, width), F32), pltpu.VMEM((8, width), F32)],
        compiler_params=params(),
        cost_estimate=estimate(21),
        name="norm_back",
    )(ssd, projected, back, sums, act, cum, info, chan, expand)


def behind_chunk(
    heads, val, valp, bc, bcp, halo_v, halo_b, info_ref, marks_ref, delta_ref, cum_ref, ssd, mixed_grad,
    sloc, pfx, entry, aloc, sfx, later, chan, bcpar, head, e_ref,
    grad_v, grad_b, raw_grad, tail_rows, head_rows, taps_grad, bias_grad, skip_grad, head_grad,
    ext_v, ext_b, slope, d_tot,
):
    i = pl.program_id(0)
    n_steps = pl.num_programs(0)
    last_step = i == n_steps - 1
    first = last_step
    width = val.shape[1]
    total_width = width + 2 * N

    @pl.when(i == 0)
    def _():
        d_tot[L:, :] = jnp.zeros((8, total_width), F32)
        taps_grad[...] = jnp.zeros_like(taps_grad)
        bias_grad[...] = jnp.zeros_like(bias_grad)
        skip_grad[...] = jnp.zeros_like(skip_grad)
        head_grad[...] = jnp.zeros_like(head_grad)

    @pl.when(i > 0)
    def _():
        d_tot[L:, :] = d_tot[0:8, :]

    load_ext(ext_v, valp, halo_v, val, first)
    load_ext(ext_b, bcp, halo_b, bc, first)
    info = info_ref[...]

    def activate(ext_ref, taps, sl, at):
        _, total = conv_tile(ext_ref, info, taps[:, sl], sl)
        sig = sigmoid(total)
        slope[:, slice(at, at + LANE)] = sig * (1.0 + total * (1.0 - sig))
        return total * sig

    xs = jnp.concatenate([activate(ext_v, chan, sl, sl.start) for sl in tiles(width)], axis=1)
    bmat = activate(ext_b, bcpar, slice(0, N), width)
    cmat = activate(ext_b, bcpar, slice(N, 2 * N), width + N)

    delta = delta_ref[...]
    cum = cum_ref[...]
    cum_t = cum.T
    keep = keep_mask(info, marks_ref[0])
    last = cum[L - 1 : L, :]
    scores = dot3(cmat, bmat, 1, 1)
    dexp = spread(delta, e_ref)
    eexp = spread(info[:, 3:4] * jnp.exp2(cum), e_ref)
    texp = spread(info[:, 4:5] * jnp.exp2(last - cum), e_ref)
    u = xs * dexp
    u_hi, u_lo = two(u)
    dy = mixed_grad[...]
    dy_hi, dy_lo = two(dy)
    skip = spread(jnp.broadcast_to(head[2:3, :], (8, LANE)), e_ref)
    state = sloc[0] + entry[...] * pfx[0, 0:1, :]
    adj = aloc[0] + later[...] * sfx[0, 0:1, :]
    tail_du = dot3(bmat, adj) * texp
    lane = lax.broadcasted_iota(jnp.int32, (1, LANE), 1)
    left = jnp.where(lane < P_SIZE, 1.0, 0.0).astype(BF16)
    right = jnp.where(lane < P_SIZE, 0.0, 1.0).astype(BF16)
    two_left = jnp.concatenate([left, left], axis=1)
    two_right = jnp.concatenate([right, right], axis=1)
    d_scores = jnp.zeros((L, L), F32)
    inner_du = []
    for q, sl in enumerate(tiles(width)):
        decays = [decay_of(keep, cum, cum_t, 2 * q + r) for r in (0, 1)]
        mix = jnp.concatenate([(scores * d).astype(BF16) for d in decays], axis=0)
        dy_both = jnp.concatenate([dy_hi[:, sl], dy_lo[:, sl]], axis=1)
        rhs = jnp.concatenate([dy_both * two_left, dy_both * two_right], axis=0)
        out = dot(mix, rhs, 0, 0)
        inner_du.append(out[:, :LANE] + out[:, LANE:])
        u_twice = jnp.concatenate([u_hi[:, sl], u_hi[:, sl]], axis=1)
        u_rows = jnp.concatenate([u_twice * two_left, u_twice * two_right], axis=0)
        d_mix = dot(dy_both, u_rows, 1, 1)
        d_scores = d_scores + d_mix[:, :L] * decays[0] + d_mix[:, L:] * decays[1]
    du = jnp.concatenate(inner_du, axis=1) + tail_du
    d_xs = dexp * du + skip[0:1, :] * dy
    d_b = dot3(d_scores, cmat, 0, 0) + dot3(u * texp, adj, 1, 1)
    d_c = dot3(d_scores, bmat) + dot3(dy * eexp, state, 1, 1)
    skip_grad[...] += fold(dy * xs)

    direct = per_head(xs * du, e_ref)
    mixed = ssd[...] - skip[0:1, :] * xs
    d_cum = per_head(dy * mixed, e_ref) - delta * direct
    at_last = jnp.sum(per_head(u * tail_du, e_ref), axis=0, keepdims=True)
    through = info[L - 1 : L, 3:4] * jnp.exp2(last)
    pair = per_head(fold(adj * state), e_ref)
    at_last = at_last + through * jnp.sum(pair, axis=0, keepdims=True)
    upper = jnp.where(lower_mask(), 1.0, 0.0).astype(BF16).T
    d_log = tri_sum(upper, d_cum) + at_last
    rate = jnp.exp(head[1:2, :])
    raw = bc[:, 2 * N : 3 * N]
    valid = lane < heads
    d_raw = (direct - d_log * rate) * sigmoid(raw + head[0:1, :])
    d_raw = jnp.where(valid, d_raw, 0.0)
    raw_grad[...] = d_raw.T[:16, :].astype(BF16)
    head_grad[0:8, :] += fold(d_raw)
    head_grad[8:16, :] += fold(jnp.where(valid, -d_log * delta * rate, 0.0))

    d_act = [d_xs[:, sl] for sl in tiles(width)] + [d_b, d_c]
    for q in range(total_width // LANE):
        sl = slice(q * LANE, (q + 1) * LANE)
        if q < width // LANE:
            ext_ref, taps, part = ext_v, chan[:, sl], sl
        else:
            part = slice(sl.start - width, sl.stop - width)
            ext_ref, taps = ext_b, bcpar[:, part]
        dt = d_act[q] * slope[:, sl]
        d_tot[0:L, sl] = dt
        bias_grad[:, sl] += fold(dt)
        for k in range(KERNEL):
            moved = ext_ref[pl.ds(8 - KERNEL + 1 + k, L), part]
            if k < KERNEL - 1:
                moved = moved * info[:, k : k + 1]
            taps_grad[8 * k : 8 * k + 8, sl] += fold(dt * moved)
        total = dt * taps[KERNEL - 1 : KERNEL, :]
        for s in range(1, KERNEL):
            total = total + taps[KERNEL - 1 - s : KERNEL - s, :] * (
                d_tot[pl.ds(s, L), sl] * info[:, 7 + s : 8 + s]
            )
        if q < width // LANE:
            grad_v[:, sl] = total.astype(BF16)
        else:
            grad_b[:, part] = total

        @pl.when(i == 0)
        def _():
            tail_rows[:, sl] = total[L - 8 :, :]

    @pl.when(last_step)
    def _():
        head_rows[...] = d_tot[0:8, :]


GROUP = 4 * L
END = 32


def remote(src, dst, send, recv, target):
    return pltpu.make_async_remote_copy(
        src_ref=src, dst_ref=dst, send_sem=send, recv_sem=recv, device_id=target,
        device_id_type=pl.DeviceIdType.MESH,
    )


def greet(targets):
    barrier = pltpu.get_barrier_semaphore()
    for target in targets:
        pl.semaphore_signal(
            barrier, inc=1, device_id=target, device_id_type=pl.DeviceIdType.MESH
        )
    return barrier


def count_rows(parts, z, gain, at, gain_grad):
    rows = jnp.zeros((parts[0].shape[0], LANE), F32)
    size = parts[0].shape[1]
    for part, k in zip(parts, at):
        lanes = pl.ds(pl.multiple_of(k * size, size), size)
        part = part * z(lanes)
        gain_grad[:, lanes] += fold(part)
        part = part * gain[0:1, lanes]
        for sl in tiles(size):
            rows = rows + part[:, sl]
    return rows


def row_dots(rows):
    ones = jnp.ones((8, LANE), BF16)
    hi, lo = two(rows)
    return dot(ones, hi, 1, 1) + dot(ones, lo, 1, 1)


def grand_kernel(heads, n, *refs):
    behind, refs = refs[:22], refs[22:]
    gate_grad, w_ref, tok, inv, gain, edge_mask, out_next = refs[:7]
    refs = refs[7:]
    in_line = n == 4
    if in_line:
        z_out, z_mid, z_mine = refs[:3]
        refs = refs[3:]
    outs, refs = refs[:9], refs[9:]
    ng_own, row_sums, gain_grad, out_last = refs[:4]
    refs = refs[4:]
    if in_line:
        z_sum, refs = refs[0], refs[1:]
    scratch, refs = refs[:4], refs[4:]
    gx, mid, send, got, nxt, last, edge, s1, r1, s2, r2, edge_s, edge_r, o_s, o_r = refs[:15]
    if in_line:
        z_got, z_on, z_last, z_s, z_r = refs[15:]
    chan, bcpar = behind[18], behind[19]
    grad_v, tail_rows = outs[0], outs[3]
    d_tot = scratch[3]
    i, n_steps = pl.program_id(0), pl.num_programs(0)
    s, c, t = lax.axis_index("shard"), lax.axis_index("context"), lax.axis_index("tensor")
    near = peers(t)
    to = [(s, c, near[0]), (s, c, near[1])]
    width = grad_v.shape[1]
    size = w_ref.shape[0] // 4
    half = GROUP // 2
    inside = mid.shape[0]

    @pl.when(i == 0)
    def _():
        pl.semaphore_wait(greet(to + beside_of(n)), 4)
        gain_grad[...] = jnp.zeros_like(gain_grad)

    def out_hop(side):
        return remote(
            out_next.at[side], out_last.at[side], o_s.at[side], o_r.at[side], to[1 - side]
        )

    @pl.when(i == 0)
    def _():
        for side in (0, 1):
            out_hop(side).start()

    if in_line:
        line = [(s, c + 1 - 2 * lax.rem(c, 2), t), (s, 3 - c, t)]
        block = z_mid.shape[1]

        def z_first(k):
            return remote(z_out.at[k], z_got.at[k], z_s.at[k], z_r.at[k], line[k])

        def z_second(k):
            return remote(z_on.at[k], z_last.at[k], z_s.at[2 + k], z_r.at[2 + k], line[1 - k])

        @pl.when(i == 0)
        def _():
            for k in (0, 1):
                z_first(k).start()

        @pl.when(i == n_steps // 2)
        def _():
            for k in (0, 1):
                z_first(k).wait()
                z_on[k] = (z_mid[k] + z_got[k, block:, :].astype(F32)).astype(BF16)
                z_second(k).start()
                z_sum[k] = z_mine[k] + z_got[k, :block, :].astype(F32)

        @pl.when(i == n_steps - 1)
        def _():
            for k in (0, 1):
                z_second(k).wait()
                z_sum[k] += z_last[k].astype(F32)

    behind_chunk(heads, *behind, *outs, *scratch)

    def first_hop(k, side):
        rows = pl.ds(side * half, half)
        return remote(
            send.at[k, rows, :], got.at[k, rows, :], s1.at[k, side], r1.at[k, side], to[side]
        )

    def second_hop(k, side):
        rows = pl.ds(side * half, half)
        return remote(
            nxt.at[k, rows, :], last.at[k, rows, :], s2.at[k, side], r2.at[k, side], to[1 - side]
        )

    def place(k, side):
        return pl.ds(pl.multiple_of((inside - 1 - k) * GROUP + side * half, half), half)

    turn = lax.rem(i, 4)
    at = pl.ds(pl.multiple_of((3 - turn) * L, L), L)
    gx[at, :width] = gate_grad[...]
    gx[at, width:] = grad_v[...]

    @pl.when(jnp.logical_and(turn == 2, i >= 6))
    def _():
        k = (i - 6) // 4
        for side in (0, 1):
            rows = slice(side * half, (side + 1) * half)
            first_hop(k, side).wait()
            nxt[k, rows, :] = (mid[k, rows, :] + got[k, rows, size:].astype(F32)).astype(BF16)
            second_hop(k, side).start()
            ng_own[place(k, side), :] += got[k, rows, :size].astype(F32)

    @pl.when(jnp.logical_and(turn == 3, i < 4 * inside))
    def _():
        k = (i - 3) // 4
        counted = jnp.where(k == 0, GROUP - END, GROUP)
        for side in (0, 1):
            rows = slice(side * half, (side + 1) * half)
            x = gx[rows, :]
            keep, go = shares_of(side, t)
            gone = dot(x, pick(w_ref, *go), 1, 1)
            send[k, rows, :] = gone.astype(BF16)
            first_hop(k, side).start()
            kept = dot(x, pick(w_ref, *keep), 1, 1)
            ng_own[place(k, side), :] = kept[:, :size]
            mid[k, rows, :] = kept[:, size:]
            row = lax.broadcasted_iota(jnp.int32, (half, 1), 0) + side * half
            scale = jnp.where(row < counted, inv[rows, :], 0.0)
            parts = [kept[:, :size], kept[:, size:], gone[:, :size], gone[:, size:]]
            sums = count_rows(
                parts, lambda lanes: tok[rows, lanes].astype(F32) * scale, gain, keep + go, gain_grad
            )
            row_sums[0, :, rows] = row_dots(sums)

    @pl.when(i == n_steps - 1)
    def _():
        before = (s, jnp.maximum(c - 1, 0), t)
        copy = remote(d_tot.at[pl.ds(0, 8), :], edge, edge_s, edge_r, before)

        @pl.when(c > 0)
        def _():
            copy.start()

        for k in range(inside):
            for side in (0, 1):
                second_hop(k, side).wait()
                rows = slice(side * half, (side + 1) * half)
                ng_own[place(k, side), :] += last[k, rows, :].astype(F32)
        for side in (0, 1):
            out_hop(side).wait()

        @pl.when(c < n - 1)
        def _():
            copy.wait_recv()
            for shift in range(1, KERNEL):
                moved = pltpu.roll(edge[...], 8 - shift, 0) * edge_mask[
                    8 * shift - 8 : 8 * shift, 0:1
                ]
                tap = slice(KERNEL - 1 - shift, KERNEL - shift)
                tail_rows[:, :width] += chan[tap, :] * moved[:, :width]
                tail_rows[:, width:] += bcpar[tap, :] * moved[:, width:]

        @pl.when(c > 0)
        def _():
            copy.wait_send()


def run_grand(
    projected, cols, halo_v, halo_b, info, marks, delta, cum, ssd, mixed_grad, sloc, pfx, entry,
    aloc, sfx, later, chan, bcpar, head, expand, heads, gate_grad, weight, tok, inv, gain, edge_mask,
    out_next, z_arrays,
):
    steps, width = ssd.shape
    count = steps // L
    groups = steps // GROUP
    inside = groups - 1
    size = D // 4
    once = lambda *dims: pl.BlockSpec(
        dims, lambda i: (0,) * len(dims), pipeline_mode=pl.Buffered(1)
    )
    turn = lambda spec: pl.BlockSpec(
        spec.block_shape, lambda i, m=spec.index_map: m(count - 1 - i)
    )
    in_group = lambda w: pl.BlockSpec((GROUP, w), lambda i: ((count - 1 - i) // 4, 0))
    chunk = pl.BlockSpec((1, N, width), lambda i: (i, 0, 0))
    few = pl.BlockSpec((1, 8, width), lambda i: (i, 0, 0))
    total = width + 2 * N
    dma = pltpu.SemaphoreType.DMA
    return pl.pallas_call(
        functools.partial(grand_kernel, heads, lax.axis_size("context")),
        grid=(count,),
        in_specs=[
            turn(row_block(width, 1)), turn(prev_block(width, 1)),
            turn(row_block(3 * N)), turn(prev_block(3 * N)),
            once(8, width), once(8, 3 * N), turn(row_block(LANE)),
            turn(pl.BlockSpec((1, 8, L), lambda i: (i, 0, 0))),
            turn(row_block(LANE)), turn(row_block(LANE)), turn(row_block(width)), turn(row_block(width)),
            turn(chunk), turn(few), once(N, width), turn(chunk), turn(few), once(N, width),
            once(8, width), once(8, 2 * N), once(8, LANE), once(2 * LANE, width),
            turn(row_block(width)), once(*weight.shape), in_group(D), in_group(1), once(8, D),
            once(24, LANE), pl.BlockSpec(memory_space=pl.ANY),
        ]
        + ([pl.BlockSpec(memory_space=pl.ANY)] + [once(*z.shape) for z in z_arrays[1:]] if z_arrays else []),
        out_specs=[
            turn(row_block(width)), turn(row_block(2 * N)),
            pl.BlockSpec((16, L), lambda i: (0, count - 1 - i)),
            whole(8, total), whole(8, total), whole(8 * KERNEL, total), whole(8, total),
            whole(8, width), whole(16, LANE),
            once(inside * GROUP, size),
            pl.BlockSpec((1, 8, GROUP), lambda i: ((count - 1 - i) // 4, 0, 0)),
            whole(8, D), pl.BlockSpec(memory_space=pl.ANY),
        ]
        + [once(*z.shape) for z in z_arrays[1:2]],
        out_shape=[
            shape(steps, width, dtype=BF16), shape(steps, 2 * N), shape(16, steps, dtype=BF16),
            shape(8, total), shape(8, total), shape(8 * KERNEL, total), shape(8, total),
            shape(8, width), shape(16, LANE),
            shape(inside * GROUP, size), shape(groups, 8, GROUP), shape(8, D),
            shape(*out_next.shape, dtype=BF16),
        ]
        + [shape(*z.shape) for z in z_arrays[1:2]],
        scratch_shapes=[
            pltpu.VMEM((8 + L, width), F32), pltpu.VMEM((8 + L, 3 * N), F32),
            pltpu.VMEM((L, total), F32), pltpu.VMEM((L + 8, total), F32),
            pltpu.VMEM((GROUP, 2 * width), BF16), pltpu.VMEM((inside, GROUP, size), F32),
            pltpu.VMEM((inside, GROUP, 2 * size), BF16), pltpu.VMEM((inside, GROUP, 2 * size), BF16),
            pltpu.VMEM((inside, GROUP, size), BF16), pltpu.VMEM((inside, GROUP, size), BF16),
            pltpu.VMEM((8, total), F32),
            dma((inside, 2)), dma((inside, 2)), dma((inside, 2)), dma((inside, 2)), dma, dma,
            dma((2,)), dma((2,)),
        ]
        + (
            [
                pltpu.VMEM(z_arrays[0].shape, BF16), pltpu.VMEM(z_arrays[1].shape, BF16),
                pltpu.VMEM(z_arrays[1].shape, BF16), dma((4,)), dma((4,)),
            ]
            if z_arrays
            else []
        ),
        compiler_params=pltpu.CompilerParams(
            dimension_semantics=("arbitrary",), vmem_limit_bytes=56 * 1024 * 1024,
            collective_id=4, has_side_effects=True,
        ),
        cost_estimate=estimate(90),
        name="behind",
    )(
        projected, projected, cols, cols, halo_v, halo_b, info, marks, delta, cum, ssd, mixed_grad,
        sloc, pfx, entry, aloc, sfx, later, chan, bcpar, head, expand,
        gate_grad, weight, tok, inv, gain, edge_mask, out_next, *z_arrays,
    )


def docs_kernel(n_bounds, scalars, info_ref, marks_ref):
    begin = scalars[n_bounds] + pl.program_id(0) * L
    limit = scalars[n_bounds + 1]

    def doc_of(position):
        found = jnp.zeros(position.shape, F32)
        for k in range(n_bounds):
            found = found + jnp.where(position >= scalars[k], 1.0, 0.0)
        return jnp.where(position < 0, -1.0, found)

    row = lax.broadcasted_iota(jnp.int32, (L, LANE), 0)
    lane = lax.broadcasted_iota(jnp.int32, (L, LANE), 1)
    offset = jnp.where(lane < KERNEL - 1, lane - KERNEL + 1, jnp.where(lane >= 8, lane - 7, 0))
    other = jnp.where(lane == 3, -1, jnp.where(lane == 4, L - 1, row + offset)) + begin
    mark = doc_of(row + begin)
    same = jnp.logical_and(doc_of(other) == mark, other < limit)
    info = jnp.where(same, 1.0, 0.0)
    info_ref[...] = jnp.where(lane == 5, mark, jnp.where(lane < 7 + KERNEL, info, 0.0))
    marks_ref[0] = doc_of(begin + lax.broadcasted_iota(jnp.int32, (8, L), 1))


def run_docs(bounds, start, steps):
    count = steps // L
    scalars = jnp.concatenate([bounds, jnp.stack([start, start + steps])]).astype(jnp.int32)
    return pl.pallas_call(
        functools.partial(docs_kernel, bounds.shape[0]),
        grid_spec=pltpu.PrefetchScalarGridSpec(
            num_scalar_prefetch=1,
            grid=(count,),
            out_specs=[
                pl.BlockSpec((L, LANE), lambda i, s: (i, 0)),
                pl.BlockSpec((1, 8, L), lambda i, s: (i, 0, 0)),
            ],
        ),
        out_shape=[shape(steps, LANE), shape(count, 8, L)],
        compiler_params=params(),
        cost_estimate=estimate(4),
        name="documents",
    )(scalars)


def peers(t):
    return t + 1 - 2 * lax.rem(t, 2), lax.rem(t + 2, 4)


def pick(w_ref, one, other):
    size = w_ref.shape[0] // 4
    at = lambda k: pl.ds(pl.multiple_of(k * size, size), size)
    return jnp.concatenate([w_ref[at(one), :], w_ref[at(other), :]], axis=0)


def shares_of(side, t):
    near = peers(t)
    return (t, near[1 - side]), (near[side], 3 - t)


def out_kernel(
    ssd, gate, sums, chan, w_ref, scaled, own, mid, send_a, send_b,
):
    i, half = pl.program_id(0), pl.num_programs(0) // 2
    t = lax.axis_index("tensor")
    width = ssd.shape[1]
    for k in range(ssd.shape[0] // L):
        rows = slice(k * L, (k + 1) * L)
        inv = jnp.broadcast_to(lax.rsqrt(sums[k, 0:1, :] / INNER + EPS), (LANE, L)).T
        for sl in tiles(width):
            g = gate[rows, sl]
            gated = ssd[rows, sl] * g * sigmoid(g)
            scaled[rows, sl] = (gated * inv * chan[KERNEL + 1 : KERNEL + 2, sl]).astype(BF16)
    x = scaled[...]
    size = own.shape[1]

    def part(side, send):
        keep, go = shares_of(side, t)
        send[...] = dot(x, pick(w_ref, *go), 1, 1).astype(BF16)
        kept = dot(x, pick(w_ref, *keep), 1, 1)
        own[...] = kept[:, :size]
        mid[...] = kept[:, size:]

    @pl.when(i < half)
    def _():
        part(0, send_a)

    @pl.when(i >= half)
    def _():
        part(1, send_b)


def run_out(ssd, projected, sums, chan, weight):
    steps, width = ssd.shape
    block = 512
    count = steps // block
    half = count // 2
    size = D // 4
    in_block = lambda w, col=0: pl.BlockSpec((block, w), lambda i: (i, col))
    return pl.pallas_call(
        out_kernel,
        grid=(count,),
        in_specs=[
            in_block(width), in_block(width, 0),
            pl.BlockSpec((block // L, 8, L), lambda i: (i, 0, 0)),
            whole(8, width), whole(*weight.shape),
        ],
        out_specs=[
            in_block(width), in_block(size), in_block(size),
            pl.BlockSpec((block, 2 * size), lambda i: (jnp.minimum(i, half - 1), 0)),
            pl.BlockSpec((block, 2 * size), lambda i: (jnp.maximum(i - half, 0), 0)),
        ],
        out_shape=[
            shape(steps, width, dtype=BF16), shape(steps, size), shape(steps, size),
            shape(steps // 2, 2 * size, dtype=BF16), shape(steps // 2, 2 * size, dtype=BF16),
        ],
        compiler_params=params(),
        cost_estimate=estimate(12),
        name="out",
    )(ssd, projected, sums, chan, weight)


def line_kernel(
    n, n_tensor, piece, zx_ref, cols_ref, zx_out, cols_out,
    local, zx_s, zx_r, core_s, core_r, col_s, col_r, group_s, group_r, bulk_s, bulk_r,
):
    s, c, t = lax.axis_index("shard"), lax.axis_index("context"), lax.axis_index("tensor")
    on = (c < n - 1, c > 0)
    to = ((s, jnp.minimum(c + 1, n - 1), t), (s, jnp.maximum(c - 1, 0), t))
    to_core = (1 - s, c, t)
    to_group = [(s, c, lax.rem(t + k, n_tensor)) for k in range(1, n_tensor)]
    beside = [(s, lax.rem(c + k, n), t) for k in (1, n - 1)]
    pl.semaphore_wait(greet([to_core] + to_group + beside), n_tensor + 2)
    rows, width = zx_ref.shape[0], cols_ref.shape[1]
    spans = [(at, min(piece, rows - at)) for at in range(0, rows, piece)]

    def block_of(way, hop):
        return jnp.maximum(c - hop, 0) if way == 0 else jnp.minimum(c + hop, n - 1)

    def has(way, hop):
        return c - hop >= 0 if way == 0 else c + hop <= n - 1

    def place(ref, block, at=0, size=rows):
        return ref.at[pl.ds(pl.multiple_of((s * n + block) * rows + at, 16), size), :]

    lanes = pl.ds(pl.multiple_of(t * width, LANE), width)

    def place_cols(block):
        return cols_out.at[pl.ds(pl.multiple_of((s * n + block) * rows, 16), rows), lanes]

    def zx_copy(way, step, p):
        at, size = spans[p]
        where = place(zx_out, block_of(way, step), at, size)
        src = zx_ref.at[pl.ds(at, size), :] if step == 0 else where
        return remote(src, where, zx_s.at[way, step, p], zx_r.at[way, step, p], to[way])

    def col_copy(way, step):
        where = place_cols(block_of(way, step))
        src = cols_ref if step == 0 else where
        return remote(src, where, col_s.at[way, step], col_r.at[way, step], to[way])

    def group_copies(way, hop):
        where = place_cols(block_of(way, hop))
        src = cols_ref if hop == 0 else where
        return [
            remote(src, where, group_s.at[k, way, hop], group_r.at[k, way, hop], target)
            for k, target in enumerate(to_group)
        ]

    def core_copy(way, hop, p):
        at, size = spans[p]
        where = place(zx_out, block_of(way, hop), at, size)
        src = zx_ref.at[pl.ds(at, size), :] if hop == 0 else where
        return remote(src, where, core_s.at[way, hop, p], core_r.at[way, hop, p], to_core)

    pieces = range(len(spans))
    for way in (0, 1):

        @pl.when(on[way])
        def _():
            col_copy(way, 0).start()
            for p in pieces:
                zx_copy(way, 0, p).start()

    for copy in group_copies(0, 0):
        copy.start()
    own_cols = pltpu.make_async_copy(cols_ref, place_cols(c), local.at[0])
    own_zx = pltpu.make_async_copy(zx_ref, place(zx_out, c), local.at[1])
    own_cols.start()
    own_zx.start()
    for p in pieces:
        core_copy(0, 0, p).start()
    start = pl.ds(pl.multiple_of(s * n * rows, 16), n * rows)
    bulk = remote(cols_out.at[start, :], cols_out.at[start, :], bulk_s, bulk_r, to_core)
    for step in range(n - 1):
        further = step < n - 2
        for way in (0, 1):

            @pl.when(has(way, step + 1))
            def _():
                col_copy(way, step).wait_recv()
                for copy in group_copies(way, step + 1):
                    copy.start()
                if further:

                    @pl.when(on[way])
                    def _():
                        col_copy(way, step + 1).start()

        if not further:
            own_cols.wait()
            for copy in group_copies(0, 0):
                copy.wait()
            for hop in range(1, n):
                for way in (0, 1):

                    @pl.when(has(way, hop))
                    def _():
                        for copy in group_copies(way, hop):
                            copy.wait()

            bulk.start()
        for p in pieces:
            for way in (0, 1):

                @pl.when(has(way, step + 1))
                def _():
                    zx_copy(way, step, p).wait_recv()
                    core_copy(way, step + 1, p).start()
                    if further:

                        @pl.when(on[way])
                        def _():
                            zx_copy(way, step + 1, p).start()

    for step in range(n - 1):
        for way in (0, 1):

            @pl.when(jnp.logical_and(on[way], has(way, step)))
            def _():
                col_copy(way, step).wait_send()
                for p in pieces:
                    zx_copy(way, step, p).wait_send()

            @pl.when(has(way, step + 1))
            def _():
                for p in pieces:
                    core_copy(way, step + 1, p).wait()

    for p in pieces:
        core_copy(0, 0, p).wait()
    bulk.wait()
    own_zx.wait()


PIECE = 64


def line_gather(zx, cols):
    n, n_tensor = lax.axis_size("context"), lax.axis_size("tensor")
    rows = zx.shape[0]
    pieces = -(-rows // PIECE)
    dma = pltpu.SemaphoreType.DMA
    return pl.pallas_call(
        functools.partial(line_kernel, n, n_tensor, PIECE),
        in_specs=[pl.BlockSpec(memory_space=pl.ANY)] * 2,
        out_specs=[pl.BlockSpec(memory_space=pl.ANY)] * 2,
        out_shape=[
            shape(2 * n * rows, zx.shape[1], dtype=BF16),
            shape(2 * n * rows, n_tensor * cols.shape[1], dtype=BF16),
        ],
        scratch_shapes=[
            dma((2,)), dma((2, n - 1, pieces)), dma((2, n - 1, pieces)),
            dma((2, n, pieces)), dma((2, n, pieces)), dma((2, n - 1)), dma((2, n - 1)),
            dma((n_tensor - 1, 2, n)), dma((n_tensor - 1, 2, n)), dma, dma,
        ],
        compiler_params=pltpu.CompilerParams(collective_id=0, has_side_effects=True),
        name="line_gather",
    )(zx, cols)


def small_sum_kernel(n, x_ref, o_ref, held, send, recv):
    s, c, t = lax.axis_index("shard"), lax.axis_index("context"), lax.axis_index("tensor")
    targets = [(s, c, lax.rem(t + k, n)) for k in range(1, n)]
    pl.semaphore_wait(greet(targets), n - 1)
    copies = [
        remote(x_ref, held.at[k], send.at[k], recv.at[k], target)
        for k, target in enumerate(targets)
    ]
    for copy in copies:
        copy.start()
    total = x_ref[...]
    for k, copy in enumerate(copies):
        copy.wait()
        total = total + held[k]
    o_ref[...] = total


def small_sum(x, collective_id):
    n = lax.axis_size("tensor")
    return pl.pallas_call(
        functools.partial(small_sum_kernel, n),
        in_specs=[pl.BlockSpec(memory_space=pltpu.VMEM)],
        out_specs=pl.BlockSpec(memory_space=pltpu.VMEM),
        out_shape=shape(*x.shape),
        scratch_shapes=[
            pltpu.VMEM((n - 1, *x.shape), F32),
            pltpu.SemaphoreType.DMA((n - 1,)), pltpu.SemaphoreType.DMA((n - 1,)),
        ],
        compiler_params=pltpu.CompilerParams(collective_id=collective_id, has_side_effects=True),
        cost_estimate=estimate(7),
        name="small_sum",
    )(x)


SLICES = 8


class Chain:
    def __init__(self, n, backward, packed, entering, got, sent, send_sem, recv_sem):
        s, c, t = lax.axis_index("shard"), lax.axis_index("context"), lax.axis_index("tensor")
        self.from_other = c < n - 1 if backward else c > 0
        self.to_other = c > 0 if backward else c < n - 1
        ahead = jnp.maximum(c - 1, 0) if backward else jnp.minimum(c + 1, n - 1)
        self.target = (s, ahead, t)
        self.refs = packed, entering, got, sent, send_sem, recv_sem

    def copy(self, j):
        _, _, got, sent, send_sem, recv_sem = self.refs
        rows = pl.ds(j * (N // SLICES), N // SLICES)
        return remote(sent.at[rows, :], got.at[rows, :], send_sem.at[j], recv_sem.at[j], self.target)

    def step(self, j):
        packed, entering, got, sent, _, _ = self.refs
        rows = slice(j * (N // SLICES), (j + 1) * (N // SLICES))

        @pl.when(self.from_other)
        def _():
            self.copy(j).wait_recv()
            entering[rows, :] = got[rows, :]

        @pl.when(jnp.logical_not(self.from_other))
        def _():
            entering[rows, :] = jnp.zeros((N // SLICES, packed.shape[1]), F32)

        @pl.when(self.to_other)
        def _():
            sent[rows, :] = packed[rows, :] + packed[N : N + 1, :] * entering[rows, :]
            self.copy(j).start()

    def finish(self):
        @pl.when(self.to_other)
        def _():
            for j in range(SLICES):
                self.copy(j).wait_send()


def beside_of(n):
    s, c, t = lax.axis_index("shard"), lax.axis_index("context"), lax.axis_index("tensor")
    return [(s, lax.rem(c + k, n), t) for k in (1, n - 1)]


def entry_kernel(
    n, packed, back, w_hbm, entry, out, bk, w_ref, buf, got, sent, load_sem, out_sem, chain_s, chain_r
):
    block = buf.shape[1]
    count = back.shape[0] // block
    load_w = pltpu.make_async_copy(w_hbm, w_ref, load_sem.at[count])
    load_w.start()

    def load(k):
        rows = pl.ds(k * block, block)
        return pltpu.make_async_copy(back.at[rows, :], bk.at[rows, :], load_sem.at[k])

    def store(k):
        return pltpu.make_async_copy(
            buf.at[k % 2], out.at[pl.ds(k * block, block), :], out_sem.at[k % 2]
        )

    for k in range(count):
        load(k).start()
    pl.semaphore_wait(greet(beside_of(n)), 2)
    chain = Chain(n, False, packed, entry, got, sent, chain_s, chain_r)
    load_w.wait()
    for k in range(count):
        load(k).wait()
        if k >= 2:
            store(k - 2).wait()
        buf[k % 2] = dot(bk[k * block : (k + 1) * block, :], w_ref[...])
        store(k).start()
        if k < SLICES:
            chain.step(k)
    for k in range(count, SLICES):
        chain.step(k)
    chain.finish()
    for k in range(max(count - 2, 0), count):
        store(k).wait()


def run_entry(packed, back, weight):
    n = lax.axis_size("context")
    steps, width = back.shape[0], weight.shape[1]
    block = 256
    dma = pltpu.SemaphoreType.DMA
    vmem = pltpu.VMEM
    inside = pl.BlockSpec(memory_space=pltpu.VMEM)
    hbm = pl.BlockSpec(memory_space=pl.ANY)
    return pl.pallas_call(
        functools.partial(entry_kernel, n),
        in_specs=[inside, hbm, hbm],
        out_specs=[inside, hbm],
        out_shape=[shape(N, width), shape(steps, width)],
        scratch_shapes=[
            vmem(back.shape, BF16), vmem(weight.shape, BF16), vmem((2, block, width), F32),
            vmem((N, width), F32), vmem((N, width), F32),
            dma((steps // block + 1,)), dma((2,)), dma((SLICES,)), dma((SLICES,)),
        ],
        compiler_params=pltpu.CompilerParams(
            vmem_limit_bytes=40 * 1024 * 1024, collective_id=6, has_side_effects=True
        ),
        cost_estimate=estimate(15),
        name="entry",
    )(packed, back, weight)


def middle_kernel(
    n, packed, send_a, send_b, mid_hbm, own_hbm, normed_hbm, gate_hbm, back_hbm, scaled_hbm, *refs
):
    if n == 4:
        later, own, next_out, z_out, z_mid, z_mine = refs[:6]
        refs = refs[6:]
    else:
        later, own, next_out, both_out = refs[:4]
        refs = refs[4:]
    (
        mid, nm, gg, bk, sc, peer_part, core_part, own_part, got, chain_got, chain_sent,
        local, core_s, core_r, f_s, f_r, chain_s, chain_r,
    ) = refs
    s, c, t = lax.axis_index("shard"), lax.axis_index("context"), lax.axis_index("tensor")
    near = peers(t)
    to = [(s, c, near[0]), (s, c, near[1])]
    to_core = (1 - s, c, t)
    loads = [
        pltpu.make_async_copy(src, dst, local.at[k])
        for k, (src, dst) in enumerate(
            [
                (normed_hbm, nm), (gate_hbm, gg), (back_hbm, bk), (scaled_hbm, sc),
                (mid_hbm, mid), (own_hbm, own),
            ]
        )
    ]
    for load in loads:
        load.start()
    pl.semaphore_wait(greet(to + [to_core] + beside_of(n)), 5)
    hops = [
        remote(src, got.at[side], f_s.at[side], f_r.at[side], to[side])
        for side, src in enumerate((send_a, send_b))
    ]
    for hop in hops:
        hop.start()
    chain = Chain(n, True, packed, later, chain_got, chain_sent, chain_s, chain_r)
    half_d = nm.shape[1] // 2
    steps = nm.shape[0]
    step = 256
    pairs = ((nm, gg), (bk, sc))

    def product(which, shard, into, m):
        left, right = pairs[which]
        lanes = pl.ds(pl.multiple_of(shard * half_d + m * step, step), step)
        acc = None
        for k in range(steps // GROUP):
            rows = slice(k * GROUP, (k + 1) * GROUP)
            part = dot(left[rows, lanes], right[rows, :], 0, 0)
            acc = part if acc is None else acc + part
        into[which, m * step : (m + 1) * step, :] = acc

    cores = [
        remote(peer_part.at[k], core_part.at[k], core_s.at[k], core_r.at[k], to_core) for k in (0, 1)
    ]
    chain.step(0)
    done = 1
    for which in (0, 1):
        loads[2 * which].wait()
        loads[2 * which + 1].wait()
        for m in range(half_d // step):
            product(which, 1 - s, peer_part, m)
            if done < SLICES:
                chain.step(done)
                done += 1
        cores[which].start()
    for which in (0, 1):
        for m in range(half_d // step):
            product(which, s, own_part, m)
            if done < SLICES:
                chain.step(done)
                done += 1
    chain.finish()
    block = half_d // n

    for which in (0, 1):
        cores[which].wait()
        if n == 4:
            first = c + 1 - 2 * lax.rem(c, 2) if which == 0 else 3 - c
            third = 3 - c if which == 0 else c + 1 - 2 * lax.rem(c, 2)

            def total(k):
                rows = pl.ds(pl.multiple_of(k * block, 8), block)
                return own_part[which, rows, :] + core_part[which, rows, :]

            z_out[which, :block, :] = total(first).astype(BF16)
            z_out[which, block:, :] = total(lax.rem(c + 2, 4)).astype(BF16)
            z_mid[which] = total(third)
            z_mine[which] = total(c)
        else:
            both_out[which] = own_part[which] + core_part[which]
    loads[4].wait()
    loads[5].wait()
    size = mid.shape[1]
    half = steps // 2
    for side in (0, 1):
        hops[side].wait()
        for k in range(half // step):
            rows = slice(k * step, (k + 1) * step)
            at = slice(side * half + k * step, side * half + (k + 1) * step)
            next_out[side, rows, :] = (mid[at, :] + got[side, rows, size:].astype(F32)).astype(BF16)
            own[at, :] += got[side, rows, :size].astype(F32)


def run_middle(packed, fan, normed, gate_grad, back, scaled):
    n = lax.axis_size("context")
    own, mid, send_a, send_b = fan
    steps, width = gate_grad.shape
    size = own.shape[1]
    half_d = D // 2
    block = half_d // n
    dma = pltpu.SemaphoreType.DMA
    vmem = pltpu.VMEM
    inside = pl.BlockSpec(memory_space=pltpu.VMEM)
    hbm = pl.BlockSpec(memory_space=pl.ANY)
    if n == 4:
        more = [
            shape(2, 2 * block, width, dtype=BF16), shape(2, block, width), shape(2, block, width)
        ]
    else:
        more = [shape(2, half_d, width)]
    pair = (2, half_d, width)
    return pl.pallas_call(
        functools.partial(middle_kernel, n),
        in_specs=[inside] + [hbm] * 8,
        out_specs=[inside] * (3 + len(more)),
        out_shape=[shape(N, width), shape(steps, size), shape(2, steps // 2, size, dtype=BF16)] + more,
        scratch_shapes=[
            vmem((steps, size), F32), vmem(normed.shape, BF16), vmem(gate_grad.shape, BF16),
            vmem(back.shape, BF16), vmem(scaled.shape, BF16),
            vmem(pair, F32), vmem(pair, F32), vmem(pair, F32), vmem((2, steps // 2, 2 * size), BF16),
            vmem((N, width), F32), vmem((N, width), F32),
            dma((6,)), dma((2,)), dma((2,)), dma((2,)), dma((2,)), dma((SLICES,)), dma((SLICES,)),
        ],
        compiler_params=pltpu.CompilerParams(
            vmem_limit_bytes=58 * 1024 * 1024, collective_id=7, has_side_effects=True
        ),
        cost_estimate=estimate(35),
        name="middle",
    )(packed, send_a, send_b, mid, own, normed, gate_grad, back, scaled)


def adam_kernel(gate_g, value_g, down_g, zx_w, zx_m, zx_v, out_w, out_m, out_v, *outs):
    zx, out = outs[:3], outs[3:]
    for k, grad in enumerate((gate_g, value_g)):
        new = adamw(
            zx_w[:, k, :], grad[...], zx_m[:, k, :], zx_v[:, k, :], RATE_MATRIX, DECAY
        )
        for ref, val in zip(zx, new):
            ref[:, k, :] = val
    new = adamw(out_w[...], down_g[...].T, out_m[...], out_v[...], RATE_MATRIX, DECAY)
    for ref, val in zip(out, new):
        ref[...] = val


def run_adam(gate_g, value_g, down_g, zx, out):
    return pl.pallas_call(
        adam_kernel,
        in_specs=[pl.BlockSpec(memory_space=pltpu.VMEM)] * 9,
        out_specs=[pl.BlockSpec(memory_space=pltpu.VMEM)] * 6,
        out_shape=[shape(*zx[0].shape)] * 3 + [shape(*out[0].shape)] * 3,
        compiler_params=pltpu.CompilerParams(vmem_limit_bytes=40 * 1024 * 1024),
        cost_estimate=estimate(6),
        name="optimizer",
    )(gate_g, value_g, down_g, *zx, *out)


PACK = 16


def tail_kernel(
    n, grad_b, grad_v, normed_hbm, w_hbm, tok_hbm, back_hbm, late_hbm,
    raw_t, fixed, gate_top, gate_end, tok_top, tok_end, inv, gain, gain_mine, w_bc, w_raw, sel_bc, sel_raw,
    late_rows, late_gain, taps_grad, bias_grad, norm_gain_grad, skip_grad, head_grad,
    tokens_out, value_out, cols_out, pack_out,
    gb, gv, nm, w_ref, tok, back, late,
    peer_part, own_part, core_part, b_got, b_next, b_last, b_full, raw_full,
    early, mid, send, got, nxt, last, gain_grad, z_out, z_got, z_on, z_last,
    ng_cols, col_peer, col_own, col_core, col_out, col_got, col_on, col_last,
    row_buf, row_held, pack, pack_other, pack_pair, pack_pieces, pack_total, pack_all,
    local, raw_s, raw_r, b_s, b_r, f_s, f_r, core_s, core_r, z_s, z_r, row_s, row_r,
    sum_s, sum_r, piece_s, piece_r, group_s, group_r,
):
    s, c, t = lax.axis_index("shard"), lax.axis_index("context"), lax.axis_index("tensor")
    near = peers(t)
    to = [(s, c, near[0]), (s, c, near[1])]
    group = [(s, c, lax.rem(t + k, 4)) for k in (1, 2, 3)]
    to_core = (1 - s, c, t)
    to_piece = [(s, lax.rem(c + k, n), t) for k in range(1, n)]
    in_line = n == 4
    line = [(s, c + 1 - 2 * lax.rem(c, 2), t), (s, 3 - c, t)] if in_line else []
    steps, width = grad_v.shape
    size = w_ref.shape[0] // 4
    share = steps // 4
    mine_lanes = pl.ds(pl.multiple_of(t * size, size), size)
    loads = [
        pltpu.make_async_copy(src, dst, local.at[k])
        for k, (src, dst) in enumerate(
            [
                (grad_b, gb), (grad_v, gv), (normed_hbm, nm), (w_hbm, w_ref),
                (tok_hbm.at[:, mine_lanes], tok), (back_hbm.at[:, mine_lanes], back), (late_hbm, late),
            ]
        )
    ]
    for load in loads:
        load.start()
    pl.semaphore_wait(greet(group + [to_core] + to_piece), n + 3)

    raw_full[t] = raw_t[...]
    raws = [
        remote(raw_t, raw_full.at[t], raw_s.at[k], raw_r.at[k], target)
        for k, target in enumerate(group)
    ]
    for copy in raws:
        copy.start()

    def rows_of(k):
        return pl.ds(pl.multiple_of(k * share, share), share)

    def lanes_of(side):
        return pl.ds(side * N, N)

    loads[0].wait()
    gb[steps - 8 :, :] = fixed[:, width:]

    def b_first(side, part):
        k = near[side] if part == 0 else 3 - t
        return remote(
            gb.at[rows_of(k), lanes_of(side)], b_got.at[side, part], b_s.at[side, part],
            b_r.at[side, part], to[side],
        )

    def b_second(side):
        return remote(
            b_next.at[side], b_last.at[side], b_s.at[side, 2], b_r.at[side, 2], to[1 - side]
        )

    def b_back(side, part):
        k = near[1 - side] if part == 2 else t
        where = b_full.at[rows_of(k), lanes_of(side)]
        return remote(
            where, where, b_s.at[side, 3 + part], b_r.at[side, 3 + part],
            to[1 - side] if part == 0 else to[side],
        )

    for side in (0, 1):
        for part in (0, 1):
            b_first(side, part).start()

    loads[1].wait()
    tail = gv[steps - 16 :, :].astype(F32)
    gv[steps - 16 :, :] = jnp.concatenate([tail[:8], fixed[:, :width]], axis=0).astype(BF16)
    loads[2].wait()
    half_d = nm.shape[1] // 2
    step = 256

    def product(shard, right, into):
        for m in range(half_d // step):
            lanes = pl.ds(pl.multiple_of(shard * half_d + m * step, step), step)
            acc = None
            for k in range(steps // GROUP):
                rows = slice(k * GROUP, (k + 1) * GROUP)
                part = dot(nm[rows, lanes], right(rows), 0, 0)
                acc = part if acc is None else acc + part
            into[m * step : (m + 1) * step, :] = acc

    product(1 - s, lambda rows: gv[rows, :], peer_part)
    core = remote(peer_part, core_part, core_s.at[0], core_r.at[0], to_core)
    core.start()

    for side in (0, 1):
        for part in (0, 1):
            b_first(side, part).wait()
        b_next[side] = gb[rows_of(near[1 - side]), lanes_of(side)] + b_got[side, 1]
        b_second(side).start()

    product(s, lambda rows: gv[rows, :], own_part)

    for side in (0, 1):
        b_second(side).wait()
        mine = gb[rows_of(t), lanes_of(side)] + b_got[side, 0] + b_last[side]
        b_full[rows_of(t), lanes_of(side)] = mine.astype(BF16)
        b_back(side, 0).start()

    block = half_d // n
    side_w = width // 2
    both = own_part
    if in_line:
        first = [c + 1 - 2 * lax.rem(c, 2), 3 - c]
        across = lax.rem(c + 2, 4)

    def block_rows(k):
        return pl.ds(pl.multiple_of(k * block, 8), block)

    def z_block(k, side):
        return both[block_rows(k), side * side_w : (side + 1) * side_w]

    def z_first(side):
        return remote(z_out.at[side], z_got.at[side], z_s.at[side], z_r.at[side], line[side])

    def z_second(side):
        return remote(z_on.at[side], z_last.at[side], z_s.at[2 + side], z_r.at[2 + side], line[1 - side])

    def col_first():
        return remote(col_out, col_got, z_s.at[4], z_r.at[4], line[0])

    def col_second():
        return remote(col_on, col_last, z_s.at[5], z_r.at[5], line[1])

    core.wait()
    both[...] = both[...] + core_part[...]
    if in_line:
        for side in (0, 1):
            z_out[side, :block, :] = z_block(first[side], side).astype(BF16)
            z_out[side, block:, :] = z_block(across, side).astype(BF16)
            z_first(side).start()
    for side in (0, 1):
        b_back(side, 0).wait()
        for part in (1, 2):
            b_back(side, part).start()

    loads[3].wait()
    half = GROUP // 2
    tail_half = END // 2

    def f_first(side):
        return remote(send.at[side], got.at[side], f_s.at[side], f_r.at[side], to[side])

    def f_second(side):
        return remote(
            nxt.at[side], last.at[side], f_s.at[2 + side], f_r.at[2 + side], to[1 - side]
        )

    gain_grad[...] = late_gain[...]
    for g in range(1, steps // GROUP):
        row_buf[:, g * GROUP : (g + 1) * GROUP] = late_rows[g]
    ends = [jnp.zeros((LANE - END, LANE), F32)]
    for side in (0, 1):
        rows = slice(side * half, (side + 1) * half)
        tail_rows = slice(side * tail_half, (side + 1) * tail_half)
        end_rows = slice(steps - END + side * tail_half, steps - END + (side + 1) * tail_half)
        x = jnp.concatenate(
            [
                jnp.concatenate([gate_top[rows, :], gv[rows, :]], axis=1),
                jnp.concatenate([gate_end[tail_rows, :], gv[end_rows, :]], axis=1),
            ],
            axis=0,
        )
        keep, go = shares_of(side, t)
        gone = dot(x, pick(w_ref, *go), 1, 1)
        send[side] = gone.astype(BF16)
        f_first(side).start()
        kept = dot(x, pick(w_ref, *keep), 1, 1)
        early[side] = kept[:, :size]
        mid[side] = kept[:, size:]
        scale = jnp.concatenate([inv[rows, :], inv[end_rows, :]], axis=0)
        parts = [kept[:, :size], kept[:, size:], gone[:, :size], gone[:, size:]]

        def z(lanes):
            values = jnp.concatenate([tok_top[rows, lanes], tok_end[tail_rows, lanes]], axis=0)
            return values.astype(F32) * scale

        sums = count_rows(parts, z, gain, keep + go, gain_grad)
        row_buf[:, rows] = row_dots(sums[:half])
        ends.append(sums[half:])
    row_buf[:, steps - LANE :] += row_dots(jnp.concatenate(ends, axis=0))

    for copy in raws:
        copy.wait()
    for side in (0, 1):
        for part in (1, 2):
            b_back(side, part).wait()
    raw_all = jnp.concatenate([raw_full[k] for k in range(4)], axis=0)

    def col_grad(rows):
        chosen = dot(b_full[rows, :], sel_bc[...]) + dot(raw_all[:, rows], sel_raw[...], 0, 0)
        return chosen.astype(BF16)

    product(1 - s, col_grad, col_peer)
    col_core_copy = remote(col_peer, col_core, core_s.at[1], core_r.at[1], to_core)
    col_core_copy.start()
    loads[4].wait()
    for k in range(steps // GROUP):
        rows = slice(k * GROUP, (k + 1) * GROUP)
        part = dot(b_full[rows, :], w_bc[...], 1, 1) + dot(raw_all[:, rows], w_raw[...], 0, 1)
        ng_cols[rows, :] = part
        part = part * (tok[rows, :].astype(F32) * inv[rows, :])
        gain_grad[:, mine_lanes] += fold(part)
        part = part * gain_mine[0:1, :]
        sums = part[:, :LANE]
        for sl in tiles(size)[1:]:
            sums = sums + part[:, sl]
        row_buf[:, rows] += row_dots(sums)
    row_copies = [
        remote(row_buf, row_held.at[k], row_s.at[k], row_r.at[k], target)
        for k, target in enumerate(group)
    ]
    for copy in row_copies:
        copy.start()

    pack[...] = jnp.zeros_like(pack)
    total = width + 2 * N
    add_up = lambda x: jnp.sum(x, axis=0, keepdims=True)
    for k in range(KERNEL):
        pack[k : k + 1, :total] = add_up(taps_grad[8 * k : 8 * k + 8, :])
    pack[KERNEL : KERNEL + 1, :total] = add_up(bias_grad[...])
    pack[KERNEL + 1 : KERNEL + 2, :width] = add_up(norm_gain_grad[...])
    pack[KERNEL + 2 : KERNEL + 3, :width] = add_up(skip_grad[...])
    pack[KERNEL + 3 : KERNEL + 4, :LANE] = add_up(head_grad[:8, :])
    pack[KERNEL + 4 : KERNEL + 5, :LANE] = add_up(head_grad[8:, :])
    pack[KERNEL + 5 : KERNEL + 6, :] = add_up(gain_grad[...])
    sum_core = remote(pack, pack_other, sum_s, sum_r, to_core)
    sum_core.start()

    for side in (0, 1):
        f_first(side).wait()
        nxt[side] = (mid[side] + got[side, :, size:].astype(F32)).astype(BF16)
        f_second(side).start()
        early[side] += got[side, :, :size].astype(F32)

    product(s, col_grad, col_own)

    sum_core.wait()
    pack_pair[...] = pack[...] + pack_other[...]
    pack_pieces[c] = pack_pair[...]
    sum_pieces = [
        remote(pack_pair, pack_pieces.at[c], piece_s.at[k], piece_r.at[k], target)
        for k, target in enumerate(to_piece)
    ]
    for copy in sum_pieces:
        copy.start()
    if in_line:
        for side in (0, 1):
            z_first(side).wait()
            z_on[side] = (
                z_block(first[1 - side], side) + z_got[side, block:, :].astype(F32)
            ).astype(BF16)
            z_second(side).start()
    col_core_copy.wait()
    col_own[...] = col_own[...] + col_core[...]
    if in_line:
        col_out[:block, :] = col_own[block_rows(first[0]), :]
        col_out[block:, :] = col_own[block_rows(across), :]
        col_first().start()

    for copy in sum_pieces:
        copy.wait()
    pack_total[...] = sum(pack_pieces[k] for k in range(1, n)) + pack_pieces[0]
    pack_all[t] = pack_total[...]
    sum_group = [
        remote(pack_total, pack_all.at[t], group_s.at[k], group_r.at[k], target)
        for k, target in enumerate(group)
    ]
    for copy in sum_group:
        copy.start()
    if in_line:
        col_first().wait()
        col_on[...] = col_own[block_rows(first[1]), :] + col_got[block:, :]
        col_second().start()

    loads[5].wait()
    loads[6].wait()
    for copy in row_copies:
        copy.wait()
    for side in (0, 1):
        f_second(side).wait()
        early[side] += last[side].astype(F32)
        at = steps - GROUP - END + side * tail_half
        late[at : at + tail_half, :] = early[side, half:, :]
    row_total = row_buf[...] + row_held[0] + row_held[1] + row_held[2]
    for k in range(steps // LANE):
        rows = slice(k * LANE, (k + 1) * LANE)
        row_dot = jnp.broadcast_to(row_total[0:1, rows] * (1.0 / D), (LANE, LANE)).T
        scale = inv[rows, :]
        for sl in tiles(size):
            if k < GROUP // LANE:
                side, at = divmod(k * LANE, half)
                main = early[side, at : at + LANE, sl]
            else:
                main = late[k * LANE - GROUP : (k + 1) * LANE - GROUP, sl]
            z_tile = tok[rows, sl].astype(F32) * scale
            change = scale * ((main + ng_cols[rows, sl]) * gain_mine[0:1, sl] - z_tile * row_dot)
            tokens_out[rows, sl] = (back[rows, sl].astype(F32) + change).astype(BF16)

    if in_line:
        for side in (0, 1):
            z_second(side).wait()
            value_out[:, side * side_w : (side + 1) * side_w] = (
                z_block(c, side) + z_got[side, :block, :].astype(F32) + z_last[side].astype(F32)
            )
        col_second().wait()
        cols_out[...] = col_own[block_rows(c), :] + col_got[:block, :] + col_last[...]
    else:
        value_out[...] = both[...]
        cols_out[...] = col_own[...]
    for copy in sum_group:
        copy.wait()
    pack_out[...] = pack_all[...]


def run_tail(
    grad_b, grad_v, normed, weight, tok, back, late, raw_t, fixed, gate_grad, inv, gain, gain_mine,
    w_bc, w_raw, sel_bc, sel_raw, late_rows, late_gain, *small,
):
    n = lax.axis_size("context")
    steps, width = grad_v.shape
    size = D // 4
    half_d = D // 2
    block = half_d // n
    side_rows = (GROUP + END) // 2
    share = steps // 4
    top = lambda w: pl.BlockSpec((GROUP, w), lambda i: (0, 0), pipeline_mode=pl.Buffered(1))
    end = lambda w: pl.BlockSpec(
        (END, w), lambda i: (steps // END - 1, 0), pipeline_mode=pl.Buffered(1)
    )
    once = lambda *dims: pl.BlockSpec(
        dims, lambda i: (0,) * len(dims), pipeline_mode=pl.Buffered(1)
    )
    full = lambda x: once(*x.shape)
    hbm = pl.BlockSpec(memory_space=pl.ANY)
    dma = pltpu.SemaphoreType.DMA
    vmem = pltpu.VMEM
    value_rows = block if n == 4 else half_d
    pair = (2, side_rows, size)
    packed = (PACK, D)
    return pl.pallas_call(
        functools.partial(tail_kernel, n),
        grid=(1,),
        in_specs=[hbm] * 7
        + [full(raw_t), full(fixed), top(width), end(width), top(D), end(D)]
        + [full(x) for x in (inv, gain, gain_mine, w_bc, w_raw, sel_bc, sel_raw)]
        + [full(x) for x in (late_rows, late_gain, *small)],
        out_specs=[
            once(steps, size), once(value_rows, width), once(value_rows, LANE), once(4, *packed)
        ],
        out_shape=[
            shape(steps, size, dtype=BF16), shape(value_rows, width), shape(value_rows, LANE),
            shape(4, *packed),
        ],
        scratch_shapes=[
            vmem((steps, 2 * N), F32), vmem((steps, width), BF16), vmem(normed.shape, BF16),
            vmem(weight.shape, BF16), vmem((steps, size), BF16), vmem((steps, size), BF16),
            vmem(late.shape, F32),
            vmem((half_d, width), F32), vmem((half_d, width), F32), vmem((half_d, width), F32),
            vmem((2, 2, share, N), F32), vmem((2, share, N), F32), vmem((2, share, N), F32),
            vmem((steps, 2 * N), BF16), vmem((4, 16, steps), BF16),
            vmem(pair, F32), vmem(pair, F32), vmem((2, side_rows, 2 * size), BF16),
            vmem((2, side_rows, 2 * size), BF16), vmem(pair, BF16), vmem(pair, BF16), vmem((8, D), F32),
            vmem((2, 2 * block, width // 2), BF16), vmem((2, 2 * block, width // 2), BF16),
            vmem((2, block, width // 2), BF16), vmem((2, block, width // 2), BF16),
            vmem((steps, size), F32),
            vmem((half_d, LANE), F32), vmem((half_d, LANE), F32), vmem((half_d, LANE), F32),
            vmem((2 * block, LANE), F32), vmem((2 * block, LANE), F32), vmem((block, LANE), F32),
            vmem((block, LANE), F32),
            vmem((8, steps), F32), vmem((3, 8, steps), F32),
            vmem(packed, F32), vmem(packed, F32), vmem(packed, F32), vmem((n, *packed), F32),
            vmem(packed, F32), vmem((4, *packed), F32),
            dma((7,)), dma((3,)), dma((3,)), dma((2, 6)), dma((2, 6)), dma((4,)), dma((4,)),
            dma((2,)), dma((2,)), dma((6,)), dma((6,)), dma((3,)), dma((3,)),
            dma, dma, dma((n - 1,)), dma((n - 1,)), dma((3,)), dma((3,)),
        ],
        compiler_params=pltpu.CompilerParams(
            dimension_semantics=("arbitrary",), vmem_limit_bytes=60 * 1024 * 1024,
            collective_id=5, has_side_effects=True,
        ),
        cost_estimate=estimate(50),
        name="tail",
    )(
        grad_b, grad_v, normed, weight, tok, back, late,
        raw_t, fixed, gate_grad, gate_grad, tok, tok, inv, gain, gain_mine, w_bc, w_raw, sel_bc, sel_raw,
        late_rows, late_gain, *small,
    )


def pad_rows(x, rows=8):
    return jnp.concatenate([x, jnp.zeros((rows - x.shape[0], x.shape[1]), x.dtype)], axis=0)


def pad_cols(x, cols=LANE):
    return jnp.concatenate([x, jnp.zeros((x.shape[0], cols - x.shape[1]), x.dtype)], axis=1)


def on_device(
    tokens, cotangent, doc_lengths, zx_weight, bcdt_weight, out_weight, input_gain, chan_params,
    bc_params, head_params, zx_first, bcdt_first, out_first, gain_first, chan_first, bc_first,
    head_first, zx_second, bcdt_second, out_second, gain_second, chan_second, bc_second, head_second,
):
    n_tensor = lax.axis_size("tensor")
    t_index = lax.axis_index("tensor")
    c_index = lax.axis_index("context")
    tok = tokens[0]
    resid = tok.astype(F32)
    back = cotangent[0]
    steps = resid.shape[0]
    inner_loc = INNER // n_tensor
    heads_loc = H // n_tensor
    share = D // n_tensor
    count = steps // L
    rows_loc = zx_weight.shape[0]
    cols_loc = bcdt_weight.shape[1]

    zx_flat = zx_weight.reshape(rows_loc, 2 * inner_loc)
    proj_w, cols_z = line_gather(zx_flat.astype(BF16), pad_cols(bcdt_weight.astype(BF16)))
    down_block, _ = lax.optimization_barrier((out_weight.astype(BF16).T, proj_w))
    down_t = lax.all_gather(down_block, ("shard", "context"), axis=0, tiled=True)
    cols_w = jnp.concatenate(
        [cols_z[:, k * LANE : k * LANE + cols_loc] for k in range(n_tensor)], axis=1
    )

    bounds = jnp.cumsum(doc_lengths[0])[:-1]
    info, marks_rows = run_docs(bounds, c_index * steps, steps)
    around = (c_index + 1) * steps + jnp.arange(1 - KERNEL, KERNEL - 1)
    near_end = jnp.sum((around[:, None] >= bounds[None, :]).astype(jnp.int32), axis=1)

    chan_loc = lax.dynamic_slice_in_dim(chan_params, t_index * inner_loc, inner_loc, 1)
    head_loc = lax.dynamic_slice_in_dim(head_params, t_index * heads_loc, heads_loc, 1)
    chan8 = pad_rows(chan_loc)
    bc8 = pad_rows(bc_params)
    head8 = pad_rows(pad_cols(head_loc))
    spread_at = lax.broadcasted_iota(jnp.int32, (2 * LANE, inner_loc), 0) % LANE
    expand = (
        spread_at == lax.broadcasted_iota(jnp.int32, (2 * LANE, inner_loc), 1) // P_SIZE
    ).astype(BF16)
    inv_rms = lax.rsqrt(jnp.mean(resid * resid, axis=1, keepdims=True) + EPS)
    normed = (resid * inv_rms * input_gain).astype(BF16)
    projected = jnp.dot(normed, proj_w, preferred_element_type=F32)
    delta_w = lax.dynamic_slice_in_dim(cols_w, 2 * N + t_index * heads_loc, heads_loc, 1)
    cols = jnp.dot(
        normed, jnp.concatenate([cols_w[:, : 2 * N], pad_cols(delta_w)], axis=1),
        preferred_element_type=F32,
    )
    edge = jnp.concatenate(
        [projected[steps - 8 :, inner_loc:], cols[steps - 8 :]], axis=1
    )
    halo = from_behind(edge, "context", 1)
    halo, down_t = lax.optimization_barrier((halo, down_t))
    halo_v, halo_b = halo[:, :inner_loc], halo[:, inner_loc:]

    act, delta, cum, sloc, pfx, final = run_prep(
        projected, cols, halo_v, halo_b, info, chan8, bc8, head8, expand, heads_loc
    )
    entry, back_scaled = run_entry(final, back, down_t)
    ssd, sums = run_ahead(
        act, delta, cum, info, marks_rows, sloc, pfx, entry, projected, back_scaled, chan8, head8,
        expand, heads_loc,
    )
    sums = small_sum(sums, 1)
    scaled, *out_fan = run_out(ssd, projected, sums, chan8, down_t)
    gate_grad, mixed_grad, aloc, sfx, first_adj, norm_gain_grad = run_norm(
        ssd, projected, back_scaled, sums, act, cum, info, chan8, expand, heads_loc
    )
    later, out_own, out_next, *z_arrays = run_middle(
        first_adj, out_fan, normed, gate_grad, back, scaled
    )
    resid_share = lax.dynamic_slice_in_dim(tok, t_index * share, share, 1).astype(F32)
    in_line = lax.axis_size("context") == 4
    total_width = inner_loc + 2 * N

    masks = []
    for s in range(1, KERNEL):
        agree = (
            near_end[KERNEL - 1 : KERNEL - 1 + s] == near_end[KERNEL - 1 - s : KERNEL - 1]
        ).astype(F32)
        masks.append(jnp.pad(agree, (8 - s, 0)))
    edge_mask = jnp.broadcast_to(jnp.concatenate(masks)[:, None], (24, LANE))
    gain8 = jnp.broadcast_to(input_gain[None], (8, D))
    (
        grad_v, grad_b, raw_t, last_rows, _, taps_grad, bias_grad, skip_grad, head_grad,
        ng_late, late_rows, late_gain, out_last, *z_sum,
    ) = run_grand(
        projected, cols, halo_v, halo_b, info, marks_rows, delta, cum, ssd, mixed_grad,
        sloc, pfx, entry, aloc, sfx, later, chan8, bc8, head8, expand, heads_loc,
        gate_grad, proj_w, tok, inv_rms, gain8, edge_mask, out_next, z_arrays if in_line else [],
    )
    out_share = out_own + out_last.reshape(steps, share).astype(F32)
    block_out = (resid_share + out_share).astype(BF16)[None]
    if in_line:
        gate_g, down_g = z_sum[0][0], z_sum[0][1]
    else:
        gate_g, down_g = [
            lax.psum_scatter(z_arrays[0][k], "context", scatter_dimension=0, tiled=True) for k in (0, 1)
        ]
    cols_rows = lax.dynamic_slice_in_dim(cols_w, t_index * share, share, 0)
    w_bc = cols_rows[:, : 2 * N]
    w_raw = jnp.pad(
        cols_rows[:, 2 * N :].reshape(share, n_tensor, heads_loc), ((0, 0), (0, 0), (0, 16 - heads_loc))
    ).reshape(share, n_tensor * 16)
    column = jnp.arange(LANE)[None, :] + t_index * cols_loc
    inside = jnp.arange(LANE)[None, :] < cols_loc
    sel_bc = jnp.logical_and(jnp.arange(2 * N)[:, None] == column, inside).astype(BF16)
    slot = jnp.arange(n_tensor * 16)[:, None]
    of_slot = jnp.where(slot % 16 < heads_loc, 2 * N + slot // 16 * heads_loc + slot % 16, -1)
    sel_raw = jnp.logical_and(of_slot == column, inside).astype(BF16)
    gain_mine = jnp.broadcast_to(
        lax.dynamic_slice_in_dim(input_gain, t_index * share, share, 0)[None], (8, share)
    )
    tokens_grad, value_g, cols_g, packed = run_tail(
        grad_b, grad_v, normed, proj_w, tok, back, ng_late, raw_t, last_rows, gate_grad, inv_rms,
        gain8, gain_mine, w_bc, w_raw, sel_bc, sel_raw, late_rows, late_gain,
        taps_grad, bias_grad, norm_gain_grad, skip_grad, head_grad,
    )
    tokens_grad = tokens_grad[None]
    cols_g = cols_g[:, :cols_loc]
    if not in_line:
        value_g = lax.psum_scatter(value_g, "context", scatter_dimension=0, tiled=True)
        cols_g = lax.psum_scatter(cols_g, "context", scatter_dimension=0, tiled=True)
    chan_g = jnp.concatenate(
        [packed[k, : KERNEL + 2, :inner_loc] for k in range(n_tensor)], axis=1
    )
    over = sum(packed[k] for k in range(n_tensor))
    bc_g = over[: KERNEL + 1, inner_loc:total_width]
    gain_g = over[KERNEL + 5]
    skip_g = jnp.sum(packed[:, KERNEL + 2, :inner_loc].reshape(H, P_SIZE), axis=1)
    head_g = jnp.concatenate(
        [packed[:, KERNEL + 3 + k, :heads_loc].reshape(1, H) for k in (0, 1)] + [skip_g[None]], axis=0
    )

    large = run_adam(
        gate_g, value_g, down_g, (zx_weight, zx_first, zx_second), (out_weight, out_first, out_second)
    )
    zx_new, out_new = large[:3], large[3:]
    bcdt_new = adamw(bcdt_weight, cols_g, bcdt_first, bcdt_second, RATE_MATRIX, DECAY)
    gain_new = adamw(input_gain, gain_g, gain_first, gain_second, RATE_SMALL, 0.0)
    chan_new = adamw(chan_params, chan_g, chan_first, chan_second, RATE_SMALL, 0.0)
    bc_new = adamw(bc_params, bc_g, bc_first, bc_second, RATE_SMALL, 0.0)
    head_new = adamw(head_params, head_g, head_first, head_second, RATE_SMALL, 0.0)
    return (
        block_out, tokens_grad, *zx_new, *bcdt_new, *out_new, *gain_new, *chan_new, *bc_new, *head_new
    )


def solution(mesh):
    big = P(("shard", "context"), None, "tensor")
    cols = P(("shard", "context"), "tensor")
    down = P("tensor", ("shard", "context"))
    rows = P("shard", "context", None)
    out_rows = P("shard", "context", "tensor")
    return jax.shard_map(
        on_device,
        mesh=mesh,
        in_specs=(
            rows, rows, P("shard", None), big, cols, down, P(), P(), P(), P(),
            big, cols, down, P(), P(), P(), P(),
            big, cols, down, P(), P(), P(), P(),
        ),
        out_specs=(
            out_rows, out_rows, big, big, big, cols, cols, cols, down, down, down,
            *([P()] * 12),
        ),
        check_vma=False,
    )
```

```python
import functools

import jax
import jax.numpy as jnp
import ml_dtypes
import numpy as np
from jax import lax
from jax.experimental import pallas as pl
from jax.experimental.pallas import tpu as pltpu
from jax.sharding import PartitionSpec as P

D = 1536
INNER = 3072
H = 48
P_SIZE = 64
N = 128
KERNEL = 4
STEP = 10

EPS = 1e-05
BETA_ONE = 0.9
BETA_TWO = 0.999
ADAM_EPS = 1e-08
DECAY = 0.1
RATE_MATRIX = 0.05
RATE_SMALL = 0.2

L = 128
LANE = 128
GROUP = 4 * L
PART = 2 * L
END = 32
LOG2E = 1.4426950408889634
F32 = jnp.float32
BF16 = jnp.bfloat16
VMEM_LIMIT = 48 * 1024 * 1024


def from_behind(block, axis, distance):
    devices = range(lax.axis_size(axis))
    route = [(i - distance, i) for i in devices if i - distance in devices]
    return lax.ppermute(block, axis, route)


def adamw(weight, grad, first, second, rate, decay):
    first_new = BETA_ONE * first + (1.0 - BETA_ONE) * grad
    second_new = BETA_TWO * second + (1.0 - BETA_TWO) * grad * grad
    scale_one = 1.0 - BETA_ONE**STEP
    scale_two = 1.0 - BETA_TWO**STEP
    update = first_new / scale_one / (jnp.sqrt(second_new / scale_two) + ADAM_EPS)
    return (weight - rate * (update + decay * weight), first_new, second_new)


def two(x):
    hi = x.astype(BF16)
    return hi, (x - hi.astype(F32)).astype(BF16)


def dot(a, b, ca=1, cb=0):
    return lax.dot_general(a, b, (((ca,), (cb,)), ((), ())), preferred_element_type=F32)


def dot3(a, b, ca=1, cb=0):
    ah, al = two(a)
    bh, bl = two(b)
    return dot(
        jnp.concatenate([ah, al, ah], axis=ca), jnp.concatenate([bh, bh, bl], axis=cb), ca, cb
    )


def tri_sum(tri, x):
    hi = x.astype(BF16)
    rest = x - hi.astype(F32)
    mid = rest.astype(BF16)
    low = (rest - mid.astype(F32)).astype(BF16)
    out = dot(tri, jnp.concatenate([hi, mid, low], axis=1))
    w = x.shape[1]
    return out[:, :w] + out[:, w : 2 * w] + out[:, 2 * w :]


def spread(x, e_ref):
    hi, lo = two(x)
    return dot(jnp.concatenate([hi, lo], axis=1), e_ref[...])


def per_head(x, e_ref):
    hi, lo = two(x)
    e = e_ref[:LANE, :]
    return dot(hi, e, 1, 1) + dot(lo, e, 1, 1)


def sigmoid(x):
    return 1.0 / (1.0 + jnp.exp(-x))


def softplus(x):
    return jnp.maximum(x, 0.0) + jnp.log1p(jnp.exp(-jnp.abs(x)))


def tiles(width):
    return [slice(k, k + LANE) for k in range(0, width, LANE)]


def fold(x):
    return jnp.sum(x.reshape(x.shape[0] // 8, 8, x.shape[1]), axis=0)


def lower_mask():
    row = lax.broadcasted_iota(jnp.int32, (L, L), 0)
    col = lax.broadcasted_iota(jnp.int32, (L, L), 1)
    return row >= col


def keep_mask(info, marks_row):
    return jnp.logical_and(lower_mask(), info[:, 5:6] == marks_row[0:1, :])


def decay_of(keep, cum, cum_t, h):
    return jnp.exp2(jnp.where(keep, cum[:, h : h + 1] - cum_t[h : h + 1, :], -1e30))


def load_ext(ext_ref, cur_ref, prev_ref, halo_ref, j, first):
    if j > 0:
        ext_ref[0:8, :] = cur_ref[j * L - 8 : j * L, :]
    else:

        @pl.when(first)
        def _():
            ext_ref[0:8, :] = halo_ref[...]

        @pl.when(jnp.logical_not(first))
        def _():
            ext_ref[0:8, :] = prev_ref[...]

    ext_ref[8 : 8 + L, :] = cur_ref[j * L : (j + 1) * L, :]


def rows_at(ref, j):
    return ref.at[j * L : (j + 1) * L, :]


def lead_at(ref, j):
    return ref.at[j : j + 1]


def conv_tile(ext_ref, info, taps, sl):
    shifted = []
    total = jnp.broadcast_to(taps[KERNEL : KERNEL + 1, :], (L, LANE))
    for k in range(KERNEL):
        val = ext_ref[pl.ds(8 - KERNEL + 1 + k, L), sl]
        if k < KERNEL - 1:
            val = val * info[:, k : k + 1]
        shifted.append(val)
        total = total + taps[k : k + 1, :] * val
    return shifted, total


def prep_chunk(
    bc, info_ref, chan, bcpar, head, e_ref, act, delta_ref, cum_ref, sloc, pfx, ext_v, ext_b, state, prod
):
    info = info_ref[...]
    width = ext_v.shape[1]
    for sl in tiles(width):
        _, total = conv_tile(ext_v, info, chan[:, sl], sl)
        act[:, sl] = total * sigmoid(total)
    for sl in tiles(2 * N):
        _, total = conv_tile(ext_b, info, bcpar[:, sl], sl)
        act[:, slice(width + sl.start, width + sl.stop)] = total * sigmoid(total)
    raw = bc[:, 2 * N : 3 * N]
    delta = softplus(raw + head[0:1, :])
    dlog = -delta * (jnp.exp(head[1:2, :]) * LOG2E)
    tri = jnp.where(lower_mask(), 1.0, 0.0).astype(BF16)
    cum = tri_sum(tri, dlog)
    delta_ref[...] = delta
    cum_ref[...] = cum
    sloc[0] = state[...]
    pfx[0] = prod[...]
    last = cum[L - 1 : L, :]
    tail = info[:, 4:5] * jnp.exp2(last - cum) * delta
    through = spread(
        jnp.broadcast_to(info[L - 1 : L, 3:4] * jnp.exp2(last), (8, LANE)), e_ref
    )
    weights = spread(tail, e_ref)
    tail_u = act[:, :width] * weights
    fresh = dot3(act[:, width : width + N], tail_u, 0, 0)
    state[...] = state[...] * through[0:1, :] + fresh
    prod[...] = prod[...] * through


def row_block(width, col=0, rows=GROUP):
    return pl.BlockSpec((rows, width), lambda i: (i, col))


def prev_block(width, col=0, rows=GROUP):
    return pl.BlockSpec((8, width), lambda i: (jnp.maximum(i * (rows // 8) - 1, 0), col))


def lead_block(*dims, rows=GROUP):
    return pl.BlockSpec((rows // L, *dims), lambda i: (i, 0, 0))


def whole(*shape):
    return pl.BlockSpec(shape, lambda i: (0,) * len(shape))


def once(*shape):
    return pl.BlockSpec(shape, lambda i: (0,) * len(shape), pipeline_mode=pl.Buffered(1))


def estimate(us):
    return pl.CostEstimate(flops=int(us * 1.1e9), bytes_accessed=int(us * 1e6), transcendentals=0)


def params(**kw):
    return pltpu.CompilerParams(
        dimension_semantics=("arbitrary",), vmem_limit_bytes=VMEM_LIMIT, **kw
    )


def shape(*dims, dtype=F32):
    return jax.ShapeDtypeStruct(dims, dtype)


def ahead_kernel(
    heads, act, delta, cum, info, marks, sloc, pfx, entry, gate, back, chan, head, e_ref, ssd, sums
):
    for j in range(act.shape[0] // L):
        ahead_chunk(
            rows_at(act, j), rows_at(delta, j), rows_at(cum, j), rows_at(info, j), lead_at(marks, j),
            lead_at(sloc, j), lead_at(pfx, j), entry, rows_at(gate, j), rows_at(back, j), chan, head,
            e_ref, rows_at(ssd, j), lead_at(sums, j),
        )


def ahead_chunk(
    act, delta_ref, cum_ref, info_ref, marks_ref, sloc, pfx, entry, gate, back, chan, head, e_ref, ssd, sums
):
    width = act.shape[1] - 2 * N
    info = info_ref[...]
    cum = cum_ref[...]
    cum_t = cum.T
    keep = keep_mask(info, marks_ref[0])
    bmat = act[:, width : width + N]
    cmat = act[:, width + N :]
    scores = dot3(cmat, bmat, 1, 1)
    xs = act[:, :width]
    u_hi, u_lo = two(xs * spread(delta_ref[...], e_ref))
    state = sloc[0] + entry[...] * pfx[0, 0:1, :]
    entering = dot3(cmat, state)
    eexp = spread(info[:, 3:4] * jnp.exp2(cum), e_ref)
    skip = spread(jnp.broadcast_to(head[2:3, :], (8, LANE)), e_ref)
    lane = lax.broadcasted_iota(jnp.int32, (1, LANE), 1)
    left = jnp.where(lane < P_SIZE, 1.0, 0.0).astype(BF16)
    right = jnp.where(lane < P_SIZE, 0.0, 1.0).astype(BF16)
    square = jnp.zeros((L, LANE), F32)
    cross = jnp.zeros((L, LANE), F32)
    for q, sl in enumerate(tiles(width)):
        mix = jnp.concatenate(
            [(scores * decay_of(keep, cum, cum_t, 2 * q + r)).astype(BF16) for r in (0, 1)], axis=1
        )
        both = jnp.concatenate([u_hi[:, sl], u_lo[:, sl]], axis=1)
        rhs = jnp.concatenate(
            [both * jnp.concatenate([m, m], axis=1) for m in (left, right)], axis=0
        )
        out = dot(mix, rhs)
        y = out[:, :LANE] + out[:, LANE:] + entering[:, sl] * eexp[:, sl]
        y = y + skip[0:1, sl] * xs[:, sl]
        ssd[:, sl] = y
        g = gate[:, sl]
        gated = y * g * sigmoid(g)
        square = square + gated * gated
        cross = cross + gated * (back[:, sl] * chan[KERNEL + 1 : KERNEL + 2, sl])
    ones = jnp.ones((8, LANE), BF16)
    rows = []
    for part in (square, cross):
        hi, lo = two(part)
        rows.append(dot(ones, hi, 1, 1) + dot(ones, lo, 1, 1))
    pick = lax.broadcasted_iota(jnp.int32, (8, LANE), 0)
    sums[0] = jnp.where(pick == 0, rows[0], jnp.where(pick == 1, rows[1], 0.0))


def run_ahead(act, delta, cum, info, marks, sloc, pfx, entry, projected, back, chan, head, expand, heads):
    steps, width = projected.shape[0], projected.shape[1] // 2
    count = steps // L
    return pl.pallas_call(
        functools.partial(ahead_kernel, heads),
        grid=(steps // GROUP,),
        in_specs=[
            row_block(width + 2 * N), row_block(LANE), row_block(LANE), row_block(LANE),
            lead_block(8, L), lead_block(N, width), lead_block(8, width),
            once(N, width), row_block(width, 0), row_block(width),
            once(8, width), once(8, LANE), once(2 * LANE, width),
        ],
        out_specs=[row_block(width), lead_block(8, L)],
        out_shape=[shape(steps, width), shape(count, 8, L)],
        compiler_params=params(),
        cost_estimate=estimate(20),
        name="ahead",
    )(act, delta, cum, info, marks, sloc, pfx, entry, projected, back, chan, head, expand)


def norm_kernel(
    heads, ssd, gate, back, sums, cmat, cum, info, chan, e_ref,
    gate_grad, mixed_grad, aloc, sfx, fin, gain_grad, state, prod,
):
    i = pl.program_id(0)

    @pl.when(i == 0)
    def _():
        state[...] = jnp.zeros_like(state)
        prod[...] = jnp.ones_like(prod)
        gain_grad[...] = jnp.zeros_like(gain_grad)

    chunks = ssd.shape[0] // L

    for j in reversed(range(chunks)):
        norm_chunk(
            rows_at(ssd, j), rows_at(gate, j), rows_at(back, j), lead_at(sums, j), rows_at(cmat, j),
            rows_at(cum, j), rows_at(info, j), chan, e_ref, rows_at(gate_grad, j),
            rows_at(mixed_grad, j), lead_at(aloc, j), lead_at(sfx, j), gain_grad, state, prod,
        )

    @pl.when(i == pl.num_programs(0) - 1)
    def _():
        fin[:N, :] = state[...]
        fin[N:, :] = prod[...]


def norm_chunk(
    ssd, gate, back, sums, cmat_ref, cum_ref, info_ref, chan, e_ref,
    gate_grad, mixed_grad, aloc, sfx, gain_grad, state, prod,
):
    width = ssd.shape[1]
    rows = sums[0]
    inv_row = lax.rsqrt(rows[0:1, :] / INNER + EPS)
    cross_row = inv_row * inv_row * inv_row * (rows[1:2, :] / INNER)
    inv = jnp.broadcast_to(inv_row, (LANE, L)).T
    cross = jnp.broadcast_to(cross_row, (LANE, L)).T
    info = info_ref[...]
    cum = cum_ref[...]
    eexp = spread(info[:, 3:4] * jnp.exp2(cum), e_ref)
    e_mixed = []
    for sl in tiles(width):
        g = gate[:, sl]
        sig = sigmoid(g)
        soft = g * sig
        y = ssd[:, sl]
        gated = y * soft
        bs = back[:, sl]
        gain = chan[KERNEL + 1 : KERNEL + 2, sl]
        normed = gated * inv
        gain_grad[:, sl] += fold(bs * normed)
        gg = inv * (bs * gain) - gated * cross
        mg = gg * soft
        mixed_grad[:, sl] = mg
        gate_grad[:, sl] = (gg * y * sig * (1.0 + g * (1.0 - sig))).astype(BF16)
        e_mixed.append(mg * eexp[:, sl])
    aloc[0] = state[...]
    sfx[0] = prod[...]
    through = spread(
        jnp.broadcast_to(info[L - 1 : L, 3:4] * jnp.exp2(cum[L - 1 : L, :]), (8, LANE)), e_ref
    )
    fresh = dot3(cmat_ref[...], jnp.concatenate(e_mixed, axis=1), 0, 0)
    state[...] = state[...] * through[0:1, :] + fresh
    prod[...] = prod[...] * through


def run_norm(ssd, projected, back, sums, act, cum, info, chan, expand, heads):
    steps, width = ssd.shape
    count = steps // L
    blocks = steps // GROUP
    turn = lambda spec: pl.BlockSpec(
        spec.block_shape, lambda i, m=spec.index_map: m(blocks - 1 - i)
    )
    c_col = width // N + 1
    return pl.pallas_call(
        functools.partial(norm_kernel, heads),
        grid=(blocks,),
        in_specs=[
            turn(row_block(width)), turn(row_block(width, 0)), turn(row_block(width)),
            turn(lead_block(8, L)),
            turn(row_block(N, c_col)), turn(row_block(LANE)), turn(row_block(LANE)),
            once(8, width), once(2 * LANE, width),
        ],
        out_specs=[
            turn(row_block(width)), turn(row_block(width)),
            turn(lead_block(N, width)),
            turn(lead_block(8, width)),
            whole(N + 8, width), whole(8, width),
        ],
        out_shape=[
            shape(steps, width, dtype=BF16), shape(steps, width),
            shape(count, N, width), shape(count, 8, width), shape(N + 8, width), shape(8, width),
        ],
        scratch_shapes=[pltpu.VMEM((N, width), F32), pltpu.VMEM((8, width), F32)],
        compiler_params=params(),
        cost_estimate=estimate(21),
        name="norm_back",
    )(ssd, projected, back, sums, act, cum, info, chan, expand)


def behind_chunk(
    heads, j, chunks, i_first, i_last, val, valp, bc, bcp, halo_v, halo_b, info_ref, marks_ref, delta_ref, cum_ref,
    ssd, mixed_grad, sloc, pfx, entry, aloc, sfx, later, chan, bcpar, head, e_ref,
    grad_v, grad_b, raw_grad, tail_rows, head_rows, taps_grad, bias_grad, skip_grad, head_grad,
    ext_v, ext_b, slope, d_tot,
):
    width = val.shape[1]
    total_width = width + 2 * N
    starts = j == chunks - 1

    if starts:

        @pl.when(i_first)
        def _():
            d_tot[0:8, :] = jnp.zeros((8, total_width), F32)
            taps_grad[...] = jnp.zeros_like(taps_grad)
            bias_grad[...] = jnp.zeros_like(bias_grad)
            skip_grad[...] = jnp.zeros_like(skip_grad)
            head_grad[...] = jnp.zeros_like(head_grad)

    d_tot[L:, :] = d_tot[0:8, :]
    load_ext(ext_v, val, valp, halo_v, j, i_last)
    load_ext(ext_b, bc, bcp, halo_b, j, i_last)
    raw = bc[j * L : (j + 1) * L, 2 * N : 3 * N]
    info_ref, marks_ref = rows_at(info_ref, j), lead_at(marks_ref, j)
    delta_ref, cum_ref, ssd = rows_at(delta_ref, j), rows_at(cum_ref, j), rows_at(ssd, j)
    mixed_grad, sloc, pfx = rows_at(mixed_grad, j), lead_at(sloc, j), lead_at(pfx, j)
    aloc, sfx = lead_at(aloc, j), lead_at(sfx, j)
    grad_v, grad_b = rows_at(grad_v, j), rows_at(grad_b, j)
    raw_grad = raw_grad.at[:, j * L : (j + 1) * L]
    info = info_ref[...]

    def activate(ext_ref, taps, sl, at):
        _, total = conv_tile(ext_ref, info, taps[:, sl], sl)
        sig = sigmoid(total)
        slope[:, slice(at, at + LANE)] = sig * (1.0 + total * (1.0 - sig))
        return total * sig

    xs = jnp.concatenate([activate(ext_v, chan, sl, sl.start) for sl in tiles(width)], axis=1)
    bmat = activate(ext_b, bcpar, slice(0, N), width)
    cmat = activate(ext_b, bcpar, slice(N, 2 * N), width + N)

    delta = delta_ref[...]
    cum = cum_ref[...]
    cum_t = cum.T
    keep = keep_mask(info, marks_ref[0])
    last = cum[L - 1 : L, :]
    scores = dot3(cmat, bmat, 1, 1)
    dexp = spread(delta, e_ref)
    eexp = spread(info[:, 3:4] * jnp.exp2(cum), e_ref)
    texp = spread(info[:, 4:5] * jnp.exp2(last - cum), e_ref)
    u = xs * dexp
    u_hi, u_lo = two(u)
    dy = mixed_grad[...]
    dy_hi, dy_lo = two(dy)
    skip = spread(jnp.broadcast_to(head[2:3, :], (8, LANE)), e_ref)
    state = sloc[0] + entry[...] * pfx[0, 0:1, :]
    adj = aloc[0] + later[...] * sfx[0, 0:1, :]
    tail_du = dot3(bmat, adj) * texp
    lane = lax.broadcasted_iota(jnp.int32, (1, LANE), 1)
    left = jnp.where(lane < P_SIZE, 1.0, 0.0).astype(BF16)
    right = jnp.where(lane < P_SIZE, 0.0, 1.0).astype(BF16)
    two_left = jnp.concatenate([left, left], axis=1)
    two_right = jnp.concatenate([right, right], axis=1)
    d_scores = jnp.zeros((L, L), F32)
    inner_du = []
    for q, sl in enumerate(tiles(width)):
        decays = [decay_of(keep, cum, cum_t, 2 * q + r) for r in (0, 1)]
        mix = jnp.concatenate([(scores * d).astype(BF16) for d in decays], axis=0)
        dy_both = jnp.concatenate([dy_hi[:, sl], dy_lo[:, sl]], axis=1)
        rhs = jnp.concatenate([dy_both * two_left, dy_both * two_right], axis=0)
        out = dot(mix, rhs, 0, 0)
        inner_du.append(out[:, :LANE] + out[:, LANE:])
        u_twice = jnp.concatenate([u_hi[:, sl], u_hi[:, sl]], axis=1)
        u_rows = jnp.concatenate([u_twice * two_left, u_twice * two_right], axis=0)
        d_mix = dot(dy_both, u_rows, 1, 1)
        d_scores = d_scores + d_mix[:, :L] * decays[0] + d_mix[:, L:] * decays[1]
    du = jnp.concatenate(inner_du, axis=1) + tail_du
    d_xs = dexp * du + skip[0:1, :] * dy
    d_b = dot3(d_scores, cmat, 0, 0) + dot3(u * texp, adj, 1, 1)
    d_c = dot3(d_scores, bmat) + dot3(dy * eexp, state, 1, 1)
    skip_grad[...] += fold(dy * xs)

    direct = per_head(xs * du, e_ref)
    mixed = ssd[...] - skip[0:1, :] * xs
    d_cum = per_head(dy * mixed, e_ref) - delta * direct
    at_last = jnp.sum(per_head(u * tail_du, e_ref), axis=0, keepdims=True)
    through = info[L - 1 : L, 3:4] * jnp.exp2(last)
    pair = per_head(fold(adj * state), e_ref)
    at_last = at_last + through * jnp.sum(pair, axis=0, keepdims=True)
    upper = jnp.where(lower_mask(), 1.0, 0.0).astype(BF16).T
    d_log = tri_sum(upper, d_cum) + at_last
    rate = jnp.exp(head[1:2, :])
    valid = lane < heads
    d_raw = (direct - d_log * rate) * sigmoid(raw + head[0:1, :])
    d_raw = jnp.where(valid, d_raw, 0.0)
    raw_grad[...] = d_raw.T[:16, :].astype(BF16)
    head_grad[0:8, :] += fold(d_raw)
    head_grad[8:16, :] += fold(jnp.where(valid, -d_log * delta * rate, 0.0))

    d_act = [d_xs[:, sl] for sl in tiles(width)] + [d_b, d_c]
    for q in range(total_width // LANE):
        sl = slice(q * LANE, (q + 1) * LANE)
        if q < width // LANE:
            ext_ref, taps, part = ext_v, chan[:, sl], sl
        else:
            part = slice(sl.start - width, sl.stop - width)
            ext_ref, taps = ext_b, bcpar[:, part]
        dt = d_act[q] * slope[:, sl]
        d_tot[0:L, sl] = dt
        bias_grad[:, sl] += fold(dt)
        for k in range(KERNEL):
            moved = ext_ref[pl.ds(8 - KERNEL + 1 + k, L), part]
            if k < KERNEL - 1:
                moved = moved * info[:, k : k + 1]
            taps_grad[8 * k : 8 * k + 8, sl] += fold(dt * moved)
        total = dt * taps[KERNEL - 1 : KERNEL, :]
        for s in range(1, KERNEL):
            total = total + taps[KERNEL - 1 - s : KERNEL - s, :] * (
                d_tot[pl.ds(s, L), sl] * info[:, 7 + s : 8 + s]
            )
        if q < width // LANE:
            grad_v[:, sl] = total.astype(BF16)
        else:
            grad_b[:, part] = total

        if starts:

            @pl.when(i_first)
            def _():
                tail_rows[:, sl] = total[L - 8 :, :]

    if j == 0:

        @pl.when(i_last)
        def _():
            head_rows[...] = d_tot[0:8, :]


def remote(src, dst, send, recv, target):
    return pltpu.make_async_remote_copy(
        src_ref=src, dst_ref=dst, send_sem=send, recv_sem=recv, device_id=target,
        device_id_type=pl.DeviceIdType.MESH,
    )


def greet(targets):
    barrier = pltpu.get_barrier_semaphore()
    for target in targets:
        pl.semaphore_signal(
            barrier, inc=1, device_id=target, device_id_type=pl.DeviceIdType.MESH
        )
    return barrier


def count_rows(parts, z, gain, at, gain_grad):
    rows = jnp.zeros((parts[0].shape[0], LANE), F32)
    size = parts[0].shape[1]
    for part, k in zip(parts, at):
        lanes = pl.ds(pl.multiple_of(k * size, size), size)
        part = part * z(lanes)
        gain_grad[:, lanes] += fold(part)
        part = part * gain[0:1, lanes]
        for sl in tiles(size):
            rows = rows + part[:, sl]
    return rows


def row_dots(rows):
    ones = jnp.ones((8, LANE), BF16)
    hi, lo = two(rows)
    return dot(ones, hi, 1, 1) + dot(ones, lo, 1, 1)


def grand_kernel(heads, n, *refs):
    behind, refs = refs[:22], refs[22:]
    gate_grad, w_ref, tok, inv, gain, edge_mask, out_next = refs[:7]
    refs = refs[7:]
    in_line = n == 4
    if in_line:
        z_out, z_mid, z_mine = refs[:3]
        refs = refs[3:]
    outs, refs = refs[:9], refs[9:]
    ng_own, row_sums, gain_grad, out_last = refs[:4]
    refs = refs[4:]
    if in_line:
        z_sum, refs = refs[0], refs[1:]
    scratch, refs = refs[:4], refs[4:]
    mid, send, got, nxt, last, edge, s1, r1, s2, r2, edge_s, edge_r, o_s, o_r = refs[:14]
    if in_line:
        z_got, z_on, z_last, z_s, z_r = refs[14:]
    chan, bcpar = behind[18], behind[19]
    grad_v, tail_rows = outs[0], outs[3]
    d_tot = scratch[3]
    i, n_steps = pl.program_id(0), pl.num_programs(0)
    s, c, t = lax.axis_index("shard"), lax.axis_index("context"), lax.axis_index("tensor")
    near = peers(t)
    to = [(s, c, near[0]), (s, c, near[1])]
    width = grad_v.shape[1]
    size = w_ref.shape[0] // 4
    inside = mid.shape[0]
    chunks = grad_v.shape[0] // L

    @pl.when(i == 0)
    def _():
        pl.semaphore_wait(greet(to + beside_of(n)), 4)
        gain_grad[...] = jnp.zeros_like(gain_grad)

    def out_hop(side):
        return remote(
            out_next.at[side], out_last.at[side], o_s.at[side], o_r.at[side], to[1 - side]
        )

    @pl.when(i == 0)
    def _():
        for side in (0, 1):
            out_hop(side).start()

    if in_line:
        line = [(s, c + 1 - 2 * lax.rem(c, 2), t), (s, 3 - c, t)]
        block = z_mid.shape[1]

        def z_first(k):
            return remote(z_out.at[k], z_got.at[k], z_s.at[k], z_r.at[k], line[k])

        def z_second(k):
            return remote(z_on.at[k], z_last.at[k], z_s.at[2 + k], z_r.at[2 + k], line[1 - k])

        @pl.when(i == 0)
        def _():
            for k in (0, 1):
                z_first(k).start()

        @pl.when(i == n_steps // 2)
        def _():
            for k in (0, 1):
                z_first(k).wait()
                z_on[k] = (z_mid[k] + z_got[k, block:, :].astype(F32)).astype(BF16)
                z_second(k).start()
                z_sum[k] = z_mine[k] + z_got[k, :block, :].astype(F32)

        @pl.when(i == n_steps - 1)
        def _():
            for k in (0, 1):
                z_second(k).wait()
                z_sum[k] += z_last[k].astype(F32)

    def first_hop(k, side):
        return remote(send.at[k], got.at[k], s1.at[k], r1.at[k], to[side])

    def second_hop(k, side):
        return remote(nxt.at[k], last.at[k], s2.at[k], r2.at[k], to[1 - side])

    def place(k):
        return pl.ds(pl.multiple_of((inside - 1 - k) * PART, PART), PART)

    for j in reversed(range(chunks)):
        behind_chunk(heads, j, chunks, i == 0, i == n_steps - 1, *behind, *outs, *scratch)

    def turn_over(k, side):
        first_hop(k, side).wait()
        nxt[k] = (mid[k] + got[k, :, size:].astype(F32)).astype(BF16)
        second_hop(k, side).start()
        ng_own[place(k), :] += got[k, :, :size].astype(F32)

    def fan(side):
        counted = jnp.where(i == 0, PART - END, PART)
        x = jnp.concatenate([gate_grad[...], grad_v[...]], axis=1)
        keep, go = shares_of(side, t)
        gone = dot(x, pick(w_ref, *go), 1, 1)
        send[i] = gone.astype(BF16)
        first_hop(i, side).start()
        kept = dot(x, pick(w_ref, *keep), 1, 1)
        ng_own[place(i), :] = kept[:, :size]
        mid[i] = kept[:, size:]
        row = lax.broadcasted_iota(jnp.int32, (PART, 1), 0)
        scale = jnp.where(row < counted, inv[...], 0.0)
        parts = [kept[:, :size], kept[:, size:], gone[:, :size], gone[:, size:]]
        sums = count_rows(
            parts, lambda lanes: tok[:, lanes].astype(F32) * scale, gain, keep + go, gain_grad
        )
        row_sums[0] = row_dots(sums)

    for side in (0, 1):
        parity = lax.rem(i, 2) == 1 - side

        @pl.when(jnp.logical_and(jnp.logical_not(parity), jnp.logical_and(i > 0, i <= inside)))
        def _():
            turn_over(i - 1, side)

        @pl.when(jnp.logical_and(parity, i < inside))
        def _():
            fan(side)

    @pl.when(i == n_steps - 1)
    def _():
        before = (s, jnp.maximum(c - 1, 0), t)
        copy = remote(d_tot.at[pl.ds(0, 8), :], edge, edge_s, edge_r, before)

        @pl.when(c > 0)
        def _():
            copy.start()

        for k in range(inside):
            second_hop(k, 1 - k % 2).wait()
            ng_own[place(k), :] += last[k].astype(F32)
        for side in (0, 1):
            out_hop(side).wait()

        @pl.when(c < n - 1)
        def _():
            copy.wait_recv()
            for shift in range(1, KERNEL):
                moved = pltpu.roll(edge[...], 8 - shift, 0) * edge_mask[
                    8 * shift - 8 : 8 * shift, 0:1
                ]
                tap = slice(KERNEL - 1 - shift, KERNEL - shift)
                tail_rows[:, :width] += chan[tap, :] * moved[:, :width]
                tail_rows[:, width:] += bcpar[tap, :] * moved[:, width:]

        @pl.when(c > 0)
        def _():
            copy.wait_send()


def run_grand(
    projected, cols, halo_v, halo_b, info, marks, delta, cum, ssd, mixed_grad, sloc, pfx, entry,
    aloc, sfx, later, chan, bcpar, head, expand, heads, gate_grad, weight, tok, inv, gain, edge_mask,
    out_next, z_arrays,
):
    steps, width = ssd.shape
    parts = steps // PART
    inside = (steps - GROUP) // PART
    size = D // 4
    turn = lambda spec: pl.BlockSpec(
        spec.block_shape, lambda i, m=spec.index_map: m(parts - 1 - i)
    )
    in_part = lambda w: pl.BlockSpec((PART, w), lambda i: (parts - 1 - i, 0))
    chunk = lead_block(N, width, rows=PART)
    few = lead_block(8, width, rows=PART)
    total = width + 2 * N
    dma = pltpu.SemaphoreType.DMA
    return pl.pallas_call(
        functools.partial(grand_kernel, heads, lax.axis_size("context")),
        grid=(parts,),
        in_specs=[
            turn(row_block(width, 1, rows=PART)), turn(prev_block(width, 1, rows=PART)),
            turn(row_block(3 * N, rows=PART)), turn(prev_block(3 * N, rows=PART)),
            once(8, width), once(8, 3 * N), turn(row_block(LANE, rows=PART)),
            turn(lead_block(8, L, rows=PART)),
            turn(row_block(LANE, rows=PART)), turn(row_block(LANE, rows=PART)), turn(row_block(width, rows=PART)), turn(row_block(width, rows=PART)),
            turn(chunk), turn(few), once(N, width), turn(chunk), turn(few), once(N, width),
            once(8, width), once(8, 2 * N), once(8, LANE), once(2 * LANE, width),
            turn(row_block(width, rows=PART)), once(*weight.shape), in_part(D), in_part(1), once(8, D),
            once(24, LANE), pl.BlockSpec(memory_space=pl.ANY),
        ]
        + ([pl.BlockSpec(memory_space=pl.ANY)] + [once(*z.shape) for z in z_arrays[1:]] if z_arrays else []),
        out_specs=[
            turn(row_block(width, rows=PART)), turn(row_block(2 * N, rows=PART)),
            pl.BlockSpec((16, PART), lambda i: (0, parts - 1 - i)),
            whole(8, total), whole(8, total), whole(8 * KERNEL, total), whole(8, total),
            whole(8, width), whole(16, LANE),
            once(inside * PART, size),
            pl.BlockSpec((1, 8, PART), lambda i: (parts - 1 - i, 0, 0)),
            whole(8, D), pl.BlockSpec(memory_space=pl.ANY),
        ]
        + [once(*z.shape) for z in z_arrays[1:2]],
        out_shape=[
            shape(steps, width, dtype=BF16), shape(steps, 2 * N), shape(16, steps, dtype=BF16),
            shape(8, total), shape(8, total), shape(8 * KERNEL, total), shape(8, total),
            shape(8, width), shape(16, LANE),
            shape(inside * PART, size), shape(parts, 8, PART), shape(8, D),
            shape(*out_next.shape, dtype=BF16),
        ]
        + [shape(*z.shape) for z in z_arrays[1:2]],
        scratch_shapes=[
            pltpu.VMEM((8 + L, width), F32), pltpu.VMEM((8 + L, 3 * N), F32),
            pltpu.VMEM((L, total), F32), pltpu.VMEM((L + 8, total), F32),
            pltpu.VMEM((inside, PART, size), F32),
            pltpu.VMEM((inside, PART, 2 * size), BF16), pltpu.VMEM((inside, PART, 2 * size), BF16),
            pltpu.VMEM((inside, PART, size), BF16), pltpu.VMEM((inside, PART, size), BF16),
            pltpu.VMEM((8, total), F32),
            dma((inside,)), dma((inside,)), dma((inside,)), dma((inside,)), dma, dma,
            dma((2,)), dma((2,)),
        ]
        + (
            [
                pltpu.VMEM(z_arrays[0].shape, BF16), pltpu.VMEM(z_arrays[1].shape, BF16),
                pltpu.VMEM(z_arrays[1].shape, BF16), dma((4,)), dma((4,)),
            ]
            if z_arrays
            else []
        ),
        compiler_params=pltpu.CompilerParams(
            dimension_semantics=("arbitrary",), vmem_limit_bytes=52 * 1024 * 1024,
            collective_id=4, has_side_effects=True,
        ),
        cost_estimate=estimate(90),
        name="behind",
    )(
        projected, projected, cols, cols, halo_v, halo_b, info, marks, delta, cum, ssd, mixed_grad,
        sloc, pfx, entry, aloc, sfx, later, chan, bcpar, head, expand,
        gate_grad, weight, tok, inv, gain, edge_mask, out_next, *z_arrays,
    )


def peers(t):
    return t + 1 - 2 * lax.rem(t, 2), lax.rem(t + 2, 4)


def pick(w_ref, one, other):
    size = w_ref.shape[0] // 4
    at = lambda k: pl.ds(pl.multiple_of(k * size, size), size)
    return jnp.concatenate([w_ref[at(one), :], w_ref[at(other), :]], axis=0)


def shares_of(side, t):
    near = peers(t)
    return (t, near[1 - side]), (near[side], 3 - t)


def out_kernel(
    ssd, gate, sums, chan, w_ref, scaled, own, mid, send_a, send_b,
):
    i, half = pl.program_id(0), pl.num_programs(0) // 2
    t = lax.axis_index("tensor")
    width = ssd.shape[1]
    for k in range(ssd.shape[0] // L):
        rows = slice(k * L, (k + 1) * L)
        inv = jnp.broadcast_to(lax.rsqrt(sums[k, 0:1, :] / INNER + EPS), (LANE, L)).T
        for sl in tiles(width):
            g = gate[rows, sl]
            gated = ssd[rows, sl] * g * sigmoid(g)
            scaled[rows, sl] = (gated * inv * chan[KERNEL + 1 : KERNEL + 2, sl]).astype(BF16)
    x = scaled[...]
    size = own.shape[1]

    def part(side, send):
        keep, go = shares_of(side, t)
        send[...] = dot(x, pick(w_ref, *go), 1, 1).astype(BF16)
        kept = dot(x, pick(w_ref, *keep), 1, 1)
        own[...] = kept[:, :size]
        mid[...] = kept[:, size:]

    @pl.when(i < half)
    def _():
        part(0, send_a)

    @pl.when(i >= half)
    def _():
        part(1, send_b)


def run_out(ssd, projected, sums, chan, weight):
    steps, width = ssd.shape
    block = 512
    count = steps // block
    half = count // 2
    size = D // 4
    in_block = lambda w, col=0: pl.BlockSpec((block, w), lambda i: (i, col))
    return pl.pallas_call(
        out_kernel,
        grid=(count,),
        in_specs=[
            in_block(width), in_block(width, 0),
            pl.BlockSpec((block // L, 8, L), lambda i: (i, 0, 0)),
            whole(8, width), whole(*weight.shape),
        ],
        out_specs=[
            in_block(width), in_block(size), in_block(size),
            pl.BlockSpec((block, 2 * size), lambda i: (jnp.minimum(i, half - 1), 0)),
            pl.BlockSpec((block, 2 * size), lambda i: (jnp.maximum(i - half, 0), 0)),
        ],
        out_shape=[
            shape(steps, width, dtype=BF16), shape(steps, size), shape(steps, size),
            shape(steps // 2, 2 * size, dtype=BF16), shape(steps // 2, 2 * size, dtype=BF16),
        ],
        compiler_params=params(),
        cost_estimate=estimate(12),
        name="out",
    )(ssd, projected, sums, chan, weight)


def line_kernel(
    n, n_tensor, piece, zx_ref, cols_ref, zx_out, cols_out,
    local, zx_s, zx_r, core_s, core_r, col_s, col_r, group_s, group_r, bulk_s, bulk_r,
):
    s, c, t = lax.axis_index("shard"), lax.axis_index("context"), lax.axis_index("tensor")
    on = (c < n - 1, c > 0)
    to = ((s, jnp.minimum(c + 1, n - 1), t), (s, jnp.maximum(c - 1, 0), t))
    to_core = (1 - s, c, t)
    to_group = [(s, c, lax.rem(t + k, n_tensor)) for k in range(1, n_tensor)]
    beside = [(s, lax.rem(c + k, n), t) for k in (1, n - 1)]
    pl.semaphore_wait(greet([to_core] + to_group + beside), n_tensor + 2)
    rows, width = zx_ref.shape[0], cols_ref.shape[1]
    spans = [(at, min(piece, rows - at)) for at in range(0, rows, piece)]

    def block_of(way, hop):
        return jnp.maximum(c - hop, 0) if way == 0 else jnp.minimum(c + hop, n - 1)

    def has(way, hop):
        return c - hop >= 0 if way == 0 else c + hop <= n - 1

    def place(ref, block, at=0, size=rows):
        return ref.at[pl.ds(pl.multiple_of((s * n + block) * rows + at, 16), size), :]

    lanes = pl.ds(pl.multiple_of(t * width, LANE), width)

    def place_cols(block):
        return cols_out.at[pl.ds(pl.multiple_of((s * n + block) * rows, 16), rows), lanes]

    def zx_copy(way, step, p):
        at, size = spans[p]
        where = place(zx_out, block_of(way, step), at, size)
        src = zx_ref.at[pl.ds(at, size), :] if step == 0 else where
        return remote(src, where, zx_s.at[way, step, p], zx_r.at[way, step, p], to[way])

    def col_copy(way, step):
        where = place_cols(block_of(way, step))
        src = cols_ref if step == 0 else where
        return remote(src, where, col_s.at[way, step], col_r.at[way, step], to[way])

    def group_copies(way, hop):
        where = place_cols(block_of(way, hop))
        src = cols_ref if hop == 0 else where
        return [
            remote(src, where, group_s.at[k, way, hop], group_r.at[k, way, hop], target)
            for k, target in enumerate(to_group)
        ]

    def core_copy(way, hop, p):
        at, size = spans[p]
        where = place(zx_out, block_of(way, hop), at, size)
        src = zx_ref.at[pl.ds(at, size), :] if hop == 0 else where
        return remote(src, where, core_s.at[way, hop, p], core_r.at[way, hop, p], to_core)

    pieces = range(len(spans))
    for way in (0, 1):

        @pl.when(on[way])
        def _():
            col_copy(way, 0).start()
            for p in pieces:
                zx_copy(way, 0, p).start()

    for copy in group_copies(0, 0):
        copy.start()
    own_cols = pltpu.make_async_copy(cols_ref, place_cols(c), local.at[0])
    own_zx = pltpu.make_async_copy(zx_ref, place(zx_out, c), local.at[1])
    own_cols.start()
    own_zx.start()
    for p in pieces:
        core_copy(0, 0, p).start()
    start = pl.ds(pl.multiple_of(s * n * rows, 16), n * rows)
    bulk = remote(cols_out.at[start, :], cols_out.at[start, :], bulk_s, bulk_r, to_core)
    for step in range(n - 1):
        further = step < n - 2
        for way in (0, 1):

            @pl.when(has(way, step + 1))
            def _():
                col_copy(way, step).wait_recv()
                for copy in group_copies(way, step + 1):
                    copy.start()
                if further:

                    @pl.when(on[way])
                    def _():
                        col_copy(way, step + 1).start()

        if not further:
            own_cols.wait()
            for copy in group_copies(0, 0):
                copy.wait()
            for hop in range(1, n):
                for way in (0, 1):

                    @pl.when(has(way, hop))
                    def _():
                        for copy in group_copies(way, hop):
                            copy.wait()

            bulk.start()
        for p in pieces:
            for way in (0, 1):

                @pl.when(has(way, step + 1))
                def _():
                    zx_copy(way, step, p).wait_recv()
                    core_copy(way, step + 1, p).start()
                    if further:

                        @pl.when(on[way])
                        def _():
                            zx_copy(way, step + 1, p).start()

    for step in range(n - 1):
        for way in (0, 1):

            @pl.when(jnp.logical_and(on[way], has(way, step)))
            def _():
                col_copy(way, step).wait_send()
                for p in pieces:
                    zx_copy(way, step, p).wait_send()

            @pl.when(has(way, step + 1))
            def _():
                for p in pieces:
                    core_copy(way, step + 1, p).wait()

    for p in pieces:
        core_copy(0, 0, p).wait()
    bulk.wait()
    own_zx.wait()


PIECE = 64


def line_gather(zx, cols):
    n, n_tensor = lax.axis_size("context"), lax.axis_size("tensor")
    rows = zx.shape[0]
    pieces = -(-rows // PIECE)
    dma = pltpu.SemaphoreType.DMA
    return pl.pallas_call(
        functools.partial(line_kernel, n, n_tensor, PIECE),
        in_specs=[pl.BlockSpec(memory_space=pl.ANY)] * 2,
        out_specs=[pl.BlockSpec(memory_space=pl.ANY)] * 2,
        out_shape=[
            shape(2 * n * rows, zx.shape[1], dtype=BF16),
            shape(2 * n * rows, n_tensor * cols.shape[1], dtype=BF16),
        ],
        scratch_shapes=[
            dma((2,)), dma((2, n - 1, pieces)), dma((2, n - 1, pieces)),
            dma((2, n, pieces)), dma((2, n, pieces)), dma((2, n - 1)), dma((2, n - 1)),
            dma((n_tensor - 1, 2, n)), dma((n_tensor - 1, 2, n)), dma, dma,
        ],
        compiler_params=pltpu.CompilerParams(collective_id=0, has_side_effects=True),
        name="line_gather",
    )(zx, cols)


def small_sum_kernel(n, x_ref, o_ref, held, send, recv):
    s, c, t = lax.axis_index("shard"), lax.axis_index("context"), lax.axis_index("tensor")
    targets = [(s, c, lax.rem(t + k, n)) for k in range(1, n)]
    pl.semaphore_wait(greet(targets), n - 1)
    copies = [
        remote(x_ref, held.at[k], send.at[k], recv.at[k], target)
        for k, target in enumerate(targets)
    ]
    for copy in copies:
        copy.start()
    total = x_ref[...]
    for k, copy in enumerate(copies):
        copy.wait()
        total = total + held[k]
    o_ref[...] = total


def small_sum(x, collective_id):
    n = lax.axis_size("tensor")
    return pl.pallas_call(
        functools.partial(small_sum_kernel, n),
        in_specs=[pl.BlockSpec(memory_space=pltpu.VMEM)],
        out_specs=pl.BlockSpec(memory_space=pltpu.VMEM),
        out_shape=shape(*x.shape),
        scratch_shapes=[
            pltpu.VMEM((n - 1, *x.shape), F32),
            pltpu.SemaphoreType.DMA((n - 1,)), pltpu.SemaphoreType.DMA((n - 1,)),
        ],
        compiler_params=pltpu.CompilerParams(collective_id=collective_id, has_side_effects=True),
        cost_estimate=estimate(7),
        name="small_sum",
    )(x)


SLICES = 8


class Chain:
    def __init__(self, n, backward, packed, entering, got, sent, send_sem, recv_sem):
        s, c, t = lax.axis_index("shard"), lax.axis_index("context"), lax.axis_index("tensor")
        self.from_other = c < n - 1 if backward else c > 0
        self.to_other = c > 0 if backward else c < n - 1
        ahead = jnp.maximum(c - 1, 0) if backward else jnp.minimum(c + 1, n - 1)
        self.target = (s, ahead, t)
        self.refs = packed, entering, got, sent, send_sem, recv_sem

    def copy(self, j):
        _, _, got, sent, send_sem, recv_sem = self.refs
        rows = pl.ds(j * (N // SLICES), N // SLICES)
        return remote(sent.at[rows, :], got.at[rows, :], send_sem.at[j], recv_sem.at[j], self.target)

    def step(self, j):
        packed, entering, got, sent, _, _ = self.refs
        rows = slice(j * (N // SLICES), (j + 1) * (N // SLICES))

        @pl.when(self.from_other)
        def _():
            self.copy(j).wait_recv()
            entering[rows, :] = got[rows, :]

        @pl.when(jnp.logical_not(self.from_other))
        def _():
            entering[rows, :] = jnp.zeros((N // SLICES, packed.shape[1]), F32)

        @pl.when(self.to_other)
        def _():
            sent[rows, :] = packed[rows, :] + packed[N : N + 1, :] * entering[rows, :]
            self.copy(j).start()

    def finish(self):
        @pl.when(self.to_other)
        def _():
            for j in range(SLICES):
                self.copy(j).wait_send()


def beside_of(n):
    s, c, t = lax.axis_index("shard"), lax.axis_index("context"), lax.axis_index("tensor")
    return [(s, lax.rem(c + k, n), t) for k in (1, n - 1)]


def entry_kernel(
    n, packed, back, w_hbm, entry, out, turned, bk, w_ref, buf, turn, got, sent, load_sem, out_sem,
    turn_sem, chain_s, chain_r,
):
    block = buf.shape[1]
    count = back.shape[0] // block
    load_w = pltpu.make_async_copy(w_hbm, w_ref, load_sem.at[count])
    load_w.start()

    def load(k):
        rows = pl.ds(k * block, block)
        return pltpu.make_async_copy(back.at[rows, :], bk.at[rows, :], load_sem.at[k])

    def store(k):
        return pltpu.make_async_copy(
            buf.at[k % 2], out.at[pl.ds(k * block, block), :], out_sem.at[k % 2]
        )

    def store_turned(k):
        return pltpu.make_async_copy(
            turn.at[k % 2], turned.at[:, pl.ds(k * block, block)], turn_sem.at[k % 2]
        )

    for k in range(count):
        load(k).start()
    pl.semaphore_wait(greet(beside_of(n)), 2)
    chain = Chain(n, False, packed, entry, got, sent, chain_s, chain_r)
    load_w.wait()
    for k in range(count):
        load(k).wait()
        if k >= 2:
            store(k - 2).wait()
            store_turned(k - 2).wait()
        rows = bk[k * block : (k + 1) * block, :]
        buf[k % 2] = dot(rows, w_ref[...])
        store(k).start()
        turn[k % 2] = rows.T
        store_turned(k).start()
        if k < SLICES:
            chain.step(k)
    for k in range(count, SLICES):
        chain.step(k)
    chain.finish()
    for k in range(max(count - 2, 0), count):
        store(k).wait()
        store_turned(k).wait()


def run_entry(packed, back, weight):
    n = lax.axis_size("context")
    steps, width = back.shape[0], weight.shape[1]
    block = 256
    dma = pltpu.SemaphoreType.DMA
    vmem = pltpu.VMEM
    inside = pl.BlockSpec(memory_space=pltpu.VMEM)
    hbm = pl.BlockSpec(memory_space=pl.ANY)
    return pl.pallas_call(
        functools.partial(entry_kernel, n),
        in_specs=[inside, hbm, hbm],
        out_specs=[inside, hbm, hbm],
        out_shape=[shape(N, width), shape(steps, width), shape(D, steps, dtype=BF16)],
        scratch_shapes=[
            vmem(back.shape, BF16), vmem(weight.shape, BF16), vmem((2, block, width), F32),
            vmem((2, D, block), BF16), vmem((N, width), F32), vmem((N, width), F32),
            dma((steps // block + 1,)), dma((2,)), dma((2,)), dma((SLICES,)), dma((SLICES,)),
        ],
        compiler_params=pltpu.CompilerParams(
            vmem_limit_bytes=40 * 1024 * 1024, collective_id=6, has_side_effects=True
        ),
        cost_estimate=estimate(15),
        name="entry",
    )(packed, back, weight)


def middle_kernel(
    n, packed, send_a, send_b, mid_hbm, own_hbm, normed_hbm, gate_hbm, back_hbm, scaled_hbm, *refs
):
    if n == 4:
        later, own, next_out, z_out, z_mid, z_mine = refs[:6]
        refs = refs[6:]
    else:
        later, own, next_out, both_out = refs[:4]
        refs = refs[4:]
    (
        mid, nm, gg, bk, sc, peer_part, core_part, own_part, got, chain_got, chain_sent,
        local, core_s, core_r, f_s, f_r, chain_s, chain_r,
    ) = refs
    s, c, t = lax.axis_index("shard"), lax.axis_index("context"), lax.axis_index("tensor")
    near = peers(t)
    to = [(s, c, near[0]), (s, c, near[1])]
    to_core = (1 - s, c, t)
    loads = [
        pltpu.make_async_copy(src, dst, local.at[k])
        for k, (src, dst) in enumerate(
            [
                (normed_hbm, nm), (gate_hbm, gg), (back_hbm, bk), (scaled_hbm, sc),
                (mid_hbm, mid), (own_hbm, own),
            ]
        )
    ]
    for load in loads:
        load.start()
    pl.semaphore_wait(greet(to + [to_core] + beside_of(n)), 5)
    hops = [
        remote(src, got.at[side], f_s.at[side], f_r.at[side], to[side])
        for side, src in enumerate((send_a, send_b))
    ]
    for hop in hops:
        hop.start()
    chain = Chain(n, True, packed, later, chain_got, chain_sent, chain_s, chain_r)
    half_d = nm.shape[0] // 2
    steps = nm.shape[1]
    step = 256
    pairs = ((nm, gg), (bk, sc))

    def product(which, shard, into, m):
        left, right = pairs[which]
        rows = pl.ds(pl.multiple_of(shard * half_d + m * step, step), step)
        into[which, m * step : (m + 1) * step, :] = dot(left[rows, :], right[...])

    cores = [
        remote(peer_part.at[k], core_part.at[k], core_s.at[k], core_r.at[k], to_core) for k in (0, 1)
    ]
    chain.step(0)
    done = 1
    for which in (0, 1):
        loads[2 * which].wait()
        loads[2 * which + 1].wait()
        for m in range(half_d // step):
            product(which, 1 - s, peer_part, m)
            if done < SLICES:
                chain.step(done)
                done += 1
        cores[which].start()
    for which in (0, 1):
        for m in range(half_d // step):
            product(which, s, own_part, m)
            if done < SLICES:
                chain.step(done)
                done += 1
    chain.finish()
    block = half_d // n

    for which in (0, 1):
        cores[which].wait()
        if n == 4:
            first = c + 1 - 2 * lax.rem(c, 2) if which == 0 else 3 - c
            third = 3 - c if which == 0 else c + 1 - 2 * lax.rem(c, 2)

            def total(k):
                rows = pl.ds(pl.multiple_of(k * block, 8), block)
                return own_part[which, rows, :] + core_part[which, rows, :]

            z_out[which, :block, :] = total(first).astype(BF16)
            z_out[which, block:, :] = total(lax.rem(c + 2, 4)).astype(BF16)
            z_mid[which] = total(third)
            z_mine[which] = total(c)
        else:
            both_out[which] = own_part[which] + core_part[which]
    loads[4].wait()
    loads[5].wait()
    size = mid.shape[1]
    half = steps // 2
    for side in (0, 1):
        hops[side].wait()
        for k in range(half // step):
            rows = slice(k * step, (k + 1) * step)
            at = slice(side * half + k * step, side * half + (k + 1) * step)
            next_out[side, rows, :] = (mid[at, :] + got[side, rows, size:].astype(F32)).astype(BF16)
            own[at, :] += got[side, rows, :size].astype(F32)


def run_middle(packed, fan, normed, gate_grad, back, scaled):
    n = lax.axis_size("context")
    own, mid, send_a, send_b = fan
    steps, width = gate_grad.shape
    size = own.shape[1]
    half_d = D // 2
    block = half_d // n
    dma = pltpu.SemaphoreType.DMA
    vmem = pltpu.VMEM
    inside = pl.BlockSpec(memory_space=pltpu.VMEM)
    hbm = pl.BlockSpec(memory_space=pl.ANY)
    if n == 4:
        more = [
            shape(2, 2 * block, width, dtype=BF16), shape(2, block, width), shape(2, block, width)
        ]
    else:
        more = [shape(2, half_d, width)]
    pair = (2, half_d, width)
    return pl.pallas_call(
        functools.partial(middle_kernel, n),
        in_specs=[inside] + [hbm] * 8,
        out_specs=[inside] * (3 + len(more)),
        out_shape=[shape(N, width), shape(steps, size), shape(2, steps // 2, size, dtype=BF16)] + more,
        scratch_shapes=[
            vmem((steps, size), F32), vmem(normed.shape, BF16), vmem(gate_grad.shape, BF16),
            vmem(back.shape, BF16), vmem(scaled.shape, BF16),
            vmem(pair, F32), vmem(pair, F32), vmem(pair, F32), vmem((2, steps // 2, 2 * size), BF16),
            vmem((N, width), F32), vmem((N, width), F32),
            dma((6,)), dma((2,)), dma((2,)), dma((2,)), dma((2,)), dma((SLICES,)), dma((SLICES,)),
        ],
        compiler_params=pltpu.CompilerParams(
            vmem_limit_bytes=54 * 1024 * 1024, collective_id=7, has_side_effects=True
        ),
        cost_estimate=estimate(35),
        name="middle",
    )(packed, send_a, send_b, mid, own, normed, gate_grad, back, scaled)


def adam_kernel(heads, cols_loc, gate_g, value_g, down_g, cols_g, packed, *refs):
    zx, out, bcdt, gain, chan, bc, head = [refs[3 * k : 3 * k + 3] for k in range(7)]
    refs = refs[21:]
    zx_new, out_new, bcdt_new, gain_new, chan_new, bc_new, head_new = [
        refs[3 * k : 3 * k + 3] for k in range(7)
    ]
    width = gate_g.shape[1]

    def put(news, olds, grad, rate, decay, at=(Ellipsis,)):
        for ref, val in zip(news, adamw(olds[0][at], grad, olds[1][at], olds[2][at], rate, decay)):
            ref[at] = val

    for k, grad in enumerate((gate_g, value_g)):
        put(zx_new, zx, grad[...], RATE_MATRIX, DECAY, (slice(None), k, slice(None)))
    put(out_new, out, down_g[...], RATE_MATRIX, DECAY)
    put(bcdt_new, bcdt, cols_g[...].T[:cols_loc, :], RATE_MATRIX, DECAY)
    over = packed[0] + packed[1] + packed[2] + packed[3]
    put(gain_new, gain, over[KERNEL + 5 : KERNEL + 6, :], RATE_SMALL, 0.0)
    put(bc_new, bc, over[: KERNEL + 1, width : width + 2 * N], RATE_SMALL, 0.0)
    grad = jnp.concatenate([packed[k, : KERNEL + 2, :width] for k in range(4)], axis=1)
    put(chan_new, chan, grad, RATE_SMALL, 0.0)
    lane = lax.broadcasted_iota(jnp.int32, (LANE, 4 * heads), 0)
    slot = lax.broadcasted_iota(jnp.int32, (LANE, 4 * heads), 1)
    channel = lax.broadcasted_iota(jnp.int32, (width, 4 * heads), 0)
    wide_slot = lax.broadcasted_iota(jnp.int32, (width, 4 * heads), 1)
    rows = jnp.zeros((8, 4 * heads), F32)
    for k in range(4):
        here = jnp.where(lane + k * heads == slot, 1.0, 0.0)
        here = jnp.where(lane < heads, here, 0.0).astype(BF16)
        wide = jnp.where(channel // P_SIZE + k * heads == wide_slot, 1.0, 0.0).astype(BF16)
        hi, lo = two(packed[k, KERNEL + 3 : KERNEL + 11, :LANE])
        at = lax.broadcasted_iota(jnp.int32, rows.shape, 0)
        rows = rows + jnp.where(at < 2, dot(hi, here) + dot(lo, here), 0.0)
        hi, lo = two(packed[k, KERNEL + 2 : KERNEL + 10, :width])
        skip = dot(hi, wide) + dot(lo, wide)
        rows = rows + jnp.where(at == 2, jnp.broadcast_to(skip[0:1, :], rows.shape), 0.0)
    put(head_new, head, rows[:3, :], RATE_SMALL, 0.0)


def run_adam(grads, olds, heads, cols_loc):
    flat = [x for group in olds for x in group]
    return pl.pallas_call(
        functools.partial(adam_kernel, heads, cols_loc),
        in_specs=[pl.BlockSpec(memory_space=pltpu.VMEM)] * (len(grads) + len(flat)),
        out_specs=[pl.BlockSpec(memory_space=pltpu.VMEM)] * len(flat),
        out_shape=[shape(*x.shape) for x in flat],
        compiler_params=pltpu.CompilerParams(vmem_limit_bytes=40 * 1024 * 1024),
        cost_estimate=estimate(8),
        name="optimizer",
    )(*grads, *flat)


def doc_of(lengths, position):
    found = jnp.zeros(position.shape, F32)
    end = 0
    for k in range(lengths.shape[1] - 1):
        end = end + lengths[0, k]
        found = found + jnp.where(position >= end, 1.0, 0.0)
    return jnp.where(position < 0, -1.0, found)


def mark_chunk(lengths, begin, limit, info_ref, marks_ref):
    row = lax.broadcasted_iota(jnp.int32, (L, LANE), 0)
    lane = lax.broadcasted_iota(jnp.int32, (L, LANE), 1)
    offset = jnp.where(lane < KERNEL - 1, lane - KERNEL + 1, jnp.where(lane >= 8, lane - 7, 0))
    other = jnp.where(lane == 3, -1, jnp.where(lane == 4, L - 1, row + offset)) + begin
    mark = doc_of(lengths, row + begin)
    same = jnp.logical_and(doc_of(lengths, other) == mark, other < limit)
    info = jnp.where(same, 1.0, 0.0)
    info_ref[...] = jnp.where(lane == 5, mark, jnp.where(lane < 7 + KERNEL, info, 0.0))
    marks_ref[0] = doc_of(lengths, begin + lax.broadcasted_iota(jnp.int32, (8, L), 1))


def norm_rows(tok, gain):
    x = tok.astype(F32)
    square = x * x
    total = square[:, :LANE]
    for sl in tiles(D)[1:]:
        total = total + square[:, sl]
    inv = lax.rsqrt(jnp.sum(total, axis=1, keepdims=True) / D + EPS)
    return (x * inv * gain[0:1, :]).astype(BF16), inv


def project_kernel(
    heads, n, cols_loc, lengths, tok, tok_end, gain, w_ref, wg_ref, chan, bcpar, head, e_ref,
    normed, normed_t, inv, projected, cols, info, marks, edge_mask, act, delta, cum, sloc, pfx, fin,
    halo_v, halo_b, ext_v, ext_b, state, prod, w_cols, prev_v, prev_b, halo_out, halo_got, h_s, h_r,
):
    i = pl.program_id(0)
    s, c, t = lax.axis_index("shard"), lax.axis_index("context"), lax.axis_index("tensor")
    width = w_ref.shape[1] // 2
    block = tok.shape[0]
    steps = block * pl.num_programs(0)
    start = c * steps
    after = (s, jnp.minimum(c + 1, n - 1), t)
    halo = remote(halo_out, halo_got, h_s, h_r, after)

    @pl.when(i == 0)
    def _():
        pl.semaphore_wait(greet(beside_of(n)), 2)
        state[...] = jnp.zeros_like(state)
        prod[...] = jnp.ones_like(prod)
        lane = lax.broadcasted_iota(jnp.int32, (4 * LANE, 3 * N), 0)
        want = lax.broadcasted_iota(jnp.int32, (4 * LANE, 3 * N), 1)
        have = lane // LANE * cols_loc + lane % LANE
        want = jnp.where(want < 2 * N, want, jnp.where(want < 2 * N + heads, want + heads * t, -1))
        chosen = jnp.logical_and(have == want, lane % LANE < cols_loc)
        select = jnp.where(chosen, 1.0, 0.0).astype(BF16)
        for k in range(0, D, block):
            w_cols[k : k + block, :] = dot(wg_ref[k : k + block, :], select).astype(BF16)
        ends, _ = norm_rows(tok_end[...], gain)
        halo_out[:, :width] = dot(ends, w_ref[:, width:])[8:, :]
        halo_out[:, width:] = dot(ends, w_cols[...])[8:, :]

        @pl.when(c < n - 1)
        def _():
            halo.start()

        row = lax.broadcasted_iota(jnp.int32, (24, LANE), 0)
        shift, at = row // 8 + 1, row % 8
        there = at - 8 + shift + start + steps
        agree = doc_of(lengths, there) == doc_of(lengths, there - shift)
        edge_mask[...] = jnp.where(jnp.logical_and(at >= 8 - shift, agree), 1.0, 0.0)

    for j in range(block // L):
        rows = slice(j * L, (j + 1) * L)
        x, scale = norm_rows(tok[rows, :], gain)
        normed[rows, :] = x
        inv[rows, :] = scale
        normed_t[:, rows] = x.T
    for k in range(0, 2 * width, 512):
        projected[:, k : k + 512] = dot(normed[...], w_ref[:, k : k + 512])
    cols[...] = dot(normed[...], w_cols[...])

    @pl.when(i == 0)
    def _():
        @pl.when(c > 0)
        def _():
            halo.wait_recv()
            halo_v[...] = halo_got[:, :width]
            halo_b[...] = halo_got[:, width:]

        @pl.when(c == 0)
        def _():
            halo_v[...] = jnp.zeros_like(halo_v)
            halo_b[...] = jnp.zeros_like(halo_b)

        @pl.when(c < n - 1)
        def _():
            halo.wait_send()

    val = projected.at[:, pl.ds(width, width)]

    for j in range(block // L):
        first = i == 0
        mark_chunk(
            lengths, start + i * block + j * L, start + steps, rows_at(info, j), lead_at(marks, j)
        )
        load_ext(ext_v, val, prev_v, halo_v, j, first)
        load_ext(ext_b, cols, prev_b, halo_b, j, first)
        prep_chunk(
            rows_at(cols, j), rows_at(info, j), chan, bcpar, head, e_ref, rows_at(act, j),
            rows_at(delta, j), rows_at(cum, j), lead_at(sloc, j), lead_at(pfx, j),
            ext_v, ext_b, state, prod,
        )
    prev_v[...] = projected[block - 8 :, width:]
    prev_b[...] = cols[block - 8 :, :]

    @pl.when(i == pl.num_programs(0) - 1)
    def _():
        fin[:N, :] = state[...]
        fin[N:, :] = prod[...]


def run_project(lengths, tok, gain, weight, w_group, chan, bcpar, head, expand, heads, cols_loc):
    steps, width = tok.shape[0], weight.shape[1] // 2
    count = steps // L
    dma = pltpu.SemaphoreType.DMA
    return pl.pallas_call(
        functools.partial(project_kernel, heads, lax.axis_size("context"), cols_loc),
        grid=(steps // GROUP,),
        in_specs=[
            pl.BlockSpec(memory_space=pltpu.SMEM), row_block(D),
            pl.BlockSpec((16, D), lambda i: (steps // 16 - 1, 0), pipeline_mode=pl.Buffered(1)),
            once(8, D), once(*weight.shape), once(*w_group.shape),
            once(8, width), once(8, 2 * N), once(8, LANE), once(2 * LANE, width),
        ],
        out_specs=[
            row_block(D), pl.BlockSpec((D, GROUP), lambda i: (0, i)), row_block(1),
            row_block(2 * width), row_block(3 * N), row_block(LANE), lead_block(8, L), once(24, LANE),
            row_block(width + 2 * N), row_block(LANE), row_block(LANE), lead_block(N, width),
            lead_block(8, width), once(N + 8, width), once(8, width), once(8, 3 * N),
        ],
        out_shape=[
            shape(steps, D, dtype=BF16), shape(D, steps, dtype=BF16), shape(steps, 1),
            shape(steps, 2 * width), shape(steps, 3 * N), shape(steps, LANE), shape(count, 8, L),
            shape(24, LANE),
            shape(steps, width + 2 * N), shape(steps, LANE), shape(steps, LANE),
            shape(count, N, width), shape(count, 8, width), shape(N + 8, width), shape(8, width),
            shape(8, 3 * N),
        ],
        scratch_shapes=[
            pltpu.VMEM((8 + L, width), F32), pltpu.VMEM((8 + L, 3 * N), F32),
            pltpu.VMEM((N, width), F32), pltpu.VMEM((8, width), F32),
            pltpu.VMEM((D, 3 * N), BF16), pltpu.VMEM((8, width), F32), pltpu.VMEM((8, 3 * N), F32),
            pltpu.VMEM((8, width + 3 * N), F32), pltpu.VMEM((8, width + 3 * N), F32), dma, dma,
        ],
        compiler_params=pltpu.CompilerParams(
            dimension_semantics=("arbitrary",), vmem_limit_bytes=48 * 1024 * 1024,
            collective_id=8, has_side_effects=True,
        ),
        cost_estimate=estimate(45),
        name="project",
    )(lengths, tok, tok, gain, weight, w_group, chan, bcpar, head, expand)


PACK = 16


def tail_kernel(
    n, grad_b, grad_v, normed_hbm, w_hbm, tok_hbm, back_hbm, late_hbm, wg_hbm,
    raw_t, fixed, gate_top, gate_end, tok_top, tok_end, inv, gain, gain_mine, sel_bc, sel_raw,
    late_rows, late_gain, taps_grad, bias_grad, norm_gain_grad, skip_grad, head_grad,
    tokens_out, value_out, cols_out, pack_out,
    gb, gv, nm, w_ref, tok, back, w_cols, col_grad,
    peer_part, own_part, core_part, b_got, b_next, b_last, b_full, raw_full,
    early, mid, send, got, nxt, last, gain_grad, z_out, z_got, z_on, z_last,
    ng, col_peer, col_own, col_core, col_out, col_got, col_on, col_last,
    row_buf, row_held, pack, pack_other, pack_pair, pack_pieces, pack_total, pack_all,
    local, raw_s, raw_r, b_s, b_r, f_s, f_r, core_s, core_r, z_s, z_r, row_s, row_r,
    sum_s, sum_r, piece_s, piece_r, group_s, group_r,
):
    s, c, t = lax.axis_index("shard"), lax.axis_index("context"), lax.axis_index("tensor")
    near = peers(t)
    to = [(s, c, near[0]), (s, c, near[1])]
    group = [(s, c, lax.rem(t + k, 4)) for k in (1, 2, 3)]
    to_core = (1 - s, c, t)
    to_piece = [(s, lax.rem(c + k, n), t) for k in range(1, n)]
    in_line = n == 4
    line = [(s, c + 1 - 2 * lax.rem(c, 2), t), (s, 3 - c, t)] if in_line else []
    steps, width = grad_v.shape
    size = w_ref.shape[0] // 4
    share = steps // 4
    mine_lanes = pl.ds(pl.multiple_of(t * size, size), size)
    loads = [
        pltpu.make_async_copy(src, dst, local.at[k])
        for k, (src, dst) in enumerate(
            [
                (grad_b, gb), (grad_v, gv), (normed_hbm, nm), (w_hbm, w_ref),
                (tok_hbm.at[:, mine_lanes], tok), (back_hbm.at[:, mine_lanes], back),
                (late_hbm, ng.at[pl.ds(GROUP, steps - GROUP), :]),
                (wg_hbm.at[mine_lanes, :], w_cols),
            ]
        )
    ]
    for load in loads:
        load.start()
    pl.semaphore_wait(greet(group + [to_core] + to_piece), n + 3)

    raw_full[t] = raw_t[...]
    raws = [
        remote(raw_t, raw_full.at[t], raw_s.at[k], raw_r.at[k], target)
        for k, target in enumerate(group)
    ]
    for copy in raws:
        copy.start()

    def rows_of(k):
        return pl.ds(pl.multiple_of(k * share, share), share)

    def lanes_of(side):
        return pl.ds(side * N, N)

    loads[0].wait()
    gb[steps - 8 :, :] = fixed[:, width:]

    def b_first(side, part):
        k = near[side] if part == 0 else 3 - t
        return remote(
            gb.at[rows_of(k), lanes_of(side)], b_got.at[side, part], b_s.at[side, part],
            b_r.at[side, part], to[side],
        )

    def b_second(side):
        return remote(
            b_next.at[side], b_last.at[side], b_s.at[side, 2], b_r.at[side, 2], to[1 - side]
        )

    def b_back(side, part):
        k = near[1 - side] if part == 2 else t
        where = b_full.at[rows_of(k), lanes_of(side)]
        return remote(
            where, where, b_s.at[side, 3 + part], b_r.at[side, 3 + part],
            to[1 - side] if part == 0 else to[side],
        )

    for side in (0, 1):
        for part in (0, 1):
            b_first(side, part).start()

    loads[1].wait()
    tail = gv[steps - 16 :, :].astype(F32)
    gv[steps - 16 :, :] = jnp.concatenate([tail[:8], fixed[:, :width]], axis=0).astype(BF16)
    loads[2].wait()
    half_d = nm.shape[0] // 2
    step = 256

    def product(shard, right, into):
        for m in range(half_d // step):
            rows = pl.ds(pl.multiple_of(shard * half_d + m * step, step), step)
            into[m * step : (m + 1) * step, :] = dot(nm[rows, :], right())

    product(1 - s, lambda: gv[...], peer_part)
    core = remote(peer_part, core_part, core_s.at[0], core_r.at[0], to_core)
    core.start()

    for side in (0, 1):
        for part in (0, 1):
            b_first(side, part).wait()
        b_next[side] = gb[rows_of(near[1 - side]), lanes_of(side)] + b_got[side, 1]
        b_second(side).start()

    product(s, lambda: gv[...], own_part)

    for side in (0, 1):
        b_second(side).wait()
        mine = gb[rows_of(t), lanes_of(side)] + b_got[side, 0] + b_last[side]
        b_full[rows_of(t), lanes_of(side)] = mine.astype(BF16)
        b_back(side, 0).start()

    block = half_d // n
    side_w = width // 2
    both = own_part
    if in_line:
        first = [c + 1 - 2 * lax.rem(c, 2), 3 - c]
        across = lax.rem(c + 2, 4)

    def block_rows(k):
        return pl.ds(pl.multiple_of(k * block, 8), block)

    def z_block(k, side):
        return both[block_rows(k), side * side_w : (side + 1) * side_w]

    def z_first(side):
        return remote(z_out.at[side], z_got.at[side], z_s.at[side], z_r.at[side], line[side])

    def z_second(side):
        return remote(z_on.at[side], z_last.at[side], z_s.at[2 + side], z_r.at[2 + side], line[1 - side])

    def col_first():
        return remote(col_out, col_got, z_s.at[4], z_r.at[4], line[0])

    def col_second():
        return remote(col_on, col_last, z_s.at[5], z_r.at[5], line[1])

    core.wait()
    both[...] = both[...] + core_part[...]
    if in_line:
        for side in (0, 1):
            z_out[side, :block, :] = z_block(first[side], side).astype(BF16)
            z_out[side, block:, :] = z_block(across, side).astype(BF16)
            z_first(side).start()
    for side in (0, 1):
        b_back(side, 0).wait()
        for part in (1, 2):
            b_back(side, part).start()

    loads[3].wait()
    half = GROUP // 2
    tail_half = END // 2

    def f_first(side):
        return remote(send.at[side], got.at[side], f_s.at[side], f_r.at[side], to[side])

    def f_second(side):
        return remote(
            nxt.at[side], last.at[side], f_s.at[2 + side], f_r.at[2 + side], to[1 - side]
        )

    gain_grad[...] = late_gain[...]
    for g in range(GROUP // PART, steps // PART):
        row_buf[:, g * PART : (g + 1) * PART] = late_rows[g]
    ends = [jnp.zeros((LANE - END, LANE), F32)]
    for side in (0, 1):
        rows = slice(side * half, (side + 1) * half)
        tail_rows = slice(side * tail_half, (side + 1) * tail_half)
        end_rows = slice(steps - END + side * tail_half, steps - END + (side + 1) * tail_half)
        x = jnp.concatenate(
            [
                jnp.concatenate([gate_top[rows, :], gv[rows, :]], axis=1),
                jnp.concatenate([gate_end[tail_rows, :], gv[end_rows, :]], axis=1),
            ],
            axis=0,
        )
        keep, go = shares_of(side, t)
        gone = dot(x, pick(w_ref, *go), 1, 1)
        send[side] = gone.astype(BF16)
        f_first(side).start()
        kept = dot(x, pick(w_ref, *keep), 1, 1)
        early[side] = kept[:, :size]
        mid[side] = kept[:, size:]
        scale = jnp.concatenate([inv[rows, :], inv[end_rows, :]], axis=0)
        parts = [kept[:, :size], kept[:, size:], gone[:, :size], gone[:, size:]]

        def z(lanes):
            values = jnp.concatenate([tok_top[rows, lanes], tok_end[tail_rows, lanes]], axis=0)
            return values.astype(F32) * scale

        sums = count_rows(parts, z, gain, keep + go, gain_grad)
        row_buf[:, rows] = row_dots(sums[:half])
        ends.append(sums[half:])
    row_buf[:, steps - LANE :] += row_dots(jnp.concatenate(ends, axis=0))

    for copy in raws:
        copy.wait()
    for side in (0, 1):
        for part in (1, 2):
            b_back(side, part).wait()
    raw_all = jnp.concatenate([raw_full[k] for k in range(4)], axis=0)

    for k in range(steps // GROUP):
        rows = slice(k * GROUP, (k + 1) * GROUP)
        chosen = dot(b_full[rows, :], sel_bc[...]) + dot(raw_all[:, rows], sel_raw[...], 0, 0)
        col_grad[rows, :] = chosen.astype(BF16)
    own_lanes = pl.ds(pl.multiple_of(t * LANE, LANE), LANE)
    product(1 - s, lambda: col_grad[:, own_lanes], col_peer)
    col_core_copy = remote(col_peer, col_core, core_s.at[1], core_r.at[1], to_core)
    col_core_copy.start()
    loads[4].wait()
    loads[6].wait()
    loads[7].wait()
    ng[steps - END :, :] = jnp.zeros((END, size), F32)
    for k in range(steps // GROUP):
        rows = slice(k * GROUP, (k + 1) * GROUP)
        part = dot(col_grad[rows, :], w_cols[...], 1, 1)
        ng[rows, :] = part if k == 0 else ng[rows, :] + part
        part = part * (tok[rows, :].astype(F32) * inv[rows, :])
        gain_grad[:, mine_lanes] += fold(part)
        part = part * gain_mine[0:1, :]
        sums = part[:, :LANE]
        for sl in tiles(size)[1:]:
            sums = sums + part[:, sl]
        row_buf[:, rows] += row_dots(sums)
    row_copies = [
        remote(row_buf, row_held.at[k], row_s.at[k], row_r.at[k], target)
        for k, target in enumerate(group)
    ]
    for copy in row_copies:
        copy.start()

    pack[...] = jnp.zeros_like(pack)
    total = width + 2 * N
    add_up = lambda x: jnp.sum(x, axis=0, keepdims=True)
    for k in range(KERNEL):
        pack[k : k + 1, :total] = add_up(taps_grad[8 * k : 8 * k + 8, :])
    pack[KERNEL : KERNEL + 1, :total] = add_up(bias_grad[...])
    pack[KERNEL + 1 : KERNEL + 2, :width] = add_up(norm_gain_grad[...])
    pack[KERNEL + 2 : KERNEL + 3, :width] = add_up(skip_grad[...])
    pack[KERNEL + 3 : KERNEL + 4, :LANE] = add_up(head_grad[:8, :])
    pack[KERNEL + 4 : KERNEL + 5, :LANE] = add_up(head_grad[8:, :])
    pack[KERNEL + 5 : KERNEL + 6, :] = add_up(gain_grad[...])
    sum_core = remote(pack, pack_other, sum_s, sum_r, to_core)
    sum_core.start()

    for side in (0, 1):
        f_first(side).wait()
        nxt[side] = (mid[side] + got[side, :, size:].astype(F32)).astype(BF16)
        f_second(side).start()
        early[side] += got[side, :, :size].astype(F32)

    product(s, lambda: col_grad[:, own_lanes], col_own)

    sum_core.wait()
    pack_pair[...] = pack[...] + pack_other[...]
    pack_pieces[c] = pack_pair[...]
    sum_pieces = [
        remote(pack_pair, pack_pieces.at[c], piece_s.at[k], piece_r.at[k], target)
        for k, target in enumerate(to_piece)
    ]
    for copy in sum_pieces:
        copy.start()
    if in_line:
        for side in (0, 1):
            z_first(side).wait()
            z_on[side] = (
                z_block(first[1 - side], side) + z_got[side, block:, :].astype(F32)
            ).astype(BF16)
            z_second(side).start()
    col_core_copy.wait()
    col_own[...] = col_own[...] + col_core[...]
    if in_line:
        col_out[:block, :] = col_own[block_rows(first[0]), :]
        col_out[block:, :] = col_own[block_rows(across), :]
        col_first().start()

    for copy in sum_pieces:
        copy.wait()
    pack_total[...] = sum(pack_pieces[k] for k in range(1, n)) + pack_pieces[0]
    pack_all[t] = pack_total[...]
    sum_group = [
        remote(pack_total, pack_all.at[t], group_s.at[k], group_r.at[k], target)
        for k, target in enumerate(group)
    ]
    for copy in sum_group:
        copy.start()
    if in_line:
        col_first().wait()
        col_on[...] = col_own[block_rows(first[1]), :] + col_got[block:, :]
        col_second().start()

    loads[5].wait()
    for copy in row_copies:
        copy.wait()
    for side in (0, 1):
        f_second(side).wait()
        early[side] += last[side].astype(F32)
        at = steps - END + side * tail_half
        ng[at : at + tail_half, :] += early[side, half:, :]
        ng[side * half : (side + 1) * half, :] += early[side, :half, :]
    row_total = row_buf[...] + row_held[0] + row_held[1] + row_held[2]
    for k in range(steps // LANE):
        rows = slice(k * LANE, (k + 1) * LANE)
        row_dot = jnp.broadcast_to(row_total[0:1, rows] * (1.0 / D), (LANE, LANE)).T
        scale = inv[rows, :]
        for sl in tiles(size):
            z_tile = tok[rows, sl].astype(F32) * scale
            change = scale * (ng[rows, sl] * gain_mine[0:1, sl] - z_tile * row_dot)
            tokens_out[rows, sl] = (back[rows, sl].astype(F32) + change).astype(BF16)

    if in_line:
        for side in (0, 1):
            z_second(side).wait()
            value_out[:, side * side_w : (side + 1) * side_w] = (
                z_block(c, side) + z_got[side, :block, :].astype(F32) + z_last[side].astype(F32)
            )
        col_second().wait()
        cols_out[...] = col_own[block_rows(c), :] + col_got[:block, :] + col_last[...]
    else:
        value_out[...] = both[...]
        cols_out[...] = col_own[...]
    for copy in sum_group:
        copy.wait()
    pack_out[...] = pack_all[...]


def run_tail(
    grad_b, grad_v, normed, weight, tok, back, late, w_group, raw_t, fixed, gate_grad, inv, gain,
    gain_mine, sel_bc, sel_raw, late_rows, late_gain, *small,
):
    n = lax.axis_size("context")
    steps, width = grad_v.shape
    size = D // 4
    half_d = D // 2
    block = half_d // n
    side_rows = (GROUP + END) // 2
    share = steps // 4
    top = lambda w: pl.BlockSpec((GROUP, w), lambda i: (0, 0), pipeline_mode=pl.Buffered(1))
    end = lambda w: pl.BlockSpec(
        (END, w), lambda i: (steps // END - 1, 0), pipeline_mode=pl.Buffered(1)
    )
    full = lambda x: once(*x.shape)
    hbm = pl.BlockSpec(memory_space=pl.ANY)
    dma = pltpu.SemaphoreType.DMA
    vmem = pltpu.VMEM
    value_rows = block if n == 4 else half_d
    pair = (2, side_rows, size)
    packed = (PACK, D)
    return pl.pallas_call(
        functools.partial(tail_kernel, n),
        grid=(1,),
        in_specs=[hbm] * 8
        + [full(raw_t), full(fixed), top(width), end(width), top(D), end(D)]
        + [full(x) for x in (inv, gain, gain_mine, sel_bc, sel_raw)]
        + [full(x) for x in (late_rows, late_gain, *small)],
        out_specs=[
            once(steps, size), once(value_rows, width), once(value_rows, LANE), once(4, *packed)
        ],
        out_shape=[
            shape(steps, size, dtype=BF16), shape(value_rows, width), shape(value_rows, LANE),
            shape(4, *packed),
        ],
        scratch_shapes=[
            vmem((steps, 2 * N), F32), vmem((steps, width), BF16), vmem(normed.shape, BF16),
            vmem(weight.shape, BF16), vmem((steps, size), BF16), vmem((steps, size), BF16),
            vmem((size, w_group.shape[1]), BF16),
            vmem((steps, w_group.shape[1]), BF16),
            vmem((half_d, width), F32), vmem((half_d, width), F32), vmem((half_d, width), F32),
            vmem((2, 2, share, N), F32), vmem((2, share, N), F32), vmem((2, share, N), F32),
            vmem((steps, 2 * N), BF16), vmem((4, 16, steps), BF16),
            vmem(pair, F32), vmem(pair, F32), vmem((2, side_rows, 2 * size), BF16),
            vmem((2, side_rows, 2 * size), BF16), vmem(pair, BF16), vmem(pair, BF16), vmem((8, D), F32),
            vmem((2, 2 * block, width // 2), BF16), vmem((2, 2 * block, width // 2), BF16),
            vmem((2, block, width // 2), BF16), vmem((2, block, width // 2), BF16),
            vmem((steps, size), F32),
            vmem((half_d, LANE), F32), vmem((half_d, LANE), F32), vmem((half_d, LANE), F32),
            vmem((2 * block, LANE), F32), vmem((2 * block, LANE), F32), vmem((block, LANE), F32),
            vmem((block, LANE), F32),
            vmem((8, steps), F32), vmem((3, 8, steps), F32),
            vmem(packed, F32), vmem(packed, F32), vmem(packed, F32), vmem((n, *packed), F32),
            vmem(packed, F32), vmem((4, *packed), F32),
            dma((8,)), dma((3,)), dma((3,)), dma((2, 6)), dma((2, 6)), dma((4,)), dma((4,)),
            dma((2,)), dma((2,)), dma((6,)), dma((6,)), dma((3,)), dma((3,)),
            dma, dma, dma((n - 1,)), dma((n - 1,)), dma((3,)), dma((3,)),
        ],
        compiler_params=pltpu.CompilerParams(
            dimension_semantics=("arbitrary",), vmem_limit_bytes=56 * 1024 * 1024,
            collective_id=5, has_side_effects=True,
        ),
        cost_estimate=estimate(50),
        name="tail",
    )(
        grad_b, grad_v, normed, weight, tok, back, late, w_group,
        raw_t, fixed, gate_grad, gate_grad, tok, tok, inv, gain, gain_mine, sel_bc, sel_raw,
        late_rows, late_gain, *small,
    )


def pad_rows(x, rows=8):
    return jnp.concatenate([x, jnp.zeros((rows - x.shape[0], x.shape[1]), x.dtype)], axis=0)


def pad_cols(x, cols=LANE):
    return jnp.concatenate([x, jnp.zeros((x.shape[0], cols - x.shape[1]), x.dtype)], axis=1)


def on_device(
    tokens, cotangent, doc_lengths, zx_weight, bcdt_weight, out_weight, input_gain, chan_params,
    bc_params, head_params, zx_first, bcdt_first, out_first, gain_first, chan_first, bc_first,
    head_first, zx_second, bcdt_second, out_second, gain_second, chan_second, bc_second, head_second,
):
    n_tensor = lax.axis_size("tensor")
    t_index = lax.axis_index("tensor")
    c_index = lax.axis_index("context")
    tok = tokens[0]
    resid = tok.astype(F32)
    back = cotangent[0]
    steps = resid.shape[0]
    inner_loc = INNER // n_tensor
    heads_loc = H // n_tensor
    share = D // n_tensor
    count = steps // L
    rows_loc = zx_weight.shape[0]
    cols_loc = bcdt_weight.shape[1]

    zx_flat = zx_weight.reshape(rows_loc, 2 * inner_loc)
    proj_w, cols_z = line_gather(zx_flat.astype(BF16), pad_cols(bcdt_weight.astype(BF16)))
    down_block, _ = lax.optimization_barrier((out_weight.astype(BF16).T, proj_w))
    down_t = lax.all_gather(down_block, ("shard", "context"), axis=0, tiled=True)
    chan_loc = lax.dynamic_slice_in_dim(chan_params, t_index * inner_loc, inner_loc, 1)
    head_loc = lax.dynamic_slice_in_dim(head_params, t_index * heads_loc, heads_loc, 1)
    chan8 = pad_rows(chan_loc)
    bc8 = pad_rows(bc_params)
    head8 = pad_rows(pad_cols(head_loc))
    spread_at = lax.broadcasted_iota(jnp.int32, (2 * LANE, inner_loc), 0) % LANE
    expand = (
        spread_at == lax.broadcasted_iota(jnp.int32, (2 * LANE, inner_loc), 1) // P_SIZE
    ).astype(BF16)
    gain8 = jnp.broadcast_to(input_gain[None], (8, D))
    (
        normed, normed_t, inv_rms, projected, cols, info, marks_rows, edge_mask,
        act, delta, cum, sloc, pfx, final, halo_v, halo_b,
    ) = run_project(
        doc_lengths, tok, gain8, proj_w, cols_z, chan8, bc8, head8, expand, heads_loc, cols_loc
    )
    entry, back_scaled, back_t = run_entry(final, back, down_t)
    ssd, sums = run_ahead(
        act, delta, cum, info, marks_rows, sloc, pfx, entry, projected, back_scaled, chan8, head8,
        expand, heads_loc,
    )
    sums = small_sum(sums, 1)
    scaled, *out_fan = run_out(ssd, projected, sums, chan8, down_t)
    gate_grad, mixed_grad, aloc, sfx, first_adj, norm_gain_grad = run_norm(
        ssd, projected, back_scaled, sums, act, cum, info, chan8, expand, heads_loc
    )
    later, out_own, out_next, *z_arrays = run_middle(
        first_adj, out_fan, normed_t, gate_grad, back_t, scaled
    )
    resid_share = lax.dynamic_slice_in_dim(tok, t_index * share, share, 1).astype(F32)
    in_line = lax.axis_size("context") == 4
    total_width = inner_loc + 2 * N

    (
        grad_v, grad_b, raw_t, last_rows, _, taps_grad, bias_grad, skip_grad, head_grad,
        ng_late, late_rows, late_gain, out_last, *z_sum,
    ) = run_grand(
        projected, cols, halo_v, halo_b, info, marks_rows, delta, cum, ssd, mixed_grad,
        sloc, pfx, entry, aloc, sfx, later, chan8, bc8, head8, expand, heads_loc,
        gate_grad, proj_w, tok, inv_rms, gain8, edge_mask, out_next, z_arrays if in_line else [],
    )
    out_share = out_own + out_last.reshape(steps, share).astype(F32)
    block_out = (resid_share + out_share).astype(BF16)[None]
    if in_line:
        gate_g, down_g = z_sum[0][0], z_sum[0][1]
    else:
        gate_g, down_g = [
            lax.psum_scatter(z_arrays[0][k], "context", scatter_dimension=0, tiled=True) for k in (0, 1)
        ]
    column = np.arange(4 * LANE)
    column = np.where(column % LANE < cols_loc, column // LANE * cols_loc + column % LANE, -1)[None, :]
    sel_bc = (np.arange(2 * N)[:, None] == column).astype(ml_dtypes.bfloat16)
    slot = np.arange(4 * 16)[:, None]
    of_slot = np.where(slot % 16 < heads_loc, 2 * N + slot // 16 * heads_loc + slot % 16, -2)
    sel_raw = (of_slot == column).astype(ml_dtypes.bfloat16)
    gain_mine = jnp.broadcast_to(
        lax.dynamic_slice_in_dim(input_gain, t_index * share, share, 0)[None], (8, share)
    )
    tokens_grad, value_g, cols_g, packed = run_tail(
        grad_b, grad_v, normed_t, proj_w, tok, back, ng_late, cols_z, raw_t, last_rows, gate_grad,
        inv_rms, gain8, gain_mine, sel_bc, sel_raw, late_rows, late_gain,
        taps_grad, bias_grad, norm_gain_grad, skip_grad, head_grad,
    )
    tokens_grad = tokens_grad[None]
    if not in_line:
        value_g = lax.psum_scatter(value_g, "context", scatter_dimension=0, tiled=True)
        cols_g = lax.psum_scatter(cols_g[:, :cols_loc], "context", scatter_dimension=0, tiled=True)
        cols_g = pad_cols(cols_g)
    flip = lambda *arrays: tuple(a.T for a in arrays)
    lift = lambda *arrays: tuple(a[None] for a in arrays)
    news = run_adam(
        (gate_g, value_g, down_g, cols_g, packed),
        (
            (zx_weight, zx_first, zx_second), flip(out_weight, out_first, out_second),
            flip(bcdt_weight, bcdt_first, bcdt_second), lift(input_gain, gain_first, gain_second),
            (chan_params, chan_first, chan_second), (bc_params, bc_first, bc_second),
            (head_params, head_first, head_second),
        ),
        heads_loc, cols_loc,
    )
    zx_new, out_new, bcdt_new, gain_new = news[:3], flip(*news[3:6]), flip(*news[6:9]), news[9:12]
    return (
        block_out, tokens_grad, *zx_new, *bcdt_new, *out_new, *[g[0] for g in gain_new], *news[12:]
    )


def solution(mesh):
    big = P(("shard", "context"), None, "tensor")
    cols = P(("shard", "context"), "tensor")
    down = P("tensor", ("shard", "context"))
    rows = P("shard", "context", None)
    out_rows = P("shard", "context", "tensor")
    return jax.shard_map(
        on_device,
        mesh=mesh,
        in_specs=(
            rows, rows, P("shard", None), big, cols, down, P(), P(), P(), P(),
            big, cols, down, P(), P(), P(), P(),
            big, cols, down, P(), P(), P(), P(),
        ),
        out_specs=(
            out_rows, out_rows, big, big, big, cols, cols, cols, down, down, down,
            *([P()] * 12),
        ),
        check_vma=False,
    )
```

```python
import functools

import jax
import jax.numpy as jnp
import ml_dtypes
import numpy as np
from jax import lax
from jax.experimental import pallas as pl
from jax.experimental.pallas import tpu as pltpu
from jax.sharding import PartitionSpec as P

D = 1536
INNER = 3072
H = 48
P_SIZE = 64
N = 128
KERNEL = 4
STEP = 10

EPS = 1e-05
BETA_ONE = 0.9
BETA_TWO = 0.999
ADAM_EPS = 1e-08
DECAY = 0.1
RATE_MATRIX = 0.05
RATE_SMALL = 0.2

L = 128
LANE = 128
GROUP = 4 * L
PART = 2 * L
END = 32
LOG2E = 1.4426950408889634
F32 = jnp.float32
BF16 = jnp.bfloat16
VMEM_LIMIT = 48 * 1024 * 1024


def from_behind(block, axis, distance):
    devices = range(lax.axis_size(axis))
    route = [(i - distance, i) for i in devices if i - distance in devices]
    return lax.ppermute(block, axis, route)


def adamw(weight, grad, first, second, rate, decay):
    first_new = BETA_ONE * first + (1.0 - BETA_ONE) * grad
    second_new = BETA_TWO * second + (1.0 - BETA_TWO) * grad * grad
    scale_one = 1.0 - BETA_ONE**STEP
    scale_two = 1.0 - BETA_TWO**STEP
    update = first_new / scale_one / (jnp.sqrt(second_new / scale_two) + ADAM_EPS)
    return (weight - rate * (update + decay * weight), first_new, second_new)


def two(x):
    hi = x.astype(BF16)
    return hi, (x - hi.astype(F32)).astype(BF16)


def dot(a, b, ca=1, cb=0):
    return lax.dot_general(a, b, (((ca,), (cb,)), ((), ())), preferred_element_type=F32)


def dot3(a, b, ca=1, cb=0):
    ah, al = two(a)
    bh, bl = two(b)
    return dot(
        jnp.concatenate([ah, al, ah], axis=ca), jnp.concatenate([bh, bh, bl], axis=cb), ca, cb
    )


def over_rows(left, lanes, right):
    total = None
    for at in range(0, left.shape[0], GROUP):
        rows = slice(at, at + GROUP)
        part = dot(left[rows, lanes], right(rows), 0, 0)
        total = part if total is None else total + part
    return total


def tri_sum(tri, x):
    hi = x.astype(BF16)
    rest = x - hi.astype(F32)
    mid = rest.astype(BF16)
    low = (rest - mid.astype(F32)).astype(BF16)
    out = dot(tri, jnp.concatenate([hi, mid, low], axis=1))
    w = x.shape[1]
    return out[:, :w] + out[:, w : 2 * w] + out[:, 2 * w :]


def spread(x, e_ref):
    hi, lo = two(x)
    return dot(jnp.concatenate([hi, lo], axis=1), e_ref[...])


def per_head(x, e_ref):
    hi, lo = two(x)
    e = e_ref[:LANE, :]
    return dot(hi, e, 1, 1) + dot(lo, e, 1, 1)


def sigmoid(x):
    return 1.0 / (1.0 + jnp.exp(-x))


def softplus(x):
    return jnp.maximum(x, 0.0) + jnp.log1p(jnp.exp(-jnp.abs(x)))


def tiles(width):
    return [slice(k, k + LANE) for k in range(0, width, LANE)]


def fold(x):
    return jnp.sum(x.reshape(x.shape[0] // 8, 8, x.shape[1]), axis=0)


def lower_mask():
    row = lax.broadcasted_iota(jnp.int32, (L, L), 0)
    col = lax.broadcasted_iota(jnp.int32, (L, L), 1)
    return row >= col


def keep_mask(info, marks_row):
    return jnp.logical_and(lower_mask(), info[:, 5:6] == marks_row[0:1, :])


def decay_of(keep, cum, cum_t, h):
    return jnp.exp2(jnp.where(keep, cum[:, h : h + 1] - cum_t[h : h + 1, :], -1e30))


def load_ext(ext_ref, cur_ref, prev_ref, halo_ref, j, first):
    if j > 0:
        ext_ref[0:8, :] = cur_ref[j * L - 8 : j * L, :]
    else:

        @pl.when(first)
        def _():
            ext_ref[0:8, :] = halo_ref[...]

        @pl.when(jnp.logical_not(first))
        def _():
            ext_ref[0:8, :] = prev_ref[...]

    ext_ref[8 : 8 + L, :] = cur_ref[j * L : (j + 1) * L, :]


def rows_at(ref, j):
    return ref.at[j * L : (j + 1) * L, :]


def lead_at(ref, j):
    return ref.at[j : j + 1]


def conv_tile(ext_ref, info, taps, sl):
    shifted = []
    total = jnp.broadcast_to(taps[KERNEL : KERNEL + 1, :], (L, LANE))
    for k in range(KERNEL):
        val = ext_ref[pl.ds(8 - KERNEL + 1 + k, L), sl]
        if k < KERNEL - 1:
            val = val * info[:, k : k + 1]
        shifted.append(val)
        total = total + taps[k : k + 1, :] * val
    return shifted, total


def prep_chunk(
    bc, info_ref, chan, bcpar, head, e_ref, act, delta_ref, cum_ref, sloc, pfx, ext_v, ext_b, state, prod
):
    info = info_ref[...]
    width = ext_v.shape[1]
    for sl in tiles(width):
        _, total = conv_tile(ext_v, info, chan[:, sl], sl)
        act[:, sl] = total * sigmoid(total)
    for sl in tiles(2 * N):
        _, total = conv_tile(ext_b, info, bcpar[:, sl], sl)
        act[:, slice(width + sl.start, width + sl.stop)] = total * sigmoid(total)
    raw = bc[:, 2 * N : 3 * N]
    delta = softplus(raw + head[0:1, :])
    dlog = -delta * (jnp.exp(head[1:2, :]) * LOG2E)
    tri = jnp.where(lower_mask(), 1.0, 0.0).astype(BF16)
    cum = tri_sum(tri, dlog)
    delta_ref[...] = delta
    cum_ref[...] = cum
    sloc[0] = state[...]
    pfx[0] = prod[...]
    last = cum[L - 1 : L, :]
    tail = info[:, 4:5] * jnp.exp2(last - cum) * delta
    through = spread(
        jnp.broadcast_to(info[L - 1 : L, 3:4] * jnp.exp2(last), (8, LANE)), e_ref
    )
    weights = spread(tail, e_ref)
    tail_u = act[:, :width] * weights
    fresh = dot3(act[:, width : width + N], tail_u, 0, 0)
    state[...] = state[...] * through[0:1, :] + fresh
    prod[...] = prod[...] * through


def row_block(width, col=0, rows=GROUP):
    return pl.BlockSpec((rows, width), lambda i: (i, col))


def prev_block(width, col=0, rows=GROUP):
    return pl.BlockSpec((8, width), lambda i: (jnp.maximum(i * (rows // 8) - 1, 0), col))


def lead_block(*dims, rows=GROUP):
    return pl.BlockSpec((rows // L, *dims), lambda i: (i, 0, 0))


def whole(*shape):
    return pl.BlockSpec(shape, lambda i: (0,) * len(shape))


def once(*shape):
    return pl.BlockSpec(shape, lambda i: (0,) * len(shape), pipeline_mode=pl.Buffered(1))


def estimate(us):
    return pl.CostEstimate(flops=int(us * 1.1e9), bytes_accessed=int(us * 1e6), transcendentals=0)


def params(**kw):
    return pltpu.CompilerParams(
        dimension_semantics=("arbitrary",), vmem_limit_bytes=VMEM_LIMIT, **kw
    )


def shape(*dims, dtype=F32):
    return jax.ShapeDtypeStruct(dims, dtype)


def ahead_kernel(
    heads, act, delta, cum, info, marks, sloc, pfx, entry, gate, back, chan, head, e_ref, ssd, sums
):
    for j in range(act.shape[0] // L):
        ahead_chunk(
            rows_at(act, j), rows_at(delta, j), rows_at(cum, j), rows_at(info, j), lead_at(marks, j),
            lead_at(sloc, j), lead_at(pfx, j), entry, rows_at(gate, j), rows_at(back, j), chan, head,
            e_ref, rows_at(ssd, j), lead_at(sums, j),
        )


def ahead_chunk(
    act, delta_ref, cum_ref, info_ref, marks_ref, sloc, pfx, entry, gate, back, chan, head, e_ref, ssd, sums
):
    width = act.shape[1] - 2 * N
    info = info_ref[...]
    cum = cum_ref[...]
    cum_t = cum.T
    keep = keep_mask(info, marks_ref[0])
    bmat = act[:, width : width + N]
    cmat = act[:, width + N :]
    scores = dot3(cmat, bmat, 1, 1)
    xs = act[:, :width]
    u_hi, u_lo = two(xs * spread(delta_ref[...], e_ref))
    state = sloc[0] + entry[...] * pfx[0, 0:1, :]
    entering = dot3(cmat, state)
    eexp = spread(info[:, 3:4] * jnp.exp2(cum), e_ref)
    skip = spread(jnp.broadcast_to(head[2:3, :], (8, LANE)), e_ref)
    lane = lax.broadcasted_iota(jnp.int32, (1, LANE), 1)
    left = jnp.where(lane < P_SIZE, 1.0, 0.0).astype(BF16)
    right = jnp.where(lane < P_SIZE, 0.0, 1.0).astype(BF16)
    square = jnp.zeros((L, LANE), F32)
    cross = jnp.zeros((L, LANE), F32)
    for q, sl in enumerate(tiles(width)):
        mix = jnp.concatenate(
            [(scores * decay_of(keep, cum, cum_t, 2 * q + r)).astype(BF16) for r in (0, 1)], axis=1
        )
        both = jnp.concatenate([u_hi[:, sl], u_lo[:, sl]], axis=1)
        rhs = jnp.concatenate(
            [both * jnp.concatenate([m, m], axis=1) for m in (left, right)], axis=0
        )
        out = dot(mix, rhs)
        y = out[:, :LANE] + out[:, LANE:] + entering[:, sl] * eexp[:, sl]
        y = y + skip[0:1, sl] * xs[:, sl]
        ssd[:, sl] = y
        g = gate[:, sl]
        gated = y * g * sigmoid(g)
        square = square + gated * gated
        cross = cross + gated * (back[:, sl] * chan[KERNEL + 1 : KERNEL + 2, sl])
    ones = jnp.ones((8, LANE), BF16)
    rows = []
    for part in (square, cross):
        hi, lo = two(part)
        rows.append(dot(ones, hi, 1, 1) + dot(ones, lo, 1, 1))
    pick = lax.broadcasted_iota(jnp.int32, (8, LANE), 0)
    sums[0] = jnp.where(pick == 0, rows[0], jnp.where(pick == 1, rows[1], 0.0))


def run_ahead(act, delta, cum, info, marks, sloc, pfx, entry, projected, back, chan, head, expand, heads):
    steps, width = projected.shape[0], projected.shape[1] // 2
    count = steps // L
    return pl.pallas_call(
        functools.partial(ahead_kernel, heads),
        grid=(steps // GROUP,),
        in_specs=[
            row_block(width + 2 * N), row_block(LANE), row_block(LANE), row_block(LANE),
            lead_block(8, L), lead_block(N, width), lead_block(8, width),
            once(N, width), row_block(width, 0), row_block(width),
            once(8, width), once(8, LANE), once(2 * LANE, width),
        ],
        out_specs=[row_block(width), lead_block(8, L)],
        out_shape=[shape(steps, width), shape(count, 8, L)],
        compiler_params=params(),
        cost_estimate=estimate(20),
        name="ahead",
    )(act, delta, cum, info, marks, sloc, pfx, entry, projected, back, chan, head, expand)


def norm_kernel(
    heads, ssd, gate, back, sums, cmat, cum, info, chan, e_ref,
    gate_grad, mixed_grad, aloc, sfx, fin, gain_grad, state, prod,
):
    i = pl.program_id(0)

    @pl.when(i == 0)
    def _():
        state[...] = jnp.zeros_like(state)
        prod[...] = jnp.ones_like(prod)
        gain_grad[...] = jnp.zeros_like(gain_grad)

    chunks = ssd.shape[0] // L

    for j in reversed(range(chunks)):
        norm_chunk(
            rows_at(ssd, j), rows_at(gate, j), rows_at(back, j), lead_at(sums, j), rows_at(cmat, j),
            rows_at(cum, j), rows_at(info, j), chan, e_ref, rows_at(gate_grad, j),
            rows_at(mixed_grad, j), lead_at(aloc, j), lead_at(sfx, j), gain_grad, state, prod,
        )

    @pl.when(i == pl.num_programs(0) - 1)
    def _():
        fin[:N, :] = state[...]
        fin[N:, :] = prod[...]


def norm_chunk(
    ssd, gate, back, sums, cmat_ref, cum_ref, info_ref, chan, e_ref,
    gate_grad, mixed_grad, aloc, sfx, gain_grad, state, prod,
):
    width = ssd.shape[1]
    rows = sums[0]
    inv_row = lax.rsqrt(rows[0:1, :] / INNER + EPS)
    cross_row = inv_row * inv_row * inv_row * (rows[1:2, :] / INNER)
    inv = jnp.broadcast_to(inv_row, (LANE, L)).T
    cross = jnp.broadcast_to(cross_row, (LANE, L)).T
    info = info_ref[...]
    cum = cum_ref[...]
    eexp = spread(info[:, 3:4] * jnp.exp2(cum), e_ref)
    e_mixed = []
    for sl in tiles(width):
        g = gate[:, sl]
        sig = sigmoid(g)
        soft = g * sig
        y = ssd[:, sl]
        gated = y * soft
        bs = back[:, sl]
        gain = chan[KERNEL + 1 : KERNEL + 2, sl]
        normed = gated * inv
        gain_grad[:, sl] += fold(bs * normed)
        gg = inv * (bs * gain) - gated * cross
        mg = gg * soft
        mixed_grad[:, sl] = mg
        gate_grad[:, sl] = (gg * y * sig * (1.0 + g * (1.0 - sig))).astype(BF16)
        e_mixed.append(mg * eexp[:, sl])
    aloc[0] = state[...]
    sfx[0] = prod[...]
    through = spread(
        jnp.broadcast_to(info[L - 1 : L, 3:4] * jnp.exp2(cum[L - 1 : L, :]), (8, LANE)), e_ref
    )
    fresh = dot3(cmat_ref[...], jnp.concatenate(e_mixed, axis=1), 0, 0)
    state[...] = state[...] * through[0:1, :] + fresh
    prod[...] = prod[...] * through


def run_norm(ssd, projected, back, sums, act, cum, info, chan, expand, heads):
    steps, width = ssd.shape
    count = steps // L
    blocks = steps // GROUP
    turn = lambda spec: pl.BlockSpec(
        spec.block_shape, lambda i, m=spec.index_map: m(blocks - 1 - i)
    )
    c_col = width // N + 1
    return pl.pallas_call(
        functools.partial(norm_kernel, heads),
        grid=(blocks,),
        in_specs=[
            turn(row_block(width)), turn(row_block(width, 0)), turn(row_block(width)),
            turn(lead_block(8, L)),
            turn(row_block(N, c_col)), turn(row_block(LANE)), turn(row_block(LANE)),
            once(8, width), once(2 * LANE, width),
        ],
        out_specs=[
            turn(row_block(width)), turn(row_block(width)),
            turn(lead_block(N, width)),
            turn(lead_block(8, width)),
            whole(N + 8, width), whole(8, width),
        ],
        out_shape=[
            shape(steps, width, dtype=BF16), shape(steps, width),
            shape(count, N, width), shape(count, 8, width), shape(N + 8, width), shape(8, width),
        ],
        scratch_shapes=[pltpu.VMEM((N, width), F32), pltpu.VMEM((8, width), F32)],
        compiler_params=params(),
        cost_estimate=estimate(21),
        name="norm_back",
    )(ssd, projected, back, sums, act, cum, info, chan, expand)


def behind_chunk(
    heads, j, chunks, i_first, i_last, val, valp, bc, bcp, halo_v, halo_b, info_ref, marks_ref, delta_ref, cum_ref,
    ssd, mixed_grad, sloc, pfx, entry, aloc, sfx, later, chan, bcpar, head, e_ref,
    grad_v, grad_b, raw_grad, tail_rows, head_rows, taps_grad, bias_grad, skip_grad, head_grad,
    ext_v, ext_b, slope, d_tot,
):
    width = val.shape[1]
    total_width = width + 2 * N
    starts = j == chunks - 1

    if starts:

        @pl.when(i_first)
        def _():
            d_tot[0:8, :] = jnp.zeros((8, total_width), F32)
            taps_grad[...] = jnp.zeros_like(taps_grad)
            bias_grad[...] = jnp.zeros_like(bias_grad)
            skip_grad[...] = jnp.zeros_like(skip_grad)
            head_grad[...] = jnp.zeros_like(head_grad)

    d_tot[L:, :] = d_tot[0:8, :]
    load_ext(ext_v, val, valp, halo_v, j, i_last)
    load_ext(ext_b, bc, bcp, halo_b, j, i_last)
    raw = bc[j * L : (j + 1) * L, 2 * N : 3 * N]
    info_ref, marks_ref = rows_at(info_ref, j), lead_at(marks_ref, j)
    delta_ref, cum_ref, ssd = rows_at(delta_ref, j), rows_at(cum_ref, j), rows_at(ssd, j)
    mixed_grad, sloc, pfx = rows_at(mixed_grad, j), lead_at(sloc, j), lead_at(pfx, j)
    aloc, sfx = lead_at(aloc, j), lead_at(sfx, j)
    grad_v, grad_b = rows_at(grad_v, j), rows_at(grad_b, j)
    raw_grad = raw_grad.at[:, j * L : (j + 1) * L]
    info = info_ref[...]

    def activate(ext_ref, taps, sl, at):
        _, total = conv_tile(ext_ref, info, taps[:, sl], sl)
        sig = sigmoid(total)
        slope[:, slice(at, at + LANE)] = sig * (1.0 + total * (1.0 - sig))
        return total * sig

    xs = jnp.concatenate([activate(ext_v, chan, sl, sl.start) for sl in tiles(width)], axis=1)
    bmat = activate(ext_b, bcpar, slice(0, N), width)
    cmat = activate(ext_b, bcpar, slice(N, 2 * N), width + N)

    delta = delta_ref[...]
    cum = cum_ref[...]
    cum_t = cum.T
    keep = keep_mask(info, marks_ref[0])
    last = cum[L - 1 : L, :]
    scores = dot3(cmat, bmat, 1, 1)
    dexp = spread(delta, e_ref)
    eexp = spread(info[:, 3:4] * jnp.exp2(cum), e_ref)
    texp = spread(info[:, 4:5] * jnp.exp2(last - cum), e_ref)
    u = xs * dexp
    u_hi, u_lo = two(u)
    dy = mixed_grad[...]
    dy_hi, dy_lo = two(dy)
    skip = spread(jnp.broadcast_to(head[2:3, :], (8, LANE)), e_ref)
    state = sloc[0] + entry[...] * pfx[0, 0:1, :]
    adj = aloc[0] + later[...] * sfx[0, 0:1, :]
    tail_du = dot3(bmat, adj) * texp
    lane = lax.broadcasted_iota(jnp.int32, (1, LANE), 1)
    left = jnp.where(lane < P_SIZE, 1.0, 0.0).astype(BF16)
    right = jnp.where(lane < P_SIZE, 0.0, 1.0).astype(BF16)
    two_left = jnp.concatenate([left, left], axis=1)
    two_right = jnp.concatenate([right, right], axis=1)
    d_scores = jnp.zeros((L, L), F32)
    inner_du = []
    for q, sl in enumerate(tiles(width)):
        decays = [decay_of(keep, cum, cum_t, 2 * q + r) for r in (0, 1)]
        mix = jnp.concatenate([(scores * d).astype(BF16) for d in decays], axis=0)
        dy_both = jnp.concatenate([dy_hi[:, sl], dy_lo[:, sl]], axis=1)
        rhs = jnp.concatenate([dy_both * two_left, dy_both * two_right], axis=0)
        out = dot(mix, rhs, 0, 0)
        inner_du.append(out[:, :LANE] + out[:, LANE:])
        u_twice = jnp.concatenate([u_hi[:, sl], u_hi[:, sl]], axis=1)
        u_rows = jnp.concatenate([u_twice * two_left, u_twice * two_right], axis=0)
        d_mix = dot(dy_both, u_rows, 1, 1)
        d_scores = d_scores + d_mix[:, :L] * decays[0] + d_mix[:, L:] * decays[1]
    du = jnp.concatenate(inner_du, axis=1) + tail_du
    d_xs = dexp * du + skip[0:1, :] * dy
    d_b = dot3(d_scores, cmat, 0, 0) + dot3(u * texp, adj, 1, 1)
    d_c = dot3(d_scores, bmat) + dot3(dy * eexp, state, 1, 1)
    skip_grad[...] += fold(dy * xs)

    direct = per_head(xs * du, e_ref)
    mixed = ssd[...] - skip[0:1, :] * xs
    d_cum = per_head(dy * mixed, e_ref) - delta * direct
    at_last = jnp.sum(per_head(u * tail_du, e_ref), axis=0, keepdims=True)
    through = info[L - 1 : L, 3:4] * jnp.exp2(last)
    pair = per_head(fold(adj * state), e_ref)
    at_last = at_last + through * jnp.sum(pair, axis=0, keepdims=True)
    upper = jnp.where(lower_mask(), 1.0, 0.0).astype(BF16).T
    d_log = tri_sum(upper, d_cum) + at_last
    rate = jnp.exp(head[1:2, :])
    valid = lane < heads
    d_raw = (direct - d_log * rate) * sigmoid(raw + head[0:1, :])
    d_raw = jnp.where(valid, d_raw, 0.0)
    raw_grad[...] = d_raw.T[:16, :].astype(BF16)
    head_grad[0:8, :] += fold(d_raw)
    head_grad[8:16, :] += fold(jnp.where(valid, -d_log * delta * rate, 0.0))

    d_act = [d_xs[:, sl] for sl in tiles(width)] + [d_b, d_c]
    for q in range(total_width // LANE):
        sl = slice(q * LANE, (q + 1) * LANE)
        if q < width // LANE:
            ext_ref, taps, part = ext_v, chan[:, sl], sl
        else:
            part = slice(sl.start - width, sl.stop - width)
            ext_ref, taps = ext_b, bcpar[:, part]
        dt = d_act[q] * slope[:, sl]
        d_tot[0:L, sl] = dt
        bias_grad[:, sl] += fold(dt)
        for k in range(KERNEL):
            moved = ext_ref[pl.ds(8 - KERNEL + 1 + k, L), part]
            if k < KERNEL - 1:
                moved = moved * info[:, k : k + 1]
            taps_grad[8 * k : 8 * k + 8, sl] += fold(dt * moved)
        total = dt * taps[KERNEL - 1 : KERNEL, :]
        for s in range(1, KERNEL):
            total = total + taps[KERNEL - 1 - s : KERNEL - s, :] * (
                d_tot[pl.ds(s, L), sl] * info[:, 7 + s : 8 + s]
            )
        if q < width // LANE:
            grad_v[:, sl] = total.astype(BF16)
        else:
            grad_b[:, part] = total

        if starts:

            @pl.when(i_first)
            def _():
                tail_rows[:, sl] = total[L - 8 :, :]

    if j == 0:

        @pl.when(i_last)
        def _():
            head_rows[...] = d_tot[0:8, :]


def remote(src, dst, send, recv, target):
    return pltpu.make_async_remote_copy(
        src_ref=src, dst_ref=dst, send_sem=send, recv_sem=recv, device_id=target,
        device_id_type=pl.DeviceIdType.MESH,
    )


def greet(targets):
    barrier = pltpu.get_barrier_semaphore()
    for target in targets:
        pl.semaphore_signal(
            barrier, inc=1, device_id=target, device_id_type=pl.DeviceIdType.MESH
        )
    return barrier


def count_rows(parts, z, gain, at, gain_grad):
    rows = jnp.zeros((parts[0].shape[0], LANE), F32)
    size = parts[0].shape[1]
    for part, k in zip(parts, at):
        lanes = pl.ds(pl.multiple_of(k * size, size), size)
        part = part * z(lanes)
        gain_grad[:, lanes] += fold(part)
        part = part * gain[0:1, lanes]
        for sl in tiles(size):
            rows = rows + part[:, sl]
    return rows


def row_dots(rows):
    ones = jnp.ones((8, LANE), BF16)
    hi, lo = two(rows)
    return dot(ones, hi, 1, 1) + dot(ones, lo, 1, 1)


def grand_kernel(heads, n, *refs):
    behind, refs = refs[:22], refs[22:]
    gate_grad, w_ref, tok, inv, gain, edge_mask, out_next = refs[:7]
    refs = refs[7:]
    in_line = n == 4
    if in_line:
        z_out, z_mid, z_mine = refs[:3]
        refs = refs[3:]
    outs, refs = refs[:9], refs[9:]
    ng_own, row_sums, gain_grad, out_last = refs[:4]
    refs = refs[4:]
    if in_line:
        z_sum, refs = refs[0], refs[1:]
    scratch, refs = refs[:4], refs[4:]
    mid, send, got, nxt, last, edge, s1, r1, s2, r2, edge_s, edge_r, o_s, o_r = refs[:14]
    if in_line:
        z_got, z_on, z_last, z_s, z_r = refs[14:]
    chan, bcpar = behind[18], behind[19]
    grad_v, tail_rows = outs[0], outs[3]
    d_tot = scratch[3]
    i, n_steps = pl.program_id(0), pl.num_programs(0)
    s, c, t = lax.axis_index("shard"), lax.axis_index("context"), lax.axis_index("tensor")
    near = peers(t)
    to = [(s, c, near[0]), (s, c, near[1])]
    width = grad_v.shape[1]
    size = w_ref.shape[0] // 4
    inside = mid.shape[0]
    chunks = grad_v.shape[0] // L

    @pl.when(i == 0)
    def _():
        pl.semaphore_wait(greet(to + beside_of(n)), 4)
        gain_grad[...] = jnp.zeros_like(gain_grad)

    def out_hop(side):
        return remote(
            out_next.at[side], out_last.at[side], o_s.at[side], o_r.at[side], to[1 - side]
        )

    @pl.when(i == 0)
    def _():
        for side in (0, 1):
            out_hop(side).start()

    if in_line:
        line = [(s, c + 1 - 2 * lax.rem(c, 2), t), (s, 3 - c, t)]
        block = z_mid.shape[1]

        def z_first(k):
            return remote(z_out.at[k], z_got.at[k], z_s.at[k], z_r.at[k], line[k])

        def z_second(k):
            return remote(z_on.at[k], z_last.at[k], z_s.at[2 + k], z_r.at[2 + k], line[1 - k])

        @pl.when(i == 0)
        def _():
            for k in (0, 1):
                z_first(k).start()

        @pl.when(i == n_steps // 2)
        def _():
            for k in (0, 1):
                z_first(k).wait()
                z_on[k] = (z_mid[k] + z_got[k, block:, :].astype(F32)).astype(BF16)
                z_second(k).start()
                z_sum[k] = z_mine[k] + z_got[k, :block, :].astype(F32)

        @pl.when(i == n_steps - 1)
        def _():
            for k in (0, 1):
                z_second(k).wait()
                z_sum[k] += z_last[k].astype(F32)

    def first_hop(k, side):
        return remote(send.at[k], got.at[k], s1.at[k], r1.at[k], to[side])

    def second_hop(k, side):
        return remote(nxt.at[k], last.at[k], s2.at[k], r2.at[k], to[1 - side])

    def place(k):
        return pl.ds(pl.multiple_of((inside - 1 - k) * PART, PART), PART)

    for j in reversed(range(chunks)):
        behind_chunk(heads, j, chunks, i == 0, i == n_steps - 1, *behind, *outs, *scratch)

    def turn_over(k, side):
        first_hop(k, side).wait()
        nxt[k] = (mid[k] + got[k, :, size:].astype(F32)).astype(BF16)
        second_hop(k, side).start()
        ng_own[place(k), :] += got[k, :, :size].astype(F32)

    def fan(side):
        counted = jnp.where(i == 0, PART - END, PART)
        x = jnp.concatenate([gate_grad[...], grad_v[...]], axis=1)
        keep, go = shares_of(side, t)
        gone = dot(x, pick(w_ref, *go), 1, 1)
        send[i] = gone.astype(BF16)
        first_hop(i, side).start()
        kept = dot(x, pick(w_ref, *keep), 1, 1)
        ng_own[place(i), :] = kept[:, :size]
        mid[i] = kept[:, size:]
        row = lax.broadcasted_iota(jnp.int32, (PART, 1), 0)
        scale = jnp.where(row < counted, inv[...], 0.0)
        parts = [kept[:, :size], kept[:, size:], gone[:, :size], gone[:, size:]]
        sums = count_rows(
            parts, lambda lanes: tok[:, lanes].astype(F32) * scale, gain, keep + go, gain_grad
        )
        row_sums[0] = row_dots(sums)

    for side in (0, 1):
        parity = lax.rem(i, 2) == 1 - side

        @pl.when(jnp.logical_and(jnp.logical_not(parity), jnp.logical_and(i > 0, i <= inside)))
        def _():
            turn_over(i - 1, side)

        @pl.when(jnp.logical_and(parity, i < inside))
        def _():
            fan(side)

    @pl.when(i == n_steps - 1)
    def _():
        before = (s, jnp.maximum(c - 1, 0), t)
        copy = remote(d_tot.at[pl.ds(0, 8), :], edge, edge_s, edge_r, before)

        @pl.when(c > 0)
        def _():
            copy.start()

        for k in range(inside):
            second_hop(k, 1 - k % 2).wait()
            ng_own[place(k), :] += last[k].astype(F32)
        for side in (0, 1):
            out_hop(side).wait()

        @pl.when(c < n - 1)
        def _():
            copy.wait_recv()
            for shift in range(1, KERNEL):
                moved = pltpu.roll(edge[...], 8 - shift, 0) * edge_mask[
                    8 * shift - 8 : 8 * shift, 0:1
                ]
                tap = slice(KERNEL - 1 - shift, KERNEL - shift)
                tail_rows[:, :width] += chan[tap, :] * moved[:, :width]
                tail_rows[:, width:] += bcpar[tap, :] * moved[:, width:]

        @pl.when(c > 0)
        def _():
            copy.wait_send()


def run_grand(
    projected, cols, halo_v, halo_b, info, marks, delta, cum, ssd, mixed_grad, sloc, pfx, entry,
    aloc, sfx, later, chan, bcpar, head, expand, heads, gate_grad, weight, tok, inv, gain, edge_mask,
    out_next, z_arrays,
):
    steps, width = ssd.shape
    parts = steps // PART
    inside = (steps - GROUP) // PART
    size = D // 4
    turn = lambda spec: pl.BlockSpec(
        spec.block_shape, lambda i, m=spec.index_map: m(parts - 1 - i)
    )
    in_part = lambda w: pl.BlockSpec((PART, w), lambda i: (parts - 1 - i, 0))
    chunk = lead_block(N, width, rows=PART)
    few = lead_block(8, width, rows=PART)
    total = width + 2 * N
    dma = pltpu.SemaphoreType.DMA
    return pl.pallas_call(
        functools.partial(grand_kernel, heads, lax.axis_size("context")),
        grid=(parts,),
        in_specs=[
            turn(row_block(width, 1, rows=PART)), turn(prev_block(width, 1, rows=PART)),
            turn(row_block(3 * N, rows=PART)), turn(prev_block(3 * N, rows=PART)),
            once(8, width), once(8, 3 * N), turn(row_block(LANE, rows=PART)),
            turn(lead_block(8, L, rows=PART)),
            turn(row_block(LANE, rows=PART)), turn(row_block(LANE, rows=PART)), turn(row_block(width, rows=PART)), turn(row_block(width, rows=PART)),
            turn(chunk), turn(few), once(N, width), turn(chunk), turn(few), once(N, width),
            once(8, width), once(8, 2 * N), once(8, LANE), once(2 * LANE, width),
            turn(row_block(width, rows=PART)), once(*weight.shape), in_part(D), in_part(1), once(8, D),
            once(24, LANE), pl.BlockSpec(memory_space=pl.ANY),
        ]
        + ([pl.BlockSpec(memory_space=pl.ANY)] + [once(*z.shape) for z in z_arrays[1:]] if z_arrays else []),
        out_specs=[
            turn(row_block(width, rows=PART)), turn(row_block(2 * N, rows=PART)),
            pl.BlockSpec((16, PART), lambda i: (0, parts - 1 - i)),
            whole(8, total), whole(8, total), whole(8 * KERNEL, total), whole(8, total),
            whole(8, width), whole(16, LANE),
            once(inside * PART, size),
            pl.BlockSpec((1, 8, PART), lambda i: (parts - 1 - i, 0, 0)),
            whole(8, D), pl.BlockSpec(memory_space=pl.ANY),
        ]
        + [once(*z.shape) for z in z_arrays[1:2]],
        out_shape=[
            shape(steps, width, dtype=BF16), shape(steps, 2 * N), shape(16, steps, dtype=BF16),
            shape(8, total), shape(8, total), shape(8 * KERNEL, total), shape(8, total),
            shape(8, width), shape(16, LANE),
            shape(inside * PART, size), shape(parts, 8, PART), shape(8, D),
            shape(*out_next.shape, dtype=BF16),
        ]
        + [shape(*z.shape) for z in z_arrays[1:2]],
        scratch_shapes=[
            pltpu.VMEM((8 + L, width), F32), pltpu.VMEM((8 + L, 3 * N), F32),
            pltpu.VMEM((L, total), F32), pltpu.VMEM((L + 8, total), F32),
            pltpu.VMEM((inside, PART, size), F32),
            pltpu.VMEM((inside, PART, 2 * size), BF16), pltpu.VMEM((inside, PART, 2 * size), BF16),
            pltpu.VMEM((inside, PART, size), BF16), pltpu.VMEM((inside, PART, size), BF16),
            pltpu.VMEM((8, total), F32),
            dma((inside,)), dma((inside,)), dma((inside,)), dma((inside,)), dma, dma,
            dma((2,)), dma((2,)),
        ]
        + (
            [
                pltpu.VMEM(z_arrays[0].shape, BF16), pltpu.VMEM(z_arrays[1].shape, BF16),
                pltpu.VMEM(z_arrays[1].shape, BF16), dma((4,)), dma((4,)),
            ]
            if z_arrays
            else []
        ),
        compiler_params=pltpu.CompilerParams(
            dimension_semantics=("arbitrary",), vmem_limit_bytes=52 * 1024 * 1024,
            collective_id=4, has_side_effects=True,
        ),
        cost_estimate=estimate(90),
        name="behind",
    )(
        projected, projected, cols, cols, halo_v, halo_b, info, marks, delta, cum, ssd, mixed_grad,
        sloc, pfx, entry, aloc, sfx, later, chan, bcpar, head, expand,
        gate_grad, weight, tok, inv, gain, edge_mask, out_next, *z_arrays,
    )


def peers(t):
    return t + 1 - 2 * lax.rem(t, 2), lax.rem(t + 2, 4)


def pick(w_ref, one, other):
    size = w_ref.shape[0] // 4
    at = lambda k: pl.ds(pl.multiple_of(k * size, size), size)
    return jnp.concatenate([w_ref[at(one), :], w_ref[at(other), :]], axis=0)


def shares_of(side, t):
    near = peers(t)
    return (t, near[1 - side]), (near[side], 3 - t)


def out_kernel(
    ssd, gate, sums, chan, w_ref, scaled, own, mid, send_a, send_b,
):
    i, half = pl.program_id(0), pl.num_programs(0) // 2
    t = lax.axis_index("tensor")
    width = ssd.shape[1]
    for k in range(ssd.shape[0] // L):
        rows = slice(k * L, (k + 1) * L)
        inv = jnp.broadcast_to(lax.rsqrt(sums[k, 0:1, :] / INNER + EPS), (LANE, L)).T
        for sl in tiles(width):
            g = gate[rows, sl]
            gated = ssd[rows, sl] * g * sigmoid(g)
            scaled[rows, sl] = (gated * inv * chan[KERNEL + 1 : KERNEL + 2, sl]).astype(BF16)
    x = scaled[...]
    size = own.shape[1]

    def part(side, send):
        keep, go = shares_of(side, t)
        send[...] = dot(x, pick(w_ref, *go), 1, 1).astype(BF16)
        kept = dot(x, pick(w_ref, *keep), 1, 1)
        own[...] = kept[:, :size]
        mid[...] = kept[:, size:]

    @pl.when(i < half)
    def _():
        part(0, send_a)

    @pl.when(i >= half)
    def _():
        part(1, send_b)


def run_out(ssd, projected, sums, chan, weight):
    steps, width = ssd.shape
    block = 512
    count = steps // block
    half = count // 2
    size = D // 4
    in_block = lambda w, col=0: pl.BlockSpec((block, w), lambda i: (i, col))
    return pl.pallas_call(
        out_kernel,
        grid=(count,),
        in_specs=[
            in_block(width), in_block(width, 0),
            pl.BlockSpec((block // L, 8, L), lambda i: (i, 0, 0)),
            whole(8, width), whole(*weight.shape),
        ],
        out_specs=[
            in_block(width), in_block(size), in_block(size),
            pl.BlockSpec((block, 2 * size), lambda i: (jnp.minimum(i, half - 1), 0)),
            pl.BlockSpec((block, 2 * size), lambda i: (jnp.maximum(i - half, 0), 0)),
        ],
        out_shape=[
            shape(steps, width, dtype=BF16), shape(steps, size), shape(steps, size),
            shape(steps // 2, 2 * size, dtype=BF16), shape(steps // 2, 2 * size, dtype=BF16),
        ],
        compiler_params=params(),
        cost_estimate=estimate(12),
        name="out",
    )(ssd, projected, sums, chan, weight)


def line_kernel(
    n, n_tensor, piece, zx_ref, cols_ref, zx_out, cols_out,
    local, zx_s, zx_r, core_s, core_r, col_s, col_r, group_s, group_r, bulk_s, bulk_r,
):
    s, c, t = lax.axis_index("shard"), lax.axis_index("context"), lax.axis_index("tensor")
    on = (c < n - 1, c > 0)
    to = ((s, jnp.minimum(c + 1, n - 1), t), (s, jnp.maximum(c - 1, 0), t))
    to_core = (1 - s, c, t)
    to_group = [(s, c, lax.rem(t + k, n_tensor)) for k in range(1, n_tensor)]
    beside = [(s, lax.rem(c + k, n), t) for k in (1, n - 1)]
    pl.semaphore_wait(greet([to_core] + to_group + beside), n_tensor + 2)
    rows, width = zx_ref.shape[0], cols_ref.shape[1]
    spans = [(at, min(piece, rows - at)) for at in range(0, rows, piece)]

    def block_of(way, hop):
        return jnp.maximum(c - hop, 0) if way == 0 else jnp.minimum(c + hop, n - 1)

    def has(way, hop):
        return c - hop >= 0 if way == 0 else c + hop <= n - 1

    def place(ref, block, at=0, size=rows):
        return ref.at[pl.ds(pl.multiple_of((s * n + block) * rows + at, 16), size), :]

    lanes = pl.ds(pl.multiple_of(t * width, LANE), width)

    def place_cols(block):
        return cols_out.at[pl.ds(pl.multiple_of((s * n + block) * rows, 16), rows), lanes]

    def zx_copy(way, step, p):
        at, size = spans[p]
        where = place(zx_out, block_of(way, step), at, size)
        src = zx_ref.at[pl.ds(at, size), :] if step == 0 else where
        return remote(src, where, zx_s.at[way, step, p], zx_r.at[way, step, p], to[way])

    def col_copy(way, step):
        where = place_cols(block_of(way, step))
        src = cols_ref if step == 0 else where
        return remote(src, where, col_s.at[way, step], col_r.at[way, step], to[way])

    def group_copies(way, hop):
        where = place_cols(block_of(way, hop))
        src = cols_ref if hop == 0 else where
        return [
            remote(src, where, group_s.at[k, way, hop], group_r.at[k, way, hop], target)
            for k, target in enumerate(to_group)
        ]

    def core_copy(way, hop, p):
        at, size = spans[p]
        where = place(zx_out, block_of(way, hop), at, size)
        src = zx_ref.at[pl.ds(at, size), :] if hop == 0 else where
        return remote(src, where, core_s.at[way, hop, p], core_r.at[way, hop, p], to_core)

    pieces = range(len(spans))
    for way in (0, 1):

        @pl.when(on[way])
        def _():
            col_copy(way, 0).start()
            for p in pieces:
                zx_copy(way, 0, p).start()

    for copy in group_copies(0, 0):
        copy.start()
    own_cols = pltpu.make_async_copy(cols_ref, place_cols(c), local.at[0])
    own_zx = pltpu.make_async_copy(zx_ref, place(zx_out, c), local.at[1])
    own_cols.start()
    own_zx.start()
    for p in pieces:
        core_copy(0, 0, p).start()
    start = pl.ds(pl.multiple_of(s * n * rows, 16), n * rows)
    bulk = remote(cols_out.at[start, :], cols_out.at[start, :], bulk_s, bulk_r, to_core)
    for step in range(n - 1):
        further = step < n - 2
        for way in (0, 1):

            @pl.when(has(way, step + 1))
            def _():
                col_copy(way, step).wait_recv()
                for copy in group_copies(way, step + 1):
                    copy.start()
                if further:

                    @pl.when(on[way])
                    def _():
                        col_copy(way, step + 1).start()

        if not further:
            own_cols.wait()
            for copy in group_copies(0, 0):
                copy.wait()
            for hop in range(1, n):
                for way in (0, 1):

                    @pl.when(has(way, hop))
                    def _():
                        for copy in group_copies(way, hop):
                            copy.wait()

            bulk.start()
        for p in pieces:
            for way in (0, 1):

                @pl.when(has(way, step + 1))
                def _():
                    zx_copy(way, step, p).wait_recv()
                    core_copy(way, step + 1, p).start()
                    if further:

                        @pl.when(on[way])
                        def _():
                            zx_copy(way, step + 1, p).start()

    for step in range(n - 1):
        for way in (0, 1):

            @pl.when(jnp.logical_and(on[way], has(way, step)))
            def _():
                col_copy(way, step).wait_send()
                for p in pieces:
                    zx_copy(way, step, p).wait_send()

            @pl.when(has(way, step + 1))
            def _():
                for p in pieces:
                    core_copy(way, step + 1, p).wait()

    for p in pieces:
        core_copy(0, 0, p).wait()
    bulk.wait()
    own_zx.wait()


PIECE = 64


def line_gather(zx, cols):
    n, n_tensor = lax.axis_size("context"), lax.axis_size("tensor")
    rows = zx.shape[0]
    pieces = -(-rows // PIECE)
    dma = pltpu.SemaphoreType.DMA
    return pl.pallas_call(
        functools.partial(line_kernel, n, n_tensor, PIECE),
        in_specs=[pl.BlockSpec(memory_space=pl.ANY)] * 2,
        out_specs=[pl.BlockSpec(memory_space=pl.ANY)] * 2,
        out_shape=[
            shape(2 * n * rows, zx.shape[1], dtype=BF16),
            shape(2 * n * rows, n_tensor * cols.shape[1], dtype=BF16),
        ],
        scratch_shapes=[
            dma((2,)), dma((2, n - 1, pieces)), dma((2, n - 1, pieces)),
            dma((2, n, pieces)), dma((2, n, pieces)), dma((2, n - 1)), dma((2, n - 1)),
            dma((n_tensor - 1, 2, n)), dma((n_tensor - 1, 2, n)), dma, dma,
        ],
        compiler_params=pltpu.CompilerParams(collective_id=0, has_side_effects=True),
        name="line_gather",
    )(zx, cols)


def small_sum_kernel(n, x_ref, o_ref, held, send, recv):
    s, c, t = lax.axis_index("shard"), lax.axis_index("context"), lax.axis_index("tensor")
    targets = [(s, c, lax.rem(t + k, n)) for k in range(1, n)]
    pl.semaphore_wait(greet(targets), n - 1)
    copies = [
        remote(x_ref, held.at[k], send.at[k], recv.at[k], target)
        for k, target in enumerate(targets)
    ]
    for copy in copies:
        copy.start()
    total = x_ref[...]
    for k, copy in enumerate(copies):
        copy.wait()
        total = total + held[k]
    o_ref[...] = total


def small_sum(x, collective_id):
    n = lax.axis_size("tensor")
    return pl.pallas_call(
        functools.partial(small_sum_kernel, n),
        in_specs=[pl.BlockSpec(memory_space=pltpu.VMEM)],
        out_specs=pl.BlockSpec(memory_space=pltpu.VMEM),
        out_shape=shape(*x.shape),
        scratch_shapes=[
            pltpu.VMEM((n - 1, *x.shape), F32),
            pltpu.SemaphoreType.DMA((n - 1,)), pltpu.SemaphoreType.DMA((n - 1,)),
        ],
        compiler_params=pltpu.CompilerParams(collective_id=collective_id, has_side_effects=True),
        cost_estimate=estimate(7),
        name="small_sum",
    )(x)


SLICES = 8


class Chain:
    def __init__(self, n, backward, packed, entering, got, sent, send_sem, recv_sem):
        s, c, t = lax.axis_index("shard"), lax.axis_index("context"), lax.axis_index("tensor")
        self.from_other = c < n - 1 if backward else c > 0
        self.to_other = c > 0 if backward else c < n - 1
        ahead = jnp.maximum(c - 1, 0) if backward else jnp.minimum(c + 1, n - 1)
        self.target = (s, ahead, t)
        self.refs = packed, entering, got, sent, send_sem, recv_sem

    def copy(self, j):
        _, _, got, sent, send_sem, recv_sem = self.refs
        rows = pl.ds(j * (N // SLICES), N // SLICES)
        return remote(sent.at[rows, :], got.at[rows, :], send_sem.at[j], recv_sem.at[j], self.target)

    def step(self, j):
        packed, entering, got, sent, _, _ = self.refs
        rows = slice(j * (N // SLICES), (j + 1) * (N // SLICES))

        @pl.when(self.from_other)
        def _():
            self.copy(j).wait_recv()
            entering[rows, :] = got[rows, :]

        @pl.when(jnp.logical_not(self.from_other))
        def _():
            entering[rows, :] = jnp.zeros((N // SLICES, packed.shape[1]), F32)

        @pl.when(self.to_other)
        def _():
            sent[rows, :] = packed[rows, :] + packed[N : N + 1, :] * entering[rows, :]
            self.copy(j).start()

    def finish(self):
        @pl.when(self.to_other)
        def _():
            for j in range(SLICES):
                self.copy(j).wait_send()


def beside_of(n):
    s, c, t = lax.axis_index("shard"), lax.axis_index("context"), lax.axis_index("tensor")
    return [(s, lax.rem(c + k, n), t) for k in (1, n - 1)]


def entry_kernel(
    n, packed, back, w_hbm, entry, out, bk, w_ref, buf, got, sent, load_sem, out_sem, chain_s, chain_r
):
    block = buf.shape[1]
    count = back.shape[0] // block
    load_w = pltpu.make_async_copy(w_hbm, w_ref, load_sem.at[count])
    load_w.start()

    def load(k):
        rows = pl.ds(k * block, block)
        return pltpu.make_async_copy(back.at[rows, :], bk.at[rows, :], load_sem.at[k])

    def store(k):
        return pltpu.make_async_copy(
            buf.at[k % 2], out.at[pl.ds(k * block, block), :], out_sem.at[k % 2]
        )

    for k in range(count):
        load(k).start()
    pl.semaphore_wait(greet(beside_of(n)), 2)
    chain = Chain(n, False, packed, entry, got, sent, chain_s, chain_r)
    load_w.wait()
    for k in range(count):
        load(k).wait()
        if k >= 2:
            store(k - 2).wait()
        buf[k % 2] = dot(bk[k * block : (k + 1) * block, :], w_ref[...])
        store(k).start()
        if k < SLICES:
            chain.step(k)
    for k in range(count, SLICES):
        chain.step(k)
    chain.finish()
    for k in range(max(count - 2, 0), count):
        store(k).wait()


def run_entry(packed, back, weight):
    n = lax.axis_size("context")
    steps, width = back.shape[0], weight.shape[1]
    block = 256
    dma = pltpu.SemaphoreType.DMA
    vmem = pltpu.VMEM
    inside = pl.BlockSpec(memory_space=pltpu.VMEM)
    hbm = pl.BlockSpec(memory_space=pl.ANY)
    return pl.pallas_call(
        functools.partial(entry_kernel, n),
        in_specs=[inside, hbm, hbm],
        out_specs=[inside, hbm],
        out_shape=[shape(N, width), shape(steps, width)],
        scratch_shapes=[
            vmem(back.shape, BF16), vmem(weight.shape, BF16), vmem((2, block, width), F32),
            vmem((N, width), F32), vmem((N, width), F32),
            dma((steps // block + 1,)), dma((2,)), dma((SLICES,)), dma((SLICES,)),
        ],
        compiler_params=pltpu.CompilerParams(
            vmem_limit_bytes=40 * 1024 * 1024, collective_id=6, has_side_effects=True
        ),
        cost_estimate=estimate(15),
        name="entry",
    )(packed, back, weight)


def middle_kernel(
    n, packed, send_a, send_b, mid_hbm, own_hbm, normed_hbm, gate_hbm, back_hbm, scaled_hbm, *refs
):
    if n == 4:
        later, own, next_out, z_out, z_mid, z_mine = refs[:6]
        refs = refs[6:]
    else:
        later, own, next_out, both_out = refs[:4]
        refs = refs[4:]
    (
        mid, nm, gg, bk, sc, peer_part, core_part, own_part, got, chain_got, chain_sent,
        local, core_s, core_r, f_s, f_r, chain_s, chain_r,
    ) = refs
    s, c, t = lax.axis_index("shard"), lax.axis_index("context"), lax.axis_index("tensor")
    near = peers(t)
    to = [(s, c, near[0]), (s, c, near[1])]
    to_core = (1 - s, c, t)
    loads = [
        pltpu.make_async_copy(src, dst, local.at[k])
        for k, (src, dst) in enumerate(
            [
                (normed_hbm, nm), (gate_hbm, gg), (back_hbm, bk), (scaled_hbm, sc),
                (mid_hbm, mid), (own_hbm, own),
            ]
        )
    ]
    for load in loads:
        load.start()
    pl.semaphore_wait(greet(to + [to_core] + beside_of(n)), 5)
    hops = [
        remote(src, got.at[side], f_s.at[side], f_r.at[side], to[side])
        for side, src in enumerate((send_a, send_b))
    ]
    for hop in hops:
        hop.start()
    chain = Chain(n, True, packed, later, chain_got, chain_sent, chain_s, chain_r)
    half_d = nm.shape[1] // 2
    steps = nm.shape[0]
    step = 256
    pairs = ((nm, gg), (bk, sc))

    def product(which, shard, into, m):
        left, right = pairs[which]
        lanes = pl.ds(pl.multiple_of(shard * half_d + m * step, step), step)
        into[which, m * step : (m + 1) * step, :] = over_rows(left, lanes, lambda rows: right[rows, :])

    cores = [
        remote(peer_part.at[k], core_part.at[k], core_s.at[k], core_r.at[k], to_core) for k in (0, 1)
    ]
    chain.step(0)
    done = 1
    for which in (0, 1):
        loads[2 * which].wait()
        loads[2 * which + 1].wait()
        for m in range(half_d // step):
            product(which, 1 - s, peer_part, m)
            if done < SLICES:
                chain.step(done)
                done += 1
        cores[which].start()
    for which in (0, 1):
        for m in range(half_d // step):
            product(which, s, own_part, m)
            if done < SLICES:
                chain.step(done)
                done += 1
    chain.finish()
    block = half_d // n

    for which in (0, 1):
        cores[which].wait()
        if n == 4:
            first = c + 1 - 2 * lax.rem(c, 2) if which == 0 else 3 - c
            third = 3 - c if which == 0 else c + 1 - 2 * lax.rem(c, 2)

            def total(k):
                rows = pl.ds(pl.multiple_of(k * block, 8), block)
                return own_part[which, rows, :] + core_part[which, rows, :]

            z_out[which, :block, :] = total(first).astype(BF16)
            z_out[which, block:, :] = total(lax.rem(c + 2, 4)).astype(BF16)
            z_mid[which] = total(third)
            z_mine[which] = total(c)
        else:
            both_out[which] = own_part[which] + core_part[which]
    loads[4].wait()
    loads[5].wait()
    size = mid.shape[1]
    half = steps // 2
    for side in (0, 1):
        hops[side].wait()
        for k in range(half // step):
            rows = slice(k * step, (k + 1) * step)
            at = slice(side * half + k * step, side * half + (k + 1) * step)
            next_out[side, rows, :] = (mid[at, :] + got[side, rows, size:].astype(F32)).astype(BF16)
            own[at, :] += got[side, rows, :size].astype(F32)


def run_middle(packed, fan, normed, gate_grad, back, scaled):
    n = lax.axis_size("context")
    own, mid, send_a, send_b = fan
    steps, width = gate_grad.shape
    size = own.shape[1]
    half_d = D // 2
    block = half_d // n
    dma = pltpu.SemaphoreType.DMA
    vmem = pltpu.VMEM
    inside = pl.BlockSpec(memory_space=pltpu.VMEM)
    hbm = pl.BlockSpec(memory_space=pl.ANY)
    if n == 4:
        more = [
            shape(2, 2 * block, width, dtype=BF16), shape(2, block, width), shape(2, block, width)
        ]
    else:
        more = [shape(2, half_d, width)]
    pair = (2, half_d, width)
    return pl.pallas_call(
        functools.partial(middle_kernel, n),
        in_specs=[inside] + [hbm] * 8,
        out_specs=[inside] * (3 + len(more)),
        out_shape=[shape(N, width), shape(steps, size), shape(2, steps // 2, size, dtype=BF16)] + more,
        scratch_shapes=[
            vmem((steps, size), F32), vmem(normed.shape, BF16), vmem(gate_grad.shape, BF16),
            vmem(back.shape, BF16), vmem(scaled.shape, BF16),
            vmem(pair, F32), vmem(pair, F32), vmem(pair, F32), vmem((2, steps // 2, 2 * size), BF16),
            vmem((N, width), F32), vmem((N, width), F32),
            dma((6,)), dma((2,)), dma((2,)), dma((2,)), dma((2,)), dma((SLICES,)), dma((SLICES,)),
        ],
        compiler_params=pltpu.CompilerParams(
            vmem_limit_bytes=54 * 1024 * 1024, collective_id=7, has_side_effects=True
        ),
        cost_estimate=estimate(35),
        name="middle",
    )(packed, send_a, send_b, mid, own, normed, gate_grad, back, scaled)


def adam_kernel(heads, cols_loc, gate_g, value_g, down_g, cols_g, packed, *refs):
    zx, out, bcdt, gain, chan, bc, head = [refs[3 * k : 3 * k + 3] for k in range(7)]
    refs = refs[21:]
    zx_new, out_new, bcdt_new, gain_new, chan_new, bc_new, head_new = [
        refs[3 * k : 3 * k + 3] for k in range(7)
    ]
    width = gate_g.shape[1]

    def put(news, olds, grad, rate, decay, at=(Ellipsis,)):
        for ref, val in zip(news, adamw(olds[0][at], grad, olds[1][at], olds[2][at], rate, decay)):
            ref[at] = val

    for k, grad in enumerate((gate_g, value_g)):
        put(zx_new, zx, grad[...], RATE_MATRIX, DECAY, (slice(None), k, slice(None)))
    put(out_new, out, down_g[...], RATE_MATRIX, DECAY)
    put(bcdt_new, bcdt, cols_g[...].T[:cols_loc, :], RATE_MATRIX, DECAY)
    over = packed[0] + packed[1] + packed[2] + packed[3]
    put(gain_new, gain, over[KERNEL + 5 : KERNEL + 6, :], RATE_SMALL, 0.0)
    put(bc_new, bc, over[: KERNEL + 1, width : width + 2 * N], RATE_SMALL, 0.0)
    grad = jnp.concatenate([packed[k, : KERNEL + 2, :width] for k in range(4)], axis=1)
    put(chan_new, chan, grad, RATE_SMALL, 0.0)
    lane = lax.broadcasted_iota(jnp.int32, (LANE, 4 * heads), 0)
    slot = lax.broadcasted_iota(jnp.int32, (LANE, 4 * heads), 1)
    channel = lax.broadcasted_iota(jnp.int32, (width, 4 * heads), 0)
    wide_slot = lax.broadcasted_iota(jnp.int32, (width, 4 * heads), 1)
    rows = jnp.zeros((8, 4 * heads), F32)
    for k in range(4):
        here = jnp.where(lane + k * heads == slot, 1.0, 0.0)
        here = jnp.where(lane < heads, here, 0.0).astype(BF16)
        wide = jnp.where(channel // P_SIZE + k * heads == wide_slot, 1.0, 0.0).astype(BF16)
        hi, lo = two(packed[k, KERNEL + 3 : KERNEL + 11, :LANE])
        at = lax.broadcasted_iota(jnp.int32, rows.shape, 0)
        rows = rows + jnp.where(at < 2, dot(hi, here) + dot(lo, here), 0.0)
        hi, lo = two(packed[k, KERNEL + 2 : KERNEL + 10, :width])
        skip = dot(hi, wide) + dot(lo, wide)
        rows = rows + jnp.where(at == 2, jnp.broadcast_to(skip[0:1, :], rows.shape), 0.0)
    put(head_new, head, rows[:3, :], RATE_SMALL, 0.0)


def run_adam(grads, olds, heads, cols_loc):
    flat = [x for group in olds for x in group]
    return pl.pallas_call(
        functools.partial(adam_kernel, heads, cols_loc),
        in_specs=[pl.BlockSpec(memory_space=pltpu.VMEM)] * (len(grads) + len(flat)),
        out_specs=[pl.BlockSpec(memory_space=pltpu.VMEM)] * len(flat),
        out_shape=[shape(*x.shape) for x in flat],
        compiler_params=pltpu.CompilerParams(vmem_limit_bytes=40 * 1024 * 1024),
        cost_estimate=estimate(8),
        name="optimizer",
    )(*grads, *flat)


def doc_of(lengths, position):
    found = jnp.zeros(position.shape, F32)
    end = 0
    for k in range(lengths.shape[1] - 1):
        end = end + lengths[0, k]
        found = found + jnp.where(position >= end, 1.0, 0.0)
    return jnp.where(position < 0, -1.0, found)


def mark_chunk(lengths, begin, limit, info_ref, marks_ref):
    row = lax.broadcasted_iota(jnp.int32, (L, LANE), 0)
    lane = lax.broadcasted_iota(jnp.int32, (L, LANE), 1)
    offset = jnp.where(lane < KERNEL - 1, lane - KERNEL + 1, jnp.where(lane >= 8, lane - 7, 0))
    other = jnp.where(lane == 3, -1, jnp.where(lane == 4, L - 1, row + offset)) + begin
    mark = doc_of(lengths, row + begin)
    same = jnp.logical_and(doc_of(lengths, other) == mark, other < limit)
    info = jnp.where(same, 1.0, 0.0)
    info_ref[...] = jnp.where(lane == 5, mark, jnp.where(lane < 7 + KERNEL, info, 0.0))
    marks_ref[0] = doc_of(lengths, begin + lax.broadcasted_iota(jnp.int32, (8, L), 1))


def norm_rows(tok, gain):
    x = tok.astype(F32)
    square = x * x
    total = square[:, :LANE]
    for sl in tiles(D)[1:]:
        total = total + square[:, sl]
    inv = lax.rsqrt(jnp.sum(total, axis=1, keepdims=True) / D + EPS)
    return (x * inv * gain[0:1, :]).astype(BF16), inv


def project_kernel(
    heads, n, cols_loc, lengths, tok, tok_end, gain, w_ref, wg_ref, chan, bcpar, head, e_ref,
    normed, inv, projected, cols, info, marks, edge_mask, act, delta, cum, sloc, pfx, fin,
    halo_v, halo_b, ext_v, ext_b, state, prod, w_cols, prev_v, prev_b, halo_out, halo_got, h_s, h_r,
):
    i = pl.program_id(0)
    s, c, t = lax.axis_index("shard"), lax.axis_index("context"), lax.axis_index("tensor")
    width = w_ref.shape[1] // 2
    block = tok.shape[0]
    steps = block * pl.num_programs(0)
    start = c * steps
    after = (s, jnp.minimum(c + 1, n - 1), t)
    halo = remote(halo_out, halo_got, h_s, h_r, after)

    @pl.when(i == 0)
    def _():
        pl.semaphore_wait(greet(beside_of(n)), 2)
        state[...] = jnp.zeros_like(state)
        prod[...] = jnp.ones_like(prod)
        lane = lax.broadcasted_iota(jnp.int32, (4 * LANE, 3 * N), 0)
        want = lax.broadcasted_iota(jnp.int32, (4 * LANE, 3 * N), 1)
        have = lane // LANE * cols_loc + lane % LANE
        want = jnp.where(want < 2 * N, want, jnp.where(want < 2 * N + heads, want + heads * t, -1))
        chosen = jnp.logical_and(have == want, lane % LANE < cols_loc)
        select = jnp.where(chosen, 1.0, 0.0).astype(BF16)
        for k in range(0, D, block):
            w_cols[k : k + block, :] = dot(wg_ref[k : k + block, :], select).astype(BF16)
        ends, _ = norm_rows(tok_end[...], gain)
        halo_out[:, :width] = dot(ends, w_ref[:, width:])[8:, :]
        halo_out[:, width:] = dot(ends, w_cols[...])[8:, :]

        @pl.when(c < n - 1)
        def _():
            halo.start()

        row = lax.broadcasted_iota(jnp.int32, (24, LANE), 0)
        shift, at = row // 8 + 1, row % 8
        there = at - 8 + shift + start + steps
        agree = doc_of(lengths, there) == doc_of(lengths, there - shift)
        edge_mask[...] = jnp.where(jnp.logical_and(at >= 8 - shift, agree), 1.0, 0.0)

    for j in range(block // L):
        rows = slice(j * L, (j + 1) * L)
        x, scale = norm_rows(tok[rows, :], gain)
        normed[rows, :] = x
        inv[rows, :] = scale
    for k in range(0, 2 * width, 512):
        projected[:, k : k + 512] = dot(normed[...], w_ref[:, k : k + 512])
    cols[...] = dot(normed[...], w_cols[...])

    @pl.when(i == 0)
    def _():
        @pl.when(c > 0)
        def _():
            halo.wait_recv()
            halo_v[...] = halo_got[:, :width]
            halo_b[...] = halo_got[:, width:]

        @pl.when(c == 0)
        def _():
            halo_v[...] = jnp.zeros_like(halo_v)
            halo_b[...] = jnp.zeros_like(halo_b)

        @pl.when(c < n - 1)
        def _():
            halo.wait_send()

    val = projected.at[:, pl.ds(width, width)]

    for j in range(block // L):
        first = i == 0
        mark_chunk(
            lengths, start + i * block + j * L, start + steps, rows_at(info, j), lead_at(marks, j)
        )
        load_ext(ext_v, val, prev_v, halo_v, j, first)
        load_ext(ext_b, cols, prev_b, halo_b, j, first)
        prep_chunk(
            rows_at(cols, j), rows_at(info, j), chan, bcpar, head, e_ref, rows_at(act, j),
            rows_at(delta, j), rows_at(cum, j), lead_at(sloc, j), lead_at(pfx, j),
            ext_v, ext_b, state, prod,
        )
    prev_v[...] = projected[block - 8 :, width:]
    prev_b[...] = cols[block - 8 :, :]

    @pl.when(i == pl.num_programs(0) - 1)
    def _():
        fin[:N, :] = state[...]
        fin[N:, :] = prod[...]


def run_project(lengths, tok, gain, weight, w_group, chan, bcpar, head, expand, heads, cols_loc):
    steps, width = tok.shape[0], weight.shape[1] // 2
    count = steps // L
    dma = pltpu.SemaphoreType.DMA
    return pl.pallas_call(
        functools.partial(project_kernel, heads, lax.axis_size("context"), cols_loc),
        grid=(steps // GROUP,),
        in_specs=[
            pl.BlockSpec(memory_space=pltpu.SMEM), row_block(D),
            pl.BlockSpec((16, D), lambda i: (steps // 16 - 1, 0), pipeline_mode=pl.Buffered(1)),
            once(8, D), once(*weight.shape), once(*w_group.shape),
            once(8, width), once(8, 2 * N), once(8, LANE), once(2 * LANE, width),
        ],
        out_specs=[
            row_block(D), row_block(1),
            row_block(2 * width), row_block(3 * N), row_block(LANE), lead_block(8, L), once(24, LANE),
            row_block(width + 2 * N), row_block(LANE), row_block(LANE), lead_block(N, width),
            lead_block(8, width), once(N + 8, width), once(8, width), once(8, 3 * N),
        ],
        out_shape=[
            shape(steps, D, dtype=BF16), shape(steps, 1),
            shape(steps, 2 * width), shape(steps, 3 * N), shape(steps, LANE), shape(count, 8, L),
            shape(24, LANE),
            shape(steps, width + 2 * N), shape(steps, LANE), shape(steps, LANE),
            shape(count, N, width), shape(count, 8, width), shape(N + 8, width), shape(8, width),
            shape(8, 3 * N),
        ],
        scratch_shapes=[
            pltpu.VMEM((8 + L, width), F32), pltpu.VMEM((8 + L, 3 * N), F32),
            pltpu.VMEM((N, width), F32), pltpu.VMEM((8, width), F32),
            pltpu.VMEM((D, 3 * N), BF16), pltpu.VMEM((8, width), F32), pltpu.VMEM((8, 3 * N), F32),
            pltpu.VMEM((8, width + 3 * N), F32), pltpu.VMEM((8, width + 3 * N), F32), dma, dma,
        ],
        compiler_params=pltpu.CompilerParams(
            dimension_semantics=("arbitrary",), vmem_limit_bytes=48 * 1024 * 1024,
            collective_id=8, has_side_effects=True,
        ),
        cost_estimate=estimate(45),
        name="project",
    )(lengths, tok, tok, gain, weight, w_group, chan, bcpar, head, expand)


PACK = 16


def tail_kernel(
    n, grad_b, grad_v, normed_hbm, w_hbm, tok_hbm, back_hbm, late_hbm, wg_hbm,
    raw_t, fixed, gate_top, gate_end, tok_top, tok_end, inv, gain, gain_mine, sel_bc, sel_raw,
    late_rows, late_gain, taps_grad, bias_grad, norm_gain_grad, skip_grad, head_grad,
    tokens_out, value_out, cols_out, pack_out,
    gb, gv, nm, w_ref, tok, back, w_cols, col_grad,
    peer_part, own_part, core_part, b_got, b_next, b_last, b_full, raw_full,
    early, mid, send, got, nxt, last, gain_grad, z_out, z_got, z_on, z_last,
    ng, col_peer, col_own, col_core, col_out, col_got, col_on, col_last,
    row_buf, row_held, pack, pack_other, pack_pair, pack_pieces, pack_total, pack_all,
    local, raw_s, raw_r, b_s, b_r, f_s, f_r, core_s, core_r, z_s, z_r, row_s, row_r,
    sum_s, sum_r, piece_s, piece_r, group_s, group_r,
):
    s, c, t = lax.axis_index("shard"), lax.axis_index("context"), lax.axis_index("tensor")
    near = peers(t)
    to = [(s, c, near[0]), (s, c, near[1])]
    group = [(s, c, lax.rem(t + k, 4)) for k in (1, 2, 3)]
    to_core = (1 - s, c, t)
    to_piece = [(s, lax.rem(c + k, n), t) for k in range(1, n)]
    in_line = n == 4
    line = [(s, c + 1 - 2 * lax.rem(c, 2), t), (s, 3 - c, t)] if in_line else []
    steps, width = grad_v.shape
    size = w_ref.shape[0] // 4
    share = steps // 4
    mine_lanes = pl.ds(pl.multiple_of(t * size, size), size)
    loads = [
        pltpu.make_async_copy(src, dst, local.at[k])
        for k, (src, dst) in enumerate(
            [
                (grad_b, gb), (grad_v, gv), (normed_hbm, nm), (w_hbm, w_ref),
                (tok_hbm.at[:, mine_lanes], tok), (back_hbm.at[:, mine_lanes], back),
                (late_hbm, ng.at[pl.ds(GROUP, steps - GROUP), :]),
                (wg_hbm.at[mine_lanes, :], w_cols),
            ]
        )
    ]
    for load in loads:
        load.start()
    pl.semaphore_wait(greet(group + [to_core] + to_piece), n + 3)

    raw_full[t] = raw_t[...]
    raws = [
        remote(raw_t, raw_full.at[t], raw_s.at[k], raw_r.at[k], target)
        for k, target in enumerate(group)
    ]
    for copy in raws:
        copy.start()

    def rows_of(k):
        return pl.ds(pl.multiple_of(k * share, share), share)

    def lanes_of(side):
        return pl.ds(side * N, N)

    loads[0].wait()
    gb[steps - 8 :, :] = fixed[:, width:]

    def b_first(side, part):
        k = near[side] if part == 0 else 3 - t
        return remote(
            gb.at[rows_of(k), lanes_of(side)], b_got.at[side, part], b_s.at[side, part],
            b_r.at[side, part], to[side],
        )

    def b_second(side):
        return remote(
            b_next.at[side], b_last.at[side], b_s.at[side, 2], b_r.at[side, 2], to[1 - side]
        )

    def b_back(side, part):
        k = near[1 - side] if part == 2 else t
        where = b_full.at[rows_of(k), lanes_of(side)]
        return remote(
            where, where, b_s.at[side, 3 + part], b_r.at[side, 3 + part],
            to[1 - side] if part == 0 else to[side],
        )

    for side in (0, 1):
        for part in (0, 1):
            b_first(side, part).start()

    loads[1].wait()
    tail = gv[steps - 16 :, :].astype(F32)
    gv[steps - 16 :, :] = jnp.concatenate([tail[:8], fixed[:, :width]], axis=0).astype(BF16)
    loads[2].wait()
    half_d = nm.shape[1] // 2
    step = 256

    def product(shard, right, into):
        for m in range(half_d // step):
            lanes = pl.ds(pl.multiple_of(shard * half_d + m * step, step), step)
            into[m * step : (m + 1) * step, :] = over_rows(nm, lanes, right)

    product(1 - s, lambda rows: gv[rows, :], peer_part)
    core = remote(peer_part, core_part, core_s.at[0], core_r.at[0], to_core)
    core.start()

    for side in (0, 1):
        for part in (0, 1):
            b_first(side, part).wait()
        b_next[side] = gb[rows_of(near[1 - side]), lanes_of(side)] + b_got[side, 1]
        b_second(side).start()

    product(s, lambda rows: gv[rows, :], own_part)

    for side in (0, 1):
        b_second(side).wait()
        mine = gb[rows_of(t), lanes_of(side)] + b_got[side, 0] + b_last[side]
        b_full[rows_of(t), lanes_of(side)] = mine.astype(BF16)
        b_back(side, 0).start()

    block = half_d // n
    side_w = width // 2
    both = own_part
    if in_line:
        first = [c + 1 - 2 * lax.rem(c, 2), 3 - c]
        across = lax.rem(c + 2, 4)

    def block_rows(k):
        return pl.ds(pl.multiple_of(k * block, 8), block)

    def z_block(k, side):
        return both[block_rows(k), side * side_w : (side + 1) * side_w]

    def z_first(side):
        return remote(z_out.at[side], z_got.at[side], z_s.at[side], z_r.at[side], line[side])

    def z_second(side):
        return remote(z_on.at[side], z_last.at[side], z_s.at[2 + side], z_r.at[2 + side], line[1 - side])

    def col_first():
        return remote(col_out, col_got, z_s.at[4], z_r.at[4], line[0])

    def col_second():
        return remote(col_on, col_last, z_s.at[5], z_r.at[5], line[1])

    core.wait()
    both[...] = both[...] + core_part[...]
    if in_line:
        for side in (0, 1):
            z_out[side, :block, :] = z_block(first[side], side).astype(BF16)
            z_out[side, block:, :] = z_block(across, side).astype(BF16)
            z_first(side).start()
    for side in (0, 1):
        b_back(side, 0).wait()
        for part in (1, 2):
            b_back(side, part).start()

    loads[3].wait()
    half = GROUP // 2
    tail_half = END // 2

    def f_first(side):
        return remote(send.at[side], got.at[side], f_s.at[side], f_r.at[side], to[side])

    def f_second(side):
        return remote(
            nxt.at[side], last.at[side], f_s.at[2 + side], f_r.at[2 + side], to[1 - side]
        )

    gain_grad[...] = late_gain[...]
    for g in range(GROUP // PART, steps // PART):
        row_buf[:, g * PART : (g + 1) * PART] = late_rows[g]
    ends = [jnp.zeros((LANE - END, LANE), F32)]
    for side in (0, 1):
        rows = slice(side * half, (side + 1) * half)
        tail_rows = slice(side * tail_half, (side + 1) * tail_half)
        end_rows = slice(steps - END + side * tail_half, steps - END + (side + 1) * tail_half)
        x = jnp.concatenate(
            [
                jnp.concatenate([gate_top[rows, :], gv[rows, :]], axis=1),
                jnp.concatenate([gate_end[tail_rows, :], gv[end_rows, :]], axis=1),
            ],
            axis=0,
        )
        keep, go = shares_of(side, t)
        gone = dot(x, pick(w_ref, *go), 1, 1)
        send[side] = gone.astype(BF16)
        f_first(side).start()
        kept = dot(x, pick(w_ref, *keep), 1, 1)
        early[side] = kept[:, :size]
        mid[side] = kept[:, size:]
        scale = jnp.concatenate([inv[rows, :], inv[end_rows, :]], axis=0)
        parts = [kept[:, :size], kept[:, size:], gone[:, :size], gone[:, size:]]

        def z(lanes):
            values = jnp.concatenate([tok_top[rows, lanes], tok_end[tail_rows, lanes]], axis=0)
            return values.astype(F32) * scale

        sums = count_rows(parts, z, gain, keep + go, gain_grad)
        row_buf[:, rows] = row_dots(sums[:half])
        ends.append(sums[half:])
    row_buf[:, steps - LANE :] += row_dots(jnp.concatenate(ends, axis=0))

    for copy in raws:
        copy.wait()
    for side in (0, 1):
        for part in (1, 2):
            b_back(side, part).wait()
    raw_all = jnp.concatenate([raw_full[k] for k in range(4)], axis=0)

    for k in range(steps // GROUP):
        rows = slice(k * GROUP, (k + 1) * GROUP)
        chosen = dot(b_full[rows, :], sel_bc[...]) + dot(raw_all[:, rows], sel_raw[...], 0, 0)
        col_grad[rows, :] = chosen.astype(BF16)
    own_lanes = pl.ds(pl.multiple_of(t * LANE, LANE), LANE)
    product(1 - s, lambda rows: col_grad[rows, own_lanes], col_peer)
    col_core_copy = remote(col_peer, col_core, core_s.at[1], core_r.at[1], to_core)
    col_core_copy.start()
    loads[4].wait()
    loads[6].wait()
    loads[7].wait()
    ng[steps - END :, :] = jnp.zeros((END, size), F32)
    for k in range(steps // GROUP):
        rows = slice(k * GROUP, (k + 1) * GROUP)
        part = dot(col_grad[rows, :], w_cols[...], 1, 1)
        ng[rows, :] = part if k == 0 else ng[rows, :] + part
        part = part * (tok[rows, :].astype(F32) * inv[rows, :])
        gain_grad[:, mine_lanes] += fold(part)
        part = part * gain_mine[0:1, :]
        sums = part[:, :LANE]
        for sl in tiles(size)[1:]:
            sums = sums + part[:, sl]
        row_buf[:, rows] += row_dots(sums)
    row_copies = [
        remote(row_buf, row_held.at[k], row_s.at[k], row_r.at[k], target)
        for k, target in enumerate(group)
    ]
    for copy in row_copies:
        copy.start()

    pack[...] = jnp.zeros_like(pack)
    total = width + 2 * N
    add_up = lambda x: jnp.sum(x, axis=0, keepdims=True)
    for k in range(KERNEL):
        pack[k : k + 1, :total] = add_up(taps_grad[8 * k : 8 * k + 8, :])
    pack[KERNEL : KERNEL + 1, :total] = add_up(bias_grad[...])
    pack[KERNEL + 1 : KERNEL + 2, :width] = add_up(norm_gain_grad[...])
    pack[KERNEL + 2 : KERNEL + 3, :width] = add_up(skip_grad[...])
    pack[KERNEL + 3 : KERNEL + 4, :LANE] = add_up(head_grad[:8, :])
    pack[KERNEL + 4 : KERNEL + 5, :LANE] = add_up(head_grad[8:, :])
    pack[KERNEL + 5 : KERNEL + 6, :] = add_up(gain_grad[...])
    sum_core = remote(pack, pack_other, sum_s, sum_r, to_core)
    sum_core.start()

    for side in (0, 1):
        f_first(side).wait()
        nxt[side] = (mid[side] + got[side, :, size:].astype(F32)).astype(BF16)
        f_second(side).start()
        early[side] += got[side, :, :size].astype(F32)

    product(s, lambda rows: col_grad[rows, own_lanes], col_own)

    sum_core.wait()
    pack_pair[...] = pack[...] + pack_other[...]
    pack_pieces[c] = pack_pair[...]
    sum_pieces = [
        remote(pack_pair, pack_pieces.at[c], piece_s.at[k], piece_r.at[k], target)
        for k, target in enumerate(to_piece)
    ]
    for copy in sum_pieces:
        copy.start()
    if in_line:
        for side in (0, 1):
            z_first(side).wait()
            z_on[side] = (
                z_block(first[1 - side], side) + z_got[side, block:, :].astype(F32)
            ).astype(BF16)
            z_second(side).start()
    col_core_copy.wait()
    col_own[...] = col_own[...] + col_core[...]
    if in_line:
        col_out[:block, :] = col_own[block_rows(first[0]), :]
        col_out[block:, :] = col_own[block_rows(across), :]
        col_first().start()

    for copy in sum_pieces:
        copy.wait()
    pack_total[...] = sum(pack_pieces[k] for k in range(1, n)) + pack_pieces[0]
    pack_all[t] = pack_total[...]
    sum_group = [
        remote(pack_total, pack_all.at[t], group_s.at[k], group_r.at[k], target)
        for k, target in enumerate(group)
    ]
    for copy in sum_group:
        copy.start()
    if in_line:
        col_first().wait()
        col_on[...] = col_own[block_rows(first[1]), :] + col_got[block:, :]
        col_second().start()

    loads[5].wait()
    for copy in row_copies:
        copy.wait()
    for side in (0, 1):
        f_second(side).wait()
        early[side] += last[side].astype(F32)
        at = steps - END + side * tail_half
        ng[at : at + tail_half, :] += early[side, half:, :]
        ng[side * half : (side + 1) * half, :] += early[side, :half, :]
    row_total = row_buf[...] + row_held[0] + row_held[1] + row_held[2]
    for k in range(steps // LANE):
        rows = slice(k * LANE, (k + 1) * LANE)
        row_dot = jnp.broadcast_to(row_total[0:1, rows] * (1.0 / D), (LANE, LANE)).T
        scale = inv[rows, :]
        for sl in tiles(size):
            z_tile = tok[rows, sl].astype(F32) * scale
            change = scale * (ng[rows, sl] * gain_mine[0:1, sl] - z_tile * row_dot)
            tokens_out[rows, sl] = (back[rows, sl].astype(F32) + change).astype(BF16)

    if in_line:
        for side in (0, 1):
            z_second(side).wait()
            value_out[:, side * side_w : (side + 1) * side_w] = (
                z_block(c, side) + z_got[side, :block, :].astype(F32) + z_last[side].astype(F32)
            )
        col_second().wait()
        cols_out[...] = col_own[block_rows(c), :] + col_got[:block, :] + col_last[...]
    else:
        value_out[...] = both[...]
        cols_out[...] = col_own[...]
    for copy in sum_group:
        copy.wait()
    pack_out[...] = pack_all[...]


def run_tail(
    grad_b, grad_v, normed, weight, tok, back, late, w_group, raw_t, fixed, gate_grad, inv, gain,
    gain_mine, sel_bc, sel_raw, late_rows, late_gain, *small,
):
    n = lax.axis_size("context")
    steps, width = grad_v.shape
    size = D // 4
    half_d = D // 2
    block = half_d // n
    side_rows = (GROUP + END) // 2
    share = steps // 4
    top = lambda w: pl.BlockSpec((GROUP, w), lambda i: (0, 0), pipeline_mode=pl.Buffered(1))
    end = lambda w: pl.BlockSpec(
        (END, w), lambda i: (steps // END - 1, 0), pipeline_mode=pl.Buffered(1)
    )
    full = lambda x: once(*x.shape)
    hbm = pl.BlockSpec(memory_space=pl.ANY)
    dma = pltpu.SemaphoreType.DMA
    vmem = pltpu.VMEM
    value_rows = block if n == 4 else half_d
    pair = (2, side_rows, size)
    packed = (PACK, D)
    return pl.pallas_call(
        functools.partial(tail_kernel, n),
        grid=(1,),
        in_specs=[hbm] * 8
        + [full(raw_t), full(fixed), top(width), end(width), top(D), end(D)]
        + [full(x) for x in (inv, gain, gain_mine, sel_bc, sel_raw)]
        + [full(x) for x in (late_rows, late_gain, *small)],
        out_specs=[
            once(steps, size), once(value_rows, width), once(value_rows, LANE), once(4, *packed)
        ],
        out_shape=[
            shape(steps, size, dtype=BF16), shape(value_rows, width), shape(value_rows, LANE),
            shape(4, *packed),
        ],
        scratch_shapes=[
            vmem((steps, 2 * N), F32), vmem((steps, width), BF16), vmem(normed.shape, BF16),
            vmem(weight.shape, BF16), vmem((steps, size), BF16), vmem((steps, size), BF16),
            vmem((size, w_group.shape[1]), BF16),
            vmem((steps, w_group.shape[1]), BF16),
            vmem((half_d, width), F32), vmem((half_d, width), F32), vmem((half_d, width), F32),
            vmem((2, 2, share, N), F32), vmem((2, share, N), F32), vmem((2, share, N), F32),
            vmem((steps, 2 * N), BF16), vmem((4, 16, steps), BF16),
            vmem(pair, F32), vmem(pair, F32), vmem((2, side_rows, 2 * size), BF16),
            vmem((2, side_rows, 2 * size), BF16), vmem(pair, BF16), vmem(pair, BF16), vmem((8, D), F32),
            vmem((2, 2 * block, width // 2), BF16), vmem((2, 2 * block, width // 2), BF16),
            vmem((2, block, width // 2), BF16), vmem((2, block, width // 2), BF16),
            vmem((steps, size), F32),
            vmem((half_d, LANE), F32), vmem((half_d, LANE), F32), vmem((half_d, LANE), F32),
            vmem((2 * block, LANE), F32), vmem((2 * block, LANE), F32), vmem((block, LANE), F32),
            vmem((block, LANE), F32),
            vmem((8, steps), F32), vmem((3, 8, steps), F32),
            vmem(packed, F32), vmem(packed, F32), vmem(packed, F32), vmem((n, *packed), F32),
            vmem(packed, F32), vmem((4, *packed), F32),
            dma((8,)), dma((3,)), dma((3,)), dma((2, 6)), dma((2, 6)), dma((4,)), dma((4,)),
            dma((2,)), dma((2,)), dma((6,)), dma((6,)), dma((3,)), dma((3,)),
            dma, dma, dma((n - 1,)), dma((n - 1,)), dma((3,)), dma((3,)),
        ],
        compiler_params=pltpu.CompilerParams(
            dimension_semantics=("arbitrary",), vmem_limit_bytes=56 * 1024 * 1024,
            collective_id=5, has_side_effects=True,
        ),
        cost_estimate=estimate(50),
        name="tail",
    )(
        grad_b, grad_v, normed, weight, tok, back, late, w_group,
        raw_t, fixed, gate_grad, gate_grad, tok, tok, inv, gain, gain_mine, sel_bc, sel_raw,
        late_rows, late_gain, *small,
    )


def pad_rows(x, rows=8):
    return jnp.concatenate([x, jnp.zeros((rows - x.shape[0], x.shape[1]), x.dtype)], axis=0)


def pad_cols(x, cols=LANE):
    return jnp.concatenate([x, jnp.zeros((x.shape[0], cols - x.shape[1]), x.dtype)], axis=1)


def on_device(
    tokens, cotangent, doc_lengths, zx_weight, bcdt_weight, out_weight, input_gain, chan_params,
    bc_params, head_params, zx_first, bcdt_first, out_first, gain_first, chan_first, bc_first,
    head_first, zx_second, bcdt_second, out_second, gain_second, chan_second, bc_second, head_second,
):
    n_tensor = lax.axis_size("tensor")
    t_index = lax.axis_index("tensor")
    c_index = lax.axis_index("context")
    tok = tokens[0]
    resid = tok.astype(F32)
    back = cotangent[0]
    steps = resid.shape[0]
    inner_loc = INNER // n_tensor
    heads_loc = H // n_tensor
    share = D // n_tensor
    count = steps // L
    rows_loc = zx_weight.shape[0]
    cols_loc = bcdt_weight.shape[1]

    zx_flat = zx_weight.reshape(rows_loc, 2 * inner_loc)
    proj_w, cols_z = line_gather(zx_flat.astype(BF16), pad_cols(bcdt_weight.astype(BF16)))
    down_block, _ = lax.optimization_barrier((out_weight.astype(BF16).T, proj_w))
    down_t = lax.all_gather(down_block, ("shard", "context"), axis=0, tiled=True)
    chan_loc = lax.dynamic_slice_in_dim(chan_params, t_index * inner_loc, inner_loc, 1)
    head_loc = lax.dynamic_slice_in_dim(head_params, t_index * heads_loc, heads_loc, 1)
    chan8 = pad_rows(chan_loc)
    bc8 = pad_rows(bc_params)
    head8 = pad_rows(pad_cols(head_loc))
    spread_at = lax.broadcasted_iota(jnp.int32, (2 * LANE, inner_loc), 0) % LANE
    expand = (
        spread_at == lax.broadcasted_iota(jnp.int32, (2 * LANE, inner_loc), 1) // P_SIZE
    ).astype(BF16)
    gain8 = jnp.broadcast_to(input_gain[None], (8, D))
    (
        normed, inv_rms, projected, cols, info, marks_rows, edge_mask,
        act, delta, cum, sloc, pfx, final, halo_v, halo_b,
    ) = run_project(
        doc_lengths, tok, gain8, proj_w, cols_z, chan8, bc8, head8, expand, heads_loc, cols_loc
    )
    entry, back_scaled = run_entry(final, back, down_t)
    ssd, sums = run_ahead(
        act, delta, cum, info, marks_rows, sloc, pfx, entry, projected, back_scaled, chan8, head8,
        expand, heads_loc,
    )
    sums = small_sum(sums, 1)
    scaled, *out_fan = run_out(ssd, projected, sums, chan8, down_t)
    gate_grad, mixed_grad, aloc, sfx, first_adj, norm_gain_grad = run_norm(
        ssd, projected, back_scaled, sums, act, cum, info, chan8, expand, heads_loc
    )
    later, out_own, out_next, *z_arrays = run_middle(
        first_adj, out_fan, normed, gate_grad, back, scaled
    )
    resid_share = lax.dynamic_slice_in_dim(tok, t_index * share, share, 1).astype(F32)
    in_line = lax.axis_size("context") == 4
    total_width = inner_loc + 2 * N

    (
        grad_v, grad_b, raw_t, last_rows, _, taps_grad, bias_grad, skip_grad, head_grad,
        ng_late, late_rows, late_gain, out_last, *z_sum,
    ) = run_grand(
        projected, cols, halo_v, halo_b, info, marks_rows, delta, cum, ssd, mixed_grad,
        sloc, pfx, entry, aloc, sfx, later, chan8, bc8, head8, expand, heads_loc,
        gate_grad, proj_w, tok, inv_rms, gain8, edge_mask, out_next, z_arrays if in_line else [],
    )
    out_share = out_own + out_last.reshape(steps, share).astype(F32)
    block_out = (resid_share + out_share).astype(BF16)[None]
    if in_line:
        gate_g, down_g = z_sum[0][0], z_sum[0][1]
    else:
        gate_g, down_g = [
            lax.psum_scatter(z_arrays[0][k], "context", scatter_dimension=0, tiled=True) for k in (0, 1)
        ]
    column = np.arange(4 * LANE)
    column = np.where(column % LANE < cols_loc, column // LANE * cols_loc + column % LANE, -1)[None, :]
    sel_bc = (np.arange(2 * N)[:, None] == column).astype(ml_dtypes.bfloat16)
    slot = np.arange(4 * 16)[:, None]
    of_slot = np.where(slot % 16 < heads_loc, 2 * N + slot // 16 * heads_loc + slot % 16, -2)
    sel_raw = (of_slot == column).astype(ml_dtypes.bfloat16)
    gain_mine = jnp.broadcast_to(
        lax.dynamic_slice_in_dim(input_gain, t_index * share, share, 0)[None], (8, share)
    )
    tokens_grad, value_g, cols_g, packed = run_tail(
        grad_b, grad_v, normed, proj_w, tok, back, ng_late, cols_z, raw_t, last_rows, gate_grad,
        inv_rms, gain8, gain_mine, sel_bc, sel_raw, late_rows, late_gain,
        taps_grad, bias_grad, norm_gain_grad, skip_grad, head_grad,
    )
    tokens_grad = tokens_grad[None]
    if not in_line:
        value_g = lax.psum_scatter(value_g, "context", scatter_dimension=0, tiled=True)
        cols_g = lax.psum_scatter(cols_g[:, :cols_loc], "context", scatter_dimension=0, tiled=True)
        cols_g = pad_cols(cols_g)
    flip = lambda *arrays: tuple(a.T for a in arrays)
    lift = lambda *arrays: tuple(a[None] for a in arrays)
    news = run_adam(
        (gate_g, value_g, down_g, cols_g, packed),
        (
            (zx_weight, zx_first, zx_second), flip(out_weight, out_first, out_second),
            flip(bcdt_weight, bcdt_first, bcdt_second), lift(input_gain, gain_first, gain_second),
            (chan_params, chan_first, chan_second), (bc_params, bc_first, bc_second),
            (head_params, head_first, head_second),
        ),
        heads_loc, cols_loc,
    )
    zx_new, out_new, bcdt_new, gain_new = news[:3], flip(*news[3:6]), flip(*news[6:9]), news[9:12]
    return (
        block_out, tokens_grad, *zx_new, *bcdt_new, *out_new, *[g[0] for g in gain_new], *news[12:]
    )


def solution(mesh):
    big = P(("shard", "context"), None, "tensor")
    cols = P(("shard", "context"), "tensor")
    down = P("tensor", ("shard", "context"))
    rows = P("shard", "context", None)
    out_rows = P("shard", "context", "tensor")
    return jax.shard_map(
        on_device,
        mesh=mesh,
        in_specs=(
            rows, rows, P("shard", None), big, cols, down, P(), P(), P(), P(),
            big, cols, down, P(), P(), P(), P(),
            big, cols, down, P(), P(), P(), P(),
        ),
        out_specs=(
            out_rows, out_rows, big, big, big, cols, cols, cols, down, down, down,
            *([P()] * 12),
        ),
        check_vma=False,
    )
```

```python
import functools

import jax
import jax.numpy as jnp
import ml_dtypes
import numpy as np
from jax import lax
from jax.experimental import pallas as pl
from jax.experimental.pallas import tpu as pltpu
from jax.sharding import PartitionSpec as P

D = 1536
INNER = 3072
H = 48
P_SIZE = 64
N = 128
KERNEL = 4
STEP = 10

EPS = 1e-05
BETA_ONE = 0.9
BETA_TWO = 0.999
ADAM_EPS = 1e-08
DECAY = 0.1
RATE_MATRIX = 0.05
RATE_SMALL = 0.2

L = 128
LANE = 128
GROUP = 4 * L
PART = 2 * L
END = 32
LOG2E = 1.4426950408889634
F32 = jnp.float32
BF16 = jnp.bfloat16
VMEM_LIMIT = 48 * 1024 * 1024


def from_behind(block, axis, distance):
    devices = range(lax.axis_size(axis))
    route = [(i - distance, i) for i in devices if i - distance in devices]
    return lax.ppermute(block, axis, route)


def adamw(weight, grad, first, second, rate, decay):
    first_new = BETA_ONE * first + (1.0 - BETA_ONE) * grad
    second_new = BETA_TWO * second + (1.0 - BETA_TWO) * grad * grad
    scale_one = 1.0 - BETA_ONE**STEP
    scale_two = 1.0 - BETA_TWO**STEP
    update = first_new / scale_one / (jnp.sqrt(second_new / scale_two) + ADAM_EPS)
    return (weight - rate * (update + decay * weight), first_new, second_new)


def two(x):
    hi = x.astype(BF16)
    return hi, (x - hi.astype(F32)).astype(BF16)


def dot(a, b, ca=1, cb=0):
    return lax.dot_general(a, b, (((ca,), (cb,)), ((), ())), preferred_element_type=F32)


def dot3(a, b, ca=1, cb=0):
    ah, al = two(a)
    bh, bl = two(b)
    return dot(
        jnp.concatenate([ah, al, ah], axis=ca), jnp.concatenate([bh, bh, bl], axis=cb), ca, cb
    )


def over_rows(left, lanes, right):
    total = None
    for at in range(0, left.shape[0], GROUP):
        rows = slice(at, at + GROUP)
        part = dot(left[rows, lanes], right(rows), 0, 0)
        total = part if total is None else total + part
    return total


def tri_sum(tri, x):
    hi = x.astype(BF16)
    rest = x - hi.astype(F32)
    mid = rest.astype(BF16)
    low = (rest - mid.astype(F32)).astype(BF16)
    out = dot(tri, jnp.concatenate([hi, mid, low], axis=1))
    w = x.shape[1]
    return out[:, :w] + out[:, w : 2 * w] + out[:, 2 * w :]


def spread(x, e_ref):
    hi, lo = two(x)
    return dot(jnp.concatenate([hi, lo], axis=1), e_ref[...])


def per_head(x, e_ref):
    hi, lo = two(x)
    e = e_ref[:LANE, :]
    return dot(hi, e, 1, 1) + dot(lo, e, 1, 1)


def sigmoid(x):
    return 1.0 / (1.0 + jnp.exp(-x))


def softplus(x):
    return jnp.maximum(x, 0.0) + jnp.log1p(jnp.exp(-jnp.abs(x)))


def tiles(width):
    return [slice(k, k + LANE) for k in range(0, width, LANE)]


def fold(x):
    return jnp.sum(x.reshape(x.shape[0] // 8, 8, x.shape[1]), axis=0)


def lower_mask():
    row = lax.broadcasted_iota(jnp.int32, (L, L), 0)
    col = lax.broadcasted_iota(jnp.int32, (L, L), 1)
    return row >= col


def keep_mask(info, marks_row):
    return jnp.logical_and(lower_mask(), info[:, 5:6] == marks_row[0:1, :])


def decay_of(keep, cum, cum_t, h):
    return jnp.exp2(jnp.where(keep, cum[:, h : h + 1] - cum_t[h : h + 1, :], -1e30))


def load_ext(ext_ref, cur_ref, prev_ref, halo_ref, j, first):
    if j > 0:
        ext_ref[0:8, :] = cur_ref[j * L - 8 : j * L, :]
    else:

        @pl.when(first)
        def _():
            ext_ref[0:8, :] = halo_ref[...]

        @pl.when(jnp.logical_not(first))
        def _():
            ext_ref[0:8, :] = prev_ref[...]

    ext_ref[8 : 8 + L, :] = cur_ref[j * L : (j + 1) * L, :]


def rows_of_chunk(ref, j):
    return ref.at[pl.ds(pl.multiple_of(j * L, L), L), :]


def lead_of_chunk(ref, j):
    return ref.at[pl.ds(j, 1)]


def load_ext_of(ext_ref, cur_ref, prev_ref, halo_ref, j, first):
    @pl.when(first)
    def _():
        ext_ref[0:8, :] = halo_ref[...]

    @pl.when(jnp.logical_and(j == 0, jnp.logical_not(first)))
    def _():
        ext_ref[0:8, :] = prev_ref[...]

    @pl.when(j > 0)
    def _():
        ext_ref[0:8, :] = cur_ref[pl.ds(pl.multiple_of(jnp.maximum(j * L - 8, 0), 8), 8), :]

    ext_ref[8 : 8 + L, :] = cur_ref[pl.ds(pl.multiple_of(j * L, L), L), :]


def rows_at(ref, j):
    return ref.at[j * L : (j + 1) * L, :]


def lead_at(ref, j):
    return ref.at[j : j + 1]


def conv_tile(ext_ref, info, taps, sl):
    shifted = []
    total = jnp.broadcast_to(taps[KERNEL : KERNEL + 1, :], (L, LANE))
    for k in range(KERNEL):
        val = ext_ref[pl.ds(8 - KERNEL + 1 + k, L), sl]
        if k < KERNEL - 1:
            val = val * info[:, k : k + 1]
        shifted.append(val)
        total = total + taps[k : k + 1, :] * val
    return shifted, total


def prep_chunk(
    bc, info_ref, chan, bcpar, head, e_ref, act, delta_ref, cum_ref, sloc, pfx, ext_v, ext_b, state, prod
):
    info = info_ref[...]
    width = ext_v.shape[1]
    for sl in tiles(width):
        _, total = conv_tile(ext_v, info, chan[:, sl], sl)
        act[:, sl] = total * sigmoid(total)
    for sl in tiles(2 * N):
        _, total = conv_tile(ext_b, info, bcpar[:, sl], sl)
        act[:, slice(width + sl.start, width + sl.stop)] = total * sigmoid(total)
    raw = bc[:, 2 * N : 3 * N]
    delta = softplus(raw + head[0:1, :])
    dlog = -delta * (jnp.exp(head[1:2, :]) * LOG2E)
    tri = jnp.where(lower_mask(), 1.0, 0.0).astype(BF16)
    cum = tri_sum(tri, dlog)
    delta_ref[...] = delta
    cum_ref[...] = cum
    sloc[0] = state[...]
    pfx[0] = prod[...]
    last = cum[L - 1 : L, :]
    tail = info[:, 4:5] * jnp.exp2(last - cum) * delta
    through = spread(
        jnp.broadcast_to(info[L - 1 : L, 3:4] * jnp.exp2(last), (8, LANE)), e_ref
    )
    weights = spread(tail, e_ref)
    tail_u = act[:, :width] * weights
    fresh = dot3(act[:, width : width + N], tail_u, 0, 0)
    state[...] = state[...] * through[0:1, :] + fresh
    prod[...] = prod[...] * through


def row_block(width, col=0, rows=GROUP):
    return pl.BlockSpec((rows, width), lambda i: (i, col))


def prev_block(width, col=0, rows=GROUP):
    return pl.BlockSpec((8, width), lambda i: (jnp.maximum(i * (rows // 8) - 1, 0), col))


def lead_block(*dims, rows=GROUP):
    return pl.BlockSpec((rows // L, *dims), lambda i: (i, 0, 0))


def whole(*shape):
    return pl.BlockSpec(shape, lambda i: (0,) * len(shape))


def once(*shape):
    return pl.BlockSpec(shape, lambda i: (0,) * len(shape), pipeline_mode=pl.Buffered(1))


def estimate(us):
    return pl.CostEstimate(flops=int(us * 1.1e9), bytes_accessed=int(us * 1e6), transcendentals=0)


def params(**kw):
    return pltpu.CompilerParams(
        dimension_semantics=("arbitrary",), vmem_limit_bytes=VMEM_LIMIT, **kw
    )


def shape(*dims, dtype=F32):
    return jax.ShapeDtypeStruct(dims, dtype)


def ahead_kernel(
    heads, act, delta, cum, info, marks, sloc, pfx, entry, gate, back, chan, head, e_ref, ssd, sums
):
    for j in range(act.shape[0] // L):
        ahead_chunk(
            rows_at(act, j), rows_at(delta, j), rows_at(cum, j), rows_at(info, j), lead_at(marks, j),
            lead_at(sloc, j), lead_at(pfx, j), entry, rows_at(gate, j), rows_at(back, j), chan, head,
            e_ref, rows_at(ssd, j), lead_at(sums, j),
        )


def ahead_chunk(
    act, delta_ref, cum_ref, info_ref, marks_ref, sloc, pfx, entry, gate, back, chan, head, e_ref, ssd, sums
):
    width = act.shape[1] - 2 * N
    info = info_ref[...]
    cum = cum_ref[...]
    cum_t = cum.T
    keep = keep_mask(info, marks_ref[0])
    bmat = act[:, width : width + N]
    cmat = act[:, width + N :]
    scores = dot3(cmat, bmat, 1, 1)
    xs = act[:, :width]
    u_hi, u_lo = two(xs * spread(delta_ref[...], e_ref))
    state = sloc[0] + entry[...] * pfx[0, 0:1, :]
    entering = dot3(cmat, state)
    eexp = spread(info[:, 3:4] * jnp.exp2(cum), e_ref)
    skip = spread(jnp.broadcast_to(head[2:3, :], (8, LANE)), e_ref)
    lane = lax.broadcasted_iota(jnp.int32, (1, LANE), 1)
    left = jnp.where(lane < P_SIZE, 1.0, 0.0).astype(BF16)
    right = jnp.where(lane < P_SIZE, 0.0, 1.0).astype(BF16)
    square = jnp.zeros((L, LANE), F32)
    cross = jnp.zeros((L, LANE), F32)
    for q, sl in enumerate(tiles(width)):
        mix = jnp.concatenate(
            [(scores * decay_of(keep, cum, cum_t, 2 * q + r)).astype(BF16) for r in (0, 1)], axis=1
        )
        both = jnp.concatenate([u_hi[:, sl], u_lo[:, sl]], axis=1)
        rhs = jnp.concatenate(
            [both * jnp.concatenate([m, m], axis=1) for m in (left, right)], axis=0
        )
        out = dot(mix, rhs)
        y = out[:, :LANE] + out[:, LANE:] + entering[:, sl] * eexp[:, sl]
        y = y + skip[0:1, sl] * xs[:, sl]
        ssd[:, sl] = y
        g = gate[:, sl]
        gated = y * g * sigmoid(g)
        square = square + gated * gated
        cross = cross + gated * (back[:, sl] * chan[KERNEL + 1 : KERNEL + 2, sl])
    ones = jnp.ones((8, LANE), BF16)
    rows = []
    for part in (square, cross):
        hi, lo = two(part)
        rows.append(dot(ones, hi, 1, 1) + dot(ones, lo, 1, 1))
    pick = lax.broadcasted_iota(jnp.int32, (8, LANE), 0)
    sums[0] = jnp.where(pick == 0, rows[0], jnp.where(pick == 1, rows[1], 0.0))


def run_ahead(act, delta, cum, info, marks, sloc, pfx, entry, projected, back, chan, head, expand, heads):
    steps, width = projected.shape[0], projected.shape[1] // 2
    count = steps // L
    return pl.pallas_call(
        functools.partial(ahead_kernel, heads),
        grid=(steps // GROUP,),
        in_specs=[
            row_block(width + 2 * N), row_block(LANE), row_block(LANE), row_block(LANE),
            lead_block(8, L), lead_block(N, width), lead_block(8, width),
            once(N, width), row_block(width, 0), row_block(width),
            once(8, width), once(8, LANE), once(2 * LANE, width),
        ],
        out_specs=[row_block(width), lead_block(8, L)],
        out_shape=[shape(steps, width), shape(count, 8, L)],
        compiler_params=params(),
        cost_estimate=estimate(20),
        name="ahead",
    )(act, delta, cum, info, marks, sloc, pfx, entry, projected, back, chan, head, expand)


def norm_kernel(
    heads, ssd, gate, back, sums, cmat, cum, info, chan, e_ref,
    gate_grad, mixed_grad, aloc, sfx, fin, gain_grad, state, prod,
):
    i = pl.program_id(0)

    @pl.when(i == 0)
    def _():
        state[...] = jnp.zeros_like(state)
        prod[...] = jnp.ones_like(prod)
        gain_grad[...] = jnp.zeros_like(gain_grad)

    chunks = ssd.shape[0] // L

    for j in reversed(range(chunks)):
        norm_chunk(
            rows_at(ssd, j), rows_at(gate, j), rows_at(back, j), lead_at(sums, j), rows_at(cmat, j),
            rows_at(cum, j), rows_at(info, j), chan, e_ref, rows_at(gate_grad, j),
            rows_at(mixed_grad, j), lead_at(aloc, j), lead_at(sfx, j), gain_grad, state, prod,
        )

    @pl.when(i == pl.num_programs(0) - 1)
    def _():
        fin[:N, :] = state[...]
        fin[N:, :] = prod[...]


def norm_chunk(
    ssd, gate, back, sums, cmat_ref, cum_ref, info_ref, chan, e_ref,
    gate_grad, mixed_grad, aloc, sfx, gain_grad, state, prod,
):
    width = ssd.shape[1]
    rows = sums[0]
    inv_row = lax.rsqrt(rows[0:1, :] / INNER + EPS)
    cross_row = inv_row * inv_row * inv_row * (rows[1:2, :] / INNER)
    inv = jnp.broadcast_to(inv_row, (LANE, L)).T
    cross = jnp.broadcast_to(cross_row, (LANE, L)).T
    info = info_ref[...]
    cum = cum_ref[...]
    eexp = spread(info[:, 3:4] * jnp.exp2(cum), e_ref)
    e_mixed = []
    for sl in tiles(width):
        g = gate[:, sl]
        sig = sigmoid(g)
        soft = g * sig
        y = ssd[:, sl]
        gated = y * soft
        bs = back[:, sl]
        gain = chan[KERNEL + 1 : KERNEL + 2, sl]
        normed = gated * inv
        gain_grad[:, sl] += fold(bs * normed)
        gg = inv * (bs * gain) - gated * cross
        mg = gg * soft
        mixed_grad[:, sl] = mg
        gate_grad[:, sl] = (gg * y * sig * (1.0 + g * (1.0 - sig))).astype(BF16)
        e_mixed.append(mg * eexp[:, sl])
    aloc[0] = state[...]
    sfx[0] = prod[...]
    through = spread(
        jnp.broadcast_to(info[L - 1 : L, 3:4] * jnp.exp2(cum[L - 1 : L, :]), (8, LANE)), e_ref
    )
    fresh = dot3(cmat_ref[...], jnp.concatenate(e_mixed, axis=1), 0, 0)
    state[...] = state[...] * through[0:1, :] + fresh
    prod[...] = prod[...] * through


def run_norm(ssd, projected, back, sums, act, cum, info, chan, expand, heads):
    steps, width = ssd.shape
    count = steps // L
    blocks = steps // GROUP
    turn = lambda spec: pl.BlockSpec(
        spec.block_shape, lambda i, m=spec.index_map: m(blocks - 1 - i)
    )
    c_col = width // N + 1
    return pl.pallas_call(
        functools.partial(norm_kernel, heads),
        grid=(blocks,),
        in_specs=[
            turn(row_block(width)), turn(row_block(width, 0)), turn(row_block(width)),
            turn(lead_block(8, L)),
            turn(row_block(N, c_col)), turn(row_block(LANE)), turn(row_block(LANE)),
            once(8, width), once(2 * LANE, width),
        ],
        out_specs=[
            turn(row_block(width)), turn(row_block(width)),
            turn(lead_block(N, width)),
            turn(lead_block(8, width)),
            whole(N + 8, width), whole(8, width),
        ],
        out_shape=[
            shape(steps, width, dtype=BF16), shape(steps, width),
            shape(count, N, width), shape(count, 8, width), shape(N + 8, width), shape(8, width),
        ],
        scratch_shapes=[pltpu.VMEM((N, width), F32), pltpu.VMEM((8, width), F32)],
        compiler_params=params(),
        cost_estimate=estimate(21),
        name="norm_back",
    )(ssd, projected, back, sums, act, cum, info, chan, expand)


def behind_chunk(
    heads, j, start, first, val, valp, bc, bcp, halo_v, halo_b, info_ref, marks_ref, delta_ref, cum_ref,
    ssd, mixed_grad, sloc, pfx, entry, aloc, sfx, later, chan, bcpar, head, e_ref,
    grad_v, grad_b, raw_grad, tail_rows, head_rows, taps_grad, bias_grad, skip_grad, head_grad,
    ext_v, ext_b, slope, d_tot,
):
    width = val.shape[1]
    total_width = width + 2 * N

    @pl.when(start)
    def _():
        d_tot[0:8, :] = jnp.zeros((8, total_width), F32)
        taps_grad[...] = jnp.zeros_like(taps_grad)
        bias_grad[...] = jnp.zeros_like(bias_grad)
        skip_grad[...] = jnp.zeros_like(skip_grad)
        head_grad[...] = jnp.zeros_like(head_grad)

    d_tot[L:, :] = d_tot[0:8, :]
    load_ext_of(ext_v, val, valp, halo_v, j, first)
    load_ext_of(ext_b, bc, bcp, halo_b, j, first)
    raw = bc[pl.ds(pl.multiple_of(j * L, L), L), 2 * N : 3 * N]
    info_ref, marks_ref = rows_of_chunk(info_ref, j), lead_of_chunk(marks_ref, j)
    delta_ref, cum_ref = rows_of_chunk(delta_ref, j), rows_of_chunk(cum_ref, j)
    ssd, mixed_grad = rows_of_chunk(ssd, j), rows_of_chunk(mixed_grad, j)
    sloc, pfx = lead_of_chunk(sloc, j), lead_of_chunk(pfx, j)
    aloc, sfx = lead_of_chunk(aloc, j), lead_of_chunk(sfx, j)
    grad_v, grad_b = rows_of_chunk(grad_v, j), rows_of_chunk(grad_b, j)
    raw_grad = raw_grad.at[:, pl.ds(pl.multiple_of(j * L, L), L)]
    info = info_ref[...]

    def activate(ext_ref, taps, sl, at):
        _, total = conv_tile(ext_ref, info, taps[:, sl], sl)
        sig = sigmoid(total)
        slope[:, slice(at, at + LANE)] = sig * (1.0 + total * (1.0 - sig))
        return total * sig

    xs = jnp.concatenate([activate(ext_v, chan, sl, sl.start) for sl in tiles(width)], axis=1)
    bmat = activate(ext_b, bcpar, slice(0, N), width)
    cmat = activate(ext_b, bcpar, slice(N, 2 * N), width + N)

    delta = delta_ref[...]
    cum = cum_ref[...]
    cum_t = cum.T
    keep = keep_mask(info, marks_ref[0])
    last = cum[L - 1 : L, :]
    scores = dot3(cmat, bmat, 1, 1)
    dexp = spread(delta, e_ref)
    eexp = spread(info[:, 3:4] * jnp.exp2(cum), e_ref)
    texp = spread(info[:, 4:5] * jnp.exp2(last - cum), e_ref)
    u = xs * dexp
    u_hi, u_lo = two(u)
    dy = mixed_grad[...]
    dy_hi, dy_lo = two(dy)
    skip = spread(jnp.broadcast_to(head[2:3, :], (8, LANE)), e_ref)
    state = sloc[0] + entry[...] * pfx[0, 0:1, :]
    adj = aloc[0] + later[...] * sfx[0, 0:1, :]
    tail_du = dot3(bmat, adj) * texp
    lane = lax.broadcasted_iota(jnp.int32, (1, LANE), 1)
    left = jnp.where(lane < P_SIZE, 1.0, 0.0).astype(BF16)
    right = jnp.where(lane < P_SIZE, 0.0, 1.0).astype(BF16)
    two_left = jnp.concatenate([left, left], axis=1)
    two_right = jnp.concatenate([right, right], axis=1)
    d_scores = jnp.zeros((L, L), F32)
    inner_du = []
    for q, sl in enumerate(tiles(width)):
        decays = [decay_of(keep, cum, cum_t, 2 * q + r) for r in (0, 1)]
        mix = jnp.concatenate([(scores * d).astype(BF16) for d in decays], axis=0)
        dy_both = jnp.concatenate([dy_hi[:, sl], dy_lo[:, sl]], axis=1)
        rhs = jnp.concatenate([dy_both * two_left, dy_both * two_right], axis=0)
        out = dot(mix, rhs, 0, 0)
        inner_du.append(out[:, :LANE] + out[:, LANE:])
        u_twice = jnp.concatenate([u_hi[:, sl], u_hi[:, sl]], axis=1)
        u_rows = jnp.concatenate([u_twice * two_left, u_twice * two_right], axis=0)
        d_mix = dot(dy_both, u_rows, 1, 1)
        d_scores = d_scores + d_mix[:, :L] * decays[0] + d_mix[:, L:] * decays[1]
    du = jnp.concatenate(inner_du, axis=1) + tail_du
    d_xs = dexp * du + skip[0:1, :] * dy
    d_b = dot3(d_scores, cmat, 0, 0) + dot3(u * texp, adj, 1, 1)
    d_c = dot3(d_scores, bmat) + dot3(dy * eexp, state, 1, 1)
    skip_grad[...] += fold(dy * xs)

    direct = per_head(xs * du, e_ref)
    mixed = ssd[...] - skip[0:1, :] * xs
    d_cum = per_head(dy * mixed, e_ref) - delta * direct
    at_last = jnp.sum(per_head(u * tail_du, e_ref), axis=0, keepdims=True)
    through = info[L - 1 : L, 3:4] * jnp.exp2(last)
    pair = per_head(fold(adj * state), e_ref)
    at_last = at_last + through * jnp.sum(pair, axis=0, keepdims=True)
    upper = jnp.where(lower_mask(), 1.0, 0.0).astype(BF16).T
    d_log = tri_sum(upper, d_cum) + at_last
    rate = jnp.exp(head[1:2, :])
    valid = lane < heads
    d_raw = (direct - d_log * rate) * sigmoid(raw + head[0:1, :])
    d_raw = jnp.where(valid, d_raw, 0.0)
    raw_grad[...] = d_raw.T[:16, :].astype(BF16)
    head_grad[0:8, :] += fold(d_raw)
    head_grad[8:16, :] += fold(jnp.where(valid, -d_log * delta * rate, 0.0))

    d_act = [d_xs[:, sl] for sl in tiles(width)] + [d_b, d_c]
    for q in range(total_width // LANE):
        sl = slice(q * LANE, (q + 1) * LANE)
        if q < width // LANE:
            ext_ref, taps, part = ext_v, chan[:, sl], sl
        else:
            part = slice(sl.start - width, sl.stop - width)
            ext_ref, taps = ext_b, bcpar[:, part]
        dt = d_act[q] * slope[:, sl]
        d_tot[0:L, sl] = dt
        bias_grad[:, sl] += fold(dt)
        for k in range(KERNEL):
            moved = ext_ref[pl.ds(8 - KERNEL + 1 + k, L), part]
            if k < KERNEL - 1:
                moved = moved * info[:, k : k + 1]
            taps_grad[8 * k : 8 * k + 8, sl] += fold(dt * moved)
        total = dt * taps[KERNEL - 1 : KERNEL, :]
        for s in range(1, KERNEL):
            total = total + taps[KERNEL - 1 - s : KERNEL - s, :] * (
                d_tot[pl.ds(s, L), sl] * info[:, 7 + s : 8 + s]
            )
        if q < width // LANE:
            grad_v[:, sl] = total.astype(BF16)
        else:
            grad_b[:, part] = total

        @pl.when(start)
        def _():
            tail_rows[:, sl] = total[L - 8 :, :]

    @pl.when(first)
    def _():
        head_rows[...] = d_tot[0:8, :]


def remote(src, dst, send, recv, target):
    return pltpu.make_async_remote_copy(
        src_ref=src, dst_ref=dst, send_sem=send, recv_sem=recv, device_id=target,
        device_id_type=pl.DeviceIdType.MESH,
    )


def greet(targets):
    barrier = pltpu.get_barrier_semaphore()
    for target in targets:
        pl.semaphore_signal(
            barrier, inc=1, device_id=target, device_id_type=pl.DeviceIdType.MESH
        )
    return barrier


def count_rows(parts, z, gain, at, gain_grad):
    rows = jnp.zeros((parts[0].shape[0], LANE), F32)
    size = parts[0].shape[1]
    for part, k in zip(parts, at):
        lanes = pl.ds(pl.multiple_of(k * size, size), size)
        part = part * z(lanes)
        gain_grad[:, lanes] += fold(part)
        part = part * gain[0:1, lanes]
        for sl in tiles(size):
            rows = rows + part[:, sl]
    return rows


def row_dots(rows):
    ones = jnp.ones((8, LANE), BF16)
    hi, lo = two(rows)
    return dot(ones, hi, 1, 1) + dot(ones, lo, 1, 1)


def grand_kernel(heads, n, *refs):
    behind, refs = refs[:22], refs[22:]
    gate_grad, w_ref, tok, inv, gain, edge_mask, out_next = refs[:7]
    refs = refs[7:]
    in_line = n == 4
    if in_line:
        z_out, z_mid, z_mine = refs[:3]
        refs = refs[3:]
    outs, refs = refs[:9], refs[9:]
    ng_own, row_sums, gain_grad, out_last = refs[:4]
    refs = refs[4:]
    if in_line:
        z_sum, refs = refs[0], refs[1:]
    scratch, refs = refs[:4], refs[4:]
    mid, send, got, nxt, last, edge, s1, r1, s2, r2, edge_s, edge_r, o_s, o_r = refs[:14]
    if in_line:
        z_got, z_on, z_last, z_s, z_r = refs[14:]
    chan, bcpar = behind[18], behind[19]
    grad_v, tail_rows = outs[0], outs[3]
    d_tot = scratch[3]
    i, n_steps = pl.program_id(0), pl.num_programs(0)
    s, c, t = lax.axis_index("shard"), lax.axis_index("context"), lax.axis_index("tensor")
    near = peers(t)
    to = [(s, c, near[0]), (s, c, near[1])]
    width = grad_v.shape[1]
    size = w_ref.shape[0] // 4
    inside = mid.shape[0]
    chunks = grad_v.shape[0] // L

    @pl.when(i == 0)
    def _():
        pl.semaphore_wait(greet(to + beside_of(n)), 4)
        gain_grad[...] = jnp.zeros_like(gain_grad)

    def out_hop(side):
        return remote(
            out_next.at[side], out_last.at[side], o_s.at[side], o_r.at[side], to[1 - side]
        )

    @pl.when(i == 0)
    def _():
        for side in (0, 1):
            out_hop(side).start()

    if in_line:
        line = [(s, c + 1 - 2 * lax.rem(c, 2), t), (s, 3 - c, t)]
        block = z_mid.shape[1]

        def z_first(k):
            return remote(z_out.at[k], z_got.at[k], z_s.at[k], z_r.at[k], line[k])

        def z_second(k):
            return remote(z_on.at[k], z_last.at[k], z_s.at[2 + k], z_r.at[2 + k], line[1 - k])

        @pl.when(i == 0)
        def _():
            for k in (0, 1):
                z_first(k).start()

        @pl.when(i == n_steps // 2)
        def _():
            for k in (0, 1):
                z_first(k).wait()
                z_on[k] = (z_mid[k] + z_got[k, block:, :].astype(F32)).astype(BF16)
                z_second(k).start()
                z_sum[k] = z_mine[k] + z_got[k, :block, :].astype(F32)

        @pl.when(i == n_steps - 1)
        def _():
            for k in (0, 1):
                z_second(k).wait()
                z_sum[k] += z_last[k].astype(F32)

    def first_hop(k, side):
        return remote(send.at[k], got.at[k], s1.at[k], r1.at[k], to[side])

    def second_hop(k, side):
        return remote(nxt.at[k], last.at[k], s2.at[k], r2.at[k], to[1 - side])

    def place(k):
        return pl.ds(pl.multiple_of((inside - 1 - k) * PART, PART), PART)

    def turn_over(k, side):
        first_hop(k, side).wait()
        nxt[k] = (mid[k] + got[k, :, size:].astype(F32)).astype(BF16)
        second_hop(k, side).start()
        ng_own[place(k), :] += got[k, :, :size].astype(F32)

    def one(step, carry):
        j = chunks - 1 - step
        behind_chunk(
            heads, j, jnp.logical_and(i == 0, step == 0),
            jnp.logical_and(i == n_steps - 1, j == 0), *behind, *outs, *scratch,
        )
        for side in (0, 1):
            ready = jnp.logical_and(step == 0, lax.rem(i, 2) == 1 - side)

            @pl.when(jnp.logical_and(ready, jnp.logical_and(i >= 2, i < inside + 2)))
            def _():
                turn_over(i - 2, side)

        return carry

    lax.fori_loop(0, chunks, one, 0)

    def fan(side):
        counted = jnp.where(i == 0, PART - END, PART)
        x = jnp.concatenate([gate_grad[...], grad_v[...]], axis=1)
        keep, go = shares_of(side, t)
        gone = dot(x, pick(w_ref, *go), 1, 1)
        send[i] = gone.astype(BF16)
        first_hop(i, side).start()
        kept = dot(x, pick(w_ref, *keep), 1, 1)
        ng_own[place(i), :] = kept[:, :size]
        mid[i] = kept[:, size:]
        row = lax.broadcasted_iota(jnp.int32, (PART, 1), 0)
        scale = jnp.where(row < counted, inv[...], 0.0)
        parts = [kept[:, :size], kept[:, size:], gone[:, :size], gone[:, size:]]
        sums = count_rows(
            parts, lambda lanes: tok[:, lanes].astype(F32) * scale, gain, keep + go, gain_grad
        )
        row_sums[0] = row_dots(sums)

    for side in (0, 1):
        parity = lax.rem(i, 2) == 1 - side

        @pl.when(jnp.logical_and(parity, i < inside))
        def _():
            fan(side)

    @pl.when(i == n_steps - 1)
    def _():
        before = (s, jnp.maximum(c - 1, 0), t)
        copy = remote(d_tot.at[pl.ds(0, 8), :], edge, edge_s, edge_r, before)

        @pl.when(c > 0)
        def _():
            copy.start()

        for k in range(inside):
            second_hop(k, 1 - k % 2).wait()
            ng_own[place(k), :] += last[k].astype(F32)
        for side in (0, 1):
            out_hop(side).wait()

        @pl.when(c < n - 1)
        def _():
            copy.wait_recv()
            for shift in range(1, KERNEL):
                moved = pltpu.roll(edge[...], 8 - shift, 0) * edge_mask[
                    8 * shift - 8 : 8 * shift, 0:1
                ]
                tap = slice(KERNEL - 1 - shift, KERNEL - shift)
                tail_rows[:, :width] += chan[tap, :] * moved[:, :width]
                tail_rows[:, width:] += bcpar[tap, :] * moved[:, width:]

        @pl.when(c > 0)
        def _():
            copy.wait_send()


def run_grand(
    projected, cols, halo_v, halo_b, info, marks, delta, cum, ssd, mixed_grad, sloc, pfx, entry,
    aloc, sfx, later, chan, bcpar, head, expand, heads, gate_grad, weight, tok, inv, gain, edge_mask,
    out_next, z_arrays,
):
    steps, width = ssd.shape
    parts = steps // PART
    inside = (steps - GROUP) // PART
    size = D // 4
    turn = lambda spec: pl.BlockSpec(
        spec.block_shape, lambda i, m=spec.index_map: m(parts - 1 - i)
    )
    in_part = lambda w: pl.BlockSpec((PART, w), lambda i: (parts - 1 - i, 0))
    chunk = lead_block(N, width, rows=PART)
    few = lead_block(8, width, rows=PART)
    total = width + 2 * N
    dma = pltpu.SemaphoreType.DMA
    return pl.pallas_call(
        functools.partial(grand_kernel, heads, lax.axis_size("context")),
        grid=(parts,),
        in_specs=[
            turn(row_block(width, 1, rows=PART)), turn(prev_block(width, 1, rows=PART)),
            turn(row_block(3 * N, rows=PART)), turn(prev_block(3 * N, rows=PART)),
            once(8, width), once(8, 3 * N), turn(row_block(LANE, rows=PART)),
            turn(lead_block(8, L, rows=PART)),
            turn(row_block(LANE, rows=PART)), turn(row_block(LANE, rows=PART)), turn(row_block(width, rows=PART)), turn(row_block(width, rows=PART)),
            turn(chunk), turn(few), once(N, width), turn(chunk), turn(few), once(N, width),
            once(8, width), once(8, 2 * N), once(8, LANE), once(2 * LANE, width),
            turn(row_block(width, rows=PART)), once(*weight.shape), in_part(D), in_part(1), once(8, D),
            once(24, LANE), pl.BlockSpec(memory_space=pl.ANY),
        ]
        + ([pl.BlockSpec(memory_space=pl.ANY)] + [once(*z.shape) for z in z_arrays[1:]] if z_arrays else []),
        out_specs=[
            turn(row_block(width, rows=PART)), turn(row_block(2 * N, rows=PART)),
            pl.BlockSpec((16, PART), lambda i: (0, parts - 1 - i)),
            whole(8, total), whole(8, total), whole(8 * KERNEL, total), whole(8, total),
            whole(8, width), whole(16, LANE),
            once(inside * PART, size),
            pl.BlockSpec((1, 8, PART), lambda i: (parts - 1 - i, 0, 0)),
            whole(8, D), pl.BlockSpec(memory_space=pl.ANY),
        ]
        + [once(*z.shape) for z in z_arrays[1:2]],
        out_shape=[
            shape(steps, width, dtype=BF16), shape(steps, 2 * N), shape(16, steps, dtype=BF16),
            shape(8, total), shape(8, total), shape(8 * KERNEL, total), shape(8, total),
            shape(8, width), shape(16, LANE),
            shape(inside * PART, size), shape(parts, 8, PART), shape(8, D),
            shape(*out_next.shape, dtype=BF16),
        ]
        + [shape(*z.shape) for z in z_arrays[1:2]],
        scratch_shapes=[
            pltpu.VMEM((8 + L, width), F32), pltpu.VMEM((8 + L, 3 * N), F32),
            pltpu.VMEM((L, total), F32), pltpu.VMEM((L + 8, total), F32),
            pltpu.VMEM((inside, PART, size), F32),
            pltpu.VMEM((inside, PART, 2 * size), BF16), pltpu.VMEM((inside, PART, 2 * size), BF16),
            pltpu.VMEM((inside, PART, size), BF16), pltpu.VMEM((inside, PART, size), BF16),
            pltpu.VMEM((8, total), F32),
            dma((inside,)), dma((inside,)), dma((inside,)), dma((inside,)), dma, dma,
            dma((2,)), dma((2,)),
        ]
        + (
            [
                pltpu.VMEM(z_arrays[0].shape, BF16), pltpu.VMEM(z_arrays[1].shape, BF16),
                pltpu.VMEM(z_arrays[1].shape, BF16), dma((4,)), dma((4,)),
            ]
            if z_arrays
            else []
        ),
        compiler_params=pltpu.CompilerParams(
            dimension_semantics=("arbitrary",), vmem_limit_bytes=52 * 1024 * 1024,
            collective_id=4, has_side_effects=True,
        ),
        cost_estimate=estimate(90),
        name="behind",
    )(
        projected, projected, cols, cols, halo_v, halo_b, info, marks, delta, cum, ssd, mixed_grad,
        sloc, pfx, entry, aloc, sfx, later, chan, bcpar, head, expand,
        gate_grad, weight, tok, inv, gain, edge_mask, out_next, *z_arrays,
    )


def peers(t):
    return t + 1 - 2 * lax.rem(t, 2), lax.rem(t + 2, 4)


def pick(w_ref, one, other):
    size = w_ref.shape[0] // 4
    at = lambda k: pl.ds(pl.multiple_of(k * size, size), size)
    return jnp.concatenate([w_ref[at(one), :], w_ref[at(other), :]], axis=0)


def shares_of(side, t):
    near = peers(t)
    return (t, near[1 - side]), (near[side], 3 - t)


def out_kernel(
    ssd, gate, sums, chan, w_ref, scaled, own, mid, send_a, send_b,
):
    i, half = pl.program_id(0), pl.num_programs(0) // 2
    t = lax.axis_index("tensor")
    width = ssd.shape[1]
    for k in range(ssd.shape[0] // L):
        rows = slice(k * L, (k + 1) * L)
        inv = jnp.broadcast_to(lax.rsqrt(sums[k, 0:1, :] / INNER + EPS), (LANE, L)).T
        for sl in tiles(width):
            g = gate[rows, sl]
            gated = ssd[rows, sl] * g * sigmoid(g)
            scaled[rows, sl] = (gated * inv * chan[KERNEL + 1 : KERNEL + 2, sl]).astype(BF16)
    x = scaled[...]
    size = own.shape[1]

    def part(side, send):
        keep, go = shares_of(side, t)
        send[...] = dot(x, pick(w_ref, *go), 1, 1).astype(BF16)
        kept = dot(x, pick(w_ref, *keep), 1, 1)
        own[...] = kept[:, :size]
        mid[...] = kept[:, size:]

    @pl.when(i < half)
    def _():
        part(0, send_a)

    @pl.when(i >= half)
    def _():
        part(1, send_b)


def run_out(ssd, projected, sums, chan, weight):
    steps, width = ssd.shape
    block = 512
    count = steps // block
    half = count // 2
    size = D // 4
    in_block = lambda w, col=0: pl.BlockSpec((block, w), lambda i: (i, col))
    return pl.pallas_call(
        out_kernel,
        grid=(count,),
        in_specs=[
            in_block(width), in_block(width, 0),
            pl.BlockSpec((block // L, 8, L), lambda i: (i, 0, 0)),
            whole(8, width), whole(*weight.shape),
        ],
        out_specs=[
            in_block(width), in_block(size), in_block(size),
            pl.BlockSpec((block, 2 * size), lambda i: (jnp.minimum(i, half - 1), 0)),
            pl.BlockSpec((block, 2 * size), lambda i: (jnp.maximum(i - half, 0), 0)),
        ],
        out_shape=[
            shape(steps, width, dtype=BF16), shape(steps, size), shape(steps, size),
            shape(steps // 2, 2 * size, dtype=BF16), shape(steps // 2, 2 * size, dtype=BF16),
        ],
        compiler_params=params(),
        cost_estimate=estimate(12),
        name="out",
    )(ssd, projected, sums, chan, weight)


def line_kernel(
    n, n_tensor, piece, zx_ref, cols_ref, zx_out, cols_out,
    local, zx_s, zx_r, core_s, core_r, col_s, col_r, group_s, group_r, bulk_s, bulk_r,
):
    s, c, t = lax.axis_index("shard"), lax.axis_index("context"), lax.axis_index("tensor")
    on = (c < n - 1, c > 0)
    to = ((s, jnp.minimum(c + 1, n - 1), t), (s, jnp.maximum(c - 1, 0), t))
    to_core = (1 - s, c, t)
    to_group = [(s, c, lax.rem(t + k, n_tensor)) for k in range(1, n_tensor)]
    beside = [(s, lax.rem(c + k, n), t) for k in (1, n - 1)]
    pl.semaphore_wait(greet([to_core] + to_group + beside), n_tensor + 2)
    rows, width = zx_ref.shape[0], cols_ref.shape[1]
    spans = [(at, min(piece, rows - at)) for at in range(0, rows, piece)]

    def block_of(way, hop):
        return jnp.maximum(c - hop, 0) if way == 0 else jnp.minimum(c + hop, n - 1)

    def has(way, hop):
        return c - hop >= 0 if way == 0 else c + hop <= n - 1

    def place(ref, block, at=0, size=rows):
        return ref.at[pl.ds(pl.multiple_of((s * n + block) * rows + at, 16), size), :]

    lanes = pl.ds(pl.multiple_of(t * width, LANE), width)

    def place_cols(block):
        return cols_out.at[pl.ds(pl.multiple_of((s * n + block) * rows, 16), rows), lanes]

    def zx_copy(way, step, p):
        at, size = spans[p]
        where = place(zx_out, block_of(way, step), at, size)
        src = zx_ref.at[pl.ds(at, size), :] if step == 0 else where
        return remote(src, where, zx_s.at[way, step, p], zx_r.at[way, step, p], to[way])

    def col_copy(way, step):
        where = place_cols(block_of(way, step))
        src = cols_ref if step == 0 else where
        return remote(src, where, col_s.at[way, step], col_r.at[way, step], to[way])

    def group_copies(way, hop):
        where = place_cols(block_of(way, hop))
        src = cols_ref if hop == 0 else where
        return [
            remote(src, where, group_s.at[k, way, hop], group_r.at[k, way, hop], target)
            for k, target in enumerate(to_group)
        ]

    def core_copy(way, hop, p):
        at, size = spans[p]
        where = place(zx_out, block_of(way, hop), at, size)
        src = zx_ref.at[pl.ds(at, size), :] if hop == 0 else where
        return remote(src, where, core_s.at[way, hop, p], core_r.at[way, hop, p], to_core)

    pieces = range(len(spans))
    for way in (0, 1):

        @pl.when(on[way])
        def _():
            col_copy(way, 0).start()
            for p in pieces:
                zx_copy(way, 0, p).start()

    for copy in group_copies(0, 0):
        copy.start()
    own_cols = pltpu.make_async_copy(cols_ref, place_cols(c), local.at[0])
    own_zx = pltpu.make_async_copy(zx_ref, place(zx_out, c), local.at[1])
    own_cols.start()
    own_zx.start()
    for p in pieces:
        core_copy(0, 0, p).start()
    start = pl.ds(pl.multiple_of(s * n * rows, 16), n * rows)
    bulk = remote(cols_out.at[start, :], cols_out.at[start, :], bulk_s, bulk_r, to_core)
    for step in range(n - 1):
        further = step < n - 2
        for way in (0, 1):

            @pl.when(has(way, step + 1))
            def _():
                col_copy(way, step).wait_recv()
                for copy in group_copies(way, step + 1):
                    copy.start()
                if further:

                    @pl.when(on[way])
                    def _():
                        col_copy(way, step + 1).start()

        if not further:
            own_cols.wait()
            for copy in group_copies(0, 0):
                copy.wait()
            for hop in range(1, n):
                for way in (0, 1):

                    @pl.when(has(way, hop))
                    def _():
                        for copy in group_copies(way, hop):
                            copy.wait()

            bulk.start()
        for p in pieces:
            for way in (0, 1):

                @pl.when(has(way, step + 1))
                def _():
                    zx_copy(way, step, p).wait_recv()
                    core_copy(way, step + 1, p).start()
                    if further:

                        @pl.when(on[way])
                        def _():
                            zx_copy(way, step + 1, p).start()

    for step in range(n - 1):
        for way in (0, 1):

            @pl.when(jnp.logical_and(on[way], has(way, step)))
            def _():
                col_copy(way, step).wait_send()
                for p in pieces:
                    zx_copy(way, step, p).wait_send()

            @pl.when(has(way, step + 1))
            def _():
                for p in pieces:
                    core_copy(way, step + 1, p).wait()

    for p in pieces:
        core_copy(0, 0, p).wait()
    bulk.wait()
    own_zx.wait()


PIECE = 64


def line_gather(zx, cols):
    n, n_tensor = lax.axis_size("context"), lax.axis_size("tensor")
    rows = zx.shape[0]
    pieces = -(-rows // PIECE)
    dma = pltpu.SemaphoreType.DMA
    return pl.pallas_call(
        functools.partial(line_kernel, n, n_tensor, PIECE),
        in_specs=[pl.BlockSpec(memory_space=pl.ANY)] * 2,
        out_specs=[pl.BlockSpec(memory_space=pl.ANY)] * 2,
        out_shape=[
            shape(2 * n * rows, zx.shape[1], dtype=BF16),
            shape(2 * n * rows, n_tensor * cols.shape[1], dtype=BF16),
        ],
        scratch_shapes=[
            dma((2,)), dma((2, n - 1, pieces)), dma((2, n - 1, pieces)),
            dma((2, n, pieces)), dma((2, n, pieces)), dma((2, n - 1)), dma((2, n - 1)),
            dma((n_tensor - 1, 2, n)), dma((n_tensor - 1, 2, n)), dma, dma,
        ],
        compiler_params=pltpu.CompilerParams(collective_id=0, has_side_effects=True),
        name="line_gather",
    )(zx, cols)


def small_sum_kernel(n, x_ref, o_ref, held, send, recv):
    s, c, t = lax.axis_index("shard"), lax.axis_index("context"), lax.axis_index("tensor")
    targets = [(s, c, lax.rem(t + k, n)) for k in range(1, n)]
    pl.semaphore_wait(greet(targets), n - 1)
    copies = [
        remote(x_ref, held.at[k], send.at[k], recv.at[k], target)
        for k, target in enumerate(targets)
    ]
    for copy in copies:
        copy.start()
    total = x_ref[...]
    for k, copy in enumerate(copies):
        copy.wait()
        total = total + held[k]
    o_ref[...] = total


def small_sum(x, collective_id):
    n = lax.axis_size("tensor")
    return pl.pallas_call(
        functools.partial(small_sum_kernel, n),
        in_specs=[pl.BlockSpec(memory_space=pltpu.VMEM)],
        out_specs=pl.BlockSpec(memory_space=pltpu.VMEM),
        out_shape=shape(*x.shape),
        scratch_shapes=[
            pltpu.VMEM((n - 1, *x.shape), F32),
            pltpu.SemaphoreType.DMA((n - 1,)), pltpu.SemaphoreType.DMA((n - 1,)),
        ],
        compiler_params=pltpu.CompilerParams(collective_id=collective_id, has_side_effects=True),
        cost_estimate=estimate(7),
        name="small_sum",
    )(x)


SLICES = 8


class Chain:
    def __init__(self, n, backward, packed, entering, got, sent, send_sem, recv_sem):
        s, c, t = lax.axis_index("shard"), lax.axis_index("context"), lax.axis_index("tensor")
        self.from_other = c < n - 1 if backward else c > 0
        self.to_other = c > 0 if backward else c < n - 1
        ahead = jnp.maximum(c - 1, 0) if backward else jnp.minimum(c + 1, n - 1)
        self.target = (s, ahead, t)
        self.refs = packed, entering, got, sent, send_sem, recv_sem

    def copy(self, j):
        _, _, got, sent, send_sem, recv_sem = self.refs
        rows = pl.ds(j * (N // SLICES), N // SLICES)
        return remote(sent.at[rows, :], got.at[rows, :], send_sem.at[j], recv_sem.at[j], self.target)

    def step(self, j):
        packed, entering, got, sent, _, _ = self.refs
        rows = slice(j * (N // SLICES), (j + 1) * (N // SLICES))

        @pl.when(self.from_other)
        def _():
            self.copy(j).wait_recv()
            entering[rows, :] = got[rows, :]

        @pl.when(jnp.logical_not(self.from_other))
        def _():
            entering[rows, :] = jnp.zeros((N // SLICES, packed.shape[1]), F32)

        @pl.when(self.to_other)
        def _():
            sent[rows, :] = packed[rows, :] + packed[N : N + 1, :] * entering[rows, :]
            self.copy(j).start()

    def finish(self):
        @pl.when(self.to_other)
        def _():
            for j in range(SLICES):
                self.copy(j).wait_send()


def beside_of(n):
    s, c, t = lax.axis_index("shard"), lax.axis_index("context"), lax.axis_index("tensor")
    return [(s, lax.rem(c + k, n), t) for k in (1, n - 1)]


def entry_kernel(
    n, packed, back, w_hbm, entry, out, bk, w_ref, buf, got, sent, load_sem, out_sem, chain_s, chain_r
):
    block = buf.shape[1]
    count = back.shape[0] // block
    load_w = pltpu.make_async_copy(w_hbm, w_ref, load_sem.at[count])
    load_w.start()

    def load(k):
        rows = pl.ds(k * block, block)
        return pltpu.make_async_copy(back.at[rows, :], bk.at[rows, :], load_sem.at[k])

    def store(k):
        return pltpu.make_async_copy(
            buf.at[k % 2], out.at[pl.ds(k * block, block), :], out_sem.at[k % 2]
        )

    for k in range(count):
        load(k).start()
    pl.semaphore_wait(greet(beside_of(n)), 2)
    chain = Chain(n, False, packed, entry, got, sent, chain_s, chain_r)
    load_w.wait()
    for k in range(count):
        load(k).wait()
        if k >= 2:
            store(k - 2).wait()
        buf[k % 2] = dot(bk[k * block : (k + 1) * block, :], w_ref[...])
        store(k).start()
        if k < SLICES:
            chain.step(k)
    for k in range(count, SLICES):
        chain.step(k)
    chain.finish()
    for k in range(max(count - 2, 0), count):
        store(k).wait()


def run_entry(packed, back, weight):
    n = lax.axis_size("context")
    steps, width = back.shape[0], weight.shape[1]
    block = 256
    dma = pltpu.SemaphoreType.DMA
    vmem = pltpu.VMEM
    inside = pl.BlockSpec(memory_space=pltpu.VMEM)
    hbm = pl.BlockSpec(memory_space=pl.ANY)
    return pl.pallas_call(
        functools.partial(entry_kernel, n),
        in_specs=[inside, hbm, hbm],
        out_specs=[inside, hbm],
        out_shape=[shape(N, width), shape(steps, width)],
        scratch_shapes=[
            vmem(back.shape, BF16), vmem(weight.shape, BF16), vmem((2, block, width), F32),
            vmem((N, width), F32), vmem((N, width), F32),
            dma((steps // block + 1,)), dma((2,)), dma((SLICES,)), dma((SLICES,)),
        ],
        compiler_params=pltpu.CompilerParams(
            vmem_limit_bytes=40 * 1024 * 1024, collective_id=6, has_side_effects=True
        ),
        cost_estimate=estimate(15),
        name="entry",
    )(packed, back, weight)


def middle_kernel(
    n, packed, send_a, send_b, mid_hbm, own_hbm, normed_hbm, gate_hbm, back_hbm, scaled_hbm, *refs
):
    if n == 4:
        later, own, next_out, z_out, z_mid, z_mine = refs[:6]
        refs = refs[6:]
    else:
        later, own, next_out, both_out = refs[:4]
        refs = refs[4:]
    (
        mid, nm, gg, bk, sc, peer_part, core_part, own_part, got, chain_got, chain_sent,
        local, core_s, core_r, f_s, f_r, chain_s, chain_r,
    ) = refs
    s, c, t = lax.axis_index("shard"), lax.axis_index("context"), lax.axis_index("tensor")
    near = peers(t)
    to = [(s, c, near[0]), (s, c, near[1])]
    to_core = (1 - s, c, t)
    loads = [
        pltpu.make_async_copy(src, dst, local.at[k])
        for k, (src, dst) in enumerate(
            [
                (normed_hbm, nm), (gate_hbm, gg), (back_hbm, bk), (scaled_hbm, sc),
                (mid_hbm, mid), (own_hbm, own),
            ]
        )
    ]
    for load in loads:
        load.start()
    pl.semaphore_wait(greet(to + [to_core] + beside_of(n)), 5)
    hops = [
        remote(src, got.at[side], f_s.at[side], f_r.at[side], to[side])
        for side, src in enumerate((send_a, send_b))
    ]
    for hop in hops:
        hop.start()
    chain = Chain(n, True, packed, later, chain_got, chain_sent, chain_s, chain_r)
    half_d = nm.shape[1] // 2
    steps = nm.shape[0]
    step = 256
    pairs = ((nm, gg), (bk, sc))

    def product(which, shard, into, m):
        left, right = pairs[which]
        lanes = pl.ds(pl.multiple_of(shard * half_d + m * step, step), step)
        into[which, m * step : (m + 1) * step, :] = over_rows(left, lanes, lambda rows: right[rows, :])

    cores = [
        remote(peer_part.at[k], core_part.at[k], core_s.at[k], core_r.at[k], to_core) for k in (0, 1)
    ]
    chain.step(0)
    done = 1
    for which in (0, 1):
        loads[2 * which].wait()
        loads[2 * which + 1].wait()
        for m in range(half_d // step):
            product(which, 1 - s, peer_part, m)
            if done < SLICES:
                chain.step(done)
                done += 1
        cores[which].start()
    for which in (0, 1):
        for m in range(half_d // step):
            product(which, s, own_part, m)
            if done < SLICES:
                chain.step(done)
                done += 1
    chain.finish()
    block = half_d // n

    for which in (0, 1):
        cores[which].wait()
        if n == 4:
            first = c + 1 - 2 * lax.rem(c, 2) if which == 0 else 3 - c
            third = 3 - c if which == 0 else c + 1 - 2 * lax.rem(c, 2)

            def total(k):
                rows = pl.ds(pl.multiple_of(k * block, 8), block)
                return own_part[which, rows, :] + core_part[which, rows, :]

            z_out[which, :block, :] = total(first).astype(BF16)
            z_out[which, block:, :] = total(lax.rem(c + 2, 4)).astype(BF16)
            z_mid[which] = total(third)
            z_mine[which] = total(c)
        else:
            both_out[which] = own_part[which] + core_part[which]
    loads[4].wait()
    loads[5].wait()
    size = mid.shape[1]
    half = steps // 2
    for side in (0, 1):
        hops[side].wait()
        for k in range(half // step):
            rows = slice(k * step, (k + 1) * step)
            at = slice(side * half + k * step, side * half + (k + 1) * step)
            next_out[side, rows, :] = (mid[at, :] + got[side, rows, size:].astype(F32)).astype(BF16)
            own[at, :] += got[side, rows, :size].astype(F32)


def run_middle(packed, fan, normed, gate_grad, back, scaled):
    n = lax.axis_size("context")
    own, mid, send_a, send_b = fan
    steps, width = gate_grad.shape
    size = own.shape[1]
    half_d = D // 2
    block = half_d // n
    dma = pltpu.SemaphoreType.DMA
    vmem = pltpu.VMEM
    inside = pl.BlockSpec(memory_space=pltpu.VMEM)
    hbm = pl.BlockSpec(memory_space=pl.ANY)
    if n == 4:
        more = [
            shape(2, 2 * block, width, dtype=BF16), shape(2, block, width), shape(2, block, width)
        ]
    else:
        more = [shape(2, half_d, width)]
    pair = (2, half_d, width)
    return pl.pallas_call(
        functools.partial(middle_kernel, n),
        in_specs=[inside] + [hbm] * 8,
        out_specs=[inside] * (3 + len(more)),
        out_shape=[shape(N, width), shape(steps, size), shape(2, steps // 2, size, dtype=BF16)] + more,
        scratch_shapes=[
            vmem((steps, size), F32), vmem(normed.shape, BF16), vmem(gate_grad.shape, BF16),
            vmem(back.shape, BF16), vmem(scaled.shape, BF16),
            vmem(pair, F32), vmem(pair, F32), vmem(pair, F32), vmem((2, steps // 2, 2 * size), BF16),
            vmem((N, width), F32), vmem((N, width), F32),
            dma((6,)), dma((2,)), dma((2,)), dma((2,)), dma((2,)), dma((SLICES,)), dma((SLICES,)),
        ],
        compiler_params=pltpu.CompilerParams(
            vmem_limit_bytes=54 * 1024 * 1024, collective_id=7, has_side_effects=True
        ),
        cost_estimate=estimate(35),
        name="middle",
    )(packed, send_a, send_b, mid, own, normed, gate_grad, back, scaled)


def adam_kernel(heads, cols_loc, gate_g, value_g, down_g, cols_g, packed, packed_gain, *refs):
    zx, out, bcdt, gain, chan, bc, head = [refs[3 * k : 3 * k + 3] for k in range(7)]
    refs = refs[21:]
    zx_new, out_new, bcdt_new, gain_new, chan_new, bc_new, head_new = [
        refs[3 * k : 3 * k + 3] for k in range(7)
    ]
    width = gate_g.shape[1]

    def put(news, olds, grad, rate, decay, at=(Ellipsis,)):
        for ref, val in zip(news, adamw(olds[0][at], grad, olds[1][at], olds[2][at], rate, decay)):
            ref[at] = val

    for k, grad in enumerate((gate_g, value_g)):
        put(zx_new, zx, grad[...], RATE_MATRIX, DECAY, (slice(None), k, slice(None)))
    put(out_new, out, down_g[...], RATE_MATRIX, DECAY)
    put(bcdt_new, bcdt, cols_g[...].T[:cols_loc, :], RATE_MATRIX, DECAY)
    over = packed[0] + packed[1] + packed[2] + packed[3]
    gains = packed_gain[0] + packed_gain[1] + packed_gain[2] + packed_gain[3]
    gains = jnp.concatenate([gains[k : k + 1, :] for k in range(D // LANE)], axis=1)
    put(gain_new, gain, gains, RATE_SMALL, 0.0)
    put(bc_new, bc, over[: KERNEL + 1, width : width + 2 * N], RATE_SMALL, 0.0)
    grad = jnp.concatenate([packed[k, : KERNEL + 2, :width] for k in range(4)], axis=1)
    put(chan_new, chan, grad, RATE_SMALL, 0.0)
    lane = lax.broadcasted_iota(jnp.int32, (LANE, 4 * heads), 0)
    slot = lax.broadcasted_iota(jnp.int32, (LANE, 4 * heads), 1)
    channel = lax.broadcasted_iota(jnp.int32, (width, 4 * heads), 0)
    wide_slot = lax.broadcasted_iota(jnp.int32, (width, 4 * heads), 1)
    rows = jnp.zeros((8, 4 * heads), F32)
    for k in range(4):
        here = jnp.where(lane + k * heads == slot, 1.0, 0.0)
        here = jnp.where(lane < heads, here, 0.0).astype(BF16)
        wide = jnp.where(channel // P_SIZE + k * heads == wide_slot, 1.0, 0.0).astype(BF16)
        hi, lo = two(packed[k, KERNEL + 3 : KERNEL + 11, :LANE])
        at = lax.broadcasted_iota(jnp.int32, rows.shape, 0)
        rows = rows + jnp.where(at < 2, dot(hi, here) + dot(lo, here), 0.0)
        hi, lo = two(packed[k, KERNEL + 2 : KERNEL + 10, :width])
        skip = dot(hi, wide) + dot(lo, wide)
        rows = rows + jnp.where(at == 2, jnp.broadcast_to(skip[0:1, :], rows.shape), 0.0)
    put(head_new, head, rows[:3, :], RATE_SMALL, 0.0)


def run_adam(grads, olds, heads, cols_loc):
    flat = [x for group in olds for x in group]
    return pl.pallas_call(
        functools.partial(adam_kernel, heads, cols_loc),
        in_specs=[pl.BlockSpec(memory_space=pltpu.VMEM)] * (len(grads) + len(flat)),
        out_specs=[pl.BlockSpec(memory_space=pltpu.VMEM)] * len(flat),
        out_shape=[shape(*x.shape) for x in flat],
        compiler_params=pltpu.CompilerParams(vmem_limit_bytes=40 * 1024 * 1024),
        cost_estimate=estimate(8),
        name="optimizer",
    )(*grads, *flat)


def doc_of(lengths, position):
    found = jnp.zeros(position.shape, F32)
    end = 0
    for k in range(lengths.shape[1] - 1):
        end = end + lengths[0, k]
        found = found + jnp.where(position >= end, 1.0, 0.0)
    return jnp.where(position < 0, -1.0, found)


def mark_chunk(lengths, begin, limit, info_ref, marks_ref):
    row = lax.broadcasted_iota(jnp.int32, (L, LANE), 0)
    lane = lax.broadcasted_iota(jnp.int32, (L, LANE), 1)
    offset = jnp.where(lane < KERNEL - 1, lane - KERNEL + 1, jnp.where(lane >= 8, lane - 7, 0))
    other = jnp.where(lane == 3, -1, jnp.where(lane == 4, L - 1, row + offset)) + begin
    mark = doc_of(lengths, row + begin)
    same = jnp.logical_and(doc_of(lengths, other) == mark, other < limit)
    info = jnp.where(same, 1.0, 0.0)
    info_ref[...] = jnp.where(lane == 5, mark, jnp.where(lane < 7 + KERNEL, info, 0.0))
    marks_ref[0] = doc_of(lengths, begin + lax.broadcasted_iota(jnp.int32, (8, L), 1))


def norm_rows(tok, gain):
    x = tok.astype(F32)
    square = x * x
    total = square[:, :LANE]
    for sl in tiles(D)[1:]:
        total = total + square[:, sl]
    inv = lax.rsqrt(jnp.sum(total, axis=1, keepdims=True) / D + EPS)
    return (x * inv * gain[0:1, :]).astype(BF16), inv


def project_kernel(
    heads, n, cols_loc, lengths, tok, tok_end, gain, w_ref, wg_ref, chan, bcpar, head, e_ref,
    normed, inv, projected, cols, info, marks, edge_mask, act, delta, cum, sloc, pfx, fin,
    halo_v, halo_b, ext_v, ext_b, state, prod, w_cols, prev_v, prev_b, halo_out, halo_got, h_s, h_r,
):
    i = pl.program_id(0)
    s, c, t = lax.axis_index("shard"), lax.axis_index("context"), lax.axis_index("tensor")
    width = w_ref.shape[1] // 2
    block = tok.shape[0]
    steps = block * pl.num_programs(0)
    start = c * steps
    after = (s, jnp.minimum(c + 1, n - 1), t)
    halo = remote(halo_out, halo_got, h_s, h_r, after)

    @pl.when(i == 0)
    def _():
        pl.semaphore_wait(greet(beside_of(n)), 2)
        state[...] = jnp.zeros_like(state)
        prod[...] = jnp.ones_like(prod)
        lane = lax.broadcasted_iota(jnp.int32, (4 * LANE, 3 * N), 0)
        want = lax.broadcasted_iota(jnp.int32, (4 * LANE, 3 * N), 1)
        have = lane // LANE * cols_loc + lane % LANE
        want = jnp.where(want < 2 * N, want, jnp.where(want < 2 * N + heads, want + heads * t, -1))
        chosen = jnp.logical_and(have == want, lane % LANE < cols_loc)
        select = jnp.where(chosen, 1.0, 0.0).astype(BF16)
        for k in range(0, D, block):
            w_cols[k : k + block, :] = dot(wg_ref[k : k + block, :], select).astype(BF16)
        ends, _ = norm_rows(tok_end[...], gain)
        halo_out[:, :width] = dot(ends, w_ref[:, width:])[8:, :]
        halo_out[:, width:] = dot(ends, w_cols[...])[8:, :]

        @pl.when(c < n - 1)
        def _():
            halo.start()

        row = lax.broadcasted_iota(jnp.int32, (24, LANE), 0)
        shift, at = row // 8 + 1, row % 8
        there = at - 8 + shift + start + steps
        agree = doc_of(lengths, there) == doc_of(lengths, there - shift)
        edge_mask[...] = jnp.where(jnp.logical_and(at >= 8 - shift, agree), 1.0, 0.0)

    for j in range(block // L):
        rows = slice(j * L, (j + 1) * L)
        x, scale = norm_rows(tok[rows, :], gain)
        normed[rows, :] = x
        inv[rows, :] = scale
    for k in range(0, 2 * width, 512):
        projected[:, k : k + 512] = dot(normed[...], w_ref[:, k : k + 512])
    cols[...] = dot(normed[...], w_cols[...])

    @pl.when(i == 0)
    def _():
        @pl.when(c > 0)
        def _():
            halo.wait_recv()
            halo_v[...] = halo_got[:, :width]
            halo_b[...] = halo_got[:, width:]

        @pl.when(c == 0)
        def _():
            halo_v[...] = jnp.zeros_like(halo_v)
            halo_b[...] = jnp.zeros_like(halo_b)

        @pl.when(c < n - 1)
        def _():
            halo.wait_send()

    val = projected.at[:, pl.ds(width, width)]

    for j in range(block // L):
        first = i == 0
        mark_chunk(
            lengths, start + i * block + j * L, start + steps, rows_at(info, j), lead_at(marks, j)
        )
        load_ext(ext_v, val, prev_v, halo_v, j, first)
        load_ext(ext_b, cols, prev_b, halo_b, j, first)
        prep_chunk(
            rows_at(cols, j), rows_at(info, j), chan, bcpar, head, e_ref, rows_at(act, j),
            rows_at(delta, j), rows_at(cum, j), lead_at(sloc, j), lead_at(pfx, j),
            ext_v, ext_b, state, prod,
        )
    prev_v[...] = projected[block - 8 :, width:]
    prev_b[...] = cols[block - 8 :, :]

    @pl.when(i == pl.num_programs(0) - 1)
    def _():
        fin[:N, :] = state[...]
        fin[N:, :] = prod[...]


def run_project(lengths, tok, gain, weight, w_group, chan, bcpar, head, expand, heads, cols_loc):
    steps, width = tok.shape[0], weight.shape[1] // 2
    count = steps // L
    dma = pltpu.SemaphoreType.DMA
    return pl.pallas_call(
        functools.partial(project_kernel, heads, lax.axis_size("context"), cols_loc),
        grid=(steps // GROUP,),
        in_specs=[
            pl.BlockSpec(memory_space=pltpu.SMEM), row_block(D),
            pl.BlockSpec((16, D), lambda i: (steps // 16 - 1, 0), pipeline_mode=pl.Buffered(1)),
            once(8, D), once(*weight.shape), once(*w_group.shape),
            once(8, width), once(8, 2 * N), once(8, LANE), once(2 * LANE, width),
        ],
        out_specs=[
            row_block(D), row_block(1),
            row_block(2 * width), row_block(3 * N), row_block(LANE), lead_block(8, L), once(24, LANE),
            row_block(width + 2 * N), row_block(LANE), row_block(LANE), lead_block(N, width),
            lead_block(8, width), once(N + 8, width), once(8, width), once(8, 3 * N),
        ],
        out_shape=[
            shape(steps, D, dtype=BF16), shape(steps, 1),
            shape(steps, 2 * width), shape(steps, 3 * N), shape(steps, LANE), shape(count, 8, L),
            shape(24, LANE),
            shape(steps, width + 2 * N), shape(steps, LANE), shape(steps, LANE),
            shape(count, N, width), shape(count, 8, width), shape(N + 8, width), shape(8, width),
            shape(8, 3 * N),
        ],
        scratch_shapes=[
            pltpu.VMEM((8 + L, width), F32), pltpu.VMEM((8 + L, 3 * N), F32),
            pltpu.VMEM((N, width), F32), pltpu.VMEM((8, width), F32),
            pltpu.VMEM((D, 3 * N), BF16), pltpu.VMEM((8, width), F32), pltpu.VMEM((8, 3 * N), F32),
            pltpu.VMEM((8, width + 3 * N), F32), pltpu.VMEM((8, width + 3 * N), F32), dma, dma,
        ],
        compiler_params=pltpu.CompilerParams(
            dimension_semantics=("arbitrary",), vmem_limit_bytes=48 * 1024 * 1024,
            collective_id=8, has_side_effects=True,
        ),
        cost_estimate=estimate(45),
        name="project",
    )(lengths, tok, tok, gain, weight, w_group, chan, bcpar, head, expand)


class AllSum:
    def __init__(self, n, refs, sems):
        s, c, t = lax.axis_index("shard"), lax.axis_index("context"), lax.axis_index("tensor")
        self.n, self.c, self.t = n, c, t
        self.mine, self.other, self.pair, self.pieces, self.total, self.every = refs
        core_s, core_r, piece_s, piece_r, group_s, group_r = sems
        self.core = remote(self.mine, self.other, core_s, core_r, (1 - s, c, t))
        self.along = [
            remote(self.pair, self.pieces.at[c], piece_s.at[k], piece_r.at[k], (s, lax.rem(c + k + 1, n), t))
            for k in range(n - 1)
        ]
        self.across = [
            remote(self.total, self.every.at[t], group_s.at[k], group_r.at[k], (s, c, lax.rem(t + k + 1, 4)))
            for k in range(3)
        ]

    def start(self):
        self.core.start()

    def after_core(self):
        self.core.wait()
        self.pair[...] = self.mine[...] + self.other[...]
        self.pieces[self.c] = self.pair[...]
        for copy in self.along:
            copy.start()

    def after_pieces(self):
        for copy in self.along:
            copy.wait()
        self.total[...] = sum(self.pieces[k] for k in range(1, self.n)) + self.pieces[0]
        self.every[self.t] = self.total[...]
        for copy in self.across:
            copy.start()

    def finish(self):
        for copy in self.across:
            copy.wait()


PACK = 16


def tail_kernel(
    n, grad_b, grad_v, normed_hbm, w_hbm, tok_hbm, back_hbm, late_hbm, wg_hbm,
    raw_t, fixed, gate_top, gate_end, tok_top, tok_end, inv, gain, gain_mine, sel_bc, sel_raw,
    late_rows, late_gain, taps_grad, bias_grad, norm_gain_grad, skip_grad, head_grad,
    tokens_out, value_out, cols_out, pack_out, gain_out,
    gb, gv, nm, w_ref, tok, back, w_cols, col_grad,
    peer_part, own_part, core_part, b_got, b_next, b_last, b_full, raw_full,
    early, mid, send, got, nxt, last, gain_grad, z_out, z_got, z_on, z_last,
    ng, col_peer, col_own, col_core, col_out, col_got, col_on, col_last,
    row_buf, row_held, *refs,
):
    tail_body(
        n, grad_b, grad_v, normed_hbm, w_hbm, tok_hbm, back_hbm, late_hbm, wg_hbm,
        raw_t, fixed, gate_top, gate_end, tok_top, tok_end, inv, gain, gain_mine, sel_bc, sel_raw,
        late_rows, late_gain, taps_grad, bias_grad, norm_gain_grad, skip_grad, head_grad,
        tokens_out, value_out, cols_out, pack_out, gain_out,
        gb, gv, nm, w_ref, tok, back, w_cols, col_grad,
        peer_part, own_part, core_part, b_got, b_next, b_last, b_full, raw_full,
        early, mid, send, got, nxt, last, gain_grad, z_out, z_got, z_on, z_last,
        ng, col_peer, col_own, col_core, col_out, col_got, col_on, col_last,
        row_buf, row_held, refs[:6], refs[6:12], *refs[12:25], refs[25:31], refs[31:37],
    )


def tail_body(
    n, grad_b, grad_v, normed_hbm, w_hbm, tok_hbm, back_hbm, late_hbm, wg_hbm,
    raw_t, fixed, gate_top, gate_end, tok_top, tok_end, inv, gain, gain_mine, sel_bc, sel_raw,
    late_rows, late_gain, taps_grad, bias_grad, norm_gain_grad, skip_grad, head_grad,
    tokens_out, value_out, cols_out, pack_out, gain_out,
    gb, gv, nm, w_ref, tok, back, w_cols, col_grad,
    peer_part, own_part, core_part, b_got, b_next, b_last, b_full, raw_full,
    early, mid, send, got, nxt, last, gain_grad, z_out, z_got, z_on, z_last,
    ng, col_peer, col_own, col_core, col_out, col_got, col_on, col_last,
    row_buf, row_held, pack_refs, gain_refs,
    local, raw_s, raw_r, b_s, b_r, f_s, f_r, core_s, core_r, z_s, z_r, row_s, row_r,
    pack_sems, gain_sems,
):
    s, c, t = lax.axis_index("shard"), lax.axis_index("context"), lax.axis_index("tensor")
    near = peers(t)
    to = [(s, c, near[0]), (s, c, near[1])]
    group = [(s, c, lax.rem(t + k, 4)) for k in (1, 2, 3)]
    to_core = (1 - s, c, t)
    to_piece = [(s, lax.rem(c + k, n), t) for k in range(1, n)]
    in_line = n == 4
    line = [(s, c + 1 - 2 * lax.rem(c, 2), t), (s, 3 - c, t)] if in_line else []
    steps, width = grad_v.shape
    size = w_ref.shape[0] // 4
    share = steps // 4
    mine_lanes = pl.ds(pl.multiple_of(t * size, size), size)
    loads = [
        pltpu.make_async_copy(src, dst, local.at[k])
        for k, (src, dst) in enumerate(
            [
                (grad_b, gb), (grad_v, gv), (normed_hbm, nm), (w_hbm, w_ref),
                (tok_hbm.at[:, mine_lanes], tok), (back_hbm.at[:, mine_lanes], back),
                (late_hbm, ng.at[pl.ds(GROUP, steps - GROUP), :]),
                (wg_hbm.at[mine_lanes, :], w_cols),
            ]
        )
    ]
    for load in loads:
        load.start()
    pl.semaphore_wait(greet(group + [to_core] + to_piece), n + 3)

    pack = pack_refs[0]
    pack[...] = jnp.zeros_like(pack)
    gain_refs[0][...] = jnp.zeros_like(gain_refs[0])
    total = width + 2 * N
    add_up = lambda x: jnp.sum(x, axis=0, keepdims=True)
    for k in range(KERNEL):
        pack[k : k + 1, :total] = add_up(taps_grad[8 * k : 8 * k + 8, :])
    pack[KERNEL : KERNEL + 1, :total] = add_up(bias_grad[...])
    pack[KERNEL + 1 : KERNEL + 2, :width] = add_up(norm_gain_grad[...])
    pack[KERNEL + 2 : KERNEL + 3, :width] = add_up(skip_grad[...])
    pack[KERNEL + 3 : KERNEL + 4, :LANE] = add_up(head_grad[:8, :])
    pack[KERNEL + 4 : KERNEL + 5, :LANE] = add_up(head_grad[8:, :])
    pack_sum = AllSum(n, pack_refs, pack_sems)
    gain_sum = AllSum(n, gain_refs, gain_sems)

    raw_full[t] = raw_t[...]
    raws = [
        remote(raw_t, raw_full.at[t], raw_s.at[k], raw_r.at[k], target)
        for k, target in enumerate(group)
    ]
    for copy in raws:
        copy.start()

    def rows_of(k):
        return pl.ds(pl.multiple_of(k * share, share), share)

    def lanes_of(side):
        return pl.ds(side * N, N)

    loads[0].wait()
    gb[steps - 8 :, :] = fixed[:, width:]

    def b_first(side, part):
        k = near[side] if part == 0 else 3 - t
        return remote(
            gb.at[rows_of(k), lanes_of(side)], b_got.at[side, part], b_s.at[side, part],
            b_r.at[side, part], to[side],
        )

    def b_second(side):
        return remote(
            b_next.at[side], b_last.at[side], b_s.at[side, 2], b_r.at[side, 2], to[1 - side]
        )

    def b_back(side, part):
        k = near[1 - side] if part == 2 else t
        where = b_full.at[rows_of(k), lanes_of(side)]
        return remote(
            where, where, b_s.at[side, 3 + part], b_r.at[side, 3 + part],
            to[1 - side] if part == 0 else to[side],
        )

    for side in (0, 1):
        for part in (0, 1):
            b_first(side, part).start()
    pack_sum.start()

    loads[1].wait()
    tail = gv[steps - 16 :, :].astype(F32)
    gv[steps - 16 :, :] = jnp.concatenate([tail[:8], fixed[:, :width]], axis=0).astype(BF16)
    loads[2].wait()
    half_d = nm.shape[1] // 2
    step = 256

    def product(shard, right, into):
        for m in range(half_d // step):
            lanes = pl.ds(pl.multiple_of(shard * half_d + m * step, step), step)
            into[m * step : (m + 1) * step, :] = over_rows(nm, lanes, right)

    product(1 - s, lambda rows: gv[rows, :], peer_part)
    core = remote(peer_part, core_part, core_s.at[0], core_r.at[0], to_core)
    core.start()

    for side in (0, 1):
        for part in (0, 1):
            b_first(side, part).wait()
        b_next[side] = gb[rows_of(near[1 - side]), lanes_of(side)] + b_got[side, 1]
        b_second(side).start()
    pack_sum.after_core()

    product(s, lambda rows: gv[rows, :], own_part)

    for side in (0, 1):
        b_second(side).wait()
        mine = gb[rows_of(t), lanes_of(side)] + b_got[side, 0] + b_last[side]
        b_full[rows_of(t), lanes_of(side)] = mine.astype(BF16)
        b_back(side, 0).start()

    block = half_d // n
    side_w = width // 2
    both = own_part
    if in_line:
        first = [c + 1 - 2 * lax.rem(c, 2), 3 - c]
        across = lax.rem(c + 2, 4)

    def block_rows(k):
        return pl.ds(pl.multiple_of(k * block, 8), block)

    def z_block(k, side):
        return both[block_rows(k), side * side_w : (side + 1) * side_w]

    def z_first(side):
        return remote(z_out.at[side], z_got.at[side], z_s.at[side], z_r.at[side], line[side])

    def z_second(side):
        return remote(z_on.at[side], z_last.at[side], z_s.at[2 + side], z_r.at[2 + side], line[1 - side])

    def col_first():
        return remote(col_out, col_got, z_s.at[4], z_r.at[4], line[0])

    def col_second():
        return remote(col_on, col_last, z_s.at[5], z_r.at[5], line[1])

    core.wait()
    both[...] = both[...] + core_part[...]
    if in_line:
        for side in (0, 1):
            z_out[side, :block, :] = z_block(first[side], side).astype(BF16)
            z_out[side, block:, :] = z_block(across, side).astype(BF16)
            z_first(side).start()
    for side in (0, 1):
        b_back(side, 0).wait()
        for part in (1, 2):
            b_back(side, part).start()

    loads[3].wait()
    pack_sum.after_pieces()
    half = GROUP // 2
    tail_half = END // 2

    def f_first(side):
        return remote(send.at[side], got.at[side], f_s.at[side], f_r.at[side], to[side])

    def f_second(side):
        return remote(
            nxt.at[side], last.at[side], f_s.at[2 + side], f_r.at[2 + side], to[1 - side]
        )

    gain_grad[...] = late_gain[...]
    for g in range(GROUP // PART, steps // PART):
        row_buf[:, g * PART : (g + 1) * PART] = late_rows[g]
    ends = [jnp.zeros((LANE - END, LANE), F32)]
    for side in (0, 1):
        rows = slice(side * half, (side + 1) * half)
        tail_rows = slice(side * tail_half, (side + 1) * tail_half)
        end_rows = slice(steps - END + side * tail_half, steps - END + (side + 1) * tail_half)
        x = jnp.concatenate(
            [
                jnp.concatenate([gate_top[rows, :], gv[rows, :]], axis=1),
                jnp.concatenate([gate_end[tail_rows, :], gv[end_rows, :]], axis=1),
            ],
            axis=0,
        )
        keep, go = shares_of(side, t)
        gone = dot(x, pick(w_ref, *go), 1, 1)
        send[side] = gone.astype(BF16)
        f_first(side).start()
        kept = dot(x, pick(w_ref, *keep), 1, 1)
        early[side] = kept[:, :size]
        mid[side] = kept[:, size:]
        scale = jnp.concatenate([inv[rows, :], inv[end_rows, :]], axis=0)
        parts = [kept[:, :size], kept[:, size:], gone[:, :size], gone[:, size:]]

        def z(lanes):
            values = jnp.concatenate([tok_top[rows, lanes], tok_end[tail_rows, lanes]], axis=0)
            return values.astype(F32) * scale

        sums = count_rows(parts, z, gain, keep + go, gain_grad)
        row_buf[:, rows] = row_dots(sums[:half])
        ends.append(sums[half:])
    row_buf[:, steps - LANE :] += row_dots(jnp.concatenate(ends, axis=0))

    for copy in raws:
        copy.wait()
    for side in (0, 1):
        for part in (1, 2):
            b_back(side, part).wait()
    raw_all = jnp.concatenate([raw_full[k] for k in range(4)], axis=0)

    for k in range(steps // GROUP):
        rows = slice(k * GROUP, (k + 1) * GROUP)
        chosen = dot(b_full[rows, :], sel_bc[...]) + dot(raw_all[:, rows], sel_raw[...], 0, 0)
        col_grad[rows, :] = chosen.astype(BF16)
    own_lanes = pl.ds(pl.multiple_of(t * LANE, LANE), LANE)
    product(1 - s, lambda rows: col_grad[rows, own_lanes], col_peer)
    col_core_copy = remote(col_peer, col_core, core_s.at[1], core_r.at[1], to_core)
    col_core_copy.start()
    loads[4].wait()
    loads[6].wait()
    loads[7].wait()
    ng[steps - END :, :] = jnp.zeros((END, size), F32)
    for k in range(steps // GROUP):
        rows = slice(k * GROUP, (k + 1) * GROUP)
        part = dot(col_grad[rows, :], w_cols[...], 1, 1)
        ng[rows, :] = part if k == 0 else ng[rows, :] + part
        part = part * (tok[rows, :].astype(F32) * inv[rows, :])
        gain_grad[:, mine_lanes] += fold(part)
        part = part * gain_mine[0:1, :]
        sums = part[:, :LANE]
        for sl in tiles(size)[1:]:
            sums = sums + part[:, sl]
        row_buf[:, rows] += row_dots(sums)
    row_copies = [
        remote(row_buf, row_held.at[k], row_s.at[k], row_r.at[k], target)
        for k, target in enumerate(group)
    ]
    for copy in row_copies:
        copy.start()

    for k in range(D // LANE):
        gain_refs[0][k : k + 1, :] = add_up(gain_grad[:, k * LANE : (k + 1) * LANE])
    gain_sum.start()

    for side in (0, 1):
        f_first(side).wait()
        nxt[side] = (mid[side] + got[side, :, size:].astype(F32)).astype(BF16)
        f_second(side).start()
        early[side] += got[side, :, :size].astype(F32)

    product(s, lambda rows: col_grad[rows, own_lanes], col_own)

    gain_sum.after_core()
    if in_line:
        for side in (0, 1):
            z_first(side).wait()
            z_on[side] = (
                z_block(first[1 - side], side) + z_got[side, block:, :].astype(F32)
            ).astype(BF16)
            z_second(side).start()
    col_core_copy.wait()
    col_own[...] = col_own[...] + col_core[...]
    if in_line:
        col_out[:block, :] = col_own[block_rows(first[0]), :]
        col_out[block:, :] = col_own[block_rows(across), :]
        col_first().start()

    gain_sum.after_pieces()
    if in_line:
        col_first().wait()
        col_on[...] = col_own[block_rows(first[1]), :] + col_got[block:, :]
        col_second().start()

    loads[5].wait()
    for copy in row_copies:
        copy.wait()
    for side in (0, 1):
        f_second(side).wait()
        early[side] += last[side].astype(F32)
        at = steps - END + side * tail_half
        ng[at : at + tail_half, :] += early[side, half:, :]
        ng[side * half : (side + 1) * half, :] += early[side, :half, :]
    row_total = row_buf[...] + row_held[0] + row_held[1] + row_held[2]
    for k in range(steps // LANE):
        rows = slice(k * LANE, (k + 1) * LANE)
        row_dot = jnp.broadcast_to(row_total[0:1, rows] * (1.0 / D), (LANE, LANE)).T
        scale = inv[rows, :]
        for sl in tiles(size):
            z_tile = tok[rows, sl].astype(F32) * scale
            change = scale * (ng[rows, sl] * gain_mine[0:1, sl] - z_tile * row_dot)
            tokens_out[rows, sl] = (back[rows, sl].astype(F32) + change).astype(BF16)

    if in_line:
        for side in (0, 1):
            z_second(side).wait()
            value_out[:, side * side_w : (side + 1) * side_w] = (
                z_block(c, side) + z_got[side, :block, :].astype(F32) + z_last[side].astype(F32)
            )
        col_second().wait()
        cols_out[...] = col_own[block_rows(c), :] + col_got[:block, :] + col_last[...]
    else:
        value_out[...] = both[...]
        cols_out[...] = col_own[...]
    pack_sum.finish()
    pack_out[...] = pack_refs[5][...]
    gain_sum.finish()
    gain_out[...] = gain_refs[5][...]


def run_tail(
    grad_b, grad_v, normed, weight, tok, back, late, w_group, raw_t, fixed, gate_grad, inv, gain,
    gain_mine, sel_bc, sel_raw, late_rows, late_gain, *small,
):
    n = lax.axis_size("context")
    steps, width = grad_v.shape
    size = D // 4
    half_d = D // 2
    block = half_d // n
    side_rows = (GROUP + END) // 2
    share = steps // 4
    top = lambda w: pl.BlockSpec((GROUP, w), lambda i: (0, 0), pipeline_mode=pl.Buffered(1))
    end = lambda w: pl.BlockSpec(
        (END, w), lambda i: (steps // END - 1, 0), pipeline_mode=pl.Buffered(1)
    )
    full = lambda x: once(*x.shape)
    hbm = pl.BlockSpec(memory_space=pl.ANY)
    dma = pltpu.SemaphoreType.DMA
    vmem = pltpu.VMEM
    value_rows = block if n == 4 else half_d
    pair = (2, side_rows, size)
    packed = (PACK, width + 2 * N)
    return pl.pallas_call(
        functools.partial(tail_kernel, n),
        grid=(1,),
        in_specs=[hbm] * 8
        + [full(raw_t), full(fixed), top(width), end(width), top(D), end(D)]
        + [full(x) for x in (inv, gain, gain_mine, sel_bc, sel_raw)]
        + [full(x) for x in (late_rows, late_gain, *small)],
        out_specs=[
            once(steps, size), once(value_rows, width), once(value_rows, LANE), once(4, *packed),
            once(4, 16, LANE),
        ],
        out_shape=[
            shape(steps, size, dtype=BF16), shape(value_rows, width), shape(value_rows, LANE),
            shape(4, *packed), shape(4, 16, LANE),
        ],
        scratch_shapes=[
            vmem((steps, 2 * N), F32), vmem((steps, width), BF16), vmem(normed.shape, BF16),
            vmem(weight.shape, BF16), vmem((steps, size), BF16), vmem((steps, size), BF16),
            vmem((size, w_group.shape[1]), BF16),
            vmem((steps, w_group.shape[1]), BF16),
            vmem((half_d, width), F32), vmem((half_d, width), F32), vmem((half_d, width), F32),
            vmem((2, 2, share, N), F32), vmem((2, share, N), F32), vmem((2, share, N), F32),
            vmem((steps, 2 * N), BF16), vmem((4, 16, steps), BF16),
            vmem(pair, F32), vmem(pair, F32), vmem((2, side_rows, 2 * size), BF16),
            vmem((2, side_rows, 2 * size), BF16), vmem(pair, BF16), vmem(pair, BF16), vmem((8, D), F32),
            vmem((2, 2 * block, width // 2), BF16), vmem((2, 2 * block, width // 2), BF16),
            vmem((2, block, width // 2), BF16), vmem((2, block, width // 2), BF16),
            vmem((steps, size), F32),
            vmem((half_d, LANE), F32), vmem((half_d, LANE), F32), vmem((half_d, LANE), F32),
            vmem((2 * block, LANE), F32), vmem((2 * block, LANE), F32), vmem((block, LANE), F32),
            vmem((block, LANE), F32),
            vmem((8, steps), F32), vmem((3, 8, steps), F32),
            *[
                vmem((*lead, *dims), F32)
                for dims in (packed, (16, LANE))
                for lead in ((), (), (), (n,), (), (4,))
            ],
            dma((8,)), dma((3,)), dma((3,)), dma((2, 6)), dma((2, 6)), dma((4,)), dma((4,)),
            dma((2,)), dma((2,)), dma((6,)), dma((6,)), dma((3,)), dma((3,)),
            *[dma, dma, dma((n - 1,)), dma((n - 1,)), dma((3,)), dma((3,))] * 2,
        ],
        compiler_params=pltpu.CompilerParams(
            dimension_semantics=("arbitrary",), vmem_limit_bytes=56 * 1024 * 1024,
            collective_id=5, has_side_effects=True,
        ),
        cost_estimate=estimate(50),
        name="tail",
    )(
        grad_b, grad_v, normed, weight, tok, back, late, w_group,
        raw_t, fixed, gate_grad, gate_grad, tok, tok, inv, gain, gain_mine, sel_bc, sel_raw,
        late_rows, late_gain, *small,
    )


def pad_rows(x, rows=8):
    return jnp.concatenate([x, jnp.zeros((rows - x.shape[0], x.shape[1]), x.dtype)], axis=0)


def pad_cols(x, cols=LANE):
    return jnp.concatenate([x, jnp.zeros((x.shape[0], cols - x.shape[1]), x.dtype)], axis=1)


def on_device(
    tokens, cotangent, doc_lengths, zx_weight, bcdt_weight, out_weight, input_gain, chan_params,
    bc_params, head_params, zx_first, bcdt_first, out_first, gain_first, chan_first, bc_first,
    head_first, zx_second, bcdt_second, out_second, gain_second, chan_second, bc_second, head_second,
):
    n_tensor = lax.axis_size("tensor")
    t_index = lax.axis_index("tensor")
    c_index = lax.axis_index("context")
    tok = tokens[0]
    resid = tok.astype(F32)
    back = cotangent[0]
    steps = resid.shape[0]
    inner_loc = INNER // n_tensor
    heads_loc = H // n_tensor
    share = D // n_tensor
    count = steps // L
    rows_loc = zx_weight.shape[0]
    cols_loc = bcdt_weight.shape[1]

    zx_flat = zx_weight.reshape(rows_loc, 2 * inner_loc)
    proj_w, cols_z = line_gather(zx_flat.astype(BF16), pad_cols(bcdt_weight.astype(BF16)))
    down_block, _ = lax.optimization_barrier((out_weight.astype(BF16).T, proj_w))
    down_t = lax.all_gather(down_block, ("shard", "context"), axis=0, tiled=True)
    chan_loc = lax.dynamic_slice_in_dim(chan_params, t_index * inner_loc, inner_loc, 1)
    head_loc = lax.dynamic_slice_in_dim(head_params, t_index * heads_loc, heads_loc, 1)
    chan8 = pad_rows(chan_loc)
    bc8 = pad_rows(bc_params)
    head8 = pad_rows(pad_cols(head_loc))
    spread_at = lax.broadcasted_iota(jnp.int32, (2 * LANE, inner_loc), 0) % LANE
    expand = (
        spread_at == lax.broadcasted_iota(jnp.int32, (2 * LANE, inner_loc), 1) // P_SIZE
    ).astype(BF16)
    gain8 = jnp.broadcast_to(input_gain[None], (8, D))
    (
        normed, inv_rms, projected, cols, info, marks_rows, edge_mask,
        act, delta, cum, sloc, pfx, final, halo_v, halo_b,
    ) = run_project(
        doc_lengths, tok, gain8, proj_w, cols_z, chan8, bc8, head8, expand, heads_loc, cols_loc
    )
    entry, back_scaled = run_entry(final, back, down_t)
    ssd, sums = run_ahead(
        act, delta, cum, info, marks_rows, sloc, pfx, entry, projected, back_scaled, chan8, head8,
        expand, heads_loc,
    )
    sums = small_sum(sums, 1)
    scaled, *out_fan = run_out(ssd, projected, sums, chan8, down_t)
    gate_grad, mixed_grad, aloc, sfx, first_adj, norm_gain_grad = run_norm(
        ssd, projected, back_scaled, sums, act, cum, info, chan8, expand, heads_loc
    )
    later, out_own, out_next, *z_arrays = run_middle(
        first_adj, out_fan, normed, gate_grad, back, scaled
    )
    resid_share = lax.dynamic_slice_in_dim(tok, t_index * share, share, 1).astype(F32)
    in_line = lax.axis_size("context") == 4
    total_width = inner_loc + 2 * N

    (
        grad_v, grad_b, raw_t, last_rows, _, taps_grad, bias_grad, skip_grad, head_grad,
        ng_late, late_rows, late_gain, out_last, *z_sum,
    ) = run_grand(
        projected, cols, halo_v, halo_b, info, marks_rows, delta, cum, ssd, mixed_grad,
        sloc, pfx, entry, aloc, sfx, later, chan8, bc8, head8, expand, heads_loc,
        gate_grad, proj_w, tok, inv_rms, gain8, edge_mask, out_next, z_arrays if in_line else [],
    )
    out_share = out_own + out_last.reshape(steps, share).astype(F32)
    block_out = (resid_share + out_share).astype(BF16)[None]
    if in_line:
        gate_g, down_g = z_sum[0][0], z_sum[0][1]
    else:
        gate_g, down_g = [
            lax.psum_scatter(z_arrays[0][k], "context", scatter_dimension=0, tiled=True) for k in (0, 1)
        ]
    column = np.arange(4 * LANE)
    column = np.where(column % LANE < cols_loc, column // LANE * cols_loc + column % LANE, -1)[None, :]
    sel_bc = (np.arange(2 * N)[:, None] == column).astype(ml_dtypes.bfloat16)
    slot = np.arange(4 * 16)[:, None]
    of_slot = np.where(slot % 16 < heads_loc, 2 * N + slot // 16 * heads_loc + slot % 16, -2)
    sel_raw = (of_slot == column).astype(ml_dtypes.bfloat16)
    gain_mine = jnp.broadcast_to(
        lax.dynamic_slice_in_dim(input_gain, t_index * share, share, 0)[None], (8, share)
    )
    tokens_grad, value_g, cols_g, packed, packed_gain = run_tail(
        grad_b, grad_v, normed, proj_w, tok, back, ng_late, cols_z, raw_t, last_rows, gate_grad,
        inv_rms, gain8, gain_mine, sel_bc, sel_raw, late_rows, late_gain,
        taps_grad, bias_grad, norm_gain_grad, skip_grad, head_grad,
    )
    tokens_grad = tokens_grad[None]
    if not in_line:
        value_g = lax.psum_scatter(value_g, "context", scatter_dimension=0, tiled=True)
        cols_g = lax.psum_scatter(cols_g[:, :cols_loc], "context", scatter_dimension=0, tiled=True)
        cols_g = pad_cols(cols_g)
    flip = lambda *arrays: tuple(a.T for a in arrays)
    lift = lambda *arrays: tuple(a[None] for a in arrays)
    news = run_adam(
        (gate_g, value_g, down_g, cols_g, packed, packed_gain),
        (
            (zx_weight, zx_first, zx_second), flip(out_weight, out_first, out_second),
            flip(bcdt_weight, bcdt_first, bcdt_second), lift(input_gain, gain_first, gain_second),
            (chan_params, chan_first, chan_second), (bc_params, bc_first, bc_second),
            (head_params, head_first, head_second),
        ),
        heads_loc, cols_loc,
    )
    zx_new, out_new, bcdt_new, gain_new = news[:3], flip(*news[3:6]), flip(*news[6:9]), news[9:12]
    return (
        block_out, tokens_grad, *zx_new, *bcdt_new, *out_new, *[g[0] for g in gain_new], *news[12:]
    )


def solution(mesh):
    big = P(("shard", "context"), None, "tensor")
    cols = P(("shard", "context"), "tensor")
    down = P("tensor", ("shard", "context"))
    rows = P("shard", "context", None)
    out_rows = P("shard", "context", "tensor")
    return jax.shard_map(
        on_device,
        mesh=mesh,
        in_specs=(
            rows, rows, P("shard", None), big, cols, down, P(), P(), P(), P(),
            big, cols, down, P(), P(), P(), P(),
            big, cols, down, P(), P(), P(), P(),
        ),
        out_specs=(
            out_rows, out_rows, big, big, big, cols, cols, cols, down, down, down,
            *([P()] * 12),
        ),
        check_vma=False,
    )
```

```python
import functools

import jax
import jax.numpy as jnp
import ml_dtypes
import numpy as np
from jax import lax
from jax.experimental import pallas as pl
from jax.experimental.pallas import tpu as pltpu
from jax.sharding import PartitionSpec as P

D = 1536
INNER = 3072
H = 48
P_SIZE = 64
N = 128
KERNEL = 4
STEP = 10

EPS = 1e-05
BETA_ONE = 0.9
BETA_TWO = 0.999
ADAM_EPS = 1e-08
DECAY = 0.1
RATE_MATRIX = 0.05
RATE_SMALL = 0.2

L = 128
LANE = 128
GROUP = 4 * L
PART = 2 * L
END = 32
LOG2E = 1.4426950408889634
F32 = jnp.float32
BF16 = jnp.bfloat16
VMEM_LIMIT = 58 * 1024 * 1024


def from_behind(block, axis, distance):
    devices = range(lax.axis_size(axis))
    route = [(i - distance, i) for i in devices if i - distance in devices]
    return lax.ppermute(block, axis, route)


def adamw(weight, grad, first, second, rate, decay):
    first_new = BETA_ONE * first + (1.0 - BETA_ONE) * grad
    second_new = BETA_TWO * second + (1.0 - BETA_TWO) * grad * grad
    scale_one = 1.0 - BETA_ONE**STEP
    scale_two = 1.0 - BETA_TWO**STEP
    update = first_new / scale_one / (jnp.sqrt(second_new / scale_two) + ADAM_EPS)
    return (weight - rate * (update + decay * weight), first_new, second_new)


def two(x):
    hi = x.astype(BF16)
    return hi, (x - hi.astype(F32)).astype(BF16)


def dot(a, b, ca=1, cb=0):
    return lax.dot_general(a, b, (((ca,), (cb,)), ((), ())), preferred_element_type=F32)


def dot3(a, b, ca=1, cb=0):
    ah, al = two(a)
    bh, bl = two(b)
    return dot(
        jnp.concatenate([ah, al, ah], axis=ca), jnp.concatenate([bh, bh, bl], axis=cb), ca, cb
    )


def over_rows(left, lanes, right):
    total = None
    for at in range(0, left.shape[0], GROUP):
        rows = slice(at, at + GROUP)
        part = dot(left[rows, lanes], right(rows), 0, 0)
        total = part if total is None else total + part
    return total


def tri_sum(tri, x):
    hi = x.astype(BF16)
    rest = x - hi.astype(F32)
    mid = rest.astype(BF16)
    low = (rest - mid.astype(F32)).astype(BF16)
    out = dot(tri, jnp.concatenate([hi, mid, low], axis=1))
    w = x.shape[1]
    return out[:, :w] + out[:, w : 2 * w] + out[:, 2 * w :]


def spread(x, e_ref):
    hi, lo = two(x)
    return dot(jnp.concatenate([hi, lo], axis=1), e_ref[...])


def per_head(x, e_ref):
    hi, lo = two(x)
    e = e_ref[:LANE, :]
    return dot(hi, e, 1, 1) + dot(lo, e, 1, 1)


def sigmoid(x):
    return 1.0 / (1.0 + jnp.exp(-x))


def softplus(x):
    return jnp.maximum(x, 0.0) + jnp.log1p(jnp.exp(-jnp.abs(x)))


def tiles(width):
    return [slice(k, k + LANE) for k in range(0, width, LANE)]


def fold(x):
    return jnp.sum(x.reshape(x.shape[0] // 8, 8, x.shape[1]), axis=0)


def lower_mask():
    row = lax.broadcasted_iota(jnp.int32, (L, L), 0)
    col = lax.broadcasted_iota(jnp.int32, (L, L), 1)
    return row >= col


def keep_mask(info, marks_row):
    return jnp.logical_and(lower_mask(), info[:, 5:6] == marks_row[0:1, :])


def decay_of(keep, cum, cum_t, h):
    return jnp.exp2(jnp.where(keep, cum[:, h : h + 1] - cum_t[h : h + 1, :], -1e30))


def load_ext(ext_ref, cur_ref, prev_ref, halo_ref, j, first):
    if j > 0:
        ext_ref[0:8, :] = cur_ref[j * L - 8 : j * L, :]
    else:

        @pl.when(first)
        def _():
            ext_ref[0:8, :] = halo_ref[...]

        @pl.when(jnp.logical_not(first))
        def _():
            ext_ref[0:8, :] = prev_ref[...]

    ext_ref[8 : 8 + L, :] = cur_ref[j * L : (j + 1) * L, :]


def rows_of_chunk(ref, j):
    return ref.at[pl.ds(pl.multiple_of(j * L, L), L), :]


def lead_of_chunk(ref, j):
    return ref.at[pl.ds(j, 1)]


def load_ext_of(ext_ref, cur_ref, prev_ref, halo_ref, j, first):
    @pl.when(first)
    def _():
        ext_ref[0:8, :] = halo_ref[...]

    @pl.when(jnp.logical_and(j == 0, jnp.logical_not(first)))
    def _():
        ext_ref[0:8, :] = prev_ref[...]

    @pl.when(j > 0)
    def _():
        ext_ref[0:8, :] = cur_ref[pl.ds(pl.multiple_of(jnp.maximum(j * L - 8, 0), 8), 8), :]

    ext_ref[8 : 8 + L, :] = cur_ref[pl.ds(pl.multiple_of(j * L, L), L), :]


def rows_at(ref, j):
    return ref.at[j * L : (j + 1) * L, :]


def lead_at(ref, j):
    return ref.at[j : j + 1]


def conv_tile(ext_ref, info, taps, sl):
    shifted = []
    total = jnp.broadcast_to(taps[KERNEL : KERNEL + 1, :], (L, LANE))
    for k in range(KERNEL):
        val = ext_ref[pl.ds(8 - KERNEL + 1 + k, L), sl]
        if k < KERNEL - 1:
            val = val * info[:, k : k + 1]
        shifted.append(val)
        total = total + taps[k : k + 1, :] * val
    return shifted, total


def prep_chunk(
    bc, info_ref, chan, bcpar, head, e_ref, act, delta_ref, cum_ref, sloc, pfx, ext_v, ext_b, state, prod
):
    info = info_ref[...]
    width = ext_v.shape[1]
    for sl in tiles(width):
        _, total = conv_tile(ext_v, info, chan[:, sl], sl)
        act[:, sl] = total * sigmoid(total)
    for sl in tiles(2 * N):
        _, total = conv_tile(ext_b, info, bcpar[:, sl], sl)
        act[:, slice(width + sl.start, width + sl.stop)] = total * sigmoid(total)
    raw = bc[:, 2 * N : 3 * N]
    delta = softplus(raw + head[0:1, :])
    dlog = -delta * (jnp.exp(head[1:2, :]) * LOG2E)
    tri = jnp.where(lower_mask(), 1.0, 0.0).astype(BF16)
    cum = tri_sum(tri, dlog)
    delta_ref[...] = delta
    cum_ref[...] = cum
    sloc[0] = state[...]
    pfx[0] = prod[...]
    last = cum[L - 1 : L, :]
    tail = info[:, 4:5] * jnp.exp2(last - cum) * delta
    through = spread(
        jnp.broadcast_to(info[L - 1 : L, 3:4] * jnp.exp2(last), (8, LANE)), e_ref
    )
    weights = spread(tail, e_ref)
    tail_u = act[:, :width] * weights
    fresh = dot3(act[:, width : width + N], tail_u, 0, 0)
    state[...] = state[...] * through[0:1, :] + fresh
    prod[...] = prod[...] * through


def row_block(width, col=0, rows=GROUP):
    return pl.BlockSpec((rows, width), lambda i: (i, col))


def prev_block(width, col=0, rows=GROUP):
    return pl.BlockSpec((8, width), lambda i: (jnp.maximum(i * (rows // 8) - 1, 0), col))


def lead_block(*dims, rows=GROUP):
    return pl.BlockSpec((rows // L, *dims), lambda i: (i, 0, 0))


def whole(*shape):
    return pl.BlockSpec(shape, lambda i: (0,) * len(shape))


def once(*shape):
    return pl.BlockSpec(shape, lambda i: (0,) * len(shape), pipeline_mode=pl.Buffered(1))


def estimate(us):
    return pl.CostEstimate(flops=int(us * 1.1e9), bytes_accessed=int(us * 1e6), transcendentals=0)


def params(**kw):
    return pltpu.CompilerParams(
        dimension_semantics=("arbitrary",), vmem_limit_bytes=VMEM_LIMIT, **kw
    )


def shape(*dims, dtype=F32):
    return jax.ShapeDtypeStruct(dims, dtype)


def ahead_kernel(
    heads, act, delta, cum, info, marks, sloc, pfx, entry, gate, back, chan, head, e_ref, ssd, sums,
    mine, held, send, recv,
):
    i = pl.program_id(0)
    s, c, t = lax.axis_index("shard"), lax.axis_index("context"), lax.axis_index("tensor")
    group = [(s, c, lax.rem(t + k, 4)) for k in (1, 2, 3)]

    @pl.when(i == 0)
    def _():
        pl.semaphore_wait(greet(group), 3)

    chunks = act.shape[0] // L
    for j in range(act.shape[0] // L):
        ahead_chunk(
            rows_at(act, j), rows_at(delta, j), rows_at(cum, j), rows_at(info, j), lead_at(marks, j),
            lead_at(sloc, j), lead_at(pfx, j), entry, rows_at(gate, j), rows_at(back, j), chan, head,
            e_ref, rows_at(ssd, j), mine.at[pl.ds(i * chunks + j, 1)],
        )

    @pl.when(i == pl.num_programs(0) - 1)
    def _():
        copies = [
            remote(mine, held.at[k], send.at[k], recv.at[k], target) for k, target in enumerate(group)
        ]
        for copy in copies:
            copy.start()
        total = mine[...]
        for k, copy in enumerate(copies):
            copy.wait()
            total = total + held[k]
        sums[...] = total


def ahead_chunk(
    act, delta_ref, cum_ref, info_ref, marks_ref, sloc, pfx, entry, gate, back, chan, head, e_ref, ssd, sums
):
    width = act.shape[1] - 2 * N
    info = info_ref[...]
    cum = cum_ref[...]
    cum_t = cum.T
    keep = keep_mask(info, marks_ref[0])
    bmat = act[:, width : width + N]
    cmat = act[:, width + N :]
    scores = dot3(cmat, bmat, 1, 1)
    xs = act[:, :width]
    u_hi, u_lo = two(xs * spread(delta_ref[...], e_ref))
    state = sloc[0] + entry[...] * pfx[0, 0:1, :]
    entering = dot3(cmat, state)
    eexp = spread(info[:, 3:4] * jnp.exp2(cum), e_ref)
    skip = spread(jnp.broadcast_to(head[2:3, :], (8, LANE)), e_ref)
    lane = lax.broadcasted_iota(jnp.int32, (1, LANE), 1)
    left = jnp.where(lane < P_SIZE, 1.0, 0.0).astype(BF16)
    right = jnp.where(lane < P_SIZE, 0.0, 1.0).astype(BF16)
    square = jnp.zeros((L, LANE), F32)
    cross = jnp.zeros((L, LANE), F32)
    for q, sl in enumerate(tiles(width)):
        mix = jnp.concatenate(
            [(scores * decay_of(keep, cum, cum_t, 2 * q + r)).astype(BF16) for r in (0, 1)], axis=1
        )
        both = jnp.concatenate([u_hi[:, sl], u_lo[:, sl]], axis=1)
        rhs = jnp.concatenate(
            [both * jnp.concatenate([m, m], axis=1) for m in (left, right)], axis=0
        )
        out = dot(mix, rhs)
        y = out[:, :LANE] + out[:, LANE:] + entering[:, sl] * eexp[:, sl]
        y = y + skip[0:1, sl] * xs[:, sl]
        ssd[:, sl] = y
        g = gate[:, sl]
        gated = y * g * sigmoid(g)
        square = square + gated * gated
        cross = cross + gated * (back[:, sl] * chan[KERNEL + 1 : KERNEL + 2, sl])
    ones = jnp.ones((8, LANE), BF16)
    rows = []
    for part in (square, cross):
        hi, lo = two(part)
        rows.append(dot(ones, hi, 1, 1) + dot(ones, lo, 1, 1))
    pick = lax.broadcasted_iota(jnp.int32, (8, LANE), 0)
    sums[0] = jnp.where(pick == 0, rows[0], jnp.where(pick == 1, rows[1], 0.0))


def run_ahead(act, delta, cum, info, marks, sloc, pfx, entry, projected, back, chan, head, expand, heads):
    steps, width = projected.shape[0], projected.shape[1] // 2
    count = steps // L
    return pl.pallas_call(
        functools.partial(ahead_kernel, heads),
        grid=(steps // GROUP,),
        in_specs=[
            row_block(width + 2 * N), row_block(LANE), row_block(LANE), row_block(LANE),
            lead_block(8, L), lead_block(N, width), lead_block(8, width),
            once(N, width), row_block(width, 0), row_block(width),
            once(KERNEL + 2, width), once(8, LANE), once(2 * LANE, width),
        ],
        out_specs=[row_block(width), once(count, 8, L)],
        out_shape=[shape(steps, width), shape(count, 8, L)],
        scratch_shapes=[
            pltpu.VMEM((count, 8, L), F32), pltpu.VMEM((3, count, 8, L), F32),
            pltpu.SemaphoreType.DMA((3,)), pltpu.SemaphoreType.DMA((3,)),
        ],
        compiler_params=params(collective_id=1, has_side_effects=True),
        cost_estimate=estimate(20),
        name="ahead",
    )(act, delta, cum, info, marks, sloc, pfx, entry, projected, back, chan, head, expand)


def norm_kernel(
    heads, ssd, gate, back, sums, cmat, cum, info, chan, e_ref,
    gate_grad, mixed_grad, aloc, sfx, fin, gain_grad, state, prod,
):
    i = pl.program_id(0)

    @pl.when(i == 0)
    def _():
        state[...] = jnp.zeros_like(state)
        prod[...] = jnp.ones_like(prod)
        gain_grad[...] = jnp.zeros_like(gain_grad)

    chunks = ssd.shape[0] // L

    for j in reversed(range(chunks)):
        norm_chunk(
            rows_at(ssd, j), rows_at(gate, j), rows_at(back, j), lead_at(sums, j), rows_at(cmat, j),
            rows_at(cum, j), rows_at(info, j), chan, e_ref, rows_at(gate_grad, j),
            rows_at(mixed_grad, j), lead_at(aloc, j), lead_at(sfx, j), gain_grad, state, prod,
        )

    @pl.when(i == pl.num_programs(0) - 1)
    def _():
        fin[:N, :] = state[...]
        fin[N:, :] = prod[...]


def norm_chunk(
    ssd, gate, back, sums, cmat_ref, cum_ref, info_ref, chan, e_ref,
    gate_grad, mixed_grad, aloc, sfx, gain_grad, state, prod,
):
    width = ssd.shape[1]
    rows = sums[0]
    inv_row = lax.rsqrt(rows[0:1, :] / INNER + EPS)
    cross_row = inv_row * inv_row * inv_row * (rows[1:2, :] / INNER)
    inv = jnp.broadcast_to(inv_row, (LANE, L)).T
    cross = jnp.broadcast_to(cross_row, (LANE, L)).T
    info = info_ref[...]
    cum = cum_ref[...]
    eexp = spread(info[:, 3:4] * jnp.exp2(cum), e_ref)
    e_mixed = []
    for sl in tiles(width):
        g = gate[:, sl]
        sig = sigmoid(g)
        soft = g * sig
        y = ssd[:, sl]
        gated = y * soft
        bs = back[:, sl]
        gain = chan[KERNEL + 1 : KERNEL + 2, sl]
        normed = gated * inv
        gain_grad[:, sl] += fold(bs * normed)
        gg = inv * (bs * gain) - gated * cross
        mg = gg * soft
        mixed_grad[:, sl] = mg
        gate_grad[:, sl] = (gg * y * sig * (1.0 + g * (1.0 - sig))).astype(BF16)
        e_mixed.append(mg * eexp[:, sl])
    aloc[0] = state[...]
    sfx[0] = prod[...]
    through = spread(
        jnp.broadcast_to(info[L - 1 : L, 3:4] * jnp.exp2(cum[L - 1 : L, :]), (8, LANE)), e_ref
    )
    fresh = dot3(cmat_ref[...], jnp.concatenate(e_mixed, axis=1), 0, 0)
    state[...] = state[...] * through[0:1, :] + fresh
    prod[...] = prod[...] * through


def run_norm(ssd, projected, back, sums, act, cum, info, chan, expand, heads):
    steps, width = ssd.shape
    count = steps // L
    blocks = steps // GROUP
    turn = lambda spec: pl.BlockSpec(
        spec.block_shape, lambda i, m=spec.index_map: m(blocks - 1 - i)
    )
    c_col = width // N + 1
    return pl.pallas_call(
        functools.partial(norm_kernel, heads),
        grid=(blocks,),
        in_specs=[
            turn(row_block(width)), turn(row_block(width, 0)), turn(row_block(width)),
            turn(lead_block(8, L)),
            turn(row_block(N, c_col)), turn(row_block(LANE)), turn(row_block(LANE)),
            once(KERNEL + 2, width), once(2 * LANE, width),
        ],
        out_specs=[
            turn(row_block(width)), turn(row_block(width)),
            turn(lead_block(N, width)),
            turn(lead_block(8, width)),
            whole(N + 8, width), whole(8, width),
        ],
        out_shape=[
            shape(steps, width, dtype=BF16), shape(steps, width),
            shape(count, N, width), shape(count, 8, width), shape(N + 8, width), shape(8, width),
        ],
        scratch_shapes=[pltpu.VMEM((N, width), F32), pltpu.VMEM((8, width), F32)],
        compiler_params=params(),
        cost_estimate=estimate(21),
        name="norm_back",
    )(ssd, projected, back, sums, act, cum, info, chan, expand)


def behind_chunk(
    heads, j, start, first, val, valp, bc, bcp, halo_v, halo_b, info_ref, marks_ref, delta_ref, cum_ref,
    ssd, mixed_grad, sloc, pfx, entry, aloc, sfx, later, chan, bcpar, head, e_ref,
    grad_v, grad_b, raw_grad, tail_rows, head_rows, taps_grad, bias_grad, skip_grad, head_grad,
    ext_v, ext_b, slope, d_tot,
):
    width = val.shape[1]
    total_width = width + 2 * N

    @pl.when(start)
    def _():
        d_tot[0:8, :] = jnp.zeros((8, total_width), F32)
        taps_grad[...] = jnp.zeros_like(taps_grad)
        bias_grad[...] = jnp.zeros_like(bias_grad)
        skip_grad[...] = jnp.zeros_like(skip_grad)
        head_grad[...] = jnp.zeros_like(head_grad)

    d_tot[L:, :] = d_tot[0:8, :]
    load_ext_of(ext_v, val, valp, halo_v, j, first)
    load_ext_of(ext_b, bc, bcp, halo_b, j, first)
    raw = bc[pl.ds(pl.multiple_of(j * L, L), L), 2 * N : 3 * N]
    info_ref, marks_ref = rows_of_chunk(info_ref, j), lead_of_chunk(marks_ref, j)
    delta_ref, cum_ref = rows_of_chunk(delta_ref, j), rows_of_chunk(cum_ref, j)
    ssd, mixed_grad = rows_of_chunk(ssd, j), rows_of_chunk(mixed_grad, j)
    sloc, pfx = lead_of_chunk(sloc, j), lead_of_chunk(pfx, j)
    aloc, sfx = lead_of_chunk(aloc, j), lead_of_chunk(sfx, j)
    grad_v, grad_b = rows_of_chunk(grad_v, j), rows_of_chunk(grad_b, j)
    raw_grad = raw_grad.at[:, pl.ds(pl.multiple_of(j * L, L), L)]
    info = info_ref[...]

    def activate(ext_ref, taps, sl, at):
        _, total = conv_tile(ext_ref, info, taps[:, sl], sl)
        sig = sigmoid(total)
        slope[:, slice(at, at + LANE)] = sig * (1.0 + total * (1.0 - sig))
        return total * sig

    xs = jnp.concatenate([activate(ext_v, chan, sl, sl.start) for sl in tiles(width)], axis=1)
    bmat = activate(ext_b, bcpar, slice(0, N), width)
    cmat = activate(ext_b, bcpar, slice(N, 2 * N), width + N)

    delta = delta_ref[...]
    cum = cum_ref[...]
    cum_t = cum.T
    keep = keep_mask(info, marks_ref[0])
    last = cum[L - 1 : L, :]
    scores = dot3(cmat, bmat, 1, 1)
    dexp = spread(delta, e_ref)
    eexp = spread(info[:, 3:4] * jnp.exp2(cum), e_ref)
    texp = spread(info[:, 4:5] * jnp.exp2(last - cum), e_ref)
    u = xs * dexp
    u_hi, u_lo = two(u)
    dy = mixed_grad[...]
    dy_hi, dy_lo = two(dy)
    skip = spread(jnp.broadcast_to(head[2:3, :], (8, LANE)), e_ref)
    state = sloc[0] + entry[...] * pfx[0, 0:1, :]
    adj = aloc[0] + later[...] * sfx[0, 0:1, :]
    tail_du = dot3(bmat, adj) * texp
    lane = lax.broadcasted_iota(jnp.int32, (1, LANE), 1)
    left = jnp.where(lane < P_SIZE, 1.0, 0.0).astype(BF16)
    right = jnp.where(lane < P_SIZE, 0.0, 1.0).astype(BF16)
    two_left = jnp.concatenate([left, left], axis=1)
    two_right = jnp.concatenate([right, right], axis=1)
    d_scores = jnp.zeros((L, L), F32)
    inner_du = []
    for q, sl in enumerate(tiles(width)):
        decays = [decay_of(keep, cum, cum_t, 2 * q + r) for r in (0, 1)]
        mix = jnp.concatenate([(scores * d).astype(BF16) for d in decays], axis=0)
        dy_both = jnp.concatenate([dy_hi[:, sl], dy_lo[:, sl]], axis=1)
        rhs = jnp.concatenate([dy_both * two_left, dy_both * two_right], axis=0)
        out = dot(mix, rhs, 0, 0)
        inner_du.append(out[:, :LANE] + out[:, LANE:])
        u_twice = jnp.concatenate([u_hi[:, sl], u_hi[:, sl]], axis=1)
        u_rows = jnp.concatenate([u_twice * two_left, u_twice * two_right], axis=0)
        d_mix = dot(dy_both, u_rows, 1, 1)
        d_scores = d_scores + d_mix[:, :L] * decays[0] + d_mix[:, L:] * decays[1]
    du = jnp.concatenate(inner_du, axis=1) + tail_du
    d_xs = dexp * du + skip[0:1, :] * dy
    d_b = dot3(d_scores, cmat, 0, 0) + dot3(u * texp, adj, 1, 1)
    d_c = dot3(d_scores, bmat) + dot3(dy * eexp, state, 1, 1)
    skip_grad[...] += fold(dy * xs)

    direct = per_head(xs * du, e_ref)
    mixed = ssd[...] - skip[0:1, :] * xs
    d_cum = per_head(dy * mixed, e_ref) - delta * direct
    at_last = jnp.sum(per_head(u * tail_du, e_ref), axis=0, keepdims=True)
    through = info[L - 1 : L, 3:4] * jnp.exp2(last)
    pair = per_head(fold(adj * state), e_ref)
    at_last = at_last + through * jnp.sum(pair, axis=0, keepdims=True)
    upper = jnp.where(lower_mask(), 1.0, 0.0).astype(BF16).T
    d_log = tri_sum(upper, d_cum) + at_last
    rate = jnp.exp(head[1:2, :])
    valid = lane < heads
    d_raw = (direct - d_log * rate) * sigmoid(raw + head[0:1, :])
    d_raw = jnp.where(valid, d_raw, 0.0)
    raw_grad[...] = d_raw.T[:16, :].astype(BF16)
    head_grad[0:8, :] += fold(d_raw)
    head_grad[8:16, :] += fold(jnp.where(valid, -d_log * delta * rate, 0.0))

    d_act = [d_xs[:, sl] for sl in tiles(width)] + [d_b, d_c]
    for q in range(total_width // LANE):
        sl = slice(q * LANE, (q + 1) * LANE)
        if q < width // LANE:
            ext_ref, taps, part = ext_v, chan[:, sl], sl
        else:
            part = slice(sl.start - width, sl.stop - width)
            ext_ref, taps = ext_b, bcpar[:, part]
        dt = d_act[q] * slope[:, sl]
        d_tot[0:L, sl] = dt
        bias_grad[:, sl] += fold(dt)
        for k in range(KERNEL):
            moved = ext_ref[pl.ds(8 - KERNEL + 1 + k, L), part]
            if k < KERNEL - 1:
                moved = moved * info[:, k : k + 1]
            taps_grad[8 * k : 8 * k + 8, sl] += fold(dt * moved)
        total = dt * taps[KERNEL - 1 : KERNEL, :]
        for s in range(1, KERNEL):
            total = total + taps[KERNEL - 1 - s : KERNEL - s, :] * (
                d_tot[pl.ds(s, L), sl] * info[:, 7 + s : 8 + s]
            )
        if q < width // LANE:
            grad_v[:, sl] = total.astype(BF16)
        else:
            grad_b[:, part] = total

        @pl.when(start)
        def _():
            tail_rows[:, sl] = total[L - 8 :, :]

    @pl.when(first)
    def _():
        head_rows[...] = d_tot[0:8, :]


def remote(src, dst, send, recv, target):
    return pltpu.make_async_remote_copy(
        src_ref=src, dst_ref=dst, send_sem=send, recv_sem=recv, device_id=target,
        device_id_type=pl.DeviceIdType.MESH,
    )


def greet(targets):
    barrier = pltpu.get_barrier_semaphore()
    for target in targets:
        pl.semaphore_signal(
            barrier, inc=1, device_id=target, device_id_type=pl.DeviceIdType.MESH
        )
    return barrier


def count_rows(parts, z, gain, at, gain_grad):
    rows = jnp.zeros((parts[0].shape[0], LANE), F32)
    size = parts[0].shape[1]
    for part, k in zip(parts, at):
        lanes = pl.ds(pl.multiple_of(k * size, size), size)
        part = part * z(lanes)
        gain_grad[:, lanes] += fold(part)
        part = part * gain[0:1, lanes]
        for sl in tiles(size):
            rows = rows + part[:, sl]
    return rows


def row_dots(rows):
    ones = jnp.ones((8, LANE), BF16)
    hi, lo = two(rows)
    return dot(ones, hi, 1, 1) + dot(ones, lo, 1, 1)


def grand_kernel(heads, n, *refs):
    behind, refs = refs[:22], refs[22:]
    gate_grad, w_ref, tok, inv, gain, edge_mask, out_next = refs[:7]
    refs = refs[7:]
    in_line = n == 4
    if in_line:
        z_out, z_mid, z_mine = refs[:3]
        refs = refs[3:]
    outs, refs = refs[:9], refs[9:]
    ng_own, row_sums, gain_grad, out_last = refs[:4]
    refs = refs[4:]
    if in_line:
        z_sum, refs = refs[0], refs[1:]
    scratch, refs = refs[:4], refs[4:]
    mid, send, got, nxt, last, edge, s1, r1, s2, r2, edge_s, edge_r, o_s, o_r = refs[:14]
    if in_line:
        z_got, z_on, z_last, z_s, z_r = refs[14:]
    chan, bcpar = behind[18], behind[19]
    grad_v, tail_rows = outs[0], outs[3]
    d_tot = scratch[3]
    i, n_steps = pl.program_id(0), pl.num_programs(0)
    s, c, t = lax.axis_index("shard"), lax.axis_index("context"), lax.axis_index("tensor")
    near = peers(t)
    to = [(s, c, near[0]), (s, c, near[1])]
    width = grad_v.shape[1]
    size = w_ref.shape[0] // 4
    inside = mid.shape[0]
    chunks = grad_v.shape[0] // L

    @pl.when(i == 0)
    def _():
        pl.semaphore_wait(greet(to + beside_of(n)), 4)
        gain_grad[...] = jnp.zeros_like(gain_grad)

    def out_hop(side):
        return remote(
            out_next.at[side], out_last.at[side], o_s.at[side], o_r.at[side], to[1 - side]
        )

    @pl.when(i == 0)
    def _():
        for side in (0, 1):
            out_hop(side).start()

    if in_line:
        line = [(s, c + 1 - 2 * lax.rem(c, 2), t), (s, 3 - c, t)]
        block = z_mid.shape[1]

        def z_first(k):
            return remote(z_out.at[k], z_got.at[k], z_s.at[k], z_r.at[k], line[k])

        def z_second(k):
            return remote(z_on.at[k], z_last.at[k], z_s.at[2 + k], z_r.at[2 + k], line[1 - k])

        @pl.when(i == 0)
        def _():
            for k in (0, 1):
                z_first(k).start()

        @pl.when(i == n_steps // 2)
        def _():
            for k in (0, 1):
                z_first(k).wait()
                z_on[k] = (z_mid[k] + z_got[k, block:, :].astype(F32)).astype(BF16)
                z_second(k).start()
                z_sum[k] = z_mine[k] + z_got[k, :block, :].astype(F32)

        @pl.when(i == n_steps - 1)
        def _():
            for k in (0, 1):
                z_second(k).wait()
                z_sum[k] += z_last[k].astype(F32)

    def first_hop(k, side):
        return remote(send.at[k], got.at[k], s1.at[k], r1.at[k], to[side])

    def second_hop(k, side):
        return remote(nxt.at[k], last.at[k], s2.at[k], r2.at[k], to[1 - side])

    def place(k):
        return pl.ds(pl.multiple_of((inside - 1 - k) * PART, PART), PART)

    def turn_over(k, side):
        first_hop(k, side).wait()
        nxt[k] = (mid[k] + got[k, :, size:].astype(F32)).astype(BF16)
        second_hop(k, side).start()
        ng_own[place(k), :] += got[k, :, :size].astype(F32)

    def one(step, carry):
        j = chunks - 1 - step
        behind_chunk(
            heads, j, jnp.logical_and(i == 0, step == 0),
            jnp.logical_and(i == n_steps - 1, j == 0), *behind, *outs, *scratch,
        )
        for side in (0, 1):
            ready = jnp.logical_and(step == 0, lax.rem(i, 2) == 1 - side)

            @pl.when(jnp.logical_and(ready, jnp.logical_and(i >= 2, i < inside + 2)))
            def _():
                turn_over(i - 2, side)

        return carry

    lax.fori_loop(0, chunks, one, 0)

    def fan(side):
        counted = jnp.where(i == 0, PART - END, PART)
        x = jnp.concatenate([gate_grad[...], grad_v[...]], axis=1)
        keep, go = shares_of(side, t)
        gone = dot(x, pick(w_ref, *go), 1, 1)
        send[i] = gone.astype(BF16)
        first_hop(i, side).start()
        kept = dot(x, pick(w_ref, *keep), 1, 1)
        ng_own[place(i), :] = kept[:, :size]
        mid[i] = kept[:, size:]
        row = lax.broadcasted_iota(jnp.int32, (PART, 1), 0)
        scale = jnp.where(row < counted, inv[...], 0.0)
        parts = [kept[:, :size], kept[:, size:], gone[:, :size], gone[:, size:]]
        sums = count_rows(
            parts, lambda lanes: tok[:, lanes].astype(F32) * scale, gain, keep + go, gain_grad
        )
        row_sums[0] = row_dots(sums)

    for side in (0, 1):
        parity = lax.rem(i, 2) == 1 - side

        @pl.when(jnp.logical_and(parity, i < inside))
        def _():
            fan(side)

    @pl.when(i == n_steps - 1)
    def _():
        before = (s, jnp.maximum(c - 1, 0), t)
        copy = remote(d_tot.at[pl.ds(0, 8), :], edge, edge_s, edge_r, before)

        @pl.when(c > 0)
        def _():
            copy.start()

        for k in range(inside):
            second_hop(k, 1 - k % 2).wait()
            ng_own[place(k), :] += last[k].astype(F32)
        for side in (0, 1):
            out_hop(side).wait()

        @pl.when(c < n - 1)
        def _():
            copy.wait_recv()
            for shift in range(1, KERNEL):
                moved = pltpu.roll(edge[...], 8 - shift, 0) * edge_mask[
                    8 * shift - 8 : 8 * shift, 0:1
                ]
                tap = slice(KERNEL - 1 - shift, KERNEL - shift)
                tail_rows[:, :width] += chan[tap, :] * moved[:, :width]
                tail_rows[:, width:] += bcpar[tap, :] * moved[:, width:]

        @pl.when(c > 0)
        def _():
            copy.wait_send()


def run_grand(
    projected, cols, halo_v, halo_b, info, marks, delta, cum, ssd, mixed_grad, sloc, pfx, entry,
    aloc, sfx, later, chan, bcpar, head, expand, heads, gate_grad, weight, tok, inv, gain, edge_mask,
    out_next, z_arrays,
):
    steps, width = ssd.shape
    parts = steps // PART
    inside = (steps - GROUP) // PART
    size = D // 4
    turn = lambda spec: pl.BlockSpec(
        spec.block_shape, lambda i, m=spec.index_map: m(parts - 1 - i)
    )
    in_part = lambda w: pl.BlockSpec((PART, w), lambda i: (parts - 1 - i, 0))
    chunk = lead_block(N, width, rows=PART)
    few = lead_block(8, width, rows=PART)
    total = width + 2 * N
    dma = pltpu.SemaphoreType.DMA
    return pl.pallas_call(
        functools.partial(grand_kernel, heads, lax.axis_size("context")),
        grid=(parts,),
        in_specs=[
            turn(row_block(width, 1, rows=PART)), turn(prev_block(width, 1, rows=PART)),
            turn(row_block(3 * N, rows=PART)), turn(prev_block(3 * N, rows=PART)),
            once(8, width), once(8, 3 * N), turn(row_block(LANE, rows=PART)),
            turn(lead_block(8, L, rows=PART)),
            turn(row_block(LANE, rows=PART)), turn(row_block(LANE, rows=PART)), turn(row_block(width, rows=PART)), turn(row_block(width, rows=PART)),
            turn(chunk), turn(few), once(N, width), turn(chunk), turn(few), once(N, width),
            once(KERNEL + 2, width), once(KERNEL + 1, 2 * N), once(8, LANE), once(2 * LANE, width),
            turn(row_block(width, rows=PART)), once(*weight.shape), in_part(D), in_part(1), once(8, D),
            once(24, LANE), pl.BlockSpec(memory_space=pl.ANY),
        ]
        + ([pl.BlockSpec(memory_space=pl.ANY)] + [once(*z.shape) for z in z_arrays[1:]] if z_arrays else []),
        out_specs=[
            turn(row_block(width, rows=PART)), turn(row_block(2 * N, rows=PART)),
            pl.BlockSpec((16, PART), lambda i: (0, parts - 1 - i)),
            whole(8, total), whole(8, total), whole(8 * KERNEL, total), whole(8, total),
            whole(8, width), whole(16, LANE),
            once(inside * PART, size),
            pl.BlockSpec((1, 8, PART), lambda i: (parts - 1 - i, 0, 0)),
            whole(8, D), pl.BlockSpec(memory_space=pl.ANY),
        ]
        + [once(*z.shape) for z in z_arrays[1:2]],
        out_shape=[
            shape(steps, width, dtype=BF16), shape(steps, 2 * N), shape(16, steps, dtype=BF16),
            shape(8, total), shape(8, total), shape(8 * KERNEL, total), shape(8, total),
            shape(8, width), shape(16, LANE),
            shape(inside * PART, size), shape(parts, 8, PART), shape(8, D),
            shape(*out_next.shape, dtype=BF16),
        ]
        + [shape(*z.shape) for z in z_arrays[1:2]],
        scratch_shapes=[
            pltpu.VMEM((8 + L, width), F32), pltpu.VMEM((8 + L, 3 * N), F32),
            pltpu.VMEM((L, total), F32), pltpu.VMEM((L + 8, total), F32),
            pltpu.VMEM((inside, PART, size), F32),
            pltpu.VMEM((inside, PART, 2 * size), BF16), pltpu.VMEM((inside, PART, 2 * size), BF16),
            pltpu.VMEM((inside, PART, size), BF16), pltpu.VMEM((inside, PART, size), BF16),
            pltpu.VMEM((8, total), F32),
            dma((inside,)), dma((inside,)), dma((inside,)), dma((inside,)), dma, dma,
            dma((2,)), dma((2,)),
        ]
        + (
            [
                pltpu.VMEM(z_arrays[0].shape, BF16), pltpu.VMEM(z_arrays[1].shape, BF16),
                pltpu.VMEM(z_arrays[1].shape, BF16), dma((4,)), dma((4,)),
            ]
            if z_arrays
            else []
        ),
        compiler_params=pltpu.CompilerParams(
            dimension_semantics=("arbitrary",), vmem_limit_bytes=52 * 1024 * 1024,
            collective_id=4, has_side_effects=True,
        ),
        cost_estimate=estimate(90),
        name="behind",
    )(
        projected, projected, cols, cols, halo_v, halo_b, info, marks, delta, cum, ssd, mixed_grad,
        sloc, pfx, entry, aloc, sfx, later, chan, bcpar, head, expand,
        gate_grad, weight, tok, inv, gain, edge_mask, out_next, *z_arrays,
    )


def peers(t):
    return t + 1 - 2 * lax.rem(t, 2), lax.rem(t + 2, 4)


def pick(w_ref, one, other):
    size = w_ref.shape[0] // 4
    at = lambda k: pl.ds(pl.multiple_of(k * size, size), size)
    return jnp.concatenate([w_ref[at(one), :], w_ref[at(other), :]], axis=0)


def shares_of(side, t):
    near = peers(t)
    return (t, near[1 - side]), (near[side], 3 - t)


def out_kernel(
    ssd, gate, sums, chan, w_ref, scaled, own, mid, send_a, send_b,
):
    i, half = pl.program_id(0), pl.num_programs(0) // 2
    t = lax.axis_index("tensor")
    width = ssd.shape[1]
    for k in range(ssd.shape[0] // L):
        rows = slice(k * L, (k + 1) * L)
        inv = jnp.broadcast_to(lax.rsqrt(sums[k, 0:1, :] / INNER + EPS), (LANE, L)).T
        for sl in tiles(width):
            g = gate[rows, sl]
            gated = ssd[rows, sl] * g * sigmoid(g)
            scaled[rows, sl] = (gated * inv * chan[KERNEL + 1 : KERNEL + 2, sl]).astype(BF16)
    x = scaled[...]
    size = own.shape[1]

    def part(side, send):
        keep, go = shares_of(side, t)
        send[...] = dot(x, pick(w_ref, *go), 1, 1).astype(BF16)
        kept = dot(x, pick(w_ref, *keep), 1, 1)
        own[...] = kept[:, :size]
        mid[...] = kept[:, size:]

    @pl.when(i < half)
    def _():
        part(0, send_a)

    @pl.when(i >= half)
    def _():
        part(1, send_b)


def run_out(ssd, projected, sums, chan, weight):
    steps, width = ssd.shape
    block = 512
    count = steps // block
    half = count // 2
    size = D // 4
    in_block = lambda w, col=0: pl.BlockSpec((block, w), lambda i: (i, col))
    return pl.pallas_call(
        out_kernel,
        grid=(count,),
        in_specs=[
            in_block(width), in_block(width, 0),
            pl.BlockSpec((block // L, 8, L), lambda i: (i, 0, 0)),
            once(KERNEL + 2, width), once(*weight.shape),
        ],
        out_specs=[
            in_block(width), in_block(size), in_block(size),
            pl.BlockSpec((block, 2 * size), lambda i: (jnp.minimum(i, half - 1), 0)),
            pl.BlockSpec((block, 2 * size), lambda i: (jnp.maximum(i - half, 0), 0)),
        ],
        out_shape=[
            shape(steps, width, dtype=BF16), shape(steps, size), shape(steps, size),
            shape(steps // 2, 2 * size, dtype=BF16), shape(steps // 2, 2 * size, dtype=BF16),
        ],
        compiler_params=params(),
        cost_estimate=estimate(12),
        name="out",
    )(ssd, projected, sums, chan, weight)


def line_kernel(
    n, n_tensor, piece, zx_raw, cols_raw, zx_out, cols_out, zx_ref, cols_ref,
    local, zx_s, zx_r, core_s, core_r, col_s, col_r, group_s, group_r, bulk_s, bulk_r,
):
    s, c, t = lax.axis_index("shard"), lax.axis_index("context"), lax.axis_index("tensor")
    on = (c < n - 1, c > 0)
    to = ((s, jnp.minimum(c + 1, n - 1), t), (s, jnp.maximum(c - 1, 0), t))
    to_core = (1 - s, c, t)
    to_group = [(s, c, lax.rem(t + k, n_tensor)) for k in range(1, n_tensor)]
    beside = [(s, lax.rem(c + k, n), t) for k in (1, n - 1)]
    barrier = greet([to_core] + to_group + beside)
    width = zx_raw.shape[2]
    for k in (0, 1):
        zx_ref[:, k * width : (k + 1) * width] = zx_raw[:, k, :].astype(BF16)
    cols_ref[...] = cols_raw[...].T.astype(BF16)
    pl.semaphore_wait(barrier, n_tensor + 2)
    rows, width = zx_ref.shape[0], cols_ref.shape[1]
    spans = [(at, min(piece, rows - at)) for at in range(0, rows, piece)]

    def block_of(way, hop):
        return jnp.maximum(c - hop, 0) if way == 0 else jnp.minimum(c + hop, n - 1)

    def has(way, hop):
        return c - hop >= 0 if way == 0 else c + hop <= n - 1

    def place(ref, block, at=0, size=rows):
        return ref.at[pl.ds(pl.multiple_of((s * n + block) * rows + at, 16), size), :]

    lanes = pl.ds(pl.multiple_of(t * width, LANE), width)

    def place_cols(block):
        return cols_out.at[pl.ds(pl.multiple_of((s * n + block) * rows, 16), rows), lanes]

    def zx_copy(way, step, p):
        at, size = spans[p]
        where = place(zx_out, block_of(way, step), at, size)
        src = zx_ref.at[pl.ds(at, size), :] if step == 0 else where
        return remote(src, where, zx_s.at[way, step, p], zx_r.at[way, step, p], to[way])

    def col_copy(way, step):
        where = place_cols(block_of(way, step))
        src = cols_ref if step == 0 else where
        return remote(src, where, col_s.at[way, step], col_r.at[way, step], to[way])

    def group_copies(way, hop):
        where = place_cols(block_of(way, hop))
        src = cols_ref if hop == 0 else where
        return [
            remote(src, where, group_s.at[k, way, hop], group_r.at[k, way, hop], target)
            for k, target in enumerate(to_group)
        ]

    def core_copy(way, hop, p):
        at, size = spans[p]
        where = place(zx_out, block_of(way, hop), at, size)
        src = zx_ref.at[pl.ds(at, size), :] if hop == 0 else where
        return remote(src, where, core_s.at[way, hop, p], core_r.at[way, hop, p], to_core)

    pieces = range(len(spans))
    for way in (0, 1):

        @pl.when(on[way])
        def _():
            col_copy(way, 0).start()
            for p in pieces:
                zx_copy(way, 0, p).start()

    for copy in group_copies(0, 0):
        copy.start()
    own_cols = pltpu.make_async_copy(cols_ref, place_cols(c), local.at[0])
    own_zx = pltpu.make_async_copy(zx_ref, place(zx_out, c), local.at[1])
    own_cols.start()
    own_zx.start()
    for p in pieces:
        core_copy(0, 0, p).start()
    start = pl.ds(pl.multiple_of(s * n * rows, 16), n * rows)
    bulk = remote(cols_out.at[start, :], cols_out.at[start, :], bulk_s, bulk_r, to_core)
    for step in range(n - 1):
        further = step < n - 2
        for way in (0, 1):

            @pl.when(has(way, step + 1))
            def _():
                col_copy(way, step).wait_recv()
                for copy in group_copies(way, step + 1):
                    copy.start()
                if further:

                    @pl.when(on[way])
                    def _():
                        col_copy(way, step + 1).start()

        if not further:
            own_cols.wait()
            for copy in group_copies(0, 0):
                copy.wait()
            for hop in range(1, n):
                for way in (0, 1):

                    @pl.when(has(way, hop))
                    def _():
                        for copy in group_copies(way, hop):
                            copy.wait()

            bulk.start()
        for p in pieces:
            for way in (0, 1):

                @pl.when(has(way, step + 1))
                def _():
                    zx_copy(way, step, p).wait_recv()
                    core_copy(way, step + 1, p).start()
                    if further:

                        @pl.when(on[way])
                        def _():
                            zx_copy(way, step + 1, p).start()

    for step in range(n - 1):
        for way in (0, 1):

            @pl.when(jnp.logical_and(on[way], has(way, step)))
            def _():
                col_copy(way, step).wait_send()
                for p in pieces:
                    zx_copy(way, step, p).wait_send()

            @pl.when(has(way, step + 1))
            def _():
                for p in pieces:
                    core_copy(way, step + 1, p).wait()

    for p in pieces:
        core_copy(0, 0, p).wait()
    bulk.wait()
    own_zx.wait()


PIECE = 64


def line_gather(zx, cols):
    n, n_tensor = lax.axis_size("context"), lax.axis_size("tensor")
    rows, width = zx.shape[0], 2 * zx.shape[2]
    pieces = -(-rows // PIECE)
    dma = pltpu.SemaphoreType.DMA
    return pl.pallas_call(
        functools.partial(line_kernel, n, n_tensor, PIECE),
        in_specs=[pl.BlockSpec(memory_space=pltpu.VMEM)] * 2,
        out_specs=[pl.BlockSpec(memory_space=pl.ANY)] * 2,
        out_shape=[
            shape(2 * n * rows, width, dtype=BF16),
            shape(2 * n * rows, n_tensor * LANE, dtype=BF16),
        ],
        scratch_shapes=[
            pltpu.VMEM((rows, width), BF16), pltpu.VMEM((rows, LANE), BF16),
            dma((2,)), dma((2, n - 1, pieces)), dma((2, n - 1, pieces)),
            dma((2, n, pieces)), dma((2, n, pieces)), dma((2, n - 1)), dma((2, n - 1)),
            dma((n_tensor - 1, 2, n)), dma((n_tensor - 1, 2, n)), dma, dma,
        ],
        compiler_params=pltpu.CompilerParams(collective_id=0, has_side_effects=True),
        name="line_gather",
    )(zx, cols)


SLICES = 8


class Chain:
    def __init__(self, n, backward, packed, entering, got, sent, send_sem, recv_sem):
        s, c, t = lax.axis_index("shard"), lax.axis_index("context"), lax.axis_index("tensor")
        self.from_other = c < n - 1 if backward else c > 0
        self.to_other = c > 0 if backward else c < n - 1
        ahead = jnp.maximum(c - 1, 0) if backward else jnp.minimum(c + 1, n - 1)
        self.target = (s, ahead, t)
        self.refs = packed, entering, got, sent, send_sem, recv_sem

    def copy(self, j):
        _, _, got, sent, send_sem, recv_sem = self.refs
        rows = pl.ds(j * (N // SLICES), N // SLICES)
        return remote(sent.at[rows, :], got.at[rows, :], send_sem.at[j], recv_sem.at[j], self.target)

    def begin(self):
        packed, entering, _, sent, _, _ = self.refs

        @pl.when(jnp.logical_not(self.from_other))
        def _():
            entering[...] = jnp.zeros_like(entering)

            @pl.when(self.to_other)
            def _():
                sent[...] = packed[:N, :]
                for j in range(SLICES):
                    self.copy(j).start()

    def step(self, j):
        packed, entering, got, sent, _, _ = self.refs
        rows = slice(j * (N // SLICES), (j + 1) * (N // SLICES))

        @pl.when(self.from_other)
        def _():
            self.copy(j).wait_recv()
            entering[rows, :] = got[rows, :]

            @pl.when(self.to_other)
            def _():
                sent[rows, :] = packed[rows, :] + packed[N : N + 1, :] * entering[rows, :]
                self.copy(j).start()

    def finish(self):
        @pl.when(self.to_other)
        def _():
            for j in range(SLICES):
                self.copy(j).wait_send()


def beside_of(n):
    s, c, t = lax.axis_index("shard"), lax.axis_index("context"), lax.axis_index("tensor")
    return [(s, lax.rem(c + k, n), t) for k in (1, n - 1)]


def entry_kernel(
    n, packed, back, w_hbm, entry, out, bk, w_ref, buf, got, sent, load_sem, out_sem, chain_s, chain_r
):
    block = buf.shape[1]
    count = back.shape[0] // block
    load_w = pltpu.make_async_copy(w_hbm, w_ref, load_sem.at[count])
    load_w.start()

    def load(k):
        rows = pl.ds(k * block, block)
        return pltpu.make_async_copy(back.at[rows, :], bk.at[rows, :], load_sem.at[k])

    def store(k):
        return pltpu.make_async_copy(
            buf.at[k % 2], out.at[pl.ds(k * block, block), :], out_sem.at[k % 2]
        )

    for k in range(count):
        load(k).start()
    pl.semaphore_wait(greet(beside_of(n)), 2)
    chain = Chain(n, False, packed, entry, got, sent, chain_s, chain_r)
    chain.begin()
    load_w.wait()
    for k in range(count):
        load(k).wait()
        if k >= 2:
            store(k - 2).wait()
        buf[k % 2] = dot(bk[k * block : (k + 1) * block, :], w_ref[...])
        store(k).start()
        if k < SLICES:
            chain.step(k)
    for k in range(count, SLICES):
        chain.step(k)
    chain.finish()
    for k in range(max(count - 2, 0), count):
        store(k).wait()


def run_entry(packed, back, weight):
    n = lax.axis_size("context")
    steps, width = back.shape[0], weight.shape[1]
    block = 256
    dma = pltpu.SemaphoreType.DMA
    vmem = pltpu.VMEM
    inside = pl.BlockSpec(memory_space=pltpu.VMEM)
    hbm = pl.BlockSpec(memory_space=pl.ANY)
    return pl.pallas_call(
        functools.partial(entry_kernel, n),
        in_specs=[inside, hbm, hbm],
        out_specs=[inside, hbm],
        out_shape=[shape(N, width), shape(steps, width)],
        scratch_shapes=[
            vmem(back.shape, BF16), vmem(weight.shape, BF16), vmem((2, block, width), F32),
            vmem((N, width), F32), vmem((N, width), F32),
            dma((steps // block + 1,)), dma((2,)), dma((SLICES,)), dma((SLICES,)),
        ],
        compiler_params=pltpu.CompilerParams(
            vmem_limit_bytes=58 * 1024 * 1024, collective_id=6, has_side_effects=True
        ),
        cost_estimate=estimate(15),
        name="entry",
    )(packed, back, weight)


def middle_kernel(
    n, packed, send_a, send_b, mid_hbm, own_hbm, normed_hbm, gate_hbm, back_hbm, scaled_hbm, *refs
):
    if n == 4:
        later, own, next_out, z_out, z_mid, z_mine = refs[:6]
        refs = refs[6:]
    else:
        later, own, next_out, both_out = refs[:4]
        refs = refs[4:]
    (
        mid, nm, gg, bk, sc, peer_part, core_part, own_part, got, chain_got, chain_sent,
        local, core_s, core_r, f_s, f_r, chain_s, chain_r,
    ) = refs
    s, c, t = lax.axis_index("shard"), lax.axis_index("context"), lax.axis_index("tensor")
    near = peers(t)
    to = [(s, c, near[0]), (s, c, near[1])]
    to_core = (1 - s, c, t)
    loads = [
        pltpu.make_async_copy(src, dst, local.at[k])
        for k, (src, dst) in enumerate(
            [
                (normed_hbm, nm), (gate_hbm, gg), (back_hbm, bk), (scaled_hbm, sc),
                (mid_hbm, mid), (own_hbm, own),
            ]
        )
    ]
    for load in loads:
        load.start()
    pl.semaphore_wait(greet(to + [to_core] + beside_of(n)), 5)
    hops = [
        remote(src, got.at[side], f_s.at[side], f_r.at[side], to[side])
        for side, src in enumerate((send_a, send_b))
    ]
    for hop in hops:
        hop.start()
    chain = Chain(n, True, packed, later, chain_got, chain_sent, chain_s, chain_r)
    half_d = nm.shape[1] // 2
    steps = nm.shape[0]
    step = 256
    pairs = ((nm, gg), (bk, sc))

    def product(which, shard, into, m):
        left, right = pairs[which]
        lanes = pl.ds(pl.multiple_of(shard * half_d + m * step, step), step)
        into[which, m * step : (m + 1) * step, :] = over_rows(left, lanes, lambda rows: right[rows, :])

    cores = [
        remote(peer_part.at[k], core_part.at[k], core_s.at[k], core_r.at[k], to_core) for k in (0, 1)
    ]
    chain.begin()
    chain.step(0)
    done = 1
    for which in (0, 1):
        loads[2 * which].wait()
        loads[2 * which + 1].wait()
        for m in range(half_d // step):
            product(which, 1 - s, peer_part, m)
            if done < SLICES:
                chain.step(done)
                done += 1
        cores[which].start()
    for which in (0, 1):
        for m in range(half_d // step):
            product(which, s, own_part, m)
            if done < SLICES:
                chain.step(done)
                done += 1
    chain.finish()
    block = half_d // n

    for which in (0, 1):
        cores[which].wait()
        if n == 4:
            first = c + 1 - 2 * lax.rem(c, 2) if which == 0 else 3 - c
            third = 3 - c if which == 0 else c + 1 - 2 * lax.rem(c, 2)

            def total(k):
                rows = pl.ds(pl.multiple_of(k * block, 8), block)
                return own_part[which, rows, :] + core_part[which, rows, :]

            z_out[which, :block, :] = total(first).astype(BF16)
            z_out[which, block:, :] = total(lax.rem(c + 2, 4)).astype(BF16)
            z_mid[which] = total(third)
            z_mine[which] = total(c)
        else:
            both_out[which] = own_part[which] + core_part[which]
    loads[4].wait()
    loads[5].wait()
    size = mid.shape[1]
    half = steps // 2
    for side in (0, 1):
        hops[side].wait()
        for k in range(half // step):
            rows = slice(k * step, (k + 1) * step)
            at = slice(side * half + k * step, side * half + (k + 1) * step)
            next_out[side, rows, :] = (mid[at, :] + got[side, rows, size:].astype(F32)).astype(BF16)
            own[at, :] += got[side, rows, :size].astype(F32)


def run_middle(packed, fan, normed, gate_grad, back, scaled):
    n = lax.axis_size("context")
    own, mid, send_a, send_b = fan
    steps, width = gate_grad.shape
    size = own.shape[1]
    half_d = D // 2
    block = half_d // n
    dma = pltpu.SemaphoreType.DMA
    vmem = pltpu.VMEM
    inside = pl.BlockSpec(memory_space=pltpu.VMEM)
    hbm = pl.BlockSpec(memory_space=pl.ANY)
    if n == 4:
        more = [
            shape(2, 2 * block, width, dtype=BF16), shape(2, block, width), shape(2, block, width)
        ]
    else:
        more = [shape(2, half_d, width)]
    pair = (2, half_d, width)
    return pl.pallas_call(
        functools.partial(middle_kernel, n),
        in_specs=[inside] + [hbm] * 8,
        out_specs=[inside] * (3 + len(more)),
        out_shape=[shape(N, width), shape(steps, size), shape(2, steps // 2, size, dtype=BF16)] + more,
        scratch_shapes=[
            vmem((steps, size), F32), vmem(normed.shape, BF16), vmem(gate_grad.shape, BF16),
            vmem(back.shape, BF16), vmem(scaled.shape, BF16),
            vmem(pair, F32), vmem(pair, F32), vmem(pair, F32), vmem((2, steps // 2, 2 * size), BF16),
            vmem((N, width), F32), vmem((N, width), F32),
            dma((6,)), dma((2,)), dma((2,)), dma((2,)), dma((2,)), dma((SLICES,)), dma((SLICES,)),
        ],
        compiler_params=pltpu.CompilerParams(
            vmem_limit_bytes=54 * 1024 * 1024, collective_id=7, has_side_effects=True
        ),
        cost_estimate=estimate(35),
        name="middle",
    )(packed, send_a, send_b, mid, own, normed, gate_grad, back, scaled)


def adam_kernel(
    heads, cols_loc, gate_g, value_g, down_g, cols_g, packed, packed_gain, resid, own, last, *refs
):
    zx, out, bcdt, gain, chan, bc, head = [refs[3 * k : 3 * k + 3] for k in range(7)]
    refs = refs[21:]
    zx_new, out_new, bcdt_new, gain_new, chan_new, bc_new, head_new = [
        refs[3 * k : 3 * k + 3] for k in range(7)
    ]
    width = gate_g.shape[1]
    block_out = refs[21]
    half = own.shape[0] // 2
    for side in (0, 1):
        for k in range(0, half, GROUP):
            rows = slice(side * half + k, side * half + k + GROUP)
            total = own[rows, :] + last[side, k : k + GROUP, :].astype(F32)
            block_out[rows, :] = (resid[rows, :].astype(F32) + total).astype(BF16)

    def put(news, olds, grad, rate, decay, at=(Ellipsis,)):
        for ref, val in zip(news, adamw(olds[0][at], grad, olds[1][at], olds[2][at], rate, decay)):
            ref[at] = val

    for k, grad in enumerate((gate_g, value_g)):
        put(zx_new, zx, grad[...], RATE_MATRIX, DECAY, (slice(None), k, slice(None)))
    put(out_new, out, down_g[...], RATE_MATRIX, DECAY)
    put(bcdt_new, bcdt, cols_g[...].T[:cols_loc, :], RATE_MATRIX, DECAY)
    over = packed[0] + packed[1] + packed[2] + packed[3]
    gains = packed_gain[0] + packed_gain[1] + packed_gain[2] + packed_gain[3]
    put(gain_new, gain, gains[: D // LANE, :], RATE_SMALL, 0.0)
    put(bc_new, bc, over[: KERNEL + 1, width : width + 2 * N], RATE_SMALL, 0.0)
    grad = jnp.concatenate([packed[k, : KERNEL + 2, :width] for k in range(4)], axis=1)
    put(chan_new, chan, grad, RATE_SMALL, 0.0)
    lane = lax.broadcasted_iota(jnp.int32, (LANE, 4 * heads), 0)
    slot = lax.broadcasted_iota(jnp.int32, (LANE, 4 * heads), 1)
    channel = lax.broadcasted_iota(jnp.int32, (width, 4 * heads), 0)
    wide_slot = lax.broadcasted_iota(jnp.int32, (width, 4 * heads), 1)
    rows = jnp.zeros((8, 4 * heads), F32)
    for k in range(4):
        here = jnp.where(lane + k * heads == slot, 1.0, 0.0)
        here = jnp.where(lane < heads, here, 0.0).astype(BF16)
        wide = jnp.where(channel // P_SIZE + k * heads == wide_slot, 1.0, 0.0).astype(BF16)
        hi, lo = two(packed[k, KERNEL + 3 : KERNEL + 11, :LANE])
        at = lax.broadcasted_iota(jnp.int32, rows.shape, 0)
        rows = rows + jnp.where(at < 2, dot(hi, here) + dot(lo, here), 0.0)
        hi, lo = two(packed[k, KERNEL + 2 : KERNEL + 10, :width])
        skip = dot(hi, wide) + dot(lo, wide)
        rows = rows + jnp.where(at == 2, jnp.broadcast_to(skip[0:1, :], rows.shape), 0.0)
    put(head_new, head, rows[:3, :], RATE_SMALL, 0.0)


def run_adam(grads, olds, heads, cols_loc):
    flat = [x for group in olds for x in group]
    return pl.pallas_call(
        functools.partial(adam_kernel, heads, cols_loc),
        in_specs=[pl.BlockSpec(memory_space=pltpu.VMEM)] * (len(grads) + len(flat)),
        out_specs=[pl.BlockSpec(memory_space=pltpu.VMEM)] * (len(flat) + 1),
        out_shape=[shape(*x.shape) for x in flat] + [shape(*grads[7].shape, dtype=BF16)],
        compiler_params=pltpu.CompilerParams(vmem_limit_bytes=40 * 1024 * 1024),
        cost_estimate=estimate(8),
        name="optimizer",
    )(*grads, *flat)


def doc_of(lengths, position):
    found = jnp.zeros(position.shape, F32)
    end = 0
    for k in range(lengths.shape[1] - 1):
        end = end + lengths[0, k]
        found = found + jnp.where(position >= end, 1.0, 0.0)
    return jnp.where(position < 0, -1.0, found)


def mark_chunk(lengths, begin, limit, info_ref, marks_ref):
    row = lax.broadcasted_iota(jnp.int32, (L, LANE), 0)
    lane = lax.broadcasted_iota(jnp.int32, (L, LANE), 1)
    offset = jnp.where(lane < KERNEL - 1, lane - KERNEL + 1, jnp.where(lane >= 8, lane - 7, 0))
    other = jnp.where(lane == 3, -1, jnp.where(lane == 4, L - 1, row + offset)) + begin
    mark = doc_of(lengths, row + begin)
    same = jnp.logical_and(doc_of(lengths, other) == mark, other < limit)
    info = jnp.where(same, 1.0, 0.0)
    info_ref[...] = jnp.where(lane == 5, mark, jnp.where(lane < 7 + KERNEL, info, 0.0))
    marks_ref[0] = doc_of(lengths, begin + lax.broadcasted_iota(jnp.int32, (8, L), 1))


def norm_rows(tok, gain):
    x = tok.astype(F32)
    square = x * x
    total = square[:, :LANE]
    for sl in tiles(D)[1:]:
        total = total + square[:, sl]
    inv = lax.rsqrt(jnp.sum(total, axis=1, keepdims=True) / D + EPS)
    return (x * inv * gain[0:1, :]).astype(BF16), inv


def project_kernel(
    heads, n, cols_loc, lengths, tok, tok_end, gain, w_ref, wg_ref, chan, bcpar, head, e_ref,
    normed, inv, projected, cols, info, marks, edge_mask, act, delta, cum, sloc, pfx, fin,
    halo_v, halo_b, ext_v, ext_b, state, prod, w_cols, prev_v, prev_b, halo_out, halo_got, h_s, h_r,
):
    i = pl.program_id(0)
    s, c, t = lax.axis_index("shard"), lax.axis_index("context"), lax.axis_index("tensor")
    width = w_ref.shape[1] // 2
    block = tok.shape[0]
    steps = block * pl.num_programs(0)
    start = c * steps
    after = (s, jnp.minimum(c + 1, n - 1), t)
    halo = remote(halo_out, halo_got, h_s, h_r, after)

    @pl.when(i == 0)
    def _():
        pl.semaphore_wait(greet(beside_of(n)), 2)
        state[...] = jnp.zeros_like(state)
        prod[...] = jnp.ones_like(prod)
        lane = lax.broadcasted_iota(jnp.int32, (4 * LANE, 3 * N), 0)
        want = lax.broadcasted_iota(jnp.int32, (4 * LANE, 3 * N), 1)
        have = lane // LANE * cols_loc + lane % LANE
        want = jnp.where(want < 2 * N, want, jnp.where(want < 2 * N + heads, want + heads * t, -1))
        chosen = jnp.logical_and(have == want, lane % LANE < cols_loc)
        select = jnp.where(chosen, 1.0, 0.0).astype(BF16)
        for k in range(0, D, block):
            w_cols[k : k + block, :] = dot(wg_ref[k : k + block, :], select).astype(BF16)
        ends, _ = norm_rows(tok_end[...], gain)
        halo_out[:, :width] = dot(ends, w_ref[:, width:])[8:, :]
        halo_out[:, width:] = dot(ends, w_cols[...])[8:, :]

        @pl.when(c < n - 1)
        def _():
            halo.start()

        row = lax.broadcasted_iota(jnp.int32, (24, LANE), 0)
        shift, at = row // 8 + 1, row % 8
        there = at - 8 + shift + start + steps
        agree = doc_of(lengths, there) == doc_of(lengths, there - shift)
        edge_mask[...] = jnp.where(jnp.logical_and(at >= 8 - shift, agree), 1.0, 0.0)

    for j in range(block // L):
        rows = slice(j * L, (j + 1) * L)
        x, scale = norm_rows(tok[rows, :], gain)
        normed[rows, :] = x
        inv[rows, :] = scale
    for k in range(0, 2 * width, 512):
        projected[:, k : k + 512] = dot(normed[...], w_ref[:, k : k + 512])
    cols[...] = dot(normed[...], w_cols[...])

    @pl.when(i == 0)
    def _():
        @pl.when(c > 0)
        def _():
            halo.wait_recv()
            halo_v[...] = halo_got[:, :width]
            halo_b[...] = halo_got[:, width:]

        @pl.when(c == 0)
        def _():
            halo_v[...] = jnp.zeros_like(halo_v)
            halo_b[...] = jnp.zeros_like(halo_b)

        @pl.when(c < n - 1)
        def _():
            halo.wait_send()

    val = projected.at[:, pl.ds(width, width)]

    for j in range(block // L):
        first = i == 0
        mark_chunk(
            lengths, start + i * block + j * L, start + steps, rows_at(info, j), lead_at(marks, j)
        )
        load_ext(ext_v, val, prev_v, halo_v, j, first)
        load_ext(ext_b, cols, prev_b, halo_b, j, first)
        prep_chunk(
            rows_at(cols, j), rows_at(info, j), chan, bcpar, head, e_ref, rows_at(act, j),
            rows_at(delta, j), rows_at(cum, j), lead_at(sloc, j), lead_at(pfx, j),
            ext_v, ext_b, state, prod,
        )
    prev_v[...] = projected[block - 8 :, width:]
    prev_b[...] = cols[block - 8 :, :]

    @pl.when(i == pl.num_programs(0) - 1)
    def _():
        fin[:N, :] = state[...]
        fin[N:, :] = prod[...]


def run_project(lengths, tok, gain, weight, w_group, chan, bcpar, head, expand, heads, cols_loc):
    steps, width = tok.shape[0], weight.shape[1] // 2
    count = steps // L
    dma = pltpu.SemaphoreType.DMA
    return pl.pallas_call(
        functools.partial(project_kernel, heads, lax.axis_size("context"), cols_loc),
        grid=(steps // GROUP,),
        in_specs=[
            pl.BlockSpec(memory_space=pltpu.SMEM), row_block(D),
            pl.BlockSpec((16, D), lambda i: (steps // 16 - 1, 0), pipeline_mode=pl.Buffered(1)),
            once(8, D), once(*weight.shape), once(*w_group.shape),
            once(KERNEL + 2, width), once(KERNEL + 1, 2 * N), once(8, LANE), once(2 * LANE, width),
        ],
        out_specs=[
            row_block(D), row_block(1),
            row_block(2 * width), row_block(3 * N), row_block(LANE), lead_block(8, L), once(24, LANE),
            row_block(width + 2 * N), row_block(LANE), row_block(LANE), lead_block(N, width),
            lead_block(8, width), once(N + 8, width), once(8, width), once(8, 3 * N),
        ],
        out_shape=[
            shape(steps, D, dtype=BF16), shape(steps, 1),
            shape(steps, 2 * width), shape(steps, 3 * N), shape(steps, LANE), shape(count, 8, L),
            shape(24, LANE),
            shape(steps, width + 2 * N), shape(steps, LANE), shape(steps, LANE),
            shape(count, N, width), shape(count, 8, width), shape(N + 8, width), shape(8, width),
            shape(8, 3 * N),
        ],
        scratch_shapes=[
            pltpu.VMEM((8 + L, width), F32), pltpu.VMEM((8 + L, 3 * N), F32),
            pltpu.VMEM((N, width), F32), pltpu.VMEM((8, width), F32),
            pltpu.VMEM((D, 3 * N), BF16), pltpu.VMEM((8, width), F32), pltpu.VMEM((8, 3 * N), F32),
            pltpu.VMEM((8, width + 3 * N), F32), pltpu.VMEM((8, width + 3 * N), F32), dma, dma,
        ],
        compiler_params=pltpu.CompilerParams(
            dimension_semantics=("arbitrary",), vmem_limit_bytes=58 * 1024 * 1024,
            collective_id=8, has_side_effects=True,
        ),
        cost_estimate=estimate(45),
        name="project",
    )(lengths, tok, tok, gain, weight, w_group, chan, bcpar, head, expand)


class AllSum:
    def __init__(self, n, refs, sems):
        s, c, t = lax.axis_index("shard"), lax.axis_index("context"), lax.axis_index("tensor")
        self.n, self.c, self.t = n, c, t
        self.mine, self.other, self.pair, self.pieces, self.total, self.every = refs
        core_s, core_r, piece_s, piece_r, group_s, group_r = sems
        self.core = remote(self.mine, self.other, core_s, core_r, (1 - s, c, t))
        self.along = [
            remote(self.pair, self.pieces.at[c], piece_s.at[k], piece_r.at[k], (s, lax.rem(c + k + 1, n), t))
            for k in range(n - 1)
        ]
        self.across = [
            remote(self.total, self.every.at[t], group_s.at[k], group_r.at[k], (s, c, lax.rem(t + k + 1, 4)))
            for k in range(3)
        ]

    def start(self):
        self.core.start()

    def after_core(self):
        self.core.wait()
        self.pair[...] = self.mine[...] + self.other[...]
        self.pieces[self.c] = self.pair[...]
        for copy in self.along:
            copy.start()

    def after_pieces(self):
        for copy in self.along:
            copy.wait()
        self.total[...] = sum(self.pieces[k] for k in range(1, self.n)) + self.pieces[0]
        self.every[self.t] = self.total[...]
        for copy in self.across:
            copy.start()

    def finish(self):
        for copy in self.across:
            copy.wait()


PACK = 16


def tail_kernel(
    n, grad_b, grad_v, normed_hbm, w_hbm, tok_hbm, back_hbm, late_hbm, wg_hbm,
    raw_t, fixed, gate_top, gate_end, tok_top, tok_end, inv, gain, sel_bc, sel_raw,
    late_rows, late_gain, taps_grad, bias_grad, norm_gain_grad, skip_grad, head_grad,
    tokens_out, value_out, cols_out, pack_out, gain_out,
    gb, gv, nm, w_ref, tok, back, w_cols, col_grad,
    peer_part, own_part, core_part, b_got, b_next, b_last, b_full, raw_full,
    early, mid, send, got, nxt, last, gain_grad, z_out, z_got, z_on, z_last,
    ng, col_peer, col_own, col_core, col_out, col_got, col_on, col_last,
    row_buf, row_held, *refs,
):
    tail_body(
        n, grad_b, grad_v, normed_hbm, w_hbm, tok_hbm, back_hbm, late_hbm, wg_hbm,
        raw_t, fixed, gate_top, gate_end, tok_top, tok_end, inv, gain, sel_bc, sel_raw,
        late_rows, late_gain, taps_grad, bias_grad, norm_gain_grad, skip_grad, head_grad,
        tokens_out, value_out, cols_out, pack_out, gain_out,
        gb, gv, nm, w_ref, tok, back, w_cols, col_grad,
        peer_part, own_part, core_part, b_got, b_next, b_last, b_full, raw_full,
        early, mid, send, got, nxt, last, gain_grad, z_out, z_got, z_on, z_last,
        ng, col_peer, col_own, col_core, col_out, col_got, col_on, col_last,
        row_buf, row_held, refs[:6], refs[6:12], *refs[12:25], refs[25:31], refs[31:37],
    )


def tail_body(
    n, grad_b, grad_v, normed_hbm, w_hbm, tok_hbm, back_hbm, late_hbm, wg_hbm,
    raw_t, fixed, gate_top, gate_end, tok_top, tok_end, inv, gain, sel_bc, sel_raw,
    late_rows, late_gain, taps_grad, bias_grad, norm_gain_grad, skip_grad, head_grad,
    tokens_out, value_out, cols_out, pack_out, gain_out,
    gb, gv, nm, w_ref, tok, back, w_cols, col_grad,
    peer_part, own_part, core_part, b_got, b_next, b_last, b_full, raw_full,
    early, mid, send, got, nxt, last, gain_grad, z_out, z_got, z_on, z_last,
    ng, col_peer, col_own, col_core, col_out, col_got, col_on, col_last,
    row_buf, row_held, pack_refs, gain_refs,
    local, raw_s, raw_r, b_s, b_r, f_s, f_r, core_s, core_r, z_s, z_r, row_s, row_r,
    pack_sems, gain_sems,
):
    s, c, t = lax.axis_index("shard"), lax.axis_index("context"), lax.axis_index("tensor")
    near = peers(t)
    to = [(s, c, near[0]), (s, c, near[1])]
    group = [(s, c, lax.rem(t + k, 4)) for k in (1, 2, 3)]
    to_core = (1 - s, c, t)
    to_piece = [(s, lax.rem(c + k, n), t) for k in range(1, n)]
    in_line = n == 4
    line = [(s, c + 1 - 2 * lax.rem(c, 2), t), (s, 3 - c, t)] if in_line else []
    steps, width = grad_v.shape
    size = w_ref.shape[0] // 4
    share = steps // 4
    mine_lanes = pl.ds(pl.multiple_of(t * size, size), size)
    loads = [
        pltpu.make_async_copy(src, dst, local.at[k])
        for k, (src, dst) in enumerate(
            [
                (grad_b, gb), (grad_v, gv), (normed_hbm, nm), (w_hbm, w_ref),
                (tok_hbm.at[:, mine_lanes], tok), (back_hbm.at[:, mine_lanes], back),
                (late_hbm, ng.at[pl.ds(GROUP, steps - GROUP), :]),
                (wg_hbm.at[mine_lanes, :], w_cols),
            ]
        )
    ]
    for load in loads[:2]:
        load.start()
    pl.semaphore_wait(greet(group + [to_core] + to_piece), n + 3)

    raw_full[t] = raw_t[...]
    raws = [
        remote(raw_t, raw_full.at[t], raw_s.at[k], raw_r.at[k], target)
        for k, target in enumerate(group)
    ]
    for copy in raws:
        copy.start()

    def rows_of(k):
        return pl.ds(pl.multiple_of(k * share, share), share)

    def lanes_of(side):
        return pl.ds(side * N, N)

    loads[0].wait()
    for load in loads[2:]:
        load.start()
    gb[steps - 8 :, :] = fixed[:, width:]

    def b_first(side, part):
        k = near[side] if part == 0 else 3 - t
        return remote(
            gb.at[rows_of(k), lanes_of(side)], b_got.at[side, part], b_s.at[side, part],
            b_r.at[side, part], to[side],
        )

    def b_second(side):
        return remote(
            b_next.at[side], b_last.at[side], b_s.at[side, 2], b_r.at[side, 2], to[1 - side]
        )

    def b_back(side, part):
        k = near[1 - side] if part == 2 else t
        where = b_full.at[rows_of(k), lanes_of(side)]
        return remote(
            where, where, b_s.at[side, 3 + part], b_r.at[side, 3 + part],
            to[1 - side] if part == 0 else to[side],
        )

    for side in (0, 1):
        for part in (0, 1):
            b_first(side, part).start()

    pack = pack_refs[0]
    pack[...] = jnp.zeros_like(pack)
    gain_refs[0][...] = jnp.zeros_like(gain_refs[0])
    total = width + 2 * N
    add_up = lambda x: jnp.sum(x, axis=0, keepdims=True)
    for k in range(KERNEL):
        pack[k : k + 1, :total] = add_up(taps_grad[8 * k : 8 * k + 8, :])
    pack[KERNEL : KERNEL + 1, :total] = add_up(bias_grad[...])
    pack[KERNEL + 1 : KERNEL + 2, :width] = add_up(norm_gain_grad[...])
    pack[KERNEL + 2 : KERNEL + 3, :width] = add_up(skip_grad[...])
    pack[KERNEL + 3 : KERNEL + 4, :LANE] = add_up(head_grad[:8, :])
    pack[KERNEL + 4 : KERNEL + 5, :LANE] = add_up(head_grad[8:, :])
    pack_sum = AllSum(n, pack_refs, pack_sems)
    gain_sum = AllSum(n, gain_refs, gain_sems)
    pack_sum.start()

    loads[1].wait()
    tail = gv[steps - 16 :, :].astype(F32)
    gv[steps - 16 :, :] = jnp.concatenate([tail[:8], fixed[:, :width]], axis=0).astype(BF16)
    loads[2].wait()
    half_d = nm.shape[1] // 2
    step = 256

    def product(shard, right, into):
        for m in range(half_d // step):
            lanes = pl.ds(pl.multiple_of(shard * half_d + m * step, step), step)
            into[m * step : (m + 1) * step, :] = over_rows(nm, lanes, right)

    product(1 - s, lambda rows: gv[rows, :], peer_part)
    core = remote(peer_part, core_part, core_s.at[0], core_r.at[0], to_core)
    core.start()

    for side in (0, 1):
        for part in (0, 1):
            b_first(side, part).wait()
        b_next[side] = gb[rows_of(near[1 - side]), lanes_of(side)] + b_got[side, 1]
        b_second(side).start()
    pack_sum.after_core()

    product(s, lambda rows: gv[rows, :], own_part)

    for side in (0, 1):
        b_second(side).wait()
        mine = gb[rows_of(t), lanes_of(side)] + b_got[side, 0] + b_last[side]
        b_full[rows_of(t), lanes_of(side)] = mine.astype(BF16)
        b_back(side, 0).start()

    block = half_d // n
    side_w = width // 2
    both = own_part
    if in_line:
        first = [c + 1 - 2 * lax.rem(c, 2), 3 - c]
        across = lax.rem(c + 2, 4)

    def block_rows(k):
        return pl.ds(pl.multiple_of(k * block, 8), block)

    def z_block(k, side):
        return both[block_rows(k), side * side_w : (side + 1) * side_w]

    def z_first(side):
        return remote(z_out.at[side], z_got.at[side], z_s.at[side], z_r.at[side], line[side])

    def z_second(side):
        return remote(z_on.at[side], z_last.at[side], z_s.at[2 + side], z_r.at[2 + side], line[1 - side])

    def col_first():
        return remote(col_out, col_got, z_s.at[4], z_r.at[4], line[0])

    def col_second():
        return remote(col_on, col_last, z_s.at[5], z_r.at[5], line[1])

    core.wait()
    both[...] = both[...] + core_part[...]
    if in_line:
        for side in (0, 1):
            z_out[side, :block, :] = z_block(first[side], side).astype(BF16)
            z_out[side, block:, :] = z_block(across, side).astype(BF16)
            z_first(side).start()
    for side in (0, 1):
        b_back(side, 0).wait()
        for part in (1, 2):
            b_back(side, part).start()

    loads[3].wait()
    pack_sum.after_pieces()
    half = GROUP // 2
    tail_half = END // 2

    def f_first(side):
        return remote(send.at[side], got.at[side], f_s.at[side], f_r.at[side], to[side])

    def f_second(side):
        return remote(
            nxt.at[side], last.at[side], f_s.at[2 + side], f_r.at[2 + side], to[1 - side]
        )

    gain_grad[...] = late_gain[...]
    for g in range(GROUP // PART, steps // PART):
        row_buf[:, g * PART : (g + 1) * PART] = late_rows[g]
    ends = [jnp.zeros((LANE - END, LANE), F32)]
    for side in (0, 1):
        rows = slice(side * half, (side + 1) * half)
        tail_rows = slice(side * tail_half, (side + 1) * tail_half)
        end_rows = slice(steps - END + side * tail_half, steps - END + (side + 1) * tail_half)
        x = jnp.concatenate(
            [
                jnp.concatenate([gate_top[rows, :], gv[rows, :]], axis=1),
                jnp.concatenate([gate_end[tail_rows, :], gv[end_rows, :]], axis=1),
            ],
            axis=0,
        )
        keep, go = shares_of(side, t)
        gone = dot(x, pick(w_ref, *go), 1, 1)
        send[side] = gone.astype(BF16)
        f_first(side).start()
        kept = dot(x, pick(w_ref, *keep), 1, 1)
        early[side] = kept[:, :size]
        mid[side] = kept[:, size:]
        scale = jnp.concatenate([inv[rows, :], inv[end_rows, :]], axis=0)
        parts = [kept[:, :size], kept[:, size:], gone[:, :size], gone[:, size:]]

        def z(lanes):
            values = jnp.concatenate([tok_top[rows, lanes], tok_end[tail_rows, lanes]], axis=0)
            return values.astype(F32) * scale

        sums = count_rows(parts, z, gain, keep + go, gain_grad)
        row_buf[:, rows] = row_dots(sums[:half])
        ends.append(sums[half:])
    row_buf[:, steps - LANE :] += row_dots(jnp.concatenate(ends, axis=0))

    for copy in raws:
        copy.wait()
    for side in (0, 1):
        for part in (1, 2):
            b_back(side, part).wait()
    raw_all = jnp.concatenate([raw_full[k] for k in range(4)], axis=0)

    for k in range(steps // GROUP):
        rows = slice(k * GROUP, (k + 1) * GROUP)
        chosen = dot(b_full[rows, :], sel_bc[...]) + dot(raw_all[:, rows], sel_raw[...], 0, 0)
        col_grad[rows, :] = chosen.astype(BF16)
    own_lanes = pl.ds(pl.multiple_of(t * LANE, LANE), LANE)
    product(1 - s, lambda rows: col_grad[rows, own_lanes], col_peer)
    col_core_copy = remote(col_peer, col_core, core_s.at[1], core_r.at[1], to_core)
    col_core_copy.start()
    gain_mine = gain[0:1, mine_lanes]
    loads[4].wait()
    loads[6].wait()
    loads[7].wait()
    ng[steps - END :, :] = jnp.zeros((END, size), F32)
    for k in range(steps // GROUP):
        rows = slice(k * GROUP, (k + 1) * GROUP)
        part = dot(col_grad[rows, :], w_cols[...], 1, 1)
        ng[rows, :] = part if k == 0 else ng[rows, :] + part
        part = part * (tok[rows, :].astype(F32) * inv[rows, :])
        gain_grad[:, mine_lanes] += fold(part)
        part = part * gain_mine
        sums = part[:, :LANE]
        for sl in tiles(size)[1:]:
            sums = sums + part[:, sl]
        row_buf[:, rows] += row_dots(sums)
    row_copies = [
        remote(row_buf, row_held.at[k], row_s.at[k], row_r.at[k], target)
        for k, target in enumerate(group)
    ]
    for copy in row_copies:
        copy.start()

    for k in range(D // LANE):
        gain_refs[0][k : k + 1, :] = add_up(gain_grad[:, k * LANE : (k + 1) * LANE])
    gain_sum.start()

    for side in (0, 1):
        f_first(side).wait()
        nxt[side] = (mid[side] + got[side, :, size:].astype(F32)).astype(BF16)
        f_second(side).start()
        early[side] += got[side, :, :size].astype(F32)

    product(s, lambda rows: col_grad[rows, own_lanes], col_own)

    gain_sum.after_core()
    if in_line:
        for side in (0, 1):
            z_first(side).wait()
            z_on[side] = (
                z_block(first[1 - side], side) + z_got[side, block:, :].astype(F32)
            ).astype(BF16)
            z_second(side).start()
    col_core_copy.wait()
    col_own[...] = col_own[...] + col_core[...]
    if in_line:
        col_out[:block, :] = col_own[block_rows(first[0]), :]
        col_out[block:, :] = col_own[block_rows(across), :]
        col_first().start()

    gain_sum.after_pieces()
    if in_line:
        col_first().wait()
        col_on[...] = col_own[block_rows(first[1]), :] + col_got[block:, :]
        col_second().start()

    loads[5].wait()
    for copy in row_copies:
        copy.wait()
    for side in (0, 1):
        f_second(side).wait()
        early[side] += last[side].astype(F32)
        at = steps - END + side * tail_half
        ng[at : at + tail_half, :] += early[side, half:, :]
        ng[side * half : (side + 1) * half, :] += early[side, :half, :]
    row_total = row_buf[...] + row_held[0] + row_held[1] + row_held[2]
    for k in range(steps // LANE):
        rows = slice(k * LANE, (k + 1) * LANE)
        row_dot = jnp.broadcast_to(row_total[0:1, rows] * (1.0 / D), (LANE, LANE)).T
        scale = inv[rows, :]
        for sl in tiles(size):
            z_tile = tok[rows, sl].astype(F32) * scale
            change = scale * (ng[rows, sl] * gain_mine[:, sl] - z_tile * row_dot)
            tokens_out[rows, sl] = (back[rows, sl].astype(F32) + change).astype(BF16)

    if in_line:
        for side in (0, 1):
            z_second(side).wait()
            value_out[:, side * side_w : (side + 1) * side_w] = (
                z_block(c, side) + z_got[side, :block, :].astype(F32) + z_last[side].astype(F32)
            )
        col_second().wait()
        cols_out[...] = col_own[block_rows(c), :] + col_got[:block, :] + col_last[...]
    else:
        value_out[...] = both[...]
        cols_out[...] = col_own[...]
    pack_sum.finish()
    pack_out[...] = pack_refs[5][...]
    gain_sum.finish()
    gain_out[...] = gain_refs[5][...]


def run_tail(
    grad_b, grad_v, normed, weight, tok, back, late, w_group, raw_t, fixed, gate_grad, inv, gain,
    sel_bc, sel_raw, late_rows, late_gain, *small,
):
    n = lax.axis_size("context")
    steps, width = grad_v.shape
    size = D // 4
    half_d = D // 2
    block = half_d // n
    side_rows = (GROUP + END) // 2
    share = steps // 4
    top = lambda w: pl.BlockSpec((GROUP, w), lambda i: (0, 0), pipeline_mode=pl.Buffered(1))
    end = lambda w: pl.BlockSpec(
        (END, w), lambda i: (steps // END - 1, 0), pipeline_mode=pl.Buffered(1)
    )
    full = lambda x: once(*x.shape)
    hbm = pl.BlockSpec(memory_space=pl.ANY)
    dma = pltpu.SemaphoreType.DMA
    vmem = pltpu.VMEM
    value_rows = block if n == 4 else half_d
    pair = (2, side_rows, size)
    packed = (PACK, width + 2 * N)
    return pl.pallas_call(
        functools.partial(tail_kernel, n),
        grid=(1,),
        in_specs=[hbm] * 8
        + [full(raw_t), full(fixed), top(width), end(width), top(D), end(D)]
        + [full(x) for x in (inv, gain, sel_bc, sel_raw)]
        + [full(x) for x in (late_rows, late_gain, *small)],
        out_specs=[
            once(steps, size), once(value_rows, width), once(value_rows, LANE), once(4, *packed),
            once(4, 16, LANE),
        ],
        out_shape=[
            shape(steps, size, dtype=BF16), shape(value_rows, width), shape(value_rows, LANE),
            shape(4, *packed), shape(4, 16, LANE),
        ],
        scratch_shapes=[
            vmem((steps, 2 * N), F32), vmem((steps, width), BF16), vmem(normed.shape, BF16),
            vmem(weight.shape, BF16), vmem((steps, size), BF16), vmem((steps, size), BF16),
            vmem((size, w_group.shape[1]), BF16),
            vmem((steps, w_group.shape[1]), BF16),
            vmem((half_d, width), F32), vmem((half_d, width), F32), vmem((half_d, width), F32),
            vmem((2, 2, share, N), F32), vmem((2, share, N), F32), vmem((2, share, N), F32),
            vmem((steps, 2 * N), BF16), vmem((4, 16, steps), BF16),
            vmem(pair, F32), vmem(pair, F32), vmem((2, side_rows, 2 * size), BF16),
            vmem((2, side_rows, 2 * size), BF16), vmem(pair, BF16), vmem(pair, BF16), vmem((8, D), F32),
            vmem((2, 2 * block, width // 2), BF16), vmem((2, 2 * block, width // 2), BF16),
            vmem((2, block, width // 2), BF16), vmem((2, block, width // 2), BF16),
            vmem((steps, size), F32),
            vmem((half_d, LANE), F32), vmem((half_d, LANE), F32), vmem((half_d, LANE), F32),
            vmem((2 * block, LANE), F32), vmem((2 * block, LANE), F32), vmem((block, LANE), F32),
            vmem((block, LANE), F32),
            vmem((8, steps), F32), vmem((3, 8, steps), F32),
            *[
                vmem((*lead, *dims), F32)
                for dims in (packed, (16, LANE))
                for lead in ((), (), (), (n,), (), (4,))
            ],
            dma((8,)), dma((3,)), dma((3,)), dma((2, 6)), dma((2, 6)), dma((4,)), dma((4,)),
            dma((2,)), dma((2,)), dma((6,)), dma((6,)), dma((3,)), dma((3,)),
            *[dma, dma, dma((n - 1,)), dma((n - 1,)), dma((3,)), dma((3,))] * 2,
        ],
        compiler_params=pltpu.CompilerParams(
            dimension_semantics=("arbitrary",), vmem_limit_bytes=56 * 1024 * 1024,
            collective_id=5, has_side_effects=True,
        ),
        cost_estimate=estimate(50),
        name="tail",
    )(
        grad_b, grad_v, normed, weight, tok, back, late, w_group,
        raw_t, fixed, gate_grad, gate_grad, tok, tok, inv, gain, sel_bc, sel_raw,
        late_rows, late_gain, *small,
    )


def pad_rows(x, rows=8):
    return jnp.concatenate([x, jnp.zeros((rows - x.shape[0], x.shape[1]), x.dtype)], axis=0)


def pad_cols(x, cols=LANE):
    return jnp.concatenate([x, jnp.zeros((x.shape[0], cols - x.shape[1]), x.dtype)], axis=1)


def on_device(
    tokens, cotangent, doc_lengths, zx_weight, bcdt_weight, out_weight, input_gain, chan_params,
    bc_params, head_params, zx_first, bcdt_first, out_first, gain_first, chan_first, bc_first,
    head_first, zx_second, bcdt_second, out_second, gain_second, chan_second, bc_second, head_second,
):
    n_tensor = lax.axis_size("tensor")
    t_index = lax.axis_index("tensor")
    c_index = lax.axis_index("context")
    tok = tokens[0]
    resid = tok.astype(F32)
    back = cotangent[0]
    steps = resid.shape[0]
    inner_loc = INNER // n_tensor
    heads_loc = H // n_tensor
    share = D // n_tensor
    count = steps // L
    rows_loc = zx_weight.shape[0]
    cols_loc = bcdt_weight.shape[1]

    cols_t = jnp.pad(bcdt_weight.T, ((0, LANE - cols_loc), (0, 0)))
    proj_w, cols_z = line_gather(zx_weight, cols_t)
    down_block, _ = lax.optimization_barrier((out_weight.astype(BF16).T, proj_w))
    down_t = lax.all_gather(down_block, ("shard", "context"), axis=0, tiled=True)
    chan_loc = lax.dynamic_slice_in_dim(chan_params, t_index * inner_loc, inner_loc, 1)
    head_loc = lax.dynamic_slice_in_dim(head_params, t_index * heads_loc, heads_loc, 1)
    chan8, bc8 = chan_loc, bc_params
    head8 = pad_rows(pad_cols(head_loc))
    spread_at = np.arange(2 * LANE)[:, None] % LANE == np.arange(inner_loc)[None, :] // P_SIZE
    expand = spread_at.astype(ml_dtypes.bfloat16)
    gain8 = jnp.broadcast_to(input_gain[None], (8, D))
    (
        normed, inv_rms, projected, cols, info, marks_rows, edge_mask,
        act, delta, cum, sloc, pfx, final, halo_v, halo_b,
    ) = run_project(
        doc_lengths, tok, gain8, proj_w, cols_z, chan8, bc8, head8, expand, heads_loc, cols_loc
    )
    entry, back_scaled = run_entry(final, back, down_t)
    ssd, sums = run_ahead(
        act, delta, cum, info, marks_rows, sloc, pfx, entry, projected, back_scaled, chan8, head8,
        expand, heads_loc,
    )
    scaled, *out_fan = run_out(ssd, projected, sums, chan8, down_t)
    gate_grad, mixed_grad, aloc, sfx, first_adj, norm_gain_grad = run_norm(
        ssd, projected, back_scaled, sums, act, cum, info, chan8, expand, heads_loc
    )
    later, out_own, out_next, *z_arrays = run_middle(
        first_adj, out_fan, normed, gate_grad, back, scaled
    )
    resid_share = lax.dynamic_slice_in_dim(tok, t_index * share, share, 1)
    in_line = lax.axis_size("context") == 4
    total_width = inner_loc + 2 * N

    (
        grad_v, grad_b, raw_t, last_rows, _, taps_grad, bias_grad, skip_grad, head_grad,
        ng_late, late_rows, late_gain, out_last, *z_sum,
    ) = run_grand(
        projected, cols, halo_v, halo_b, info, marks_rows, delta, cum, ssd, mixed_grad,
        sloc, pfx, entry, aloc, sfx, later, chan8, bc8, head8, expand, heads_loc,
        gate_grad, proj_w, tok, inv_rms, gain8, edge_mask, out_next, z_arrays if in_line else [],
    )
    if in_line:
        gate_g, down_g = z_sum[0][0], z_sum[0][1]
    else:
        gate_g, down_g = [
            lax.psum_scatter(z_arrays[0][k], "context", scatter_dimension=0, tiled=True) for k in (0, 1)
        ]
    column = np.arange(4 * LANE)
    column = np.where(column % LANE < cols_loc, column // LANE * cols_loc + column % LANE, -1)[None, :]
    sel_bc = (np.arange(2 * N)[:, None] == column).astype(ml_dtypes.bfloat16)
    slot = np.arange(4 * 16)[:, None]
    of_slot = np.where(slot % 16 < heads_loc, 2 * N + slot // 16 * heads_loc + slot % 16, -2)
    sel_raw = (of_slot == column).astype(ml_dtypes.bfloat16)
    tokens_grad, value_g, cols_g, packed, packed_gain = run_tail(
        grad_b, grad_v, normed, proj_w, tok, back, ng_late, cols_z, raw_t, last_rows, gate_grad,
        inv_rms, gain8, sel_bc, sel_raw, late_rows, late_gain,
        taps_grad, bias_grad, norm_gain_grad, skip_grad, head_grad,
    )
    tokens_grad = tokens_grad[None]
    if not in_line:
        value_g = lax.psum_scatter(value_g, "context", scatter_dimension=0, tiled=True)
        cols_g = lax.psum_scatter(cols_g[:, :cols_loc], "context", scatter_dimension=0, tiled=True)
        cols_g = pad_cols(cols_g)
    flip = lambda *arrays: tuple(a.T for a in arrays)
    lift = lambda *arrays: tuple(a.reshape(D // LANE, LANE) for a in arrays)
    news = run_adam(
        (gate_g, value_g, down_g, cols_g, packed, packed_gain, resid_share, out_own, out_last),
        (
            (zx_weight, zx_first, zx_second), flip(out_weight, out_first, out_second),
            flip(bcdt_weight, bcdt_first, bcdt_second), lift(input_gain, gain_first, gain_second),
            (chan_params, chan_first, chan_second), (bc_params, bc_first, bc_second),
            (head_params, head_first, head_second),
        ),
        heads_loc, cols_loc,
    )
    zx_new, out_new, bcdt_new, gain_new = news[:3], flip(*news[3:6]), flip(*news[6:9]), news[9:12]
    block_out = news[21][None]
    return (
        block_out, tokens_grad, *zx_new, *bcdt_new, *out_new, *[g.reshape(D) for g in gain_new], *news[12:21]
    )


def solution(mesh):
    big = P(("shard", "context"), None, "tensor")
    cols = P(("shard", "context"), "tensor")
    down = P("tensor", ("shard", "context"))
    rows = P("shard", "context", None)
    out_rows = P("shard", "context", "tensor")
    return jax.shard_map(
        on_device,
        mesh=mesh,
        in_specs=(
            rows, rows, P("shard", None), big, cols, down, P(), P(), P(), P(),
            big, cols, down, P(), P(), P(), P(),
            big, cols, down, P(), P(), P(), P(),
        ),
        out_specs=(
            out_rows, out_rows, big, big, big, cols, cols, cols, down, down, down,
            *([P()] * 12),
        ),
        check_vma=False,
    )
```

```python
import functools

import jax
import jax.numpy as jnp
import ml_dtypes
import numpy as np
from jax import lax
from jax.experimental import pallas as pl
from jax.experimental.pallas import tpu as pltpu
from jax.sharding import PartitionSpec as P

D = 1536
INNER = 3072
H = 48
P_SIZE = 64
N = 128
KERNEL = 4
STEP = 10

EPS = 1e-05
BETA_ONE = 0.9
BETA_TWO = 0.999
ADAM_EPS = 1e-08
DECAY = 0.1
RATE_MATRIX = 0.05
RATE_SMALL = 0.2

L = 128
LANE = 128
GROUP = 4 * L
PART = 2 * L
END = 32
LOG2E = 1.4426950408889634
F32 = jnp.float32
BF16 = jnp.bfloat16
VMEM_LIMIT = 58 * 1024 * 1024


def from_behind(block, axis, distance):
    devices = range(lax.axis_size(axis))
    route = [(i - distance, i) for i in devices if i - distance in devices]
    return lax.ppermute(block, axis, route)


def adamw(weight, grad, first, second, rate, decay):
    first_new = BETA_ONE * first + (1.0 - BETA_ONE) * grad
    second_new = BETA_TWO * second + (1.0 - BETA_TWO) * grad * grad
    scale_one = 1.0 - BETA_ONE**STEP
    scale_two = 1.0 - BETA_TWO**STEP
    update = first_new / scale_one / (jnp.sqrt(second_new / scale_two) + ADAM_EPS)
    return (weight - rate * (update + decay * weight), first_new, second_new)


def two(x):
    hi = x.astype(BF16)
    return hi, (x - hi.astype(F32)).astype(BF16)


def dot(a, b, ca=1, cb=0):
    return lax.dot_general(a, b, (((ca,), (cb,)), ((), ())), preferred_element_type=F32)


def dot3(a, b, ca=1, cb=0):
    ah, al = two(a)
    bh, bl = two(b)
    return dot(
        jnp.concatenate([ah, al, ah], axis=ca), jnp.concatenate([bh, bh, bl], axis=cb), ca, cb
    )


def over_rows(left, lanes, right):
    total = None
    for at in range(0, left.shape[0], GROUP):
        rows = slice(at, at + GROUP)
        part = dot(left[rows, lanes], right(rows), 0, 0)
        total = part if total is None else total + part
    return total


def tri_sum(tri, x):
    hi = x.astype(BF16)
    rest = x - hi.astype(F32)
    mid = rest.astype(BF16)
    low = (rest - mid.astype(F32)).astype(BF16)
    out = dot(tri, jnp.concatenate([hi, mid, low], axis=1))
    w = x.shape[1]
    return out[:, :w] + out[:, w : 2 * w] + out[:, 2 * w :]


def spread(x, e_ref):
    hi, lo = two(x)
    return dot(jnp.concatenate([hi, lo], axis=1), e_ref[...])


def per_head(x, e_ref):
    hi, lo = two(x)
    e = e_ref[:LANE, :]
    return dot(hi, e, 1, 1) + dot(lo, e, 1, 1)


def sigmoid(x):
    return 1.0 / (1.0 + jnp.exp(-x))


def softplus(x):
    return jnp.maximum(x, 0.0) + jnp.log1p(jnp.exp(-jnp.abs(x)))


def tiles(width):
    return [slice(k, k + LANE) for k in range(0, width, LANE)]


def fold(x):
    return jnp.sum(x.reshape(x.shape[0] // 8, 8, x.shape[1]), axis=0)


def lower_mask():
    row = lax.broadcasted_iota(jnp.int32, (L, L), 0)
    col = lax.broadcasted_iota(jnp.int32, (L, L), 1)
    return row >= col


def keep_mask(info, marks_row):
    return jnp.logical_and(lower_mask(), info[:, 5:6] == marks_row[0:1, :])


def decay_of(keep, cum, cum_t, h):
    return jnp.exp2(jnp.where(keep, cum[:, h : h + 1] - cum_t[h : h + 1, :], -1e30))


def load_ext(ext_ref, cur_ref, prev_ref, halo_ref, j, first):
    if j > 0:
        ext_ref[0:8, :] = cur_ref[j * L - 8 : j * L, :]
    else:

        @pl.when(first)
        def _():
            ext_ref[0:8, :] = halo_ref[...]

        @pl.when(jnp.logical_not(first))
        def _():
            ext_ref[0:8, :] = prev_ref[...]

    ext_ref[8 : 8 + L, :] = cur_ref[j * L : (j + 1) * L, :]


def rows_of_chunk(ref, j):
    return ref.at[pl.ds(pl.multiple_of(j * L, L), L), :]


def lead_of_chunk(ref, j):
    return ref.at[pl.ds(j, 1)]


def load_ext_of(ext_ref, cur_ref, prev_ref, halo_ref, j, first):
    @pl.when(first)
    def _():
        ext_ref[0:8, :] = halo_ref[...]

    @pl.when(jnp.logical_and(j == 0, jnp.logical_not(first)))
    def _():
        ext_ref[0:8, :] = prev_ref[...]

    @pl.when(j > 0)
    def _():
        ext_ref[0:8, :] = cur_ref[pl.ds(pl.multiple_of(jnp.maximum(j * L - 8, 0), 8), 8), :]

    ext_ref[8 : 8 + L, :] = cur_ref[pl.ds(pl.multiple_of(j * L, L), L), :]


def rows_at(ref, j):
    return ref.at[j * L : (j + 1) * L, :]


def lead_at(ref, j):
    return ref.at[j : j + 1]


def conv_tile(ext_ref, info, taps, sl):
    shifted = []
    total = jnp.broadcast_to(taps[KERNEL : KERNEL + 1, :], (L, LANE))
    for k in range(KERNEL):
        val = ext_ref[pl.ds(8 - KERNEL + 1 + k, L), sl]
        if k < KERNEL - 1:
            val = val * info[:, k : k + 1]
        shifted.append(val)
        total = total + taps[k : k + 1, :] * val
    return shifted, total


def prep_chunk(
    bc, info_ref, chan, bcpar, head, e_ref, act, delta_ref, cum_ref, sloc, pfx, ext_v, ext_b, state, prod
):
    info = info_ref[...]
    width = ext_v.shape[1]
    for sl in tiles(width):
        _, total = conv_tile(ext_v, info, chan[:, sl], sl)
        act[:, sl] = total * sigmoid(total)
    for sl in tiles(2 * N):
        _, total = conv_tile(ext_b, info, bcpar[:, sl], sl)
        act[:, slice(width + sl.start, width + sl.stop)] = total * sigmoid(total)
    raw = bc[:, 2 * N : 3 * N]
    delta = softplus(raw + head[0:1, :])
    dlog = -delta * (jnp.exp(head[1:2, :]) * LOG2E)
    tri = jnp.where(lower_mask(), 1.0, 0.0).astype(BF16)
    cum = tri_sum(tri, dlog)
    delta_ref[...] = delta
    cum_ref[...] = cum
    sloc[0] = state[...]
    pfx[0] = prod[...]
    last = cum[L - 1 : L, :]
    tail = info[:, 4:5] * jnp.exp2(last - cum) * delta
    through = spread(
        jnp.broadcast_to(info[L - 1 : L, 3:4] * jnp.exp2(last), (8, LANE)), e_ref
    )
    weights = spread(tail, e_ref)
    tail_u = act[:, :width] * weights
    fresh = dot3(act[:, width : width + N], tail_u, 0, 0)
    state[...] = state[...] * through[0:1, :] + fresh
    prod[...] = prod[...] * through


def row_block(width, col=0, rows=GROUP):
    return pl.BlockSpec((rows, width), lambda i: (i, col))


def prev_block(width, col=0, rows=GROUP):
    return pl.BlockSpec((8, width), lambda i: (jnp.maximum(i * (rows // 8) - 1, 0), col))


def lead_block(*dims, rows=GROUP):
    return pl.BlockSpec((rows // L, *dims), lambda i: (i, 0, 0))


def whole(*shape):
    return pl.BlockSpec(shape, lambda i: (0,) * len(shape))


def once(*shape):
    return pl.BlockSpec(shape, lambda i: (0,) * len(shape), pipeline_mode=pl.Buffered(1))


def estimate(us):
    return pl.CostEstimate(flops=int(us * 1.1e9), bytes_accessed=int(us * 1e6), transcendentals=0)


def params(**kw):
    return pltpu.CompilerParams(
        dimension_semantics=("arbitrary",), vmem_limit_bytes=VMEM_LIMIT, **kw
    )


def shape(*dims, dtype=F32):
    return jax.ShapeDtypeStruct(dims, dtype)


def ahead_kernel(
    heads, act, delta, cum, info, marks, sloc, pfx, entry, gate, back, chan, head, e_ref, ssd, sums,
    mine, held, send, recv,
):
    i = pl.program_id(0)
    s, c, t = lax.axis_index("shard"), lax.axis_index("context"), lax.axis_index("tensor")
    group = [(s, c, lax.rem(t + k, 4)) for k in (1, 2, 3)]

    @pl.when(i == 0)
    def _():
        pl.semaphore_wait(greet(group), 3)

    chunks = act.shape[0] // L
    for j in range(act.shape[0] // L):
        ahead_chunk(
            rows_at(act, j), rows_at(delta, j), rows_at(cum, j), rows_at(info, j), lead_at(marks, j),
            lead_at(sloc, j), lead_at(pfx, j), entry, rows_at(gate, j), rows_at(back, j), chan, head,
            e_ref, rows_at(ssd, j), mine.at[pl.ds(i * chunks + j, 1)],
        )

    @pl.when(i == pl.num_programs(0) - 1)
    def _():
        copies = [
            remote(mine, held.at[k], send.at[k], recv.at[k], target) for k, target in enumerate(group)
        ]
        for copy in copies:
            copy.start()
        total = mine[...]
        for k, copy in enumerate(copies):
            copy.wait()
            total = total + held[k]
        sums[...] = total


def ahead_chunk(
    act, delta_ref, cum_ref, info_ref, marks_ref, sloc, pfx, entry, gate, back, chan, head, e_ref, ssd, sums
):
    width = act.shape[1] - 2 * N
    info = info_ref[...]
    cum = cum_ref[...]
    cum_t = cum.T
    keep = keep_mask(info, marks_ref[0])
    bmat = act[:, width : width + N]
    cmat = act[:, width + N :]
    scores = dot3(cmat, bmat, 1, 1)
    xs = act[:, :width]
    u_hi, u_lo = two(xs * spread(delta_ref[...], e_ref))
    state = sloc[0] + entry[...] * pfx[0, 0:1, :]
    entering = dot3(cmat, state)
    eexp = spread(info[:, 3:4] * jnp.exp2(cum), e_ref)
    skip = spread(jnp.broadcast_to(head[2:3, :], (8, LANE)), e_ref)
    lane = lax.broadcasted_iota(jnp.int32, (1, LANE), 1)
    left = jnp.where(lane < P_SIZE, 1.0, 0.0).astype(BF16)
    right = jnp.where(lane < P_SIZE, 0.0, 1.0).astype(BF16)
    square = jnp.zeros((L, LANE), F32)
    cross = jnp.zeros((L, LANE), F32)
    for q, sl in enumerate(tiles(width)):
        mix = jnp.concatenate(
            [(scores * decay_of(keep, cum, cum_t, 2 * q + r)).astype(BF16) for r in (0, 1)], axis=1
        )
        both = jnp.concatenate([u_hi[:, sl], u_lo[:, sl]], axis=1)
        rhs = jnp.concatenate(
            [both * jnp.concatenate([m, m], axis=1) for m in (left, right)], axis=0
        )
        out = dot(mix, rhs)
        y = out[:, :LANE] + out[:, LANE:] + entering[:, sl] * eexp[:, sl]
        y = y + skip[0:1, sl] * xs[:, sl]
        ssd[:, sl] = y
        g = gate[:, sl]
        gated = y * g * sigmoid(g)
        square = square + gated * gated
        cross = cross + gated * (back[:, sl] * chan[KERNEL + 1 : KERNEL + 2, sl])
    ones = jnp.ones((8, LANE), BF16)
    rows = []
    for part in (square, cross):
        hi, lo = two(part)
        rows.append(dot(ones, hi, 1, 1) + dot(ones, lo, 1, 1))
    pick = lax.broadcasted_iota(jnp.int32, (8, LANE), 0)
    sums[0] = jnp.where(pick == 0, rows[0], jnp.where(pick == 1, rows[1], 0.0))


def run_ahead(act, delta, cum, info, marks, sloc, pfx, entry, projected, back, chan, head, expand, heads):
    steps, width = projected.shape[0], projected.shape[1] // 2
    count = steps // L
    return pl.pallas_call(
        functools.partial(ahead_kernel, heads),
        grid=(steps // GROUP,),
        in_specs=[
            row_block(width + 2 * N), row_block(LANE), row_block(LANE), row_block(LANE),
            lead_block(8, L), lead_block(N, width), lead_block(8, width),
            once(N, width), row_block(width, 0), row_block(width),
            once(KERNEL + 2, width), once(8, LANE), once(2 * LANE, width),
        ],
        out_specs=[row_block(width), once(count, 8, L)],
        out_shape=[shape(steps, width), shape(count, 8, L)],
        scratch_shapes=[
            pltpu.VMEM((count, 8, L), F32), pltpu.VMEM((3, count, 8, L), F32),
            pltpu.SemaphoreType.DMA((3,)), pltpu.SemaphoreType.DMA((3,)),
        ],
        compiler_params=params(collective_id=1, has_side_effects=True),
        cost_estimate=estimate(20),
        name="ahead",
    )(act, delta, cum, info, marks, sloc, pfx, entry, projected, back, chan, head, expand)


def norm_kernel(
    heads, ssd, gate, back, sums, cmat, cum, info, chan, e_ref,
    gate_grad, mixed_grad, aloc, sfx, fin, gain_grad, state, prod,
):
    i = pl.program_id(0)

    @pl.when(i == 0)
    def _():
        state[...] = jnp.zeros_like(state)
        prod[...] = jnp.ones_like(prod)
        gain_grad[...] = jnp.zeros_like(gain_grad)

    chunks = ssd.shape[0] // L

    for j in reversed(range(chunks)):
        norm_chunk(
            rows_at(ssd, j), rows_at(gate, j), rows_at(back, j), lead_at(sums, j), rows_at(cmat, j),
            rows_at(cum, j), rows_at(info, j), chan, e_ref, rows_at(gate_grad, j),
            rows_at(mixed_grad, j), lead_at(aloc, j), lead_at(sfx, j), gain_grad, state, prod,
        )

    @pl.when(i == pl.num_programs(0) - 1)
    def _():
        fin[:N, :] = state[...]
        fin[N:, :] = prod[...]


def norm_chunk(
    ssd, gate, back, sums, cmat_ref, cum_ref, info_ref, chan, e_ref,
    gate_grad, mixed_grad, aloc, sfx, gain_grad, state, prod,
):
    width = ssd.shape[1]
    rows = sums[0]
    inv_row = lax.rsqrt(rows[0:1, :] / INNER + EPS)
    cross_row = inv_row * inv_row * inv_row * (rows[1:2, :] / INNER)
    inv = jnp.broadcast_to(inv_row, (LANE, L)).T
    cross = jnp.broadcast_to(cross_row, (LANE, L)).T
    info = info_ref[...]
    cum = cum_ref[...]
    eexp = spread(info[:, 3:4] * jnp.exp2(cum), e_ref)
    e_mixed = []
    for sl in tiles(width):
        g = gate[:, sl]
        sig = sigmoid(g)
        soft = g * sig
        y = ssd[:, sl]
        gated = y * soft
        bs = back[:, sl]
        gain = chan[KERNEL + 1 : KERNEL + 2, sl]
        normed = gated * inv
        gain_grad[:, sl] += fold(bs * normed)
        gg = inv * (bs * gain) - gated * cross
        mg = gg * soft
        mixed_grad[:, sl] = mg
        gate_grad[:, sl] = (gg * y * sig * (1.0 + g * (1.0 - sig))).astype(BF16)
        e_mixed.append(mg * eexp[:, sl])
    aloc[0] = state[...]
    sfx[0] = prod[...]
    through = spread(
        jnp.broadcast_to(info[L - 1 : L, 3:4] * jnp.exp2(cum[L - 1 : L, :]), (8, LANE)), e_ref
    )
    fresh = dot3(cmat_ref[...], jnp.concatenate(e_mixed, axis=1), 0, 0)
    state[...] = state[...] * through[0:1, :] + fresh
    prod[...] = prod[...] * through


def run_norm(ssd, projected, back, sums, act, cum, info, chan, expand, heads):
    steps, width = ssd.shape
    count = steps // L
    blocks = steps // GROUP
    turn = lambda spec: pl.BlockSpec(
        spec.block_shape, lambda i, m=spec.index_map: m(blocks - 1 - i)
    )
    c_col = width // N + 1
    return pl.pallas_call(
        functools.partial(norm_kernel, heads),
        grid=(blocks,),
        in_specs=[
            turn(row_block(width)), turn(row_block(width, 0)), turn(row_block(width)),
            turn(lead_block(8, L)),
            turn(row_block(N, c_col)), turn(row_block(LANE)), turn(row_block(LANE)),
            once(KERNEL + 2, width), once(2 * LANE, width),
        ],
        out_specs=[
            turn(row_block(width)), turn(row_block(width)),
            turn(lead_block(N, width)),
            turn(lead_block(8, width)),
            whole(N + 8, width), whole(8, width),
        ],
        out_shape=[
            shape(steps, width, dtype=BF16), shape(steps, width),
            shape(count, N, width), shape(count, 8, width), shape(N + 8, width), shape(8, width),
        ],
        scratch_shapes=[pltpu.VMEM((N, width), F32), pltpu.VMEM((8, width), F32)],
        compiler_params=params(),
        cost_estimate=estimate(21),
        name="norm_back",
    )(ssd, projected, back, sums, act, cum, info, chan, expand)


def behind_chunk(
    heads, j, start, first, val, valp, bc, bcp, halo_v, halo_b, info_ref, marks_ref, delta_ref, cum_ref,
    ssd, mixed_grad, sloc, pfx, entry, aloc, sfx, later, chan, bcpar, head, e_ref,
    grad_v, grad_b, raw_grad, tail_rows, head_rows, taps_grad, bias_grad, skip_grad, head_grad,
    ext_v, ext_b, slope, d_tot,
):
    width = val.shape[1]
    total_width = width + 2 * N

    @pl.when(start)
    def _():
        d_tot[0:8, :] = jnp.zeros((8, total_width), F32)
        taps_grad[...] = jnp.zeros_like(taps_grad)
        bias_grad[...] = jnp.zeros_like(bias_grad)
        skip_grad[...] = jnp.zeros_like(skip_grad)
        head_grad[...] = jnp.zeros_like(head_grad)

    d_tot[L:, :] = d_tot[0:8, :]
    load_ext_of(ext_v, val, valp, halo_v, j, first)
    load_ext_of(ext_b, bc, bcp, halo_b, j, first)
    raw = bc[pl.ds(pl.multiple_of(j * L, L), L), 2 * N : 3 * N]
    info_ref, marks_ref = rows_of_chunk(info_ref, j), lead_of_chunk(marks_ref, j)
    delta_ref, cum_ref = rows_of_chunk(delta_ref, j), rows_of_chunk(cum_ref, j)
    ssd, mixed_grad = rows_of_chunk(ssd, j), rows_of_chunk(mixed_grad, j)
    sloc, pfx = lead_of_chunk(sloc, j), lead_of_chunk(pfx, j)
    aloc, sfx = lead_of_chunk(aloc, j), lead_of_chunk(sfx, j)
    grad_v, grad_b = rows_of_chunk(grad_v, j), rows_of_chunk(grad_b, j)
    raw_grad = raw_grad.at[:, pl.ds(pl.multiple_of(j * L, L), L)]
    info = info_ref[...]

    def activate(ext_ref, taps, sl, at):
        _, total = conv_tile(ext_ref, info, taps[:, sl], sl)
        sig = sigmoid(total)
        slope[:, slice(at, at + LANE)] = sig * (1.0 + total * (1.0 - sig))
        return total * sig

    xs = jnp.concatenate([activate(ext_v, chan, sl, sl.start) for sl in tiles(width)], axis=1)
    bmat = activate(ext_b, bcpar, slice(0, N), width)
    cmat = activate(ext_b, bcpar, slice(N, 2 * N), width + N)

    delta = delta_ref[...]
    cum = cum_ref[...]
    cum_t = cum.T
    keep = keep_mask(info, marks_ref[0])
    last = cum[L - 1 : L, :]
    scores = dot3(cmat, bmat, 1, 1)
    dexp = spread(delta, e_ref)
    eexp = spread(info[:, 3:4] * jnp.exp2(cum), e_ref)
    texp = spread(info[:, 4:5] * jnp.exp2(last - cum), e_ref)
    u = xs * dexp
    u_hi, u_lo = two(u)
    dy = mixed_grad[...]
    dy_hi, dy_lo = two(dy)
    skip = spread(jnp.broadcast_to(head[2:3, :], (8, LANE)), e_ref)
    state = sloc[0] + entry[...] * pfx[0, 0:1, :]
    adj = aloc[0] + later[...] * sfx[0, 0:1, :]
    tail_du = dot3(bmat, adj) * texp
    lane = lax.broadcasted_iota(jnp.int32, (1, LANE), 1)
    left = jnp.where(lane < P_SIZE, 1.0, 0.0).astype(BF16)
    right = jnp.where(lane < P_SIZE, 0.0, 1.0).astype(BF16)
    two_left = jnp.concatenate([left, left], axis=1)
    two_right = jnp.concatenate([right, right], axis=1)
    d_scores = jnp.zeros((L, L), F32)
    inner_du = []
    for q, sl in enumerate(tiles(width)):
        decays = [decay_of(keep, cum, cum_t, 2 * q + r) for r in (0, 1)]
        mix = jnp.concatenate([(scores * d).astype(BF16) for d in decays], axis=0)
        dy_both = jnp.concatenate([dy_hi[:, sl], dy_lo[:, sl]], axis=1)
        rhs = jnp.concatenate([dy_both * two_left, dy_both * two_right], axis=0)
        out = dot(mix, rhs, 0, 0)
        inner_du.append(out[:, :LANE] + out[:, LANE:])
        u_twice = jnp.concatenate([u_hi[:, sl], u_hi[:, sl]], axis=1)
        u_rows = jnp.concatenate([u_twice * two_left, u_twice * two_right], axis=0)
        d_mix = dot(dy_both, u_rows, 1, 1)
        d_scores = d_scores + d_mix[:, :L] * decays[0] + d_mix[:, L:] * decays[1]
    du = jnp.concatenate(inner_du, axis=1) + tail_du
    d_xs = dexp * du + skip[0:1, :] * dy
    d_b = dot3(d_scores, cmat, 0, 0) + dot3(u * texp, adj, 1, 1)
    d_c = dot3(d_scores, bmat) + dot3(dy * eexp, state, 1, 1)
    skip_grad[...] += fold(dy * xs)

    direct = per_head(xs * du, e_ref)
    mixed = ssd[...] - skip[0:1, :] * xs
    d_cum = per_head(dy * mixed, e_ref) - delta * direct
    at_last = jnp.sum(per_head(u * tail_du, e_ref), axis=0, keepdims=True)
    through = info[L - 1 : L, 3:4] * jnp.exp2(last)
    pair = per_head(fold(adj * state), e_ref)
    at_last = at_last + through * jnp.sum(pair, axis=0, keepdims=True)
    upper = jnp.where(lower_mask(), 1.0, 0.0).astype(BF16).T
    d_log = tri_sum(upper, d_cum) + at_last
    rate = jnp.exp(head[1:2, :])
    valid = lane < heads
    d_raw = (direct - d_log * rate) * sigmoid(raw + head[0:1, :])
    d_raw = jnp.where(valid, d_raw, 0.0)
    raw_grad[...] = d_raw.T[:16, :].astype(BF16)
    head_grad[0:8, :] += fold(d_raw)
    head_grad[8:16, :] += fold(jnp.where(valid, -d_log * delta * rate, 0.0))

    d_act = [d_xs[:, sl] for sl in tiles(width)] + [d_b, d_c]
    for q in range(total_width // LANE):
        sl = slice(q * LANE, (q + 1) * LANE)
        if q < width // LANE:
            ext_ref, taps, part = ext_v, chan[:, sl], sl
        else:
            part = slice(sl.start - width, sl.stop - width)
            ext_ref, taps = ext_b, bcpar[:, part]
        dt = d_act[q] * slope[:, sl]
        d_tot[0:L, sl] = dt
        bias_grad[:, sl] += fold(dt)
        for k in range(KERNEL):
            moved = ext_ref[pl.ds(8 - KERNEL + 1 + k, L), part]
            if k < KERNEL - 1:
                moved = moved * info[:, k : k + 1]
            taps_grad[8 * k : 8 * k + 8, sl] += fold(dt * moved)
        total = dt * taps[KERNEL - 1 : KERNEL, :]
        for s in range(1, KERNEL):
            total = total + taps[KERNEL - 1 - s : KERNEL - s, :] * (
                d_tot[pl.ds(s, L), sl] * info[:, 7 + s : 8 + s]
            )
        if q < width // LANE:
            grad_v[:, sl] = total.astype(BF16)
        else:
            grad_b[:, part] = total

        @pl.when(start)
        def _():
            tail_rows[:, sl] = total[L - 8 :, :]

    @pl.when(first)
    def _():
        head_rows[...] = d_tot[0:8, :]


def remote(src, dst, send, recv, target):
    return pltpu.make_async_remote_copy(
        src_ref=src, dst_ref=dst, send_sem=send, recv_sem=recv, device_id=target,
        device_id_type=pl.DeviceIdType.MESH,
    )


def greet(targets):
    barrier = pltpu.get_barrier_semaphore()
    for target in targets:
        pl.semaphore_signal(
            barrier, inc=1, device_id=target, device_id_type=pl.DeviceIdType.MESH
        )
    return barrier


def count_rows(parts, z, gain, at, gain_grad):
    rows = jnp.zeros((parts[0].shape[0], LANE), F32)
    size = parts[0].shape[1]
    for part, k in zip(parts, at):
        lanes = pl.ds(pl.multiple_of(k * size, size), size)
        part = part * z(lanes)
        gain_grad[:, lanes] += fold(part)
        part = part * gain[0:1, lanes]
        for sl in tiles(size):
            rows = rows + part[:, sl]
    return rows


def row_dots(rows):
    ones = jnp.ones((8, LANE), BF16)
    hi, lo = two(rows)
    return dot(ones, hi, 1, 1) + dot(ones, lo, 1, 1)


def grand_kernel(heads, n, *refs):
    behind, refs = refs[:22], refs[22:]
    gate_grad, w_ref, tok, inv, gain, edge_mask, out_next = refs[:7]
    refs = refs[7:]
    in_line = n == 4
    if in_line:
        z_out, z_mid, z_mine = refs[:3]
        refs = refs[3:]
    outs, refs = refs[:9], refs[9:]
    ng_own, row_sums, gain_grad, out_last = refs[:4]
    refs = refs[4:]
    if in_line:
        z_sum, refs = refs[0], refs[1:]
    scratch, refs = refs[:4], refs[4:]
    mid, send, got, nxt, last, edge, s1, r1, s2, r2, edge_s, edge_r, o_s, o_r = refs[:14]
    if in_line:
        z_got, z_on, z_last, z_s, z_r = refs[14:]
    chan, bcpar = behind[18], behind[19]
    grad_v, tail_rows = outs[0], outs[3]
    d_tot = scratch[3]
    i, n_steps = pl.program_id(0), pl.num_programs(0)
    s, c, t = lax.axis_index("shard"), lax.axis_index("context"), lax.axis_index("tensor")
    near = peers(t)
    to = [(s, c, near[0]), (s, c, near[1])]
    width = grad_v.shape[1]
    size = w_ref.shape[0] // 4
    inside = mid.shape[0]
    chunks = grad_v.shape[0] // L

    @pl.when(i == 0)
    def _():
        pl.semaphore_wait(greet(to + beside_of(n)), 4)
        gain_grad[...] = jnp.zeros_like(gain_grad)

    def out_hop(side):
        return remote(
            out_next.at[side], out_last.at[side], o_s.at[side], o_r.at[side], to[1 - side]
        )

    @pl.when(i == 0)
    def _():
        for side in (0, 1):
            out_hop(side).start()

    if in_line:
        line = [(s, c + 1 - 2 * lax.rem(c, 2), t), (s, 3 - c, t)]
        block = z_mid.shape[1]

        def z_first(k):
            return remote(z_out.at[k], z_got.at[k], z_s.at[k], z_r.at[k], line[k])

        def z_second(k):
            return remote(z_on.at[k], z_last.at[k], z_s.at[2 + k], z_r.at[2 + k], line[1 - k])

        @pl.when(i == 0)
        def _():
            for k in (0, 1):
                z_first(k).start()

        @pl.when(i == n_steps // 2)
        def _():
            for k in (0, 1):
                z_first(k).wait()
                z_on[k] = (z_mid[k] + z_got[k, block:, :].astype(F32)).astype(BF16)
                z_second(k).start()
                z_sum[k] = z_mine[k] + z_got[k, :block, :].astype(F32)

        @pl.when(i == n_steps - 1)
        def _():
            for k in (0, 1):
                z_second(k).wait()
                z_sum[k] += z_last[k].astype(F32)

    def first_hop(k, side):
        return remote(send.at[k], got.at[k], s1.at[k], r1.at[k], to[side])

    def second_hop(k, side):
        return remote(nxt.at[k], last.at[k], s2.at[k], r2.at[k], to[1 - side])

    def place(k):
        return pl.ds(pl.multiple_of((inside - 1 - k) * PART, PART), PART)

    def turn_over(k, side):
        first_hop(k, side).wait()
        nxt[k] = (mid[k] + got[k, :, size:].astype(F32)).astype(BF16)
        second_hop(k, side).start()
        ng_own[place(k), :] += got[k, :, :size].astype(F32)

    def one(step, carry):
        j = chunks - 1 - step
        behind_chunk(
            heads, j, jnp.logical_and(i == 0, step == 0),
            jnp.logical_and(i == n_steps - 1, j == 0), *behind, *outs, *scratch,
        )
        for side in (0, 1):
            ready = jnp.logical_and(step == 0, lax.rem(i, 2) == 1 - side)

            @pl.when(jnp.logical_and(ready, jnp.logical_and(i >= 2, i < inside + 2)))
            def _():
                turn_over(i - 2, side)

        return carry

    lax.fori_loop(0, chunks, one, 0)

    def fan(side):
        counted = jnp.where(i == 0, PART - END, PART)
        x = jnp.concatenate([gate_grad[...], grad_v[...]], axis=1)
        keep, go = shares_of(side, t)
        gone = dot(x, pick(w_ref, *go), 1, 1)
        send[i] = gone.astype(BF16)
        first_hop(i, side).start()
        kept = dot(x, pick(w_ref, *keep), 1, 1)
        ng_own[place(i), :] = kept[:, :size]
        mid[i] = kept[:, size:]
        row = lax.broadcasted_iota(jnp.int32, (PART, 1), 0)
        scale = jnp.where(row < counted, inv[...], 0.0)
        parts = [kept[:, :size], kept[:, size:], gone[:, :size], gone[:, size:]]
        sums = count_rows(
            parts, lambda lanes: tok[:, lanes].astype(F32) * scale, gain, keep + go, gain_grad
        )
        row_sums[0] = row_dots(sums)

    for side in (0, 1):
        parity = lax.rem(i, 2) == 1 - side

        @pl.when(jnp.logical_and(parity, i < inside))
        def _():
            fan(side)

    @pl.when(i == n_steps - 1)
    def _():
        before = (s, jnp.maximum(c - 1, 0), t)
        copy = remote(d_tot.at[pl.ds(0, 8), :], edge, edge_s, edge_r, before)

        @pl.when(c > 0)
        def _():
            copy.start()

        for k in range(inside):
            second_hop(k, 1 - k % 2).wait()
            ng_own[place(k), :] += last[k].astype(F32)
        for side in (0, 1):
            out_hop(side).wait()

        @pl.when(c < n - 1)
        def _():
            copy.wait_recv()
            for shift in range(1, KERNEL):
                moved = pltpu.roll(edge[...], 8 - shift, 0) * edge_mask[
                    8 * shift - 8 : 8 * shift, 0:1
                ]
                tap = slice(KERNEL - 1 - shift, KERNEL - shift)
                tail_rows[:, :width] += chan[tap, :] * moved[:, :width]
                tail_rows[:, width:] += bcpar[tap, :] * moved[:, width:]

        @pl.when(c > 0)
        def _():
            copy.wait_send()


def run_grand(
    projected, cols, halo_v, halo_b, info, marks, delta, cum, ssd, mixed_grad, sloc, pfx, entry,
    aloc, sfx, later, chan, bcpar, head, expand, heads, gate_grad, weight, tok, inv, gain, edge_mask,
    out_next, z_arrays,
):
    steps, width = ssd.shape
    parts = steps // PART
    inside = (steps - GROUP) // PART
    size = D // 4
    turn = lambda spec: pl.BlockSpec(
        spec.block_shape, lambda i, m=spec.index_map: m(parts - 1 - i)
    )
    in_part = lambda w: pl.BlockSpec((PART, w), lambda i: (parts - 1 - i, 0))
    chunk = lead_block(N, width, rows=PART)
    few = lead_block(8, width, rows=PART)
    total = width + 2 * N
    dma = pltpu.SemaphoreType.DMA
    return pl.pallas_call(
        functools.partial(grand_kernel, heads, lax.axis_size("context")),
        grid=(parts,),
        in_specs=[
            turn(row_block(width, 1, rows=PART)), turn(prev_block(width, 1, rows=PART)),
            turn(row_block(3 * N, rows=PART)), turn(prev_block(3 * N, rows=PART)),
            once(8, width), once(8, 3 * N), turn(row_block(LANE, rows=PART)),
            turn(lead_block(8, L, rows=PART)),
            turn(row_block(LANE, rows=PART)), turn(row_block(LANE, rows=PART)), turn(row_block(width, rows=PART)), turn(row_block(width, rows=PART)),
            turn(chunk), turn(few), once(N, width), turn(chunk), turn(few), once(N, width),
            once(KERNEL + 2, width), once(KERNEL + 1, 2 * N), once(8, LANE), once(2 * LANE, width),
            turn(row_block(width, rows=PART)), once(*weight.shape), in_part(D), in_part(1), once(8, D),
            once(24, LANE), pl.BlockSpec(memory_space=pl.ANY),
        ]
        + ([pl.BlockSpec(memory_space=pl.ANY)] + [once(*z.shape) for z in z_arrays[1:]] if z_arrays else []),
        out_specs=[
            turn(row_block(width, rows=PART)), turn(row_block(2 * N, rows=PART)),
            pl.BlockSpec((16, PART), lambda i: (0, parts - 1 - i)),
            whole(8, total), whole(8, total), whole(8 * KERNEL, total), whole(8, total),
            whole(8, width), whole(16, LANE),
            once(inside * PART, size),
            pl.BlockSpec((1, 8, PART), lambda i: (parts - 1 - i, 0, 0)),
            whole(8, D), pl.BlockSpec(memory_space=pl.ANY),
        ]
        + [once(*z.shape) for z in z_arrays[1:2]],
        out_shape=[
            shape(steps, width, dtype=BF16), shape(steps, 2 * N), shape(16, steps, dtype=BF16),
            shape(8, total), shape(8, total), shape(8 * KERNEL, total), shape(8, total),
            shape(8, width), shape(16, LANE),
            shape(inside * PART, size), shape(parts, 8, PART), shape(8, D),
            shape(*out_next.shape, dtype=BF16),
        ]
        + [shape(*z.shape) for z in z_arrays[1:2]],
        scratch_shapes=[
            pltpu.VMEM((8 + L, width), F32), pltpu.VMEM((8 + L, 3 * N), F32),
            pltpu.VMEM((L, total), F32), pltpu.VMEM((L + 8, total), F32),
            pltpu.VMEM((inside, PART, size), F32),
            pltpu.VMEM((inside, PART, 2 * size), BF16), pltpu.VMEM((inside, PART, 2 * size), BF16),
            pltpu.VMEM((inside, PART, size), BF16), pltpu.VMEM((inside, PART, size), BF16),
            pltpu.VMEM((8, total), F32),
            dma((inside,)), dma((inside,)), dma((inside,)), dma((inside,)), dma, dma,
            dma((2,)), dma((2,)),
        ]
        + (
            [
                pltpu.VMEM(z_arrays[0].shape, BF16), pltpu.VMEM(z_arrays[1].shape, BF16),
                pltpu.VMEM(z_arrays[1].shape, BF16), dma((4,)), dma((4,)),
            ]
            if z_arrays
            else []
        ),
        compiler_params=pltpu.CompilerParams(
            dimension_semantics=("arbitrary",), vmem_limit_bytes=52 * 1024 * 1024,
            collective_id=4, has_side_effects=True,
        ),
        cost_estimate=estimate(90),
        name="behind",
    )(
        projected, projected, cols, cols, halo_v, halo_b, info, marks, delta, cum, ssd, mixed_grad,
        sloc, pfx, entry, aloc, sfx, later, chan, bcpar, head, expand,
        gate_grad, weight, tok, inv, gain, edge_mask, out_next, *z_arrays,
    )


def peers(t):
    return t + 1 - 2 * lax.rem(t, 2), lax.rem(t + 2, 4)


def pick(w_ref, one, other):
    size = w_ref.shape[0] // 4
    at = lambda k: pl.ds(pl.multiple_of(k * size, size), size)
    return jnp.concatenate([w_ref[at(one), :], w_ref[at(other), :]], axis=0)


def shares_of(side, t):
    near = peers(t)
    return (t, near[1 - side]), (near[side], 3 - t)


def out_kernel(
    ssd, gate, sums, chan, w_ref, scaled, own, mid, send_a, send_b,
):
    i, half = pl.program_id(0), pl.num_programs(0) // 2
    t = lax.axis_index("tensor")
    width = ssd.shape[1]
    for k in range(ssd.shape[0] // L):
        rows = slice(k * L, (k + 1) * L)
        inv = jnp.broadcast_to(lax.rsqrt(sums[k, 0:1, :] / INNER + EPS), (LANE, L)).T
        for sl in tiles(width):
            g = gate[rows, sl]
            gated = ssd[rows, sl] * g * sigmoid(g)
            scaled[rows, sl] = (gated * inv * chan[KERNEL + 1 : KERNEL + 2, sl]).astype(BF16)
    x = scaled[...]
    size = own.shape[1]

    def part(side, send):
        keep, go = shares_of(side, t)
        send[...] = dot(x, pick(w_ref, *go), 1, 1).astype(BF16)
        kept = dot(x, pick(w_ref, *keep), 1, 1)
        own[...] = kept[:, :size]
        mid[...] = kept[:, size:]

    @pl.when(i < half)
    def _():
        part(0, send_a)

    @pl.when(i >= half)
    def _():
        part(1, send_b)


def run_out(ssd, projected, sums, chan, weight):
    steps, width = ssd.shape
    block = 512
    count = steps // block
    half = count // 2
    size = D // 4
    in_block = lambda w, col=0: pl.BlockSpec((block, w), lambda i: (i, col))
    return pl.pallas_call(
        out_kernel,
        grid=(count,),
        in_specs=[
            in_block(width), in_block(width, 0),
            pl.BlockSpec((block // L, 8, L), lambda i: (i, 0, 0)),
            once(KERNEL + 2, width), once(*weight.shape),
        ],
        out_specs=[
            in_block(width), in_block(size), in_block(size),
            pl.BlockSpec((block, 2 * size), lambda i: (jnp.minimum(i, half - 1), 0)),
            pl.BlockSpec((block, 2 * size), lambda i: (jnp.maximum(i - half, 0), 0)),
        ],
        out_shape=[
            shape(steps, width, dtype=BF16), shape(steps, size), shape(steps, size),
            shape(steps // 2, 2 * size, dtype=BF16), shape(steps // 2, 2 * size, dtype=BF16),
        ],
        compiler_params=params(),
        cost_estimate=estimate(12),
        name="out",
    )(ssd, projected, sums, chan, weight)


def line_kernel(
    n, n_tensor, piece, zx_raw, cols_raw, zx_out, cols_out, zx_ref, cols_ref,
    local, zx_s, zx_r, core_s, core_r, col_s, col_r, group_s, group_r, bulk_s, bulk_r,
):
    s, c, t = lax.axis_index("shard"), lax.axis_index("context"), lax.axis_index("tensor")
    on = (c < n - 1, c > 0)
    to = ((s, jnp.minimum(c + 1, n - 1), t), (s, jnp.maximum(c - 1, 0), t))
    to_core = (1 - s, c, t)
    to_group = [(s, c, lax.rem(t + k, n_tensor)) for k in range(1, n_tensor)]
    beside = [(s, lax.rem(c + k, n), t) for k in (1, n - 1)]
    barrier = greet([to_core] + to_group + beside)
    width = zx_raw.shape[2]
    for k in (0, 1):
        zx_ref[:, k * width : (k + 1) * width] = zx_raw[:, k, :].astype(BF16)
    gap = jnp.zeros((LANE - cols_raw.shape[0], cols_raw.shape[1]), F32)
    cols_ref[...] = jnp.concatenate([cols_raw[...], gap], axis=0).T.astype(BF16)
    pl.semaphore_wait(barrier, n_tensor + 2)
    rows, width = zx_ref.shape[0], cols_ref.shape[1]
    spans = [(at, min(piece, rows - at)) for at in range(0, rows, piece)]

    def block_of(way, hop):
        return jnp.maximum(c - hop, 0) if way == 0 else jnp.minimum(c + hop, n - 1)

    def has(way, hop):
        return c - hop >= 0 if way == 0 else c + hop <= n - 1

    def place(ref, block, at=0, size=rows):
        return ref.at[pl.ds(pl.multiple_of((s * n + block) * rows + at, 16), size), :]

    lanes = pl.ds(pl.multiple_of(t * width, LANE), width)

    def place_cols(block):
        return cols_out.at[pl.ds(pl.multiple_of((s * n + block) * rows, 16), rows), lanes]

    def zx_copy(way, step, p):
        at, size = spans[p]
        where = place(zx_out, block_of(way, step), at, size)
        src = zx_ref.at[pl.ds(at, size), :] if step == 0 else where
        return remote(src, where, zx_s.at[way, step, p], zx_r.at[way, step, p], to[way])

    def col_copy(way, step):
        where = place_cols(block_of(way, step))
        src = cols_ref if step == 0 else where
        return remote(src, where, col_s.at[way, step], col_r.at[way, step], to[way])

    def group_copies(way, hop):
        where = place_cols(block_of(way, hop))
        src = cols_ref if hop == 0 else where
        return [
            remote(src, where, group_s.at[k, way, hop], group_r.at[k, way, hop], target)
            for k, target in enumerate(to_group)
        ]

    def core_copy(way, hop, p):
        at, size = spans[p]
        where = place(zx_out, block_of(way, hop), at, size)
        src = zx_ref.at[pl.ds(at, size), :] if hop == 0 else where
        return remote(src, where, core_s.at[way, hop, p], core_r.at[way, hop, p], to_core)

    pieces = range(len(spans))
    for way in (0, 1):

        @pl.when(on[way])
        def _():
            col_copy(way, 0).start()
            for p in pieces:
                zx_copy(way, 0, p).start()

    for copy in group_copies(0, 0):
        copy.start()
    own_cols = pltpu.make_async_copy(cols_ref, place_cols(c), local.at[0])
    own_zx = pltpu.make_async_copy(zx_ref, place(zx_out, c), local.at[1])
    own_cols.start()
    own_zx.start()
    for p in pieces:
        core_copy(0, 0, p).start()
    start = pl.ds(pl.multiple_of(s * n * rows, 16), n * rows)
    bulk = remote(cols_out.at[start, :], cols_out.at[start, :], bulk_s, bulk_r, to_core)
    for step in range(n - 1):
        further = step < n - 2
        for way in (0, 1):

            @pl.when(has(way, step + 1))
            def _():
                col_copy(way, step).wait_recv()
                for copy in group_copies(way, step + 1):
                    copy.start()
                if further:

                    @pl.when(on[way])
                    def _():
                        col_copy(way, step + 1).start()

        if not further:
            own_cols.wait()
            for copy in group_copies(0, 0):
                copy.wait()
            for hop in range(1, n):
                for way in (0, 1):

                    @pl.when(has(way, hop))
                    def _():
                        for copy in group_copies(way, hop):
                            copy.wait()

            bulk.start()
        for p in pieces:
            for way in (0, 1):

                @pl.when(has(way, step + 1))
                def _():
                    zx_copy(way, step, p).wait_recv()
                    core_copy(way, step + 1, p).start()
                    if further:

                        @pl.when(on[way])
                        def _():
                            zx_copy(way, step + 1, p).start()

    for step in range(n - 1):
        for way in (0, 1):

            @pl.when(jnp.logical_and(on[way], has(way, step)))
            def _():
                col_copy(way, step).wait_send()
                for p in pieces:
                    zx_copy(way, step, p).wait_send()

            @pl.when(has(way, step + 1))
            def _():
                for p in pieces:
                    core_copy(way, step + 1, p).wait()

    for p in pieces:
        core_copy(0, 0, p).wait()
    bulk.wait()
    own_zx.wait()


PIECE = 64


def line_gather(zx, cols):
    n, n_tensor = lax.axis_size("context"), lax.axis_size("tensor")
    rows, width = zx.shape[0], 2 * zx.shape[2]
    pieces = -(-rows // PIECE)
    dma = pltpu.SemaphoreType.DMA
    return pl.pallas_call(
        functools.partial(line_kernel, n, n_tensor, PIECE),
        in_specs=[pl.BlockSpec(memory_space=pltpu.VMEM)] * 2,
        out_specs=[pl.BlockSpec(memory_space=pl.ANY)] * 2,
        out_shape=[
            shape(2 * n * rows, width, dtype=BF16),
            shape(2 * n * rows, n_tensor * LANE, dtype=BF16),
        ],
        scratch_shapes=[
            pltpu.VMEM((rows, width), BF16), pltpu.VMEM((rows, LANE), BF16),
            dma((2,)), dma((2, n - 1, pieces)), dma((2, n - 1, pieces)),
            dma((2, n, pieces)), dma((2, n, pieces)), dma((2, n - 1)), dma((2, n - 1)),
            dma((n_tensor - 1, 2, n)), dma((n_tensor - 1, 2, n)), dma, dma,
        ],
        compiler_params=pltpu.CompilerParams(collective_id=0, has_side_effects=True),
        name="line_gather",
    )(zx, cols)


SLICES = 8


class Chain:
    def __init__(self, n, backward, packed, entering, got, sent, send_sem, recv_sem):
        s, c, t = lax.axis_index("shard"), lax.axis_index("context"), lax.axis_index("tensor")
        self.from_other = c < n - 1 if backward else c > 0
        self.to_other = c > 0 if backward else c < n - 1
        ahead = jnp.maximum(c - 1, 0) if backward else jnp.minimum(c + 1, n - 1)
        self.target = (s, ahead, t)
        self.refs = packed, entering, got, sent, send_sem, recv_sem

    def copy(self, j):
        _, _, got, sent, send_sem, recv_sem = self.refs
        rows = pl.ds(j * (N // SLICES), N // SLICES)
        return remote(sent.at[rows, :], got.at[rows, :], send_sem.at[j], recv_sem.at[j], self.target)

    def begin(self):
        packed, entering, _, sent, _, _ = self.refs

        @pl.when(jnp.logical_not(self.from_other))
        def _():
            entering[...] = jnp.zeros_like(entering)

            @pl.when(self.to_other)
            def _():
                sent[...] = packed[:N, :]
                for j in range(SLICES):
                    self.copy(j).start()

    def step(self, j):
        packed, entering, got, sent, _, _ = self.refs
        rows = slice(j * (N // SLICES), (j + 1) * (N // SLICES))

        @pl.when(self.from_other)
        def _():
            self.copy(j).wait_recv()
            entering[rows, :] = got[rows, :]

            @pl.when(self.to_other)
            def _():
                sent[rows, :] = packed[rows, :] + packed[N : N + 1, :] * entering[rows, :]
                self.copy(j).start()

    def finish(self):
        @pl.when(self.to_other)
        def _():
            for j in range(SLICES):
                self.copy(j).wait_send()


def beside_of(n):
    s, c, t = lax.axis_index("shard"), lax.axis_index("context"), lax.axis_index("tensor")
    return [(s, lax.rem(c + k, n), t) for k in (1, n - 1)]


def entry_kernel(
    n, packed, back, w_hbm, entry, out, bk, w_ref, buf, got, sent, load_sem, out_sem, chain_s, chain_r
):
    block = buf.shape[1]
    count = back.shape[0] // block
    load_w = pltpu.make_async_copy(w_hbm, w_ref, load_sem.at[count])
    load_w.start()

    def load(k):
        rows = pl.ds(k * block, block)
        return pltpu.make_async_copy(back.at[rows, :], bk.at[rows, :], load_sem.at[k])

    def store(k):
        return pltpu.make_async_copy(
            buf.at[k % 2], out.at[pl.ds(k * block, block), :], out_sem.at[k % 2]
        )

    for k in range(count):
        load(k).start()
    pl.semaphore_wait(greet(beside_of(n)), 2)
    chain = Chain(n, False, packed, entry, got, sent, chain_s, chain_r)
    chain.begin()
    load_w.wait()
    for k in range(count):
        load(k).wait()
        if k >= 2:
            store(k - 2).wait()
        buf[k % 2] = dot(bk[k * block : (k + 1) * block, :], w_ref[...])
        store(k).start()
        if k < SLICES:
            chain.step(k)
    for k in range(count, SLICES):
        chain.step(k)
    chain.finish()
    for k in range(max(count - 2, 0), count):
        store(k).wait()


def run_entry(packed, back, weight):
    n = lax.axis_size("context")
    steps, width = back.shape[0], weight.shape[1]
    block = 256
    dma = pltpu.SemaphoreType.DMA
    vmem = pltpu.VMEM
    inside = pl.BlockSpec(memory_space=pltpu.VMEM)
    hbm = pl.BlockSpec(memory_space=pl.ANY)
    return pl.pallas_call(
        functools.partial(entry_kernel, n),
        in_specs=[inside, hbm, hbm],
        out_specs=[inside, hbm],
        out_shape=[shape(N, width), shape(steps, width)],
        scratch_shapes=[
            vmem(back.shape, BF16), vmem(weight.shape, BF16), vmem((2, block, width), F32),
            vmem((N, width), F32), vmem((N, width), F32),
            dma((steps // block + 1,)), dma((2,)), dma((SLICES,)), dma((SLICES,)),
        ],
        compiler_params=pltpu.CompilerParams(
            vmem_limit_bytes=58 * 1024 * 1024, collective_id=6, has_side_effects=True
        ),
        cost_estimate=estimate(15),
        name="entry",
    )(packed, back, weight)


def middle_kernel(
    n, packed, send_a, send_b, mid_hbm, own_hbm, normed_hbm, gate_hbm, back_hbm, scaled_hbm, *refs
):
    if n == 4:
        later, own, next_out, z_out, z_mid, z_mine = refs[:6]
        refs = refs[6:]
    else:
        later, own, next_out, both_out = refs[:4]
        refs = refs[4:]
    (
        mid, nm, gg, bk, sc, peer_part, core_part, own_part, got, chain_got, chain_sent,
        local, core_s, core_r, f_s, f_r, chain_s, chain_r,
    ) = refs
    s, c, t = lax.axis_index("shard"), lax.axis_index("context"), lax.axis_index("tensor")
    near = peers(t)
    to = [(s, c, near[0]), (s, c, near[1])]
    to_core = (1 - s, c, t)
    loads = [
        pltpu.make_async_copy(src, dst, local.at[k])
        for k, (src, dst) in enumerate(
            [
                (normed_hbm, nm), (gate_hbm, gg), (back_hbm, bk), (scaled_hbm, sc),
                (mid_hbm, mid), (own_hbm, own),
            ]
        )
    ]
    for load in loads:
        load.start()
    pl.semaphore_wait(greet(to + [to_core] + beside_of(n)), 5)
    hops = [
        remote(src, got.at[side], f_s.at[side], f_r.at[side], to[side])
        for side, src in enumerate((send_a, send_b))
    ]
    for hop in hops:
        hop.start()
    chain = Chain(n, True, packed, later, chain_got, chain_sent, chain_s, chain_r)
    half_d = nm.shape[1] // 2
    steps = nm.shape[0]
    step = 256
    pairs = ((nm, gg), (bk, sc))

    def product(which, shard, into, m):
        left, right = pairs[which]
        lanes = pl.ds(pl.multiple_of(shard * half_d + m * step, step), step)
        into[which, m * step : (m + 1) * step, :] = over_rows(left, lanes, lambda rows: right[rows, :])

    cores = [
        remote(peer_part.at[k], core_part.at[k], core_s.at[k], core_r.at[k], to_core) for k in (0, 1)
    ]
    chain.begin()
    chain.step(0)
    done = 1
    for which in (0, 1):
        loads[2 * which].wait()
        loads[2 * which + 1].wait()
        for m in range(half_d // step):
            product(which, 1 - s, peer_part, m)
            if done < SLICES:
                chain.step(done)
                done += 1
        cores[which].start()
    for which in (0, 1):
        for m in range(half_d // step):
            product(which, s, own_part, m)
            if done < SLICES:
                chain.step(done)
                done += 1
    chain.finish()
    block = half_d // n

    for which in (0, 1):
        cores[which].wait()
        if n == 4:
            first = c + 1 - 2 * lax.rem(c, 2) if which == 0 else 3 - c
            third = 3 - c if which == 0 else c + 1 - 2 * lax.rem(c, 2)

            def total(k):
                rows = pl.ds(pl.multiple_of(k * block, 8), block)
                return own_part[which, rows, :] + core_part[which, rows, :]

            z_out[which, :block, :] = total(first).astype(BF16)
            z_out[which, block:, :] = total(lax.rem(c + 2, 4)).astype(BF16)
            z_mid[which] = total(third)
            z_mine[which] = total(c)
        else:
            both_out[which] = own_part[which] + core_part[which]
    loads[4].wait()
    loads[5].wait()
    size = mid.shape[1]
    half = steps // 2
    for side in (0, 1):
        hops[side].wait()
        for k in range(half // step):
            rows = slice(k * step, (k + 1) * step)
            at = slice(side * half + k * step, side * half + (k + 1) * step)
            next_out[side, rows, :] = (mid[at, :] + got[side, rows, size:].astype(F32)).astype(BF16)
            own[at, :] += got[side, rows, :size].astype(F32)


def run_middle(packed, fan, normed, gate_grad, back, scaled):
    n = lax.axis_size("context")
    own, mid, send_a, send_b = fan
    steps, width = gate_grad.shape
    size = own.shape[1]
    half_d = D // 2
    block = half_d // n
    dma = pltpu.SemaphoreType.DMA
    vmem = pltpu.VMEM
    inside = pl.BlockSpec(memory_space=pltpu.VMEM)
    hbm = pl.BlockSpec(memory_space=pl.ANY)
    if n == 4:
        more = [
            shape(2, 2 * block, width, dtype=BF16), shape(2, block, width), shape(2, block, width)
        ]
    else:
        more = [shape(2, half_d, width)]
    pair = (2, half_d, width)
    return pl.pallas_call(
        functools.partial(middle_kernel, n),
        in_specs=[inside] + [hbm] * 8,
        out_specs=[inside] * (3 + len(more)),
        out_shape=[shape(N, width), shape(steps, size), shape(2, steps // 2, size, dtype=BF16)] + more,
        scratch_shapes=[
            vmem((steps, size), F32), vmem(normed.shape, BF16), vmem(gate_grad.shape, BF16),
            vmem(back.shape, BF16), vmem(scaled.shape, BF16),
            vmem(pair, F32), vmem(pair, F32), vmem(pair, F32), vmem((2, steps // 2, 2 * size), BF16),
            vmem((N, width), F32), vmem((N, width), F32),
            dma((6,)), dma((2,)), dma((2,)), dma((2,)), dma((2,)), dma((SLICES,)), dma((SLICES,)),
        ],
        compiler_params=pltpu.CompilerParams(
            vmem_limit_bytes=54 * 1024 * 1024, collective_id=7, has_side_effects=True
        ),
        cost_estimate=estimate(35),
        name="middle",
    )(packed, send_a, send_b, mid, own, normed, gate_grad, back, scaled)


def adam_kernel(
    heads, cols_loc, table, gate_g, value_g, down_g, cols_g, packed, packed_gain, resid, own, last, *refs
):
    zx, out, bcdt, gain, chan, bc, head = [refs[3 * k : 3 * k + 3] for k in range(7)]
    refs = refs[21:]
    zx_new, out_new, bcdt_new, gain_new, chan_new, bc_new, head_new = [
        refs[3 * k : 3 * k + 3] for k in range(7)
    ]
    width = value_g.shape[1]
    refs[21][...] = (resid[...].astype(F32) + own[...] + last[0].astype(F32)).astype(BF16)

    def put(news, olds, grad, rate, decay, at=(Ellipsis,)):
        for ref, val in zip(news, adamw(olds[0][at], grad, olds[1][at], olds[2][at], rate, decay)):
            ref[at] = val

    for k, grad in enumerate((gate_g[0], value_g[...])):
        put(zx_new, zx, grad, RATE_MATRIX, DECAY, (slice(None), k, slice(None)))
    put(out_new, out, down_g[0], RATE_MATRIX, DECAY)

    @pl.when(pl.program_id(0) == 0)
    def _():
        put(bcdt_new, bcdt, cols_g[...].T[:cols_loc, :], RATE_MATRIX, DECAY)
        adam_small(
            heads, width, packed, packed_gain, put, gain, chan, bc, head, gain_new, chan_new, bc_new, head_new
        )


def adam_small(
    heads, width, packed, packed_gain, put, gain, chan, bc, head, gain_new, chan_new, bc_new, head_new
):
    over = packed[0] + packed[1] + packed[2] + packed[3]
    gains = packed_gain[0] + packed_gain[1] + packed_gain[2] + packed_gain[3]
    put(gain_new, gain, gains[: D // LANE, :], RATE_SMALL, 0.0)
    put(bc_new, bc, over[: KERNEL + 1, width : width + 2 * N], RATE_SMALL, 0.0)
    grad = jnp.concatenate([packed[k, : KERNEL + 2, :width] for k in range(4)], axis=1)
    put(chan_new, chan, grad, RATE_SMALL, 0.0)
    lane = lax.broadcasted_iota(jnp.int32, (LANE, 4 * heads), 0)
    slot = lax.broadcasted_iota(jnp.int32, (LANE, 4 * heads), 1)
    channel = lax.broadcasted_iota(jnp.int32, (width, 4 * heads), 0)
    wide_slot = lax.broadcasted_iota(jnp.int32, (width, 4 * heads), 1)
    rows = jnp.zeros((8, 4 * heads), F32)
    for k in range(4):
        here = jnp.where(lane + k * heads == slot, 1.0, 0.0)
        here = jnp.where(lane < heads, here, 0.0).astype(BF16)
        wide = jnp.where(channel // P_SIZE + k * heads == wide_slot, 1.0, 0.0).astype(BF16)
        hi, lo = two(packed[k, KERNEL + 3 : KERNEL + 11, :LANE])
        at = lax.broadcasted_iota(jnp.int32, rows.shape, 0)
        rows = rows + jnp.where(at < 2, dot(hi, here) + dot(lo, here), 0.0)
        hi, lo = two(packed[k, KERNEL + 2 : KERNEL + 10, :width])
        skip = dot(hi, wide) + dot(lo, wide)
        rows = rows + jnp.where(at == 2, jnp.broadcast_to(skip[0:1, :], rows.shape), 0.0)
    put(head_new, head, rows[:3, :], RATE_SMALL, 0.0)


def run_adam(pair, value_g, cols_g, packed, packed_gain, tok, own, last, t_index, olds, heads, cols_loc):
    rows, width = value_g.shape
    steps, size = own.shape
    count = 4 if rows % 32 == 0 else 2
    block, span = rows // count, steps // count
    half = count // 2
    one = lambda k: pl.BlockSpec((1, block, width), lambda i, t: (k, i, 0))
    some = pl.BlockSpec((block, width), lambda i, t: (i, 0))
    large = pl.BlockSpec((block, 2, width), lambda i, t: (i, 0, 0))
    tokens = pl.BlockSpec((span, size), lambda i, t: (i, 0))
    every = lambda x: pl.BlockSpec(x.shape, lambda i, t: (0,) * x.ndim, pipeline_mode=pl.Buffered(1))
    flat = [x for group in olds for x in group]
    specs = [large] * 3 + [some] * 3 + [every(x) for x in flat[6:]]
    return pl.pallas_call(
        functools.partial(adam_kernel, heads, cols_loc),
        grid_spec=pltpu.PrefetchScalarGridSpec(
            num_scalar_prefetch=1,
            grid=(count,),
            in_specs=[
                one(0), some, one(1), every(cols_g), every(packed), every(packed_gain),
                pl.BlockSpec((span, size), lambda i, t: (i, t[0])), tokens,
                pl.BlockSpec((1, span, size), lambda i, t: (i // half, i % half, 0)),
            ]
            + specs,
            out_specs=specs + [tokens],
        ),
        out_shape=[shape(*x.shape) for x in flat] + [shape(steps, size, dtype=BF16)],
        compiler_params=params(),
        cost_estimate=estimate(8),
        name="optimizer",
    )(
        jnp.full((1,), t_index, jnp.int32), pair, value_g, pair, cols_g, packed, packed_gain, tok, own,
        last, *flat,
    )


def doc_of(lengths, position):
    found = jnp.zeros(position.shape, F32)
    end = 0
    for k in range(lengths.shape[1] - 1):
        end = end + lengths[0, k]
        found = found + jnp.where(position >= end, 1.0, 0.0)
    return jnp.where(position < 0, -1.0, found)


def mark_chunk(lengths, begin, limit, info_ref, marks_ref):
    row = lax.broadcasted_iota(jnp.int32, (L, LANE), 0)
    lane = lax.broadcasted_iota(jnp.int32, (L, LANE), 1)
    offset = jnp.where(lane < KERNEL - 1, lane - KERNEL + 1, jnp.where(lane >= 8, lane - 7, 0))
    other = jnp.where(lane == 3, -1, jnp.where(lane == 4, L - 1, row + offset)) + begin
    mark = doc_of(lengths, row + begin)
    same = jnp.logical_and(doc_of(lengths, other) == mark, other < limit)
    info = jnp.where(same, 1.0, 0.0)
    info_ref[...] = jnp.where(lane == 5, mark, jnp.where(lane < 7 + KERNEL, info, 0.0))
    marks_ref[0] = doc_of(lengths, begin + lax.broadcasted_iota(jnp.int32, (8, L), 1))


def norm_rows(tok, gain):
    x = tok.astype(F32)
    square = x * x
    total = square[:, :LANE]
    for sl in tiles(D)[1:]:
        total = total + square[:, sl]
    inv = lax.rsqrt(jnp.sum(total, axis=1, keepdims=True) / D + EPS)
    return (x * inv * gain[0:1, :]).astype(BF16), inv


def project_kernel(
    heads, n, cols_loc, lengths, tok, tok_end, gain, w_ref, wg_ref, chan, bcpar, head, e_ref,
    normed, inv, projected, cols, info, marks, edge_mask, act, delta, cum, sloc, pfx, fin,
    halo_v, halo_b, ext_v, ext_b, state, prod, w_cols, prev_v, prev_b, halo_out, halo_got, h_s, h_r,
):
    i = pl.program_id(0)
    s, c, t = lax.axis_index("shard"), lax.axis_index("context"), lax.axis_index("tensor")
    width = w_ref.shape[1] // 2
    block = tok.shape[0]
    steps = block * pl.num_programs(0)
    start = c * steps
    after = (s, jnp.minimum(c + 1, n - 1), t)
    halo = remote(halo_out, halo_got, h_s, h_r, after)

    @pl.when(i == 0)
    def _():
        pl.semaphore_wait(greet(beside_of(n)), 2)
        state[...] = jnp.zeros_like(state)
        prod[...] = jnp.ones_like(prod)
        lane = lax.broadcasted_iota(jnp.int32, (4 * LANE, 3 * N), 0)
        want = lax.broadcasted_iota(jnp.int32, (4 * LANE, 3 * N), 1)
        have = lane // LANE * cols_loc + lane % LANE
        want = jnp.where(want < 2 * N, want, jnp.where(want < 2 * N + heads, want + heads * t, -1))
        chosen = jnp.logical_and(have == want, lane % LANE < cols_loc)
        select = jnp.where(chosen, 1.0, 0.0).astype(BF16)
        for k in range(0, D, block):
            w_cols[k : k + block, :] = dot(wg_ref[k : k + block, :], select).astype(BF16)
        ends, _ = norm_rows(tok_end[...], gain)
        halo_out[:, :width] = dot(ends, w_ref[:, width:])[8:, :]
        halo_out[:, width:] = dot(ends, w_cols[...])[8:, :]

        @pl.when(c < n - 1)
        def _():
            halo.start()

        row = lax.broadcasted_iota(jnp.int32, (24, LANE), 0)
        shift, at = row // 8 + 1, row % 8
        there = at - 8 + shift + start + steps
        agree = doc_of(lengths, there) == doc_of(lengths, there - shift)
        edge_mask[...] = jnp.where(jnp.logical_and(at >= 8 - shift, agree), 1.0, 0.0)

    for j in range(block // L):
        rows = slice(j * L, (j + 1) * L)
        x, scale = norm_rows(tok[rows, :], gain)
        normed[rows, :] = x
        inv[rows, :] = scale
    for k in range(0, 2 * width, 512):
        projected[:, k : k + 512] = dot(normed[...], w_ref[:, k : k + 512])
    cols[...] = dot(normed[...], w_cols[...])

    @pl.when(i == 0)
    def _():
        @pl.when(c > 0)
        def _():
            halo.wait_recv()
            halo_v[...] = halo_got[:, :width]
            halo_b[...] = halo_got[:, width:]

        @pl.when(c == 0)
        def _():
            halo_v[...] = jnp.zeros_like(halo_v)
            halo_b[...] = jnp.zeros_like(halo_b)

        @pl.when(c < n - 1)
        def _():
            halo.wait_send()

    val = projected.at[:, pl.ds(width, width)]

    for j in range(block // L):
        first = i == 0
        mark_chunk(
            lengths, start + i * block + j * L, start + steps, rows_at(info, j), lead_at(marks, j)
        )
        load_ext(ext_v, val, prev_v, halo_v, j, first)
        load_ext(ext_b, cols, prev_b, halo_b, j, first)
        prep_chunk(
            rows_at(cols, j), rows_at(info, j), chan, bcpar, head, e_ref, rows_at(act, j),
            rows_at(delta, j), rows_at(cum, j), lead_at(sloc, j), lead_at(pfx, j),
            ext_v, ext_b, state, prod,
        )
    prev_v[...] = projected[block - 8 :, width:]
    prev_b[...] = cols[block - 8 :, :]

    @pl.when(i == pl.num_programs(0) - 1)
    def _():
        fin[:N, :] = state[...]
        fin[N:, :] = prod[...]


def run_project(lengths, tok, gain, weight, w_group, chan, bcpar, head, expand, heads, cols_loc):
    steps, width = tok.shape[0], weight.shape[1] // 2
    count = steps // L
    dma = pltpu.SemaphoreType.DMA
    return pl.pallas_call(
        functools.partial(project_kernel, heads, lax.axis_size("context"), cols_loc),
        grid=(steps // GROUP,),
        in_specs=[
            pl.BlockSpec(memory_space=pltpu.SMEM), row_block(D),
            pl.BlockSpec((16, D), lambda i: (steps // 16 - 1, 0), pipeline_mode=pl.Buffered(1)),
            once(8, D), once(*weight.shape), once(*w_group.shape),
            once(KERNEL + 2, width), once(KERNEL + 1, 2 * N), once(8, LANE), once(2 * LANE, width),
        ],
        out_specs=[
            row_block(D), row_block(1),
            row_block(2 * width), row_block(3 * N), row_block(LANE), lead_block(8, L), once(24, LANE),
            row_block(width + 2 * N), row_block(LANE), row_block(LANE), lead_block(N, width),
            lead_block(8, width), once(N + 8, width), once(8, width), once(8, 3 * N),
        ],
        out_shape=[
            shape(steps, D, dtype=BF16), shape(steps, 1),
            shape(steps, 2 * width), shape(steps, 3 * N), shape(steps, LANE), shape(count, 8, L),
            shape(24, LANE),
            shape(steps, width + 2 * N), shape(steps, LANE), shape(steps, LANE),
            shape(count, N, width), shape(count, 8, width), shape(N + 8, width), shape(8, width),
            shape(8, 3 * N),
        ],
        scratch_shapes=[
            pltpu.VMEM((8 + L, width), F32), pltpu.VMEM((8 + L, 3 * N), F32),
            pltpu.VMEM((N, width), F32), pltpu.VMEM((8, width), F32),
            pltpu.VMEM((D, 3 * N), BF16), pltpu.VMEM((8, width), F32), pltpu.VMEM((8, 3 * N), F32),
            pltpu.VMEM((8, width + 3 * N), F32), pltpu.VMEM((8, width + 3 * N), F32), dma, dma,
        ],
        compiler_params=pltpu.CompilerParams(
            dimension_semantics=("arbitrary",), vmem_limit_bytes=58 * 1024 * 1024,
            collective_id=8, has_side_effects=True,
        ),
        cost_estimate=estimate(45),
        name="project",
    )(lengths, tok, tok, gain, weight, w_group, chan, bcpar, head, expand)


class AllSum:
    def __init__(self, n, refs, sems):
        s, c, t = lax.axis_index("shard"), lax.axis_index("context"), lax.axis_index("tensor")
        self.n, self.c, self.t = n, c, t
        self.mine, self.other, self.pair, self.pieces, self.total, self.every = refs
        core_s, core_r, piece_s, piece_r, group_s, group_r = sems
        self.core = remote(self.mine, self.other, core_s, core_r, (1 - s, c, t))
        self.along = [
            remote(self.pair, self.pieces.at[c], piece_s.at[k], piece_r.at[k], (s, lax.rem(c + k + 1, n), t))
            for k in range(n - 1)
        ]
        self.across = [
            remote(self.total, self.every.at[t], group_s.at[k], group_r.at[k], (s, c, lax.rem(t + k + 1, 4)))
            for k in range(3)
        ]

    def start(self):
        self.core.start()

    def after_core(self):
        self.core.wait()
        self.pair[...] = self.mine[...] + self.other[...]
        self.pieces[self.c] = self.pair[...]
        for copy in self.along:
            copy.start()

    def after_pieces(self):
        for copy in self.along:
            copy.wait()
        self.total[...] = sum(self.pieces[k] for k in range(1, self.n)) + self.pieces[0]
        self.every[self.t] = self.total[...]
        for copy in self.across:
            copy.start()

    def finish(self):
        for copy in self.across:
            copy.wait()


PACK = 16


def tail_kernel(
    n, grad_b, grad_v, normed_hbm, w_hbm, tok_hbm, back_hbm, late_hbm, wg_hbm,
    raw_t, fixed, gate_top, gate_end, tok_top, tok_end, inv, gain, sel_bc, sel_raw,
    late_rows, late_gain, taps_grad, bias_grad, norm_gain_grad, skip_grad, head_grad,
    tokens_out, value_out, cols_out, pack_out, gain_out,
    gb, gv, nm, w_ref, tok, back, w_cols, col_grad,
    peer_part, own_part, core_part, b_got, b_next, b_last, b_full, raw_full,
    early, mid, send, got, nxt, last, gain_grad, z_out, z_got, z_on, z_last,
    ng, col_peer, col_own, col_core, col_out, col_got, col_on, col_last,
    row_buf, row_held, *refs,
):
    tail_body(
        n, grad_b, grad_v, normed_hbm, w_hbm, tok_hbm, back_hbm, late_hbm, wg_hbm,
        raw_t, fixed, gate_top, gate_end, tok_top, tok_end, inv, gain, sel_bc, sel_raw,
        late_rows, late_gain, taps_grad, bias_grad, norm_gain_grad, skip_grad, head_grad,
        tokens_out, value_out, cols_out, pack_out, gain_out,
        gb, gv, nm, w_ref, tok, back, w_cols, col_grad,
        peer_part, own_part, core_part, b_got, b_next, b_last, b_full, raw_full,
        early, mid, send, got, nxt, last, gain_grad, z_out, z_got, z_on, z_last,
        ng, col_peer, col_own, col_core, col_out, col_got, col_on, col_last,
        row_buf, row_held, refs[:6], refs[6:12], *refs[12:25], refs[25:31], refs[31:37],
    )


def tail_body(
    n, grad_b, grad_v, normed_hbm, w_hbm, tok_hbm, back_hbm, late_hbm, wg_hbm,
    raw_t, fixed, gate_top, gate_end, tok_top, tok_end, inv, gain, sel_bc, sel_raw,
    late_rows, late_gain, taps_grad, bias_grad, norm_gain_grad, skip_grad, head_grad,
    tokens_out, value_out, cols_out, pack_out, gain_out,
    gb, gv, nm, w_ref, tok, back, w_cols, col_grad,
    peer_part, own_part, core_part, b_got, b_next, b_last, b_full, raw_full,
    early, mid, send, got, nxt, last, gain_grad, z_out, z_got, z_on, z_last,
    ng, col_peer, col_own, col_core, col_out, col_got, col_on, col_last,
    row_buf, row_held, pack_refs, gain_refs,
    local, raw_s, raw_r, b_s, b_r, f_s, f_r, core_s, core_r, z_s, z_r, row_s, row_r,
    pack_sems, gain_sems,
):
    s, c, t = lax.axis_index("shard"), lax.axis_index("context"), lax.axis_index("tensor")
    near = peers(t)
    to = [(s, c, near[0]), (s, c, near[1])]
    group = [(s, c, lax.rem(t + k, 4)) for k in (1, 2, 3)]
    to_core = (1 - s, c, t)
    to_piece = [(s, lax.rem(c + k, n), t) for k in range(1, n)]
    in_line = n == 4
    line = [(s, c + 1 - 2 * lax.rem(c, 2), t), (s, 3 - c, t)] if in_line else []
    steps, width = grad_v.shape
    size = w_ref.shape[0] // 4
    share = steps // 4
    mine_lanes = pl.ds(pl.multiple_of(t * size, size), size)
    loads = [
        pltpu.make_async_copy(src, dst, local.at[k])
        for k, (src, dst) in enumerate(
            [
                (grad_b, gb), (grad_v, gv), (normed_hbm, nm), (w_hbm, w_ref),
                (tok_hbm.at[:, mine_lanes], tok), (back_hbm.at[:, mine_lanes], back),
                (late_hbm, ng.at[pl.ds(GROUP, steps - GROUP), :]),
                (wg_hbm.at[mine_lanes, :], w_cols),
            ]
        )
    ]
    for load in loads[:2]:
        load.start()
    pl.semaphore_wait(greet(group + [to_core] + to_piece), n + 3)

    raw_full[t] = raw_t[...]
    raws = [
        remote(raw_t, raw_full.at[t], raw_s.at[k], raw_r.at[k], target)
        for k, target in enumerate(group)
    ]
    for copy in raws:
        copy.start()

    def rows_of(k):
        return pl.ds(pl.multiple_of(k * share, share), share)

    def lanes_of(side):
        return pl.ds(side * N, N)

    loads[0].wait()
    for load in loads[2:]:
        load.start()
    gb[steps - 8 :, :] = fixed[:, width:]

    def b_first(side, part):
        k = near[side] if part == 0 else 3 - t
        return remote(
            gb.at[rows_of(k), lanes_of(side)], b_got.at[side, part], b_s.at[side, part],
            b_r.at[side, part], to[side],
        )

    def b_second(side):
        return remote(
            b_next.at[side], b_last.at[side], b_s.at[side, 2], b_r.at[side, 2], to[1 - side]
        )

    def b_back(side, part):
        k = near[1 - side] if part == 2 else t
        where = b_full.at[rows_of(k), lanes_of(side)]
        return remote(
            where, where, b_s.at[side, 3 + part], b_r.at[side, 3 + part],
            to[1 - side] if part == 0 else to[side],
        )

    for side in (0, 1):
        for part in (0, 1):
            b_first(side, part).start()

    pack = pack_refs[0]
    pack[...] = jnp.zeros_like(pack)
    gain_refs[0][...] = jnp.zeros_like(gain_refs[0])
    total = width + 2 * N
    add_up = lambda x: jnp.sum(x, axis=0, keepdims=True)
    for k in range(KERNEL):
        pack[k : k + 1, :total] = add_up(taps_grad[8 * k : 8 * k + 8, :])
    pack[KERNEL : KERNEL + 1, :total] = add_up(bias_grad[...])
    pack[KERNEL + 1 : KERNEL + 2, :width] = add_up(norm_gain_grad[...])
    pack[KERNEL + 2 : KERNEL + 3, :width] = add_up(skip_grad[...])
    pack[KERNEL + 3 : KERNEL + 4, :LANE] = add_up(head_grad[:8, :])
    pack[KERNEL + 4 : KERNEL + 5, :LANE] = add_up(head_grad[8:, :])
    pack_sum = AllSum(n, pack_refs, pack_sems)
    gain_sum = AllSum(n, gain_refs, gain_sems)
    pack_sum.start()

    loads[1].wait()
    tail = gv[steps - 16 :, :].astype(F32)
    gv[steps - 16 :, :] = jnp.concatenate([tail[:8], fixed[:, :width]], axis=0).astype(BF16)
    loads[2].wait()
    half_d = nm.shape[1] // 2
    step = 256

    def product(shard, right, into):
        for m in range(half_d // step):
            lanes = pl.ds(pl.multiple_of(shard * half_d + m * step, step), step)
            into[m * step : (m + 1) * step, :] = over_rows(nm, lanes, right)

    product(1 - s, lambda rows: gv[rows, :], peer_part)
    core = remote(peer_part, core_part, core_s.at[0], core_r.at[0], to_core)
    core.start()

    for side in (0, 1):
        for part in (0, 1):
            b_first(side, part).wait()
        b_next[side] = gb[rows_of(near[1 - side]), lanes_of(side)] + b_got[side, 1]
        b_second(side).start()
    pack_sum.after_core()

    product(s, lambda rows: gv[rows, :], own_part)

    for side in (0, 1):
        b_second(side).wait()
        mine = gb[rows_of(t), lanes_of(side)] + b_got[side, 0] + b_last[side]
        b_full[rows_of(t), lanes_of(side)] = mine.astype(BF16)
        b_back(side, 0).start()

    block = half_d // n
    side_w = width // 2
    both = own_part
    if in_line:
        first = [c + 1 - 2 * lax.rem(c, 2), 3 - c]
        across = lax.rem(c + 2, 4)

    def block_rows(k):
        return pl.ds(pl.multiple_of(k * block, 8), block)

    def z_block(k, side):
        return both[block_rows(k), side * side_w : (side + 1) * side_w]

    def z_first(side):
        return remote(z_out.at[side], z_got.at[side], z_s.at[side], z_r.at[side], line[side])

    def z_second(side):
        return remote(z_on.at[side], z_last.at[side], z_s.at[2 + side], z_r.at[2 + side], line[1 - side])

    def col_first():
        return remote(col_out, col_got, z_s.at[4], z_r.at[4], line[0])

    def col_second():
        return remote(col_on, col_last, z_s.at[5], z_r.at[5], line[1])

    core.wait()
    both[...] = both[...] + core_part[...]
    if in_line:
        for side in (0, 1):
            z_out[side, :block, :] = z_block(first[side], side).astype(BF16)
            z_out[side, block:, :] = z_block(across, side).astype(BF16)
            z_first(side).start()
    for side in (0, 1):
        b_back(side, 0).wait()
        for part in (1, 2):
            b_back(side, part).start()

    loads[3].wait()
    pack_sum.after_pieces()
    half = GROUP // 2
    tail_half = END // 2

    def f_first(side):
        return remote(send.at[side], got.at[side], f_s.at[side], f_r.at[side], to[side])

    def f_second(side):
        return remote(
            nxt.at[side], last.at[side], f_s.at[2 + side], f_r.at[2 + side], to[1 - side]
        )

    gain_grad[...] = late_gain[...]
    for g in range(GROUP // PART, steps // PART):
        row_buf[:, g * PART : (g + 1) * PART] = late_rows[g]
    ends = [jnp.zeros((LANE - END, LANE), F32)]
    for side in (0, 1):
        rows = slice(side * half, (side + 1) * half)
        tail_rows = slice(side * tail_half, (side + 1) * tail_half)
        end_rows = slice(steps - END + side * tail_half, steps - END + (side + 1) * tail_half)
        x = jnp.concatenate(
            [
                jnp.concatenate([gate_top[rows, :], gv[rows, :]], axis=1),
                jnp.concatenate([gate_end[tail_rows, :], gv[end_rows, :]], axis=1),
            ],
            axis=0,
        )
        keep, go = shares_of(side, t)
        gone = dot(x, pick(w_ref, *go), 1, 1)
        send[side] = gone.astype(BF16)
        f_first(side).start()
        kept = dot(x, pick(w_ref, *keep), 1, 1)
        early[side] = kept[:, :size]
        mid[side] = kept[:, size:]
        scale = jnp.concatenate([inv[rows, :], inv[end_rows, :]], axis=0)
        parts = [kept[:, :size], kept[:, size:], gone[:, :size], gone[:, size:]]

        def z(lanes):
            values = jnp.concatenate([tok_top[rows, lanes], tok_end[tail_rows, lanes]], axis=0)
            return values.astype(F32) * scale

        sums = count_rows(parts, z, gain, keep + go, gain_grad)
        row_buf[:, rows] = row_dots(sums[:half])
        ends.append(sums[half:])
    row_buf[:, steps - LANE :] += row_dots(jnp.concatenate(ends, axis=0))

    for copy in raws:
        copy.wait()
    for side in (0, 1):
        for part in (1, 2):
            b_back(side, part).wait()
    raw_all = jnp.concatenate([raw_full[k] for k in range(4)], axis=0)

    for k in range(steps // GROUP):
        rows = slice(k * GROUP, (k + 1) * GROUP)
        chosen = dot(b_full[rows, :], sel_bc[...]) + dot(raw_all[:, rows], sel_raw[...], 0, 0)
        col_grad[rows, :] = chosen.astype(BF16)
    own_lanes = pl.ds(pl.multiple_of(t * LANE, LANE), LANE)
    product(1 - s, lambda rows: col_grad[rows, own_lanes], col_peer)
    col_core_copy = remote(col_peer, col_core, core_s.at[1], core_r.at[1], to_core)
    col_core_copy.start()
    gain_mine = gain[0:1, mine_lanes]
    loads[4].wait()
    loads[6].wait()
    loads[7].wait()
    ng[steps - END :, :] = jnp.zeros((END, size), F32)
    for k in range(steps // GROUP):
        rows = slice(k * GROUP, (k + 1) * GROUP)
        part = dot(col_grad[rows, :], w_cols[...], 1, 1)
        ng[rows, :] = part if k == 0 else ng[rows, :] + part
        part = part * (tok[rows, :].astype(F32) * inv[rows, :])
        gain_grad[:, mine_lanes] += fold(part)
        part = part * gain_mine
        sums = part[:, :LANE]
        for sl in tiles(size)[1:]:
            sums = sums + part[:, sl]
        row_buf[:, rows] += row_dots(sums)
    row_copies = [
        remote(row_buf, row_held.at[k], row_s.at[k], row_r.at[k], target)
        for k, target in enumerate(group)
    ]
    for copy in row_copies:
        copy.start()

    for k in range(D // LANE):
        gain_refs[0][k : k + 1, :] = add_up(gain_grad[:, k * LANE : (k + 1) * LANE])
    gain_sum.start()

    for side in (0, 1):
        f_first(side).wait()
        nxt[side] = (mid[side] + got[side, :, size:].astype(F32)).astype(BF16)
        f_second(side).start()
        early[side] += got[side, :, :size].astype(F32)

    product(s, lambda rows: col_grad[rows, own_lanes], col_own)

    gain_sum.after_core()
    if in_line:
        for side in (0, 1):
            z_first(side).wait()
            z_on[side] = (
                z_block(first[1 - side], side) + z_got[side, block:, :].astype(F32)
            ).astype(BF16)
            z_second(side).start()
    col_core_copy.wait()
    col_own[...] = col_own[...] + col_core[...]
    if in_line:
        col_out[:block, :] = col_own[block_rows(first[0]), :]
        col_out[block:, :] = col_own[block_rows(across), :]
        col_first().start()

    gain_sum.after_pieces()
    if in_line:
        col_first().wait()
        col_on[...] = col_own[block_rows(first[1]), :] + col_got[block:, :]
        col_second().start()

    loads[5].wait()
    for copy in row_copies:
        copy.wait()
    for side in (0, 1):
        f_second(side).wait()
        early[side] += last[side].astype(F32)
        at = steps - END + side * tail_half
        ng[at : at + tail_half, :] += early[side, half:, :]
        ng[side * half : (side + 1) * half, :] += early[side, :half, :]
    row_total = row_buf[...] + row_held[0] + row_held[1] + row_held[2]
    for k in range(steps // LANE):
        rows = slice(k * LANE, (k + 1) * LANE)
        row_dot = jnp.broadcast_to(row_total[0:1, rows] * (1.0 / D), (LANE, LANE)).T
        scale = inv[rows, :]
        for sl in tiles(size):
            z_tile = tok[rows, sl].astype(F32) * scale
            change = scale * (ng[rows, sl] * gain_mine[:, sl] - z_tile * row_dot)
            tokens_out[rows, sl] = (back[rows, sl].astype(F32) + change).astype(BF16)

    if in_line:
        for side in (0, 1):
            z_second(side).wait()
            value_out[:, side * side_w : (side + 1) * side_w] = (
                z_block(c, side) + z_got[side, :block, :].astype(F32) + z_last[side].astype(F32)
            )
        col_second().wait()
        cols_out[...] = col_own[block_rows(c), :] + col_got[:block, :] + col_last[...]
    else:
        value_out[...] = both[...]
        cols_out[...] = col_own[...]
    pack_sum.finish()
    pack_out[...] = pack_refs[5][...]
    gain_sum.finish()
    gain_out[...] = gain_refs[5][...]


def run_tail(
    grad_b, grad_v, normed, weight, tok, back, late, w_group, raw_t, fixed, gate_grad, inv, gain,
    sel_bc, sel_raw, late_rows, late_gain, *small,
):
    n = lax.axis_size("context")
    steps, width = grad_v.shape
    size = D // 4
    half_d = D // 2
    block = half_d // n
    side_rows = (GROUP + END) // 2
    share = steps // 4
    top = lambda w: pl.BlockSpec((GROUP, w), lambda i: (0, 0), pipeline_mode=pl.Buffered(1))
    end = lambda w: pl.BlockSpec(
        (END, w), lambda i: (steps // END - 1, 0), pipeline_mode=pl.Buffered(1)
    )
    full = lambda x: once(*x.shape)
    hbm = pl.BlockSpec(memory_space=pl.ANY)
    dma = pltpu.SemaphoreType.DMA
    vmem = pltpu.VMEM
    value_rows = block if n == 4 else half_d
    pair = (2, side_rows, size)
    packed = (PACK, width + 2 * N)
    return pl.pallas_call(
        functools.partial(tail_kernel, n),
        grid=(1,),
        in_specs=[hbm] * 8
        + [full(raw_t), full(fixed), top(width), end(width), top(D), end(D)]
        + [full(x) for x in (inv, gain, sel_bc, sel_raw)]
        + [full(x) for x in (late_rows, late_gain, *small)],
        out_specs=[
            once(steps, size), once(value_rows, width), once(value_rows, LANE), once(4, *packed),
            once(4, 16, LANE),
        ],
        out_shape=[
            shape(steps, size, dtype=BF16), shape(value_rows, width), shape(value_rows, LANE),
            shape(4, *packed), shape(4, 16, LANE),
        ],
        scratch_shapes=[
            vmem((steps, 2 * N), F32), vmem((steps, width), BF16), vmem(normed.shape, BF16),
            vmem(weight.shape, BF16), vmem((steps, size), BF16), vmem((steps, size), BF16),
            vmem((size, w_group.shape[1]), BF16),
            vmem((steps, w_group.shape[1]), BF16),
            vmem((half_d, width), F32), vmem((half_d, width), F32), vmem((half_d, width), F32),
            vmem((2, 2, share, N), F32), vmem((2, share, N), F32), vmem((2, share, N), F32),
            vmem((steps, 2 * N), BF16), vmem((4, 16, steps), BF16),
            vmem(pair, F32), vmem(pair, F32), vmem((2, side_rows, 2 * size), BF16),
            vmem((2, side_rows, 2 * size), BF16), vmem(pair, BF16), vmem(pair, BF16), vmem((8, D), F32),
            vmem((2, 2 * block, width // 2), BF16), vmem((2, 2 * block, width // 2), BF16),
            vmem((2, block, width // 2), BF16), vmem((2, block, width // 2), BF16),
            vmem((steps, size), F32),
            vmem((half_d, LANE), F32), vmem((half_d, LANE), F32), vmem((half_d, LANE), F32),
            vmem((2 * block, LANE), F32), vmem((2 * block, LANE), F32), vmem((block, LANE), F32),
            vmem((block, LANE), F32),
            vmem((8, steps), F32), vmem((3, 8, steps), F32),
            *[
                vmem((*lead, *dims), F32)
                for dims in (packed, (16, LANE))
                for lead in ((), (), (), (n,), (), (4,))
            ],
            dma((8,)), dma((3,)), dma((3,)), dma((2, 6)), dma((2, 6)), dma((4,)), dma((4,)),
            dma((2,)), dma((2,)), dma((6,)), dma((6,)), dma((3,)), dma((3,)),
            *[dma, dma, dma((n - 1,)), dma((n - 1,)), dma((3,)), dma((3,))] * 2,
        ],
        compiler_params=pltpu.CompilerParams(
            dimension_semantics=("arbitrary",), vmem_limit_bytes=56 * 1024 * 1024,
            collective_id=5, has_side_effects=True,
        ),
        cost_estimate=estimate(50),
        name="tail",
    )(
        grad_b, grad_v, normed, weight, tok, back, late, w_group,
        raw_t, fixed, gate_grad, gate_grad, tok, tok, inv, gain, sel_bc, sel_raw,
        late_rows, late_gain, *small,
    )


def pad_rows(x, rows=8):
    return jnp.concatenate([x, jnp.zeros((rows - x.shape[0], x.shape[1]), x.dtype)], axis=0)


def pad_cols(x, cols=LANE):
    return jnp.concatenate([x, jnp.zeros((x.shape[0], cols - x.shape[1]), x.dtype)], axis=1)


def on_device(
    tokens, cotangent, doc_lengths, zx_weight, bcdt_weight, out_weight, input_gain, chan_params,
    bc_params, head_params, zx_first, bcdt_first, out_first, gain_first, chan_first, bc_first,
    head_first, zx_second, bcdt_second, out_second, gain_second, chan_second, bc_second, head_second,
):
    n_tensor = lax.axis_size("tensor")
    t_index = lax.axis_index("tensor")
    c_index = lax.axis_index("context")
    tok = tokens[0]
    resid = tok.astype(F32)
    back = cotangent[0]
    steps = resid.shape[0]
    inner_loc = INNER // n_tensor
    heads_loc = H // n_tensor
    share = D // n_tensor
    count = steps // L
    rows_loc = zx_weight.shape[0]
    cols_loc = bcdt_weight.shape[1]

    proj_w, cols_z = line_gather(zx_weight, bcdt_weight.T)
    down_block, _ = lax.optimization_barrier((out_weight.astype(BF16).T, proj_w))
    down_t = lax.all_gather(down_block, ("shard", "context"), axis=0, tiled=True)
    chan_loc = lax.dynamic_slice_in_dim(chan_params, t_index * inner_loc, inner_loc, 1)
    head_loc = lax.dynamic_slice_in_dim(head_params, t_index * heads_loc, heads_loc, 1)
    chan8, bc8 = chan_loc, bc_params
    head8 = pad_rows(pad_cols(head_loc))
    spread_at = np.arange(2 * LANE)[:, None] % LANE == np.arange(inner_loc)[None, :] // P_SIZE
    expand = spread_at.astype(ml_dtypes.bfloat16)
    gain8 = jnp.broadcast_to(input_gain[None], (8, D))
    (
        normed, inv_rms, projected, cols, info, marks_rows, edge_mask,
        act, delta, cum, sloc, pfx, final, halo_v, halo_b,
    ) = run_project(
        doc_lengths, tok, gain8, proj_w, cols_z, chan8, bc8, head8, expand, heads_loc, cols_loc
    )
    entry, back_scaled = run_entry(final, back, down_t)
    ssd, sums = run_ahead(
        act, delta, cum, info, marks_rows, sloc, pfx, entry, projected, back_scaled, chan8, head8,
        expand, heads_loc,
    )
    scaled, *out_fan = run_out(ssd, projected, sums, chan8, down_t)
    gate_grad, mixed_grad, aloc, sfx, first_adj, norm_gain_grad = run_norm(
        ssd, projected, back_scaled, sums, act, cum, info, chan8, expand, heads_loc
    )
    later, out_own, out_next, *z_arrays = run_middle(
        first_adj, out_fan, normed, gate_grad, back, scaled
    )
    in_line = lax.axis_size("context") == 4
    total_width = inner_loc + 2 * N

    (
        grad_v, grad_b, raw_t, last_rows, _, taps_grad, bias_grad, skip_grad, head_grad,
        ng_late, late_rows, late_gain, out_last, *z_sum,
    ) = run_grand(
        projected, cols, halo_v, halo_b, info, marks_rows, delta, cum, ssd, mixed_grad,
        sloc, pfx, entry, aloc, sfx, later, chan8, bc8, head8, expand, heads_loc,
        gate_grad, proj_w, tok, inv_rms, gain8, edge_mask, out_next, z_arrays if in_line else [],
    )
    if in_line:
        pair_g = z_sum[0]
    else:
        pair_g = jnp.stack(
            [lax.psum_scatter(z_arrays[0][k], "context", scatter_dimension=0, tiled=True) for k in (0, 1)]
        )
    column = np.arange(4 * LANE)
    column = np.where(column % LANE < cols_loc, column // LANE * cols_loc + column % LANE, -1)[None, :]
    sel_bc = (np.arange(2 * N)[:, None] == column).astype(ml_dtypes.bfloat16)
    slot = np.arange(4 * 16)[:, None]
    of_slot = np.where(slot % 16 < heads_loc, 2 * N + slot // 16 * heads_loc + slot % 16, -2)
    sel_raw = (of_slot == column).astype(ml_dtypes.bfloat16)
    tokens_grad, value_g, cols_g, packed, packed_gain = run_tail(
        grad_b, grad_v, normed, proj_w, tok, back, ng_late, cols_z, raw_t, last_rows, gate_grad,
        inv_rms, gain8, sel_bc, sel_raw, late_rows, late_gain,
        taps_grad, bias_grad, norm_gain_grad, skip_grad, head_grad,
    )
    tokens_grad = tokens_grad[None]
    if not in_line:
        value_g = lax.psum_scatter(value_g, "context", scatter_dimension=0, tiled=True)
        cols_g = lax.psum_scatter(cols_g[:, :cols_loc], "context", scatter_dimension=0, tiled=True)
        cols_g = pad_cols(cols_g)
    flip = lambda *arrays: tuple(a.T for a in arrays)
    lift = lambda *arrays: tuple(a.reshape(D // LANE, LANE) for a in arrays)
    news = run_adam(
        pair_g, value_g, cols_g, packed, packed_gain, tok, out_own, out_last, t_index,
        (
            (zx_weight, zx_first, zx_second), flip(out_weight, out_first, out_second),
            flip(bcdt_weight, bcdt_first, bcdt_second), lift(input_gain, gain_first, gain_second),
            (chan_params, chan_first, chan_second), (bc_params, bc_first, bc_second),
            (head_params, head_first, head_second),
        ),
        heads_loc, cols_loc,
    )
    zx_new, out_new, bcdt_new, gain_new = news[:3], flip(*news[3:6]), flip(*news[6:9]), news[9:12]
    block_out = news[21][None]
    return (
        block_out, tokens_grad, *zx_new, *bcdt_new, *out_new, *[g.reshape(D) for g in gain_new], *news[12:21]
    )


def solution(mesh):
    big = P(("shard", "context"), None, "tensor")
    cols = P(("shard", "context"), "tensor")
    down = P("tensor", ("shard", "context"))
    rows = P("shard", "context", None)
    out_rows = P("shard", "context", "tensor")
    return jax.shard_map(
        on_device,
        mesh=mesh,
        in_specs=(
            rows, rows, P("shard", None), big, cols, down, P(), P(), P(), P(),
            big, cols, down, P(), P(), P(), P(),
            big, cols, down, P(), P(), P(), P(),
        ),
        out_specs=(
            out_rows, out_rows, big, big, big, cols, cols, cols, down, down, down,
            *([P()] * 12),
        ),
        check_vma=False,
    )
```

```python
import functools

import jax
import jax.numpy as jnp
import ml_dtypes
import numpy as np
from jax import lax
from jax.experimental import pallas as pl
from jax.experimental.pallas import tpu as pltpu
from jax.sharding import PartitionSpec as P

D = 1536
INNER = 3072
H = 48
P_SIZE = 64
N = 128
KERNEL = 4
STEP = 10

EPS = 1e-05
BETA_ONE = 0.9
BETA_TWO = 0.999
ADAM_EPS = 1e-08
DECAY = 0.1
RATE_MATRIX = 0.05
RATE_SMALL = 0.2

L = 128
LANE = 128
GROUP = 4 * L
PART = 2 * L
END = 32
LOG2E = 1.4426950408889634
F32 = jnp.float32
BF16 = jnp.bfloat16
VMEM_LIMIT = 58 * 1024 * 1024


def from_behind(block, axis, distance):
    devices = range(lax.axis_size(axis))
    route = [(i - distance, i) for i in devices if i - distance in devices]
    return lax.ppermute(block, axis, route)


def adamw(weight, grad, first, second, rate, decay):
    first_new = BETA_ONE * first + (1.0 - BETA_ONE) * grad
    second_new = BETA_TWO * second + (1.0 - BETA_TWO) * grad * grad
    scale_one = 1.0 - BETA_ONE**STEP
    scale_two = 1.0 - BETA_TWO**STEP
    update = first_new / scale_one / (jnp.sqrt(second_new / scale_two) + ADAM_EPS)
    return (weight - rate * (update + decay * weight), first_new, second_new)


def two(x):
    hi = x.astype(BF16)
    return hi, (x - hi.astype(F32)).astype(BF16)


def dot(a, b, ca=1, cb=0):
    return lax.dot_general(a, b, (((ca,), (cb,)), ((), ())), preferred_element_type=F32)


def dot3(a, b, ca=1, cb=0):
    ah, al = two(a)
    bh, bl = two(b)
    return dot(
        jnp.concatenate([ah, al, ah], axis=ca), jnp.concatenate([bh, bh, bl], axis=cb), ca, cb
    )


def over_rows(left, lanes, right):
    total = None
    for at in range(0, left.shape[0], GROUP):
        rows = slice(at, at + GROUP)
        part = dot(left[rows, lanes], right(rows), 0, 0)
        total = part if total is None else total + part
    return total


def tri_sum(tri, x):
    hi = x.astype(BF16)
    rest = x - hi.astype(F32)
    mid = rest.astype(BF16)
    low = (rest - mid.astype(F32)).astype(BF16)
    out = dot(tri, jnp.concatenate([hi, mid, low], axis=1))
    w = x.shape[1]
    return out[:, :w] + out[:, w : 2 * w] + out[:, 2 * w :]


def spread(x, e_ref):
    hi, lo = two(x)
    return dot(jnp.concatenate([hi, lo], axis=1), e_ref[...])


def per_head(x, e_ref):
    hi, lo = two(x)
    e = e_ref[:LANE, :]
    return dot(hi, e, 1, 1) + dot(lo, e, 1, 1)


def sigmoid(x):
    return 1.0 / (1.0 + jnp.exp(-x))


def softplus(x):
    return jnp.maximum(x, 0.0) + jnp.log1p(jnp.exp(-jnp.abs(x)))


def tiles(width):
    return [slice(k, k + LANE) for k in range(0, width, LANE)]


def fold(x):
    return jnp.sum(x.reshape(x.shape[0] // 8, 8, x.shape[1]), axis=0)


def lower_mask():
    row = lax.broadcasted_iota(jnp.int32, (L, L), 0)
    col = lax.broadcasted_iota(jnp.int32, (L, L), 1)
    return row >= col


def keep_mask(info, marks_row):
    return jnp.logical_and(lower_mask(), info[:, 5:6] == marks_row[0:1, :])


def decay_of(keep, cum, cum_t, h):
    return jnp.exp2(jnp.where(keep, cum[:, h : h + 1] - cum_t[h : h + 1, :], -1e30))


def load_ext(ext_ref, cur_ref, prev_ref, halo_ref, j, first):
    if j > 0:
        ext_ref[0:8, :] = cur_ref[j * L - 8 : j * L, :]
    else:

        @pl.when(first)
        def _():
            ext_ref[0:8, :] = halo_ref[...]

        @pl.when(jnp.logical_not(first))
        def _():
            ext_ref[0:8, :] = prev_ref[...]

    ext_ref[8 : 8 + L, :] = cur_ref[j * L : (j + 1) * L, :]


def rows_of_chunk(ref, j):
    return ref.at[pl.ds(pl.multiple_of(j * L, L), L), :]


def lead_of_chunk(ref, j):
    return ref.at[pl.ds(j, 1)]


def load_ext_of(ext_ref, cur_ref, prev_ref, halo_ref, j, first):
    @pl.when(first)
    def _():
        ext_ref[0:8, :] = halo_ref[...]

    @pl.when(jnp.logical_and(j == 0, jnp.logical_not(first)))
    def _():
        ext_ref[0:8, :] = prev_ref[...]

    @pl.when(j > 0)
    def _():
        ext_ref[0:8, :] = cur_ref[pl.ds(pl.multiple_of(jnp.maximum(j * L - 8, 0), 8), 8), :]

    ext_ref[8 : 8 + L, :] = cur_ref[pl.ds(pl.multiple_of(j * L, L), L), :]


def rows_at(ref, j):
    return ref.at[j * L : (j + 1) * L, :]


def lead_at(ref, j):
    return ref.at[j : j + 1]


def conv_tile(ext_ref, info, taps, sl):
    shifted = []
    total = jnp.broadcast_to(taps[KERNEL : KERNEL + 1, :], (L, LANE))
    for k in range(KERNEL):
        val = ext_ref[pl.ds(8 - KERNEL + 1 + k, L), sl]
        if k < KERNEL - 1:
            val = val * info[:, k : k + 1]
        shifted.append(val)
        total = total + taps[k : k + 1, :] * val
    return shifted, total


def prep_chunk(
    bc, info_ref, chan, bcpar, head, e_ref, act, delta_ref, cum_ref, sloc, pfx, ext_v, ext_b, state, prod
):
    info = info_ref[...]
    width = ext_v.shape[1]
    for sl in tiles(width):
        _, total = conv_tile(ext_v, info, chan[:, sl], sl)
        act[:, sl] = total * sigmoid(total)
    for sl in tiles(2 * N):
        _, total = conv_tile(ext_b, info, bcpar[:, sl], sl)
        act[:, slice(width + sl.start, width + sl.stop)] = total * sigmoid(total)
    raw = bc[:, 2 * N : 3 * N]
    delta = softplus(raw + head[0:1, :])
    dlog = -delta * (jnp.exp(head[1:2, :]) * LOG2E)
    tri = jnp.where(lower_mask(), 1.0, 0.0).astype(BF16)
    cum = tri_sum(tri, dlog)
    delta_ref[...] = delta
    cum_ref[...] = cum
    sloc[0] = state[...]
    pfx[0] = prod[...]
    last = cum[L - 1 : L, :]
    tail = info[:, 4:5] * jnp.exp2(last - cum) * delta
    through = spread(
        jnp.broadcast_to(info[L - 1 : L, 3:4] * jnp.exp2(last), (8, LANE)), e_ref
    )
    weights = spread(tail, e_ref)
    tail_u = act[:, :width] * weights
    fresh = dot3(act[:, width : width + N], tail_u, 0, 0)
    state[...] = state[...] * through[0:1, :] + fresh
    prod[...] = prod[...] * through


def row_block(width, col=0, rows=GROUP):
    return pl.BlockSpec((rows, width), lambda i: (i, col))


def prev_block(width, col=0, rows=GROUP):
    return pl.BlockSpec((8, width), lambda i: (jnp.maximum(i * (rows // 8) - 1, 0), col))


def lead_block(*dims, rows=GROUP):
    return pl.BlockSpec((rows // L, *dims), lambda i: (i, 0, 0))


def whole(*shape):
    return pl.BlockSpec(shape, lambda i: (0,) * len(shape))


def once(*shape):
    return pl.BlockSpec(shape, lambda i: (0,) * len(shape), pipeline_mode=pl.Buffered(1))


def estimate(us):
    return pl.CostEstimate(flops=int(us * 1.1e9), bytes_accessed=int(us * 1e6), transcendentals=0)


def params(**kw):
    return pltpu.CompilerParams(
        dimension_semantics=("arbitrary",), vmem_limit_bytes=VMEM_LIMIT, **kw
    )


def shape(*dims, dtype=F32):
    return jax.ShapeDtypeStruct(dims, dtype)


def ahead_kernel(
    heads, act, delta, cum, info, marks, sloc, pfx, entry, gate, back, chan, head, e_ref, ssd, sums,
    mine, held, send, recv,
):
    i = pl.program_id(0)
    s, c, t = lax.axis_index("shard"), lax.axis_index("context"), lax.axis_index("tensor")
    group = [(s, c, lax.rem(t + k, 4)) for k in (1, 2, 3)]

    @pl.when(i == 0)
    def _():
        pl.semaphore_wait(greet(group), 3)

    chunks = act.shape[0] // L
    for j in range(act.shape[0] // L):
        ahead_chunk(
            rows_at(act, j), rows_at(delta, j), rows_at(cum, j), rows_at(info, j), lead_at(marks, j),
            lead_at(sloc, j), lead_at(pfx, j), entry, rows_at(gate, j), rows_at(back, j), chan, head,
            e_ref, rows_at(ssd, j), mine.at[pl.ds(i * chunks + j, 1)],
        )

    @pl.when(i == pl.num_programs(0) - 1)
    def _():
        copies = [
            remote(mine, held.at[k], send.at[k], recv.at[k], target) for k, target in enumerate(group)
        ]
        for copy in copies:
            copy.start()
        total = mine[...]
        for k, copy in enumerate(copies):
            copy.wait()
            total = total + held[k]
        sums[...] = total


def ahead_chunk(
    act, delta_ref, cum_ref, info_ref, marks_ref, sloc, pfx, entry, gate, back, chan, head, e_ref, ssd, sums
):
    width = act.shape[1] - 2 * N
    info = info_ref[...]
    cum = cum_ref[...]
    cum_t = cum.T
    keep = keep_mask(info, marks_ref[0])
    bmat = act[:, width : width + N]
    cmat = act[:, width + N :]
    scores = dot3(cmat, bmat, 1, 1)
    xs = act[:, :width]
    u_hi, u_lo = two(xs * spread(delta_ref[...], e_ref))
    state = sloc[0] + entry[...] * pfx[0, 0:1, :]
    entering = dot3(cmat, state)
    eexp = spread(info[:, 3:4] * jnp.exp2(cum), e_ref)
    skip = spread(jnp.broadcast_to(head[2:3, :], (8, LANE)), e_ref)
    lane = lax.broadcasted_iota(jnp.int32, (1, LANE), 1)
    left = jnp.where(lane < P_SIZE, 1.0, 0.0).astype(BF16)
    right = jnp.where(lane < P_SIZE, 0.0, 1.0).astype(BF16)
    square = jnp.zeros((L, LANE), F32)
    cross = jnp.zeros((L, LANE), F32)
    for q, sl in enumerate(tiles(width)):
        mix = jnp.concatenate(
            [(scores * decay_of(keep, cum, cum_t, 2 * q + r)).astype(BF16) for r in (0, 1)], axis=1
        )
        both = jnp.concatenate([u_hi[:, sl], u_lo[:, sl]], axis=1)
        rhs = jnp.concatenate(
            [both * jnp.concatenate([m, m], axis=1) for m in (left, right)], axis=0
        )
        out = dot(mix, rhs)
        y = out[:, :LANE] + out[:, LANE:] + entering[:, sl] * eexp[:, sl]
        y = y + skip[0:1, sl] * xs[:, sl]
        ssd[:, sl] = y
        g = gate[:, sl]
        gated = y * g * sigmoid(g)
        square = square + gated * gated
        cross = cross + gated * (back[:, sl] * chan[KERNEL + 1 : KERNEL + 2, sl])
    ones = jnp.ones((8, LANE), BF16)
    rows = []
    for part in (square, cross):
        hi, lo = two(part)
        rows.append(dot(ones, hi, 1, 1) + dot(ones, lo, 1, 1))
    pick = lax.broadcasted_iota(jnp.int32, (8, LANE), 0)
    sums[0] = jnp.where(pick == 0, rows[0], jnp.where(pick == 1, rows[1], 0.0))


def run_ahead(act, delta, cum, info, marks, sloc, pfx, entry, projected, back, chan, head, expand, heads):
    steps, width = projected.shape[0], projected.shape[1] // 2
    count = steps // L
    return pl.pallas_call(
        functools.partial(ahead_kernel, heads),
        grid=(steps // GROUP,),
        in_specs=[
            row_block(width + 2 * N), row_block(LANE), row_block(LANE), row_block(LANE),
            lead_block(8, L), lead_block(N, width), lead_block(8, width),
            once(N, width), row_block(width, 0), row_block(width),
            once(KERNEL + 2, width), once(8, LANE), once(2 * LANE, width),
        ],
        out_specs=[row_block(width), once(count, 8, L)],
        out_shape=[shape(steps, width), shape(count, 8, L)],
        scratch_shapes=[
            pltpu.VMEM((count, 8, L), F32), pltpu.VMEM((3, count, 8, L), F32),
            pltpu.SemaphoreType.DMA((3,)), pltpu.SemaphoreType.DMA((3,)),
        ],
        compiler_params=params(collective_id=1, has_side_effects=True),
        cost_estimate=estimate(20),
        name="ahead",
    )(act, delta, cum, info, marks, sloc, pfx, entry, projected, back, chan, head, expand)


def norm_kernel(
    heads, ssd, gate, back, sums, cmat, cum, info, chan, e_ref,
    gate_grad, mixed_grad, aloc, sfx, fin, gain_grad, state, prod,
):
    i = pl.program_id(0)

    @pl.when(i == 0)
    def _():
        state[...] = jnp.zeros_like(state)
        prod[...] = jnp.ones_like(prod)
        gain_grad[...] = jnp.zeros_like(gain_grad)

    chunks = ssd.shape[0] // L

    for j in reversed(range(chunks)):
        norm_chunk(
            rows_at(ssd, j), rows_at(gate, j), rows_at(back, j), lead_at(sums, j), rows_at(cmat, j),
            rows_at(cum, j), rows_at(info, j), chan, e_ref, rows_at(gate_grad, j),
            rows_at(mixed_grad, j), lead_at(aloc, j), lead_at(sfx, j), gain_grad, state, prod,
        )

    @pl.when(i == pl.num_programs(0) - 1)
    def _():
        fin[:N, :] = state[...]
        fin[N:, :] = prod[...]


def norm_chunk(
    ssd, gate, back, sums, cmat_ref, cum_ref, info_ref, chan, e_ref,
    gate_grad, mixed_grad, aloc, sfx, gain_grad, state, prod,
):
    width = ssd.shape[1]
    rows = sums[0]
    inv_row = lax.rsqrt(rows[0:1, :] / INNER + EPS)
    cross_row = inv_row * inv_row * inv_row * (rows[1:2, :] / INNER)
    inv = jnp.broadcast_to(inv_row, (LANE, L)).T
    cross = jnp.broadcast_to(cross_row, (LANE, L)).T
    info = info_ref[...]
    cum = cum_ref[...]
    eexp = spread(info[:, 3:4] * jnp.exp2(cum), e_ref)
    e_mixed = []
    for sl in tiles(width):
        g = gate[:, sl]
        sig = sigmoid(g)
        soft = g * sig
        y = ssd[:, sl]
        gated = y * soft
        bs = back[:, sl]
        gain = chan[KERNEL + 1 : KERNEL + 2, sl]
        normed = gated * inv
        gain_grad[:, sl] += fold(bs * normed)
        gg = inv * (bs * gain) - gated * cross
        mg = gg * soft
        mixed_grad[:, sl] = mg
        gate_grad[:, sl] = (gg * y * sig * (1.0 + g * (1.0 - sig))).astype(BF16)
        e_mixed.append(mg * eexp[:, sl])
    aloc[0] = state[...]
    sfx[0] = prod[...]
    through = spread(
        jnp.broadcast_to(info[L - 1 : L, 3:4] * jnp.exp2(cum[L - 1 : L, :]), (8, LANE)), e_ref
    )
    fresh = dot3(cmat_ref[...], jnp.concatenate(e_mixed, axis=1), 0, 0)
    state[...] = state[...] * through[0:1, :] + fresh
    prod[...] = prod[...] * through


def run_norm(ssd, projected, back, sums, act, cum, info, chan, expand, heads):
    steps, width = ssd.shape
    count = steps // L
    blocks = steps // GROUP
    turn = lambda spec: pl.BlockSpec(
        spec.block_shape, lambda i, m=spec.index_map: m(blocks - 1 - i)
    )
    c_col = width // N + 1
    return pl.pallas_call(
        functools.partial(norm_kernel, heads),
        grid=(blocks,),
        in_specs=[
            turn(row_block(width)), turn(row_block(width, 0)), turn(row_block(width)),
            turn(lead_block(8, L)),
            turn(row_block(N, c_col)), turn(row_block(LANE)), turn(row_block(LANE)),
            once(KERNEL + 2, width), once(2 * LANE, width),
        ],
        out_specs=[
            turn(row_block(width)), turn(row_block(width)),
            turn(lead_block(N, width)),
            turn(lead_block(8, width)),
            whole(N + 8, width), whole(8, width),
        ],
        out_shape=[
            shape(steps, width, dtype=BF16), shape(steps, width),
            shape(count, N, width), shape(count, 8, width), shape(N + 8, width), shape(8, width),
        ],
        scratch_shapes=[pltpu.VMEM((N, width), F32), pltpu.VMEM((8, width), F32)],
        compiler_params=params(),
        cost_estimate=estimate(21),
        name="norm_back",
    )(ssd, projected, back, sums, act, cum, info, chan, expand)


def behind_chunk(
    heads, j, start, first, val, valp, bc, bcp, halo_v, halo_b, info_ref, marks_ref, delta_ref, cum_ref,
    ssd, mixed_grad, sloc, pfx, entry, aloc, sfx, later, chan, bcpar, head, e_ref,
    grad_v, grad_b, raw_grad, tail_rows, head_rows, taps_grad, bias_grad, skip_grad, head_grad,
    ext_v, ext_b, slope, d_tot,
):
    width = val.shape[1]
    total_width = width + 2 * N

    @pl.when(start)
    def _():
        d_tot[0:8, :] = jnp.zeros((8, total_width), F32)
        taps_grad[...] = jnp.zeros_like(taps_grad)
        bias_grad[...] = jnp.zeros_like(bias_grad)
        skip_grad[...] = jnp.zeros_like(skip_grad)
        head_grad[...] = jnp.zeros_like(head_grad)

    d_tot[L:, :] = d_tot[0:8, :]
    load_ext_of(ext_v, val, valp, halo_v, j, first)
    load_ext_of(ext_b, bc, bcp, halo_b, j, first)
    raw = bc[pl.ds(pl.multiple_of(j * L, L), L), 2 * N : 3 * N]
    info_ref, marks_ref = rows_of_chunk(info_ref, j), lead_of_chunk(marks_ref, j)
    delta_ref, cum_ref = rows_of_chunk(delta_ref, j), rows_of_chunk(cum_ref, j)
    ssd, mixed_grad = rows_of_chunk(ssd, j), rows_of_chunk(mixed_grad, j)
    sloc, pfx = lead_of_chunk(sloc, j), lead_of_chunk(pfx, j)
    aloc, sfx = lead_of_chunk(aloc, j), lead_of_chunk(sfx, j)
    grad_v, grad_b = rows_of_chunk(grad_v, j), rows_of_chunk(grad_b, j)
    raw_grad = raw_grad.at[:, pl.ds(pl.multiple_of(j * L, L), L)]
    info = info_ref[...]

    def activate(ext_ref, taps, sl, at):
        _, total = conv_tile(ext_ref, info, taps[:, sl], sl)
        sig = sigmoid(total)
        slope[:, slice(at, at + LANE)] = sig * (1.0 + total * (1.0 - sig))
        return total * sig

    xs = jnp.concatenate([activate(ext_v, chan, sl, sl.start) for sl in tiles(width)], axis=1)
    bmat = activate(ext_b, bcpar, slice(0, N), width)
    cmat = activate(ext_b, bcpar, slice(N, 2 * N), width + N)

    delta = delta_ref[...]
    cum = cum_ref[...]
    cum_t = cum.T
    keep = keep_mask(info, marks_ref[0])
    last = cum[L - 1 : L, :]
    scores = dot3(cmat, bmat, 1, 1)
    dexp = spread(delta, e_ref)
    eexp = spread(info[:, 3:4] * jnp.exp2(cum), e_ref)
    texp = spread(info[:, 4:5] * jnp.exp2(last - cum), e_ref)
    u = xs * dexp
    u_hi, u_lo = two(u)
    dy = mixed_grad[...]
    dy_hi, dy_lo = two(dy)
    skip = spread(jnp.broadcast_to(head[2:3, :], (8, LANE)), e_ref)
    state = sloc[0] + entry[...] * pfx[0, 0:1, :]
    adj = aloc[0] + later[...] * sfx[0, 0:1, :]
    tail_du = dot3(bmat, adj) * texp
    lane = lax.broadcasted_iota(jnp.int32, (1, LANE), 1)
    left = jnp.where(lane < P_SIZE, 1.0, 0.0).astype(BF16)
    right = jnp.where(lane < P_SIZE, 0.0, 1.0).astype(BF16)
    two_left = jnp.concatenate([left, left], axis=1)
    two_right = jnp.concatenate([right, right], axis=1)
    d_scores = jnp.zeros((L, L), F32)
    inner_du = []
    for q, sl in enumerate(tiles(width)):
        decays = [decay_of(keep, cum, cum_t, 2 * q + r) for r in (0, 1)]
        mix = jnp.concatenate([(scores * d).astype(BF16) for d in decays], axis=0)
        dy_both = jnp.concatenate([dy_hi[:, sl], dy_lo[:, sl]], axis=1)
        rhs = jnp.concatenate([dy_both * two_left, dy_both * two_right], axis=0)
        out = dot(mix, rhs, 0, 0)
        inner_du.append(out[:, :LANE] + out[:, LANE:])
        u_twice = jnp.concatenate([u_hi[:, sl], u_hi[:, sl]], axis=1)
        u_rows = jnp.concatenate([u_twice * two_left, u_twice * two_right], axis=0)
        d_mix = dot(dy_both, u_rows, 1, 1)
        d_scores = d_scores + d_mix[:, :L] * decays[0] + d_mix[:, L:] * decays[1]
    du = jnp.concatenate(inner_du, axis=1) + tail_du
    d_xs = dexp * du + skip[0:1, :] * dy
    d_b = dot3(d_scores, cmat, 0, 0) + dot3(u * texp, adj, 1, 1)
    d_c = dot3(d_scores, bmat) + dot3(dy * eexp, state, 1, 1)
    skip_grad[...] += fold(dy * xs)

    direct = per_head(xs * du, e_ref)
    mixed = ssd[...] - skip[0:1, :] * xs
    d_cum = per_head(dy * mixed, e_ref) - delta * direct
    at_last = jnp.sum(per_head(u * tail_du, e_ref), axis=0, keepdims=True)
    through = info[L - 1 : L, 3:4] * jnp.exp2(last)
    pair = per_head(fold(adj * state), e_ref)
    at_last = at_last + through * jnp.sum(pair, axis=0, keepdims=True)
    upper = jnp.where(lower_mask(), 1.0, 0.0).astype(BF16).T
    d_log = tri_sum(upper, d_cum) + at_last
    rate = jnp.exp(head[1:2, :])
    valid = lane < heads
    d_raw = (direct - d_log * rate) * sigmoid(raw + head[0:1, :])
    d_raw = jnp.where(valid, d_raw, 0.0)
    raw_grad[...] = d_raw.T[:16, :].astype(BF16)
    head_grad[0:8, :] += fold(d_raw)
    head_grad[8:16, :] += fold(jnp.where(valid, -d_log * delta * rate, 0.0))

    d_act = [d_xs[:, sl] for sl in tiles(width)] + [d_b, d_c]
    for q in range(total_width // LANE):
        sl = slice(q * LANE, (q + 1) * LANE)
        if q < width // LANE:
            ext_ref, taps, part = ext_v, chan[:, sl], sl
        else:
            part = slice(sl.start - width, sl.stop - width)
            ext_ref, taps = ext_b, bcpar[:, part]
        dt = d_act[q] * slope[:, sl]
        d_tot[0:L, sl] = dt
        bias_grad[:, sl] += fold(dt)
        for k in range(KERNEL):
            moved = ext_ref[pl.ds(8 - KERNEL + 1 + k, L), part]
            if k < KERNEL - 1:
                moved = moved * info[:, k : k + 1]
            taps_grad[8 * k : 8 * k + 8, sl] += fold(dt * moved)
        total = dt * taps[KERNEL - 1 : KERNEL, :]
        for s in range(1, KERNEL):
            total = total + taps[KERNEL - 1 - s : KERNEL - s, :] * (
                d_tot[pl.ds(s, L), sl] * info[:, 7 + s : 8 + s]
            )
        if q < width // LANE:
            grad_v[:, sl] = total.astype(BF16)
        else:
            grad_b[:, part] = total

        @pl.when(start)
        def _():
            tail_rows[:, sl] = total[L - 8 :, :]

    @pl.when(first)
    def _():
        head_rows[...] = d_tot[0:8, :]


def remote(src, dst, send, recv, target):
    return pltpu.make_async_remote_copy(
        src_ref=src, dst_ref=dst, send_sem=send, recv_sem=recv, device_id=target,
        device_id_type=pl.DeviceIdType.MESH,
    )


def greet(targets):
    barrier = pltpu.get_barrier_semaphore()
    for target in targets:
        pl.semaphore_signal(
            barrier, inc=1, device_id=target, device_id_type=pl.DeviceIdType.MESH
        )
    return barrier


def count_rows(parts, z, gain, at, gain_grad):
    rows = jnp.zeros((parts[0].shape[0], LANE), F32)
    size = parts[0].shape[1]
    for part, k in zip(parts, at):
        lanes = pl.ds(pl.multiple_of(k * size, size), size)
        part = part * z(lanes)
        gain_grad[:, lanes] += fold(part)
        part = part * gain[0:1, lanes]
        for sl in tiles(size):
            rows = rows + part[:, sl]
    return rows


def row_dots(rows):
    ones = jnp.ones((8, LANE), BF16)
    hi, lo = two(rows)
    return dot(ones, hi, 1, 1) + dot(ones, lo, 1, 1)


def grand_kernel(heads, n, *refs):
    behind, refs = refs[:22], refs[22:]
    gate_grad, w_ref, tok, inv, gain, edge_mask, out_next = refs[:7]
    refs = refs[7:]
    in_line = n == 4
    if in_line:
        z_out, z_mid, z_mine = refs[:3]
        refs = refs[3:]
    outs, refs = refs[:9], refs[9:]
    ng_own, row_sums, gain_grad, out_last = refs[:4]
    refs = refs[4:]
    if in_line:
        z_sum, refs = refs[0], refs[1:]
    scratch, refs = refs[:4], refs[4:]
    mid, send, got, nxt, last, edge, s1, r1, s2, r2, edge_s, edge_r, o_s, o_r = refs[:14]
    if in_line:
        z_got, z_on, z_last, z_s, z_r = refs[14:]
    chan, bcpar = behind[18], behind[19]
    grad_v, tail_rows = outs[0], outs[3]
    d_tot = scratch[3]
    i, n_steps = pl.program_id(0), pl.num_programs(0)
    s, c, t = lax.axis_index("shard"), lax.axis_index("context"), lax.axis_index("tensor")
    near = peers(t)
    to = [(s, c, near[0]), (s, c, near[1])]
    width = grad_v.shape[1]
    size = w_ref.shape[0] // 4
    inside = mid.shape[0]
    chunks = grad_v.shape[0] // L

    @pl.when(i == 0)
    def _():
        pl.semaphore_wait(greet(to + beside_of(n)), 4)
        gain_grad[...] = jnp.zeros_like(gain_grad)

    def out_hop(side):
        return remote(
            out_next.at[side], out_last.at[side], o_s.at[side], o_r.at[side], to[1 - side]
        )

    @pl.when(i == 0)
    def _():
        for side in (0, 1):
            out_hop(side).start()

    if in_line:
        line = [(s, c + 1 - 2 * lax.rem(c, 2), t), (s, 3 - c, t)]
        block = z_mid.shape[1]

        def z_first(k):
            return remote(z_out.at[k], z_got.at[k], z_s.at[k], z_r.at[k], line[k])

        def z_second(k):
            return remote(z_on.at[k], z_last.at[k], z_s.at[2 + k], z_r.at[2 + k], line[1 - k])

        @pl.when(i == 0)
        def _():
            for k in (0, 1):
                z_first(k).start()

        @pl.when(i == n_steps // 2)
        def _():
            for k in (0, 1):
                z_first(k).wait()
                z_on[k] = (z_mid[k] + z_got[k, block:, :].astype(F32)).astype(BF16)
                z_second(k).start()
                z_sum[k] = z_mine[k] + z_got[k, :block, :].astype(F32)

        @pl.when(i == n_steps - 1)
        def _():
            for k in (0, 1):
                z_second(k).wait()
                z_sum[k] += z_last[k].astype(F32)

    def first_hop(k, side):
        return remote(send.at[k], got.at[k], s1.at[k], r1.at[k], to[side])

    def second_hop(k, side):
        return remote(nxt.at[k], last.at[k], s2.at[k], r2.at[k], to[1 - side])

    def place(k):
        return pl.ds(pl.multiple_of((inside - 1 - k) * PART, PART), PART)

    def turn_over(k, side):
        first_hop(k, side).wait()
        nxt[k] = (mid[k] + got[k, :, size:].astype(F32)).astype(BF16)
        second_hop(k, side).start()
        ng_own[place(k), :] += got[k, :, :size].astype(F32)

    def one(step, carry):
        j = chunks - 1 - step
        behind_chunk(
            heads, j, jnp.logical_and(i == 0, step == 0),
            jnp.logical_and(i == n_steps - 1, j == 0), *behind, *outs, *scratch,
        )
        for side in (0, 1):
            ready = jnp.logical_and(step == 0, lax.rem(i, 2) == 1 - side)

            @pl.when(jnp.logical_and(ready, jnp.logical_and(i >= 2, i < inside + 2)))
            def _():
                turn_over(i - 2, side)

        return carry

    lax.fori_loop(0, chunks, one, 0)

    def fan(side):
        counted = jnp.where(i == 0, PART - END, PART)
        x = jnp.concatenate([gate_grad[...], grad_v[...]], axis=1)
        keep, go = shares_of(side, t)
        gone = dot(x, pick(w_ref, *go), 1, 1)
        send[i] = gone.astype(BF16)
        first_hop(i, side).start()
        kept = dot(x, pick(w_ref, *keep), 1, 1)
        ng_own[place(i), :] = kept[:, :size]
        mid[i] = kept[:, size:]
        row = lax.broadcasted_iota(jnp.int32, (PART, 1), 0)
        scale = jnp.where(row < counted, inv[...], 0.0)
        parts = [kept[:, :size], kept[:, size:], gone[:, :size], gone[:, size:]]
        sums = count_rows(
            parts, lambda lanes: tok[:, lanes].astype(F32) * scale, gain, keep + go, gain_grad
        )
        row_sums[0] = row_dots(sums)

    for side in (0, 1):
        parity = lax.rem(i, 2) == 1 - side

        @pl.when(jnp.logical_and(parity, i < inside))
        def _():
            fan(side)

    @pl.when(i == n_steps - 1)
    def _():
        before = (s, jnp.maximum(c - 1, 0), t)
        copy = remote(d_tot.at[pl.ds(0, 8), :], edge, edge_s, edge_r, before)

        @pl.when(c > 0)
        def _():
            copy.start()

        for k in range(inside):
            second_hop(k, 1 - k % 2).wait()
            ng_own[place(k), :] += last[k].astype(F32)
        for side in (0, 1):
            out_hop(side).wait()

        @pl.when(c < n - 1)
        def _():
            copy.wait_recv()
            for shift in range(1, KERNEL):
                moved = pltpu.roll(edge[...], 8 - shift, 0) * edge_mask[
                    8 * shift - 8 : 8 * shift, 0:1
                ]
                tap = slice(KERNEL - 1 - shift, KERNEL - shift)
                tail_rows[:, :width] += chan[tap, :] * moved[:, :width]
                tail_rows[:, width:] += bcpar[tap, :] * moved[:, width:]

        @pl.when(c > 0)
        def _():
            copy.wait_send()


def run_grand(
    projected, cols, halo_v, halo_b, info, marks, delta, cum, ssd, mixed_grad, sloc, pfx, entry,
    aloc, sfx, later, chan, bcpar, head, expand, heads, gate_grad, weight, tok, inv, gain, edge_mask,
    out_next, z_arrays,
):
    steps, width = ssd.shape
    parts = steps // PART
    inside = (steps - GROUP) // PART
    size = D // 4
    turn = lambda spec: pl.BlockSpec(
        spec.block_shape, lambda i, m=spec.index_map: m(parts - 1 - i)
    )
    in_part = lambda w: pl.BlockSpec((PART, w), lambda i: (parts - 1 - i, 0))
    chunk = lead_block(N, width, rows=PART)
    few = lead_block(8, width, rows=PART)
    total = width + 2 * N
    dma = pltpu.SemaphoreType.DMA
    return pl.pallas_call(
        functools.partial(grand_kernel, heads, lax.axis_size("context")),
        grid=(parts,),
        in_specs=[
            turn(row_block(width, 1, rows=PART)), turn(prev_block(width, 1, rows=PART)),
            turn(row_block(3 * N, rows=PART)), turn(prev_block(3 * N, rows=PART)),
            once(8, width), once(8, 3 * N), turn(row_block(LANE, rows=PART)),
            turn(lead_block(8, L, rows=PART)),
            turn(row_block(LANE, rows=PART)), turn(row_block(LANE, rows=PART)), turn(row_block(width, rows=PART)), turn(row_block(width, rows=PART)),
            turn(chunk), turn(few), once(N, width), turn(chunk), turn(few), once(N, width),
            once(KERNEL + 2, width), once(KERNEL + 1, 2 * N), once(8, LANE), once(2 * LANE, width),
            turn(row_block(width, rows=PART)), once(*weight.shape), in_part(D), in_part(1), once(8, D),
            once(24, LANE), pl.BlockSpec(memory_space=pl.ANY),
        ]
        + ([pl.BlockSpec(memory_space=pl.ANY)] + [once(*z.shape) for z in z_arrays[1:]] if z_arrays else []),
        out_specs=[
            turn(row_block(width, rows=PART)), turn(row_block(2 * N, rows=PART)),
            pl.BlockSpec((16, PART), lambda i: (0, parts - 1 - i)),
            whole(8, total), whole(8, total), whole(8 * KERNEL, total), whole(8, total),
            whole(8, width), whole(16, LANE),
            once(inside * PART, size),
            pl.BlockSpec((1, 8, PART), lambda i: (parts - 1 - i, 0, 0)),
            whole(8, D), pl.BlockSpec(memory_space=pl.ANY),
        ]
        + [once(*z.shape) for z in z_arrays[1:2]],
        out_shape=[
            shape(steps, width, dtype=BF16), shape(steps, 2 * N), shape(16, steps, dtype=BF16),
            shape(8, total), shape(8, total), shape(8 * KERNEL, total), shape(8, total),
            shape(8, width), shape(16, LANE),
            shape(inside * PART, size), shape(parts, 8, PART), shape(8, D),
            shape(*out_next.shape, dtype=BF16),
        ]
        + [shape(*z.shape) for z in z_arrays[1:2]],
        scratch_shapes=[
            pltpu.VMEM((8 + L, width), F32), pltpu.VMEM((8 + L, 3 * N), F32),
            pltpu.VMEM((L, total), F32), pltpu.VMEM((L + 8, total), F32),
            pltpu.VMEM((inside, PART, size), F32),
            pltpu.VMEM((inside, PART, 2 * size), BF16), pltpu.VMEM((inside, PART, 2 * size), BF16),
            pltpu.VMEM((inside, PART, size), BF16), pltpu.VMEM((inside, PART, size), BF16),
            pltpu.VMEM((8, total), F32),
            dma((inside,)), dma((inside,)), dma((inside,)), dma((inside,)), dma, dma,
            dma((2,)), dma((2,)),
        ]
        + (
            [
                pltpu.VMEM(z_arrays[0].shape, BF16), pltpu.VMEM(z_arrays[1].shape, BF16),
                pltpu.VMEM(z_arrays[1].shape, BF16), dma((4,)), dma((4,)),
            ]
            if z_arrays
            else []
        ),
        compiler_params=pltpu.CompilerParams(
            dimension_semantics=("arbitrary",), vmem_limit_bytes=52 * 1024 * 1024,
            collective_id=4, has_side_effects=True,
        ),
        cost_estimate=estimate(90),
        name="behind",
    )(
        projected, projected, cols, cols, halo_v, halo_b, info, marks, delta, cum, ssd, mixed_grad,
        sloc, pfx, entry, aloc, sfx, later, chan, bcpar, head, expand,
        gate_grad, weight, tok, inv, gain, edge_mask, out_next, *z_arrays,
    )


def peers(t):
    return t + 1 - 2 * lax.rem(t, 2), lax.rem(t + 2, 4)


def pick(w_ref, one, other):
    size = w_ref.shape[0] // 4
    at = lambda k: pl.ds(pl.multiple_of(k * size, size), size)
    return jnp.concatenate([w_ref[at(one), :], w_ref[at(other), :]], axis=0)


def shares_of(side, t):
    near = peers(t)
    return (t, near[1 - side]), (near[side], 3 - t)


def out_kernel(
    ssd, gate, sums, chan, w_ref, scaled, own, mid, send_a, send_b,
):
    i, half = pl.program_id(0), pl.num_programs(0) // 2
    t = lax.axis_index("tensor")
    width = ssd.shape[1]
    for k in range(ssd.shape[0] // L):
        rows = slice(k * L, (k + 1) * L)
        inv = jnp.broadcast_to(lax.rsqrt(sums[k, 0:1, :] / INNER + EPS), (LANE, L)).T
        for sl in tiles(width):
            g = gate[rows, sl]
            gated = ssd[rows, sl] * g * sigmoid(g)
            scaled[rows, sl] = (gated * inv * chan[KERNEL + 1 : KERNEL + 2, sl]).astype(BF16)
    x = scaled[...]
    size = own.shape[1]

    def part(side, send):
        keep, go = shares_of(side, t)
        send[...] = dot(x, pick(w_ref, *go), 1, 1).astype(BF16)
        kept = dot(x, pick(w_ref, *keep), 1, 1)
        own[...] = kept[:, :size]
        mid[...] = kept[:, size:]

    @pl.when(i < half)
    def _():
        part(0, send_a)

    @pl.when(i >= half)
    def _():
        part(1, send_b)


def run_out(ssd, projected, sums, chan, weight):
    steps, width = ssd.shape
    block = 512
    count = steps // block
    half = count // 2
    size = D // 4
    in_block = lambda w, col=0: pl.BlockSpec((block, w), lambda i: (i, col))
    return pl.pallas_call(
        out_kernel,
        grid=(count,),
        in_specs=[
            in_block(width), in_block(width, 0),
            pl.BlockSpec((block // L, 8, L), lambda i: (i, 0, 0)),
            once(KERNEL + 2, width), once(*weight.shape),
        ],
        out_specs=[
            in_block(width), in_block(size), in_block(size),
            pl.BlockSpec((block, 2 * size), lambda i: (jnp.minimum(i, half - 1), 0)),
            pl.BlockSpec((block, 2 * size), lambda i: (jnp.maximum(i - half, 0), 0)),
        ],
        out_shape=[
            shape(steps, width, dtype=BF16), shape(steps, size), shape(steps, size),
            shape(steps // 2, 2 * size, dtype=BF16), shape(steps // 2, 2 * size, dtype=BF16),
        ],
        compiler_params=params(),
        cost_estimate=estimate(12),
        name="out",
    )(ssd, projected, sums, chan, weight)


def line_kernel(
    n, n_tensor, piece, zx_raw, cols_raw, tok_hbm, gain, lengths,
    zx_out, cols_out, normed_out, inv_out, info_out, marks_out, edge_out,
    zx_ref, cols_ref, tok, normed, inv, info, marks, edge, work_s,
    local, zx_s, zx_r, core_s, core_r, col_s, col_r, group_s, group_r, bulk_s, bulk_r,
):
    load_tok = pltpu.make_async_copy(tok_hbm, tok, work_s.at[0])
    load_tok.start()
    s, c, t = lax.axis_index("shard"), lax.axis_index("context"), lax.axis_index("tensor")
    on = (c < n - 1, c > 0)
    to = ((s, jnp.minimum(c + 1, n - 1), t), (s, jnp.maximum(c - 1, 0), t))
    to_core = (1 - s, c, t)
    to_group = [(s, c, lax.rem(t + k, n_tensor)) for k in range(1, n_tensor)]
    beside = [(s, lax.rem(c + k, n), t) for k in (1, n - 1)]
    barrier = greet([to_core] + to_group + beside)
    width = zx_raw.shape[2]
    for k in (0, 1):
        zx_ref[:, k * width : (k + 1) * width] = zx_raw[:, k, :].astype(BF16)
    gap = jnp.zeros((LANE - cols_raw.shape[0], cols_raw.shape[1]), F32)
    cols_ref[...] = jnp.concatenate([cols_raw[...], gap], axis=0).T.astype(BF16)
    pl.semaphore_wait(barrier, n_tensor + 2)
    rows, width = zx_ref.shape[0], cols_ref.shape[1]
    spans = [(at, min(piece, rows - at)) for at in range(0, rows, piece)]

    def block_of(way, hop):
        return jnp.maximum(c - hop, 0) if way == 0 else jnp.minimum(c + hop, n - 1)

    def has(way, hop):
        return c - hop >= 0 if way == 0 else c + hop <= n - 1

    def place(ref, block, at=0, size=rows):
        return ref.at[pl.ds(pl.multiple_of((s * n + block) * rows + at, 16), size), :]

    lanes = pl.ds(pl.multiple_of(t * width, LANE), width)

    def place_cols(block):
        return cols_out.at[pl.ds(pl.multiple_of((s * n + block) * rows, 16), rows), lanes]

    def zx_copy(way, step, p):
        at, size = spans[p]
        where = place(zx_out, block_of(way, step), at, size)
        src = zx_ref.at[pl.ds(at, size), :] if step == 0 else where
        return remote(src, where, zx_s.at[way, step, p], zx_r.at[way, step, p], to[way])

    def col_copy(way, step):
        where = place_cols(block_of(way, step))
        src = cols_ref if step == 0 else where
        return remote(src, where, col_s.at[way, step], col_r.at[way, step], to[way])

    def group_copies(way, hop):
        where = place_cols(block_of(way, hop))
        src = cols_ref if hop == 0 else where
        return [
            remote(src, where, group_s.at[k, way, hop], group_r.at[k, way, hop], target)
            for k, target in enumerate(to_group)
        ]

    def core_copy(way, hop, p):
        at, size = spans[p]
        where = place(zx_out, block_of(way, hop), at, size)
        src = zx_ref.at[pl.ds(at, size), :] if hop == 0 else where
        return remote(src, where, core_s.at[way, hop, p], core_r.at[way, hop, p], to_core)

    pieces = range(len(spans))
    for way in (0, 1):

        @pl.when(on[way])
        def _():
            col_copy(way, 0).start()
            for p in pieces:
                zx_copy(way, 0, p).start()

    for copy in group_copies(0, 0):
        copy.start()
    own_cols = pltpu.make_async_copy(cols_ref, place_cols(c), local.at[0])
    own_zx = pltpu.make_async_copy(zx_ref, place(zx_out, c), local.at[1])
    own_cols.start()
    own_zx.start()
    for p in pieces:
        core_copy(0, 0, p).start()
    load_tok.wait()
    steps = tok.shape[0]
    begin = c * steps

    def work(j, carry):
        x, scale = norm_rows(rows_of_chunk(tok, j)[...], gain)
        rows_of_chunk(normed, j)[...] = x
        rows_of_chunk(inv, j)[...] = scale
        mark_chunk(
            lengths, begin + j * L, begin + steps, rows_of_chunk(info, j), lead_of_chunk(marks, j)
        )
        return carry

    lax.fori_loop(0, steps // L, work, 0)
    row = lax.broadcasted_iota(jnp.int32, (24, LANE), 0)
    shift, at_row = row // 8 + 1, row % 8
    there = at_row - 8 + shift + begin + steps
    agree = doc_of(lengths, there) == doc_of(lengths, there - shift)
    edge[...] = jnp.where(jnp.logical_and(at_row >= 8 - shift, agree), 1.0, 0.0)
    stores = [
        pltpu.make_async_copy(src, dst, work_s.at[k + 1])
        for k, (src, dst) in enumerate(
            [
                (normed, normed_out), (inv, inv_out), (info, info_out), (marks, marks_out),
                (edge, edge_out),
            ]
        )
    ]
    for store in stores:
        store.start()

    start = pl.ds(pl.multiple_of(s * n * rows, 16), n * rows)
    bulk = remote(cols_out.at[start, :], cols_out.at[start, :], bulk_s, bulk_r, to_core)
    for step in range(n - 1):
        further = step < n - 2
        for way in (0, 1):

            @pl.when(has(way, step + 1))
            def _():
                col_copy(way, step).wait_recv()
                for copy in group_copies(way, step + 1):
                    copy.start()
                if further:

                    @pl.when(on[way])
                    def _():
                        col_copy(way, step + 1).start()

        if not further:
            own_cols.wait()
            for copy in group_copies(0, 0):
                copy.wait()
            for hop in range(1, n):
                for way in (0, 1):

                    @pl.when(has(way, hop))
                    def _():
                        for copy in group_copies(way, hop):
                            copy.wait()

            bulk.start()
        for p in pieces:
            for way in (0, 1):

                @pl.when(has(way, step + 1))
                def _():
                    zx_copy(way, step, p).wait_recv()
                    core_copy(way, step + 1, p).start()
                    if further:

                        @pl.when(on[way])
                        def _():
                            zx_copy(way, step + 1, p).start()

    for step in range(n - 1):
        for way in (0, 1):

            @pl.when(jnp.logical_and(on[way], has(way, step)))
            def _():
                col_copy(way, step).wait_send()
                for p in pieces:
                    zx_copy(way, step, p).wait_send()

            @pl.when(has(way, step + 1))
            def _():
                for p in pieces:
                    core_copy(way, step + 1, p).wait()

    for p in pieces:
        core_copy(0, 0, p).wait()
    bulk.wait()
    own_zx.wait()
    for store in stores:
        store.wait()


PIECE = 64


def line_gather(zx, cols, tok, gain, lengths):
    n, n_tensor = lax.axis_size("context"), lax.axis_size("tensor")
    rows, width = zx.shape[0], 2 * zx.shape[2]
    pieces = -(-rows // PIECE)
    dma = pltpu.SemaphoreType.DMA
    steps = tok.shape[0]
    made = [
        shape(steps, D, dtype=BF16), shape(steps, 1), shape(steps, LANE), shape(steps // L, 8, L),
        shape(24, LANE),
    ]
    return pl.pallas_call(
        functools.partial(line_kernel, n, n_tensor, PIECE),
        in_specs=[pl.BlockSpec(memory_space=pltpu.VMEM)] * 2
        + [
            pl.BlockSpec(memory_space=pl.ANY), pl.BlockSpec(memory_space=pltpu.VMEM),
            pl.BlockSpec(memory_space=pltpu.SMEM),
        ],
        out_specs=[pl.BlockSpec(memory_space=pl.ANY)] * (2 + len(made)),
        out_shape=[
            shape(2 * n * rows, width, dtype=BF16),
            shape(2 * n * rows, n_tensor * LANE, dtype=BF16),
            *made,
        ],
        scratch_shapes=[
            pltpu.VMEM((rows, width), BF16), pltpu.VMEM((rows, LANE), BF16),
            pltpu.VMEM(tok.shape, BF16), *[pltpu.VMEM(m.shape, m.dtype) for m in made], dma((6,)),
            dma((2,)), dma((2, n - 1, pieces)), dma((2, n - 1, pieces)),
            dma((2, n, pieces)), dma((2, n, pieces)), dma((2, n - 1)), dma((2, n - 1)),
            dma((n_tensor - 1, 2, n)), dma((n_tensor - 1, 2, n)), dma, dma,
        ],
        compiler_params=pltpu.CompilerParams(
            vmem_limit_bytes=40 * 1024 * 1024, collective_id=0, has_side_effects=True
        ),
        name="line_gather",
    )(zx, cols, tok, gain, lengths)


SLICES = 8


class Chain:
    def __init__(self, n, backward, packed, entering, got, sent, send_sem, recv_sem):
        s, c, t = lax.axis_index("shard"), lax.axis_index("context"), lax.axis_index("tensor")
        self.from_other = c < n - 1 if backward else c > 0
        self.to_other = c > 0 if backward else c < n - 1
        ahead = jnp.maximum(c - 1, 0) if backward else jnp.minimum(c + 1, n - 1)
        self.target = (s, ahead, t)
        self.refs = packed, entering, got, sent, send_sem, recv_sem

    def copy(self, j):
        _, _, got, sent, send_sem, recv_sem = self.refs
        rows = pl.ds(j * (N // SLICES), N // SLICES)
        return remote(sent.at[rows, :], got.at[rows, :], send_sem.at[j], recv_sem.at[j], self.target)

    def begin(self):
        packed, entering, _, sent, _, _ = self.refs

        @pl.when(jnp.logical_not(self.from_other))
        def _():
            entering[...] = jnp.zeros_like(entering)

            @pl.when(self.to_other)
            def _():
                sent[...] = packed[:N, :]
                for j in range(SLICES):
                    self.copy(j).start()

    def step(self, j):
        packed, entering, got, sent, _, _ = self.refs
        rows = slice(j * (N // SLICES), (j + 1) * (N // SLICES))

        @pl.when(self.from_other)
        def _():
            self.copy(j).wait_recv()
            entering[rows, :] = got[rows, :]

            @pl.when(self.to_other)
            def _():
                sent[rows, :] = packed[rows, :] + packed[N : N + 1, :] * entering[rows, :]
                self.copy(j).start()

    def finish(self):
        @pl.when(self.to_other)
        def _():
            for j in range(SLICES):
                self.copy(j).wait_send()


def beside_of(n):
    s, c, t = lax.axis_index("shard"), lax.axis_index("context"), lax.axis_index("tensor")
    return [(s, lax.rem(c + k, n), t) for k in (1, n - 1)]


def entry_kernel(
    n, packed, back, w_hbm, entry, out, bk, w_ref, buf, got, sent, load_sem, out_sem, chain_s, chain_r
):
    block = buf.shape[1]
    count = back.shape[0] // block
    load_w = pltpu.make_async_copy(w_hbm, w_ref, load_sem.at[count])
    load_w.start()

    def load(k):
        rows = pl.ds(k * block, block)
        return pltpu.make_async_copy(back.at[rows, :], bk.at[rows, :], load_sem.at[k])

    def store(k):
        return pltpu.make_async_copy(
            buf.at[k % 2], out.at[pl.ds(k * block, block), :], out_sem.at[k % 2]
        )

    for k in range(count):
        load(k).start()
    pl.semaphore_wait(greet(beside_of(n)), 2)
    chain = Chain(n, False, packed, entry, got, sent, chain_s, chain_r)
    chain.begin()
    load_w.wait()
    for k in range(count):
        load(k).wait()
        if k >= 2:
            store(k - 2).wait()
        buf[k % 2] = dot(bk[k * block : (k + 1) * block, :], w_ref[...])
        store(k).start()
        if k < SLICES:
            chain.step(k)
    for k in range(count, SLICES):
        chain.step(k)
    chain.finish()
    for k in range(max(count - 2, 0), count):
        store(k).wait()


def run_entry(packed, back, weight):
    n = lax.axis_size("context")
    steps, width = back.shape[0], weight.shape[1]
    block = 256
    dma = pltpu.SemaphoreType.DMA
    vmem = pltpu.VMEM
    inside = pl.BlockSpec(memory_space=pltpu.VMEM)
    hbm = pl.BlockSpec(memory_space=pl.ANY)
    return pl.pallas_call(
        functools.partial(entry_kernel, n),
        in_specs=[inside, hbm, hbm],
        out_specs=[inside, hbm],
        out_shape=[shape(N, width), shape(steps, width)],
        scratch_shapes=[
            vmem(back.shape, BF16), vmem(weight.shape, BF16), vmem((2, block, width), F32),
            vmem((N, width), F32), vmem((N, width), F32),
            dma((steps // block + 1,)), dma((2,)), dma((SLICES,)), dma((SLICES,)),
        ],
        compiler_params=pltpu.CompilerParams(
            vmem_limit_bytes=58 * 1024 * 1024, collective_id=6, has_side_effects=True
        ),
        cost_estimate=estimate(15),
        name="entry",
    )(packed, back, weight)


def middle_kernel(
    n, packed, send_a, send_b, mid_hbm, own_hbm, normed_hbm, gate_hbm, back_hbm, scaled_hbm, *refs
):
    if n == 4:
        later, own, next_out, z_out, z_mid, z_mine = refs[:6]
        refs = refs[6:]
    else:
        later, own, next_out, both_out = refs[:4]
        refs = refs[4:]
    (
        mid, nm, gg, bk, sc, peer_part, core_part, own_part, got, chain_got, chain_sent,
        local, core_s, core_r, f_s, f_r, chain_s, chain_r,
    ) = refs
    s, c, t = lax.axis_index("shard"), lax.axis_index("context"), lax.axis_index("tensor")
    near = peers(t)
    to = [(s, c, near[0]), (s, c, near[1])]
    to_core = (1 - s, c, t)
    loads = [
        pltpu.make_async_copy(src, dst, local.at[k])
        for k, (src, dst) in enumerate(
            [
                (normed_hbm, nm), (gate_hbm, gg), (back_hbm, bk), (scaled_hbm, sc),
                (mid_hbm, mid), (own_hbm, own),
            ]
        )
    ]
    for load in loads:
        load.start()
    pl.semaphore_wait(greet(to + [to_core] + beside_of(n)), 5)
    hops = [
        remote(src, got.at[side], f_s.at[side], f_r.at[side], to[side])
        for side, src in enumerate((send_a, send_b))
    ]
    for hop in hops:
        hop.start()
    chain = Chain(n, True, packed, later, chain_got, chain_sent, chain_s, chain_r)
    half_d = nm.shape[1] // 2
    steps = nm.shape[0]
    step = 256
    pairs = ((nm, gg), (bk, sc))

    def product(which, shard, into, m):
        left, right = pairs[which]
        lanes = pl.ds(pl.multiple_of(shard * half_d + m * step, step), step)
        into[which, m * step : (m + 1) * step, :] = over_rows(left, lanes, lambda rows: right[rows, :])

    cores = [
        remote(peer_part.at[k], core_part.at[k], core_s.at[k], core_r.at[k], to_core) for k in (0, 1)
    ]
    chain.begin()
    chain.step(0)
    done = 1
    for which in (0, 1):
        loads[2 * which].wait()
        loads[2 * which + 1].wait()
        for m in range(half_d // step):
            product(which, 1 - s, peer_part, m)
            if done < SLICES:
                chain.step(done)
                done += 1
        cores[which].start()
    for which in (0, 1):
        for m in range(half_d // step):
            product(which, s, own_part, m)
            if done < SLICES:
                chain.step(done)
                done += 1
    chain.finish()
    block = half_d // n

    for which in (0, 1):
        cores[which].wait()
        if n == 4:
            first = c + 1 - 2 * lax.rem(c, 2) if which == 0 else 3 - c
            third = 3 - c if which == 0 else c + 1 - 2 * lax.rem(c, 2)

            def total(k):
                rows = pl.ds(pl.multiple_of(k * block, 8), block)
                return own_part[which, rows, :] + core_part[which, rows, :]

            z_out[which, :block, :] = total(first).astype(BF16)
            z_out[which, block:, :] = total(lax.rem(c + 2, 4)).astype(BF16)
            z_mid[which] = total(third)
            z_mine[which] = total(c)
        else:
            both_out[which] = own_part[which] + core_part[which]
    loads[4].wait()
    loads[5].wait()
    size = mid.shape[1]
    half = steps // 2
    for side in (0, 1):
        hops[side].wait()
        for k in range(half // step):
            rows = slice(k * step, (k + 1) * step)
            at = slice(side * half + k * step, side * half + (k + 1) * step)
            next_out[side, rows, :] = (mid[at, :] + got[side, rows, size:].astype(F32)).astype(BF16)
            own[at, :] += got[side, rows, :size].astype(F32)


def run_middle(packed, fan, normed, gate_grad, back, scaled):
    n = lax.axis_size("context")
    own, mid, send_a, send_b = fan
    steps, width = gate_grad.shape
    size = own.shape[1]
    half_d = D // 2
    block = half_d // n
    dma = pltpu.SemaphoreType.DMA
    vmem = pltpu.VMEM
    inside = pl.BlockSpec(memory_space=pltpu.VMEM)
    hbm = pl.BlockSpec(memory_space=pl.ANY)
    if n == 4:
        more = [
            shape(2, 2 * block, width, dtype=BF16), shape(2, block, width), shape(2, block, width)
        ]
    else:
        more = [shape(2, half_d, width)]
    pair = (2, half_d, width)
    return pl.pallas_call(
        functools.partial(middle_kernel, n),
        in_specs=[inside] + [hbm] * 8,
        out_specs=[inside] * (3 + len(more)),
        out_shape=[shape(N, width), shape(steps, size), shape(2, steps // 2, size, dtype=BF16)] + more,
        scratch_shapes=[
            vmem((steps, size), F32), vmem(normed.shape, BF16), vmem(gate_grad.shape, BF16),
            vmem(back.shape, BF16), vmem(scaled.shape, BF16),
            vmem(pair, F32), vmem(pair, F32), vmem(pair, F32), vmem((2, steps // 2, 2 * size), BF16),
            vmem((N, width), F32), vmem((N, width), F32),
            dma((6,)), dma((2,)), dma((2,)), dma((2,)), dma((2,)), dma((SLICES,)), dma((SLICES,)),
        ],
        compiler_params=pltpu.CompilerParams(
            vmem_limit_bytes=54 * 1024 * 1024, collective_id=7, has_side_effects=True
        ),
        cost_estimate=estimate(35),
        name="middle",
    )(packed, send_a, send_b, mid, own, normed, gate_grad, back, scaled)


def adam_kernel(
    heads, cols_loc, table, gate_g, value_g, down_g, cols_g, packed, packed_gain, resid, own, last, *refs
):
    zx, out, bcdt, gain, chan, bc, head = [refs[3 * k : 3 * k + 3] for k in range(7)]
    refs = refs[21:]
    zx_new, out_new, bcdt_new, gain_new, chan_new, bc_new, head_new = [
        refs[3 * k : 3 * k + 3] for k in range(7)
    ]
    width = value_g.shape[1]
    refs[21][...] = (resid[...].astype(F32) + own[...] + last[0].astype(F32)).astype(BF16)

    def put(news, olds, grad, rate, decay, at=(Ellipsis,)):
        for ref, val in zip(news, adamw(olds[0][at], grad, olds[1][at], olds[2][at], rate, decay)):
            ref[at] = val

    for k, grad in enumerate((gate_g[0], value_g[...])):
        put(zx_new, zx, grad, RATE_MATRIX, DECAY, (slice(None), k, slice(None)))
    put(out_new, out, down_g[0], RATE_MATRIX, DECAY)

    @pl.when(pl.program_id(0) == 0)
    def _():
        put(bcdt_new, bcdt, cols_g[...].T[:cols_loc, :], RATE_MATRIX, DECAY)
        adam_small(
            heads, width, packed, packed_gain, put, gain, chan, bc, head, gain_new, chan_new, bc_new, head_new
        )


def adam_small(
    heads, width, packed, packed_gain, put, gain, chan, bc, head, gain_new, chan_new, bc_new, head_new
):
    over = packed[0] + packed[1] + packed[2] + packed[3]
    gains = packed_gain[0] + packed_gain[1] + packed_gain[2] + packed_gain[3]
    put(gain_new, gain, gains[: D // LANE, :], RATE_SMALL, 0.0)
    put(bc_new, bc, over[: KERNEL + 1, width : width + 2 * N], RATE_SMALL, 0.0)
    grad = jnp.concatenate([packed[k, : KERNEL + 2, :width] for k in range(4)], axis=1)
    put(chan_new, chan, grad, RATE_SMALL, 0.0)
    lane = lax.broadcasted_iota(jnp.int32, (LANE, 4 * heads), 0)
    slot = lax.broadcasted_iota(jnp.int32, (LANE, 4 * heads), 1)
    channel = lax.broadcasted_iota(jnp.int32, (width, 4 * heads), 0)
    wide_slot = lax.broadcasted_iota(jnp.int32, (width, 4 * heads), 1)
    rows = jnp.zeros((8, 4 * heads), F32)
    for k in range(4):
        here = jnp.where(lane + k * heads == slot, 1.0, 0.0)
        here = jnp.where(lane < heads, here, 0.0).astype(BF16)
        wide = jnp.where(channel // P_SIZE + k * heads == wide_slot, 1.0, 0.0).astype(BF16)
        hi, lo = two(packed[k, KERNEL + 3 : KERNEL + 11, :LANE])
        at = lax.broadcasted_iota(jnp.int32, rows.shape, 0)
        rows = rows + jnp.where(at < 2, dot(hi, here) + dot(lo, here), 0.0)
        hi, lo = two(packed[k, KERNEL + 2 : KERNEL + 10, :width])
        skip = dot(hi, wide) + dot(lo, wide)
        rows = rows + jnp.where(at == 2, jnp.broadcast_to(skip[0:1, :], rows.shape), 0.0)
    put(head_new, head, rows[:3, :], RATE_SMALL, 0.0)


def run_adam(pair, value_g, cols_g, packed, packed_gain, tok, own, last, t_index, olds, heads, cols_loc):
    rows, width = value_g.shape
    steps, size = own.shape
    count = 4 if rows % 32 == 0 else 2
    block, span = rows // count, steps // count
    half = count // 2
    one = lambda k: pl.BlockSpec((1, block, width), lambda i, t: (k, i, 0))
    some = pl.BlockSpec((block, width), lambda i, t: (i, 0))
    large = pl.BlockSpec((block, 2, width), lambda i, t: (i, 0, 0))
    tokens = pl.BlockSpec((span, size), lambda i, t: (i, 0))
    every = lambda x: pl.BlockSpec(x.shape, lambda i, t: (0,) * x.ndim, pipeline_mode=pl.Buffered(1))
    flat = [x for group in olds for x in group]
    specs = [large] * 3 + [some] * 3 + [every(x) for x in flat[6:]]
    return pl.pallas_call(
        functools.partial(adam_kernel, heads, cols_loc),
        grid_spec=pltpu.PrefetchScalarGridSpec(
            num_scalar_prefetch=1,
            grid=(count,),
            in_specs=[
                one(0), some, one(1), every(cols_g), every(packed), every(packed_gain),
                pl.BlockSpec((span, size), lambda i, t: (i, t[0])), tokens,
                pl.BlockSpec((1, span, size), lambda i, t: (i // half, i % half, 0)),
            ]
            + specs,
            out_specs=specs + [tokens],
        ),
        out_shape=[shape(*x.shape) for x in flat] + [shape(steps, size, dtype=BF16)],
        compiler_params=params(),
        cost_estimate=estimate(8),
        name="optimizer",
    )(
        jnp.full((1,), t_index, jnp.int32), pair, value_g, pair, cols_g, packed, packed_gain, tok, own,
        last, *flat,
    )


def doc_of(lengths, position):
    found = jnp.zeros(position.shape, F32)
    end = 0
    for k in range(lengths.shape[1] - 1):
        end = end + lengths[0, k]
        found = found + jnp.where(position >= end, 1.0, 0.0)
    return jnp.where(position < 0, -1.0, found)


def mark_chunk(lengths, begin, limit, info_ref, marks_ref):
    row = lax.broadcasted_iota(jnp.int32, (L, LANE), 0)
    lane = lax.broadcasted_iota(jnp.int32, (L, LANE), 1)
    offset = jnp.where(lane < KERNEL - 1, lane - KERNEL + 1, jnp.where(lane >= 8, lane - 7, 0))
    other = jnp.where(lane == 3, -1, jnp.where(lane == 4, L - 1, row + offset)) + begin
    mark = doc_of(lengths, row + begin)
    same = jnp.logical_and(doc_of(lengths, other) == mark, other < limit)
    info = jnp.where(same, 1.0, 0.0)
    info_ref[...] = jnp.where(lane == 5, mark, jnp.where(lane < 7 + KERNEL, info, 0.0))
    marks_ref[0] = doc_of(lengths, begin + lax.broadcasted_iota(jnp.int32, (8, L), 1))


def norm_rows(tok, gain):
    x = tok.astype(F32)
    square = x * x
    total = square[:, :LANE]
    for sl in tiles(D)[1:]:
        total = total + square[:, sl]
    inv = lax.rsqrt(jnp.sum(total, axis=1, keepdims=True) / D + EPS)
    return (x * inv * gain[0:1, :]).astype(BF16), inv


def project_kernel(
    heads, n, cols_loc, normed, ends, w_ref, wg_ref, chan, bcpar, head, e_ref, info,
    projected, cols, act, delta, cum, sloc, pfx, fin,
    halo_v, halo_b, ext_v, ext_b, state, prod, w_cols, prev_v, prev_b, halo_out, halo_got, h_s, h_r,
):
    i = pl.program_id(0)
    s, c, t = lax.axis_index("shard"), lax.axis_index("context"), lax.axis_index("tensor")
    width = w_ref.shape[1] // 2
    block = normed.shape[0]
    after = (s, jnp.minimum(c + 1, n - 1), t)
    halo = remote(halo_out, halo_got, h_s, h_r, after)

    @pl.when(i == 0)
    def _():
        pl.semaphore_wait(greet(beside_of(n)), 2)
        state[...] = jnp.zeros_like(state)
        prod[...] = jnp.ones_like(prod)
        lane = lax.broadcasted_iota(jnp.int32, (4 * LANE, 3 * N), 0)
        want = lax.broadcasted_iota(jnp.int32, (4 * LANE, 3 * N), 1)
        have = lane // LANE * cols_loc + lane % LANE
        want = jnp.where(want < 2 * N, want, jnp.where(want < 2 * N + heads, want + heads * t, -1))
        chosen = jnp.logical_and(have == want, lane % LANE < cols_loc)
        select = jnp.where(chosen, 1.0, 0.0).astype(BF16)
        for k in range(0, D, block):
            w_cols[k : k + block, :] = dot(wg_ref[k : k + block, :], select).astype(BF16)
        halo_out[:, :width] = dot(ends[...], w_ref[:, width:])[8:, :]
        halo_out[:, width:] = dot(ends[...], w_cols[...])[8:, :]

        @pl.when(c < n - 1)
        def _():
            halo.start()

    for k in range(0, 2 * width, 512):
        projected[:, k : k + 512] = dot(normed[...], w_ref[:, k : k + 512])
    cols[...] = dot(normed[...], w_cols[...])

    @pl.when(i == 0)
    def _():
        @pl.when(c > 0)
        def _():
            halo.wait_recv()
            halo_v[...] = halo_got[:, :width]
            halo_b[...] = halo_got[:, width:]

        @pl.when(c == 0)
        def _():
            halo_v[...] = jnp.zeros_like(halo_v)
            halo_b[...] = jnp.zeros_like(halo_b)

        @pl.when(c < n - 1)
        def _():
            halo.wait_send()

    val = projected.at[:, pl.ds(width, width)]

    for j in range(block // L):
        first = i == 0
        load_ext(ext_v, val, prev_v, halo_v, j, first)
        load_ext(ext_b, cols, prev_b, halo_b, j, first)
        prep_chunk(
            rows_at(cols, j), rows_at(info, j), chan, bcpar, head, e_ref, rows_at(act, j),
            rows_at(delta, j), rows_at(cum, j), lead_at(sloc, j), lead_at(pfx, j),
            ext_v, ext_b, state, prod,
        )
    prev_v[...] = projected[block - 8 :, width:]
    prev_b[...] = cols[block - 8 :, :]

    @pl.when(i == pl.num_programs(0) - 1)
    def _():
        fin[:N, :] = state[...]
        fin[N:, :] = prod[...]


def run_project(normed, weight, w_group, chan, bcpar, head, expand, info, heads, cols_loc):
    steps, width = normed.shape[0], weight.shape[1] // 2
    count = steps // L
    dma = pltpu.SemaphoreType.DMA
    return pl.pallas_call(
        functools.partial(project_kernel, heads, lax.axis_size("context"), cols_loc),
        grid=(steps // GROUP,),
        in_specs=[
            row_block(D),
            pl.BlockSpec((16, D), lambda i: (steps // 16 - 1, 0), pipeline_mode=pl.Buffered(1)),
            once(*weight.shape), once(*w_group.shape),
            once(KERNEL + 2, width), once(KERNEL + 1, 2 * N), once(8, LANE), once(2 * LANE, width),
            row_block(LANE),
        ],
        out_specs=[
            row_block(2 * width), row_block(3 * N),
            row_block(width + 2 * N), row_block(LANE), row_block(LANE), lead_block(N, width),
            lead_block(8, width), once(N + 8, width), once(8, width), once(8, 3 * N),
        ],
        out_shape=[
            shape(steps, 2 * width), shape(steps, 3 * N),
            shape(steps, width + 2 * N), shape(steps, LANE), shape(steps, LANE),
            shape(count, N, width), shape(count, 8, width), shape(N + 8, width), shape(8, width),
            shape(8, 3 * N),
        ],
        scratch_shapes=[
            pltpu.VMEM((8 + L, width), F32), pltpu.VMEM((8 + L, 3 * N), F32),
            pltpu.VMEM((N, width), F32), pltpu.VMEM((8, width), F32),
            pltpu.VMEM((D, 3 * N), BF16), pltpu.VMEM((8, width), F32), pltpu.VMEM((8, 3 * N), F32),
            pltpu.VMEM((8, width + 3 * N), F32), pltpu.VMEM((8, width + 3 * N), F32), dma, dma,
        ],
        compiler_params=pltpu.CompilerParams(
            dimension_semantics=("arbitrary",), vmem_limit_bytes=58 * 1024 * 1024,
            collective_id=8, has_side_effects=True,
        ),
        cost_estimate=estimate(45),
        name="project",
    )(normed, normed, weight, w_group, chan, bcpar, head, expand, info)


class AllSum:
    def __init__(self, n, refs, sems):
        s, c, t = lax.axis_index("shard"), lax.axis_index("context"), lax.axis_index("tensor")
        self.n, self.c, self.t = n, c, t
        self.mine, self.other, self.pair, self.pieces, self.total, self.every = refs
        core_s, core_r, piece_s, piece_r, group_s, group_r = sems
        self.core = remote(self.mine, self.other, core_s, core_r, (1 - s, c, t))
        self.along = [
            remote(self.pair, self.pieces.at[c], piece_s.at[k], piece_r.at[k], (s, lax.rem(c + k + 1, n), t))
            for k in range(n - 1)
        ]
        self.across = [
            remote(self.total, self.every.at[t], group_s.at[k], group_r.at[k], (s, c, lax.rem(t + k + 1, 4)))
            for k in range(3)
        ]

    def start(self):
        self.core.start()

    def after_core(self):
        self.core.wait()
        self.pair[...] = self.mine[...] + self.other[...]
        self.pieces[self.c] = self.pair[...]
        for copy in self.along:
            copy.start()

    def after_pieces(self):
        for copy in self.along:
            copy.wait()
        self.total[...] = sum(self.pieces[k] for k in range(1, self.n)) + self.pieces[0]
        self.every[self.t] = self.total[...]
        for copy in self.across:
            copy.start()

    def finish(self):
        for copy in self.across:
            copy.wait()


PACK = 16


def tail_kernel(
    n, grad_b, grad_v, normed_hbm, w_hbm, tok_hbm, back_hbm, late_hbm, wg_hbm,
    raw_t, fixed, gate_top, gate_end, tok_top, tok_end, inv, gain, sel_bc, sel_raw,
    late_rows, late_gain, taps_grad, bias_grad, norm_gain_grad, skip_grad, head_grad,
    tokens_out, value_out, cols_out, pack_out, gain_out,
    gb, gv, nm, w_ref, tok, back, w_cols, col_grad,
    peer_part, own_part, core_part, b_got, b_next, b_last, b_full, raw_full,
    early, mid, send, got, nxt, last, gain_grad, z_out, z_got, z_on, z_last,
    ng, col_peer, col_own, col_core, col_out, col_got, col_on, col_last,
    row_buf, row_held, *refs,
):
    tail_body(
        n, grad_b, grad_v, normed_hbm, w_hbm, tok_hbm, back_hbm, late_hbm, wg_hbm,
        raw_t, fixed, gate_top, gate_end, tok_top, tok_end, inv, gain, sel_bc, sel_raw,
        late_rows, late_gain, taps_grad, bias_grad, norm_gain_grad, skip_grad, head_grad,
        tokens_out, value_out, cols_out, pack_out, gain_out,
        gb, gv, nm, w_ref, tok, back, w_cols, col_grad,
        peer_part, own_part, core_part, b_got, b_next, b_last, b_full, raw_full,
        early, mid, send, got, nxt, last, gain_grad, z_out, z_got, z_on, z_last,
        ng, col_peer, col_own, col_core, col_out, col_got, col_on, col_last,
        row_buf, row_held, refs[:6], refs[6:12], *refs[12:25], refs[25:31], refs[31:37],
    )


def tail_body(
    n, grad_b, grad_v, normed_hbm, w_hbm, tok_hbm, back_hbm, late_hbm, wg_hbm,
    raw_t, fixed, gate_top, gate_end, tok_top, tok_end, inv, gain, sel_bc, sel_raw,
    late_rows, late_gain, taps_grad, bias_grad, norm_gain_grad, skip_grad, head_grad,
    tokens_out, value_out, cols_out, pack_out, gain_out,
    gb, gv, nm, w_ref, tok, back, w_cols, col_grad,
    peer_part, own_part, core_part, b_got, b_next, b_last, b_full, raw_full,
    early, mid, send, got, nxt, last, gain_grad, z_out, z_got, z_on, z_last,
    ng, col_peer, col_own, col_core, col_out, col_got, col_on, col_last,
    row_buf, row_held, pack_refs, gain_refs,
    local, raw_s, raw_r, b_s, b_r, f_s, f_r, core_s, core_r, z_s, z_r, row_s, row_r,
    pack_sems, gain_sems,
):
    s, c, t = lax.axis_index("shard"), lax.axis_index("context"), lax.axis_index("tensor")
    near = peers(t)
    to = [(s, c, near[0]), (s, c, near[1])]
    group = [(s, c, lax.rem(t + k, 4)) for k in (1, 2, 3)]
    to_core = (1 - s, c, t)
    to_piece = [(s, lax.rem(c + k, n), t) for k in range(1, n)]
    in_line = n == 4
    line = [(s, c + 1 - 2 * lax.rem(c, 2), t), (s, 3 - c, t)] if in_line else []
    steps, width = grad_v.shape
    size = w_ref.shape[0] // 4
    share = steps // 4
    mine_lanes = pl.ds(pl.multiple_of(t * size, size), size)
    loads = [
        pltpu.make_async_copy(src, dst, local.at[k])
        for k, (src, dst) in enumerate(
            [
                (grad_b, gb), (grad_v, gv), (normed_hbm, nm), (w_hbm, w_ref),
                (tok_hbm.at[:, mine_lanes], tok), (back_hbm.at[:, mine_lanes], back),
                (late_hbm, ng.at[pl.ds(GROUP, steps - GROUP), :]),
                (wg_hbm.at[mine_lanes, :], w_cols),
            ]
        )
    ]
    for load in loads[:2]:
        load.start()
    pl.semaphore_wait(greet(group + [to_core] + to_piece), n + 3)

    raw_full[t] = raw_t[...]
    raws = [
        remote(raw_t, raw_full.at[t], raw_s.at[k], raw_r.at[k], target)
        for k, target in enumerate(group)
    ]
    for copy in raws:
        copy.start()

    def rows_of(k):
        return pl.ds(pl.multiple_of(k * share, share), share)

    def lanes_of(side):
        return pl.ds(side * N, N)

    loads[0].wait()
    for load in loads[2:]:
        load.start()
    gb[steps - 8 :, :] = fixed[:, width:]

    def b_first(side, part):
        k = near[side] if part == 0 else 3 - t
        return remote(
            gb.at[rows_of(k), lanes_of(side)], b_got.at[side, part], b_s.at[side, part],
            b_r.at[side, part], to[side],
        )

    def b_second(side):
        return remote(
            b_next.at[side], b_last.at[side], b_s.at[side, 2], b_r.at[side, 2], to[1 - side]
        )

    def b_back(side, part):
        k = near[1 - side] if part == 2 else t
        where = b_full.at[rows_of(k), lanes_of(side)]
        return remote(
            where, where, b_s.at[side, 3 + part], b_r.at[side, 3 + part],
            to[1 - side] if part == 0 else to[side],
        )

    for side in (0, 1):
        for part in (0, 1):
            b_first(side, part).start()

    pack = pack_refs[0]
    pack[...] = jnp.zeros_like(pack)
    gain_refs[0][...] = jnp.zeros_like(gain_refs[0])
    total = width + 2 * N
    add_up = lambda x: jnp.sum(x, axis=0, keepdims=True)
    for k in range(KERNEL):
        pack[k : k + 1, :total] = add_up(taps_grad[8 * k : 8 * k + 8, :])
    pack[KERNEL : KERNEL + 1, :total] = add_up(bias_grad[...])
    pack[KERNEL + 1 : KERNEL + 2, :width] = add_up(norm_gain_grad[...])
    pack[KERNEL + 2 : KERNEL + 3, :width] = add_up(skip_grad[...])
    pack[KERNEL + 3 : KERNEL + 4, :LANE] = add_up(head_grad[:8, :])
    pack[KERNEL + 4 : KERNEL + 5, :LANE] = add_up(head_grad[8:, :])
    pack_sum = AllSum(n, pack_refs, pack_sems)
    gain_sum = AllSum(n, gain_refs, gain_sems)
    pack_sum.start()

    loads[1].wait()
    tail = gv[steps - 16 :, :].astype(F32)
    gv[steps - 16 :, :] = jnp.concatenate([tail[:8], fixed[:, :width]], axis=0).astype(BF16)
    loads[2].wait()
    half_d = nm.shape[1] // 2
    step = 256

    def product(shard, right, into):
        for m in range(half_d // step):
            lanes = pl.ds(pl.multiple_of(shard * half_d + m * step, step), step)
            into[m * step : (m + 1) * step, :] = over_rows(nm, lanes, right)

    product(1 - s, lambda rows: gv[rows, :], peer_part)
    core = remote(peer_part, core_part, core_s.at[0], core_r.at[0], to_core)
    core.start()

    for side in (0, 1):
        for part in (0, 1):
            b_first(side, part).wait()
        b_next[side] = gb[rows_of(near[1 - side]), lanes_of(side)] + b_got[side, 1]
        b_second(side).start()
    pack_sum.after_core()

    product(s, lambda rows: gv[rows, :], own_part)

    for side in (0, 1):
        b_second(side).wait()
        mine = gb[rows_of(t), lanes_of(side)] + b_got[side, 0] + b_last[side]
        b_full[rows_of(t), lanes_of(side)] = mine.astype(BF16)
        b_back(side, 0).start()

    block = half_d // n
    side_w = width // 2
    both = own_part
    if in_line:
        first = [c + 1 - 2 * lax.rem(c, 2), 3 - c]
        across = lax.rem(c + 2, 4)

    def block_rows(k):
        return pl.ds(pl.multiple_of(k * block, 8), block)

    def z_block(k, side):
        return both[block_rows(k), side * side_w : (side + 1) * side_w]

    def z_first(side):
        return remote(z_out.at[side], z_got.at[side], z_s.at[side], z_r.at[side], line[side])

    def z_second(side):
        return remote(z_on.at[side], z_last.at[side], z_s.at[2 + side], z_r.at[2 + side], line[1 - side])

    def col_first():
        return remote(col_out, col_got, z_s.at[4], z_r.at[4], line[0])

    def col_second():
        return remote(col_on, col_last, z_s.at[5], z_r.at[5], line[1])

    core.wait()
    both[...] = both[...] + core_part[...]
    if in_line:
        for side in (0, 1):
            z_out[side, :block, :] = z_block(first[side], side).astype(BF16)
            z_out[side, block:, :] = z_block(across, side).astype(BF16)
            z_first(side).start()
    for side in (0, 1):
        b_back(side, 0).wait()
        for part in (1, 2):
            b_back(side, part).start()

    loads[3].wait()
    pack_sum.after_pieces()
    half = GROUP // 2
    tail_half = END // 2

    def f_first(side):
        return remote(send.at[side], got.at[side], f_s.at[side], f_r.at[side], to[side])

    def f_second(side):
        return remote(
            nxt.at[side], last.at[side], f_s.at[2 + side], f_r.at[2 + side], to[1 - side]
        )

    gain_grad[...] = late_gain[...]
    for g in range(GROUP // PART, steps // PART):
        row_buf[:, g * PART : (g + 1) * PART] = late_rows[g]
    ends = [jnp.zeros((LANE - END, LANE), F32)]
    for side in (0, 1):
        rows = slice(side * half, (side + 1) * half)
        tail_rows = slice(side * tail_half, (side + 1) * tail_half)
        end_rows = slice(steps - END + side * tail_half, steps - END + (side + 1) * tail_half)
        x = jnp.concatenate(
            [
                jnp.concatenate([gate_top[rows, :], gv[rows, :]], axis=1),
                jnp.concatenate([gate_end[tail_rows, :], gv[end_rows, :]], axis=1),
            ],
            axis=0,
        )
        keep, go = shares_of(side, t)
        gone = dot(x, pick(w_ref, *go), 1, 1)
        send[side] = gone.astype(BF16)
        f_first(side).start()
        kept = dot(x, pick(w_ref, *keep), 1, 1)
        early[side] = kept[:, :size]
        mid[side] = kept[:, size:]
        scale = jnp.concatenate([inv[rows, :], inv[end_rows, :]], axis=0)
        parts = [kept[:, :size], kept[:, size:], gone[:, :size], gone[:, size:]]

        def z(lanes):
            values = jnp.concatenate([tok_top[rows, lanes], tok_end[tail_rows, lanes]], axis=0)
            return values.astype(F32) * scale

        sums = count_rows(parts, z, gain, keep + go, gain_grad)
        row_buf[:, rows] = row_dots(sums[:half])
        ends.append(sums[half:])
    row_buf[:, steps - LANE :] += row_dots(jnp.concatenate(ends, axis=0))

    for copy in raws:
        copy.wait()
    for side in (0, 1):
        for part in (1, 2):
            b_back(side, part).wait()
    raw_all = jnp.concatenate([raw_full[k] for k in range(4)], axis=0)

    for k in range(steps // GROUP):
        rows = slice(k * GROUP, (k + 1) * GROUP)
        chosen = dot(b_full[rows, :], sel_bc[...]) + dot(raw_all[:, rows], sel_raw[...], 0, 0)
        col_grad[rows, :] = chosen.astype(BF16)
    own_lanes = pl.ds(pl.multiple_of(t * LANE, LANE), LANE)
    product(1 - s, lambda rows: col_grad[rows, own_lanes], col_peer)
    col_core_copy = remote(col_peer, col_core, core_s.at[1], core_r.at[1], to_core)
    col_core_copy.start()
    gain_mine = gain[0:1, mine_lanes]
    loads[4].wait()
    loads[6].wait()
    loads[7].wait()
    ng[steps - END :, :] = jnp.zeros((END, size), F32)
    for k in range(steps // GROUP):
        rows = slice(k * GROUP, (k + 1) * GROUP)
        part = dot(col_grad[rows, :], w_cols[...], 1, 1)
        ng[rows, :] = part if k == 0 else ng[rows, :] + part
        part = part * (tok[rows, :].astype(F32) * inv[rows, :])
        gain_grad[:, mine_lanes] += fold(part)
        part = part * gain_mine
        sums = part[:, :LANE]
        for sl in tiles(size)[1:]:
            sums = sums + part[:, sl]
        row_buf[:, rows] += row_dots(sums)
    row_copies = [
        remote(row_buf, row_held.at[k], row_s.at[k], row_r.at[k], target)
        for k, target in enumerate(group)
    ]
    for copy in row_copies:
        copy.start()

    for k in range(D // LANE):
        gain_refs[0][k : k + 1, :] = add_up(gain_grad[:, k * LANE : (k + 1) * LANE])
    gain_sum.start()

    for side in (0, 1):
        f_first(side).wait()
        nxt[side] = (mid[side] + got[side, :, size:].astype(F32)).astype(BF16)
        f_second(side).start()
        early[side] += got[side, :, :size].astype(F32)

    product(s, lambda rows: col_grad[rows, own_lanes], col_own)

    gain_sum.after_core()
    if in_line:
        for side in (0, 1):
            z_first(side).wait()
            z_on[side] = (
                z_block(first[1 - side], side) + z_got[side, block:, :].astype(F32)
            ).astype(BF16)
            z_second(side).start()
    col_core_copy.wait()
    col_own[...] = col_own[...] + col_core[...]
    if in_line:
        col_out[:block, :] = col_own[block_rows(first[0]), :]
        col_out[block:, :] = col_own[block_rows(across), :]
        col_first().start()

    gain_sum.after_pieces()
    if in_line:
        col_first().wait()
        col_on[...] = col_own[block_rows(first[1]), :] + col_got[block:, :]
        col_second().start()

    loads[5].wait()
    for copy in row_copies:
        copy.wait()
    for side in (0, 1):
        f_second(side).wait()
        early[side] += last[side].astype(F32)
        at = steps - END + side * tail_half
        ng[at : at + tail_half, :] += early[side, half:, :]
        ng[side * half : (side + 1) * half, :] += early[side, :half, :]
    row_total = row_buf[...] + row_held[0] + row_held[1] + row_held[2]
    for k in range(steps // LANE):
        rows = slice(k * LANE, (k + 1) * LANE)
        row_dot = jnp.broadcast_to(row_total[0:1, rows] * (1.0 / D), (LANE, LANE)).T
        scale = inv[rows, :]
        for sl in tiles(size):
            z_tile = tok[rows, sl].astype(F32) * scale
            change = scale * (ng[rows, sl] * gain_mine[:, sl] - z_tile * row_dot)
            tokens_out[rows, sl] = (back[rows, sl].astype(F32) + change).astype(BF16)

    if in_line:
        for side in (0, 1):
            z_second(side).wait()
            value_out[:, side * side_w : (side + 1) * side_w] = (
                z_block(c, side) + z_got[side, :block, :].astype(F32) + z_last[side].astype(F32)
            )
        col_second().wait()
        cols_out[...] = col_own[block_rows(c), :] + col_got[:block, :] + col_last[...]
    else:
        value_out[...] = both[...]
        cols_out[...] = col_own[...]
    pack_sum.finish()
    pack_out[...] = pack_refs[5][...]
    gain_sum.finish()
    gain_out[...] = gain_refs[5][...]


def run_tail(
    grad_b, grad_v, normed, weight, tok, back, late, w_group, raw_t, fixed, gate_grad, inv, gain,
    sel_bc, sel_raw, late_rows, late_gain, *small,
):
    n = lax.axis_size("context")
    steps, width = grad_v.shape
    size = D // 4
    half_d = D // 2
    block = half_d // n
    side_rows = (GROUP + END) // 2
    share = steps // 4
    top = lambda w: pl.BlockSpec((GROUP, w), lambda i: (0, 0), pipeline_mode=pl.Buffered(1))
    end = lambda w: pl.BlockSpec(
        (END, w), lambda i: (steps // END - 1, 0), pipeline_mode=pl.Buffered(1)
    )
    full = lambda x: once(*x.shape)
    hbm = pl.BlockSpec(memory_space=pl.ANY)
    dma = pltpu.SemaphoreType.DMA
    vmem = pltpu.VMEM
    value_rows = block if n == 4 else half_d
    pair = (2, side_rows, size)
    packed = (PACK, width + 2 * N)
    return pl.pallas_call(
        functools.partial(tail_kernel, n),
        grid=(1,),
        in_specs=[hbm] * 8
        + [full(raw_t), full(fixed), top(width), end(width), top(D), end(D)]
        + [full(x) for x in (inv, gain, sel_bc, sel_raw)]
        + [full(x) for x in (late_rows, late_gain, *small)],
        out_specs=[
            once(steps, size), once(value_rows, width), once(value_rows, LANE), once(4, *packed),
            once(4, 16, LANE),
        ],
        out_shape=[
            shape(steps, size, dtype=BF16), shape(value_rows, width), shape(value_rows, LANE),
            shape(4, *packed), shape(4, 16, LANE),
        ],
        scratch_shapes=[
            vmem((steps, 2 * N), F32), vmem((steps, width), BF16), vmem(normed.shape, BF16),
            vmem(weight.shape, BF16), vmem((steps, size), BF16), vmem((steps, size), BF16),
            vmem((size, w_group.shape[1]), BF16),
            vmem((steps, w_group.shape[1]), BF16),
            vmem((half_d, width), F32), vmem((half_d, width), F32), vmem((half_d, width), F32),
            vmem((2, 2, share, N), F32), vmem((2, share, N), F32), vmem((2, share, N), F32),
            vmem((steps, 2 * N), BF16), vmem((4, 16, steps), BF16),
            vmem(pair, F32), vmem(pair, F32), vmem((2, side_rows, 2 * size), BF16),
            vmem((2, side_rows, 2 * size), BF16), vmem(pair, BF16), vmem(pair, BF16), vmem((8, D), F32),
            vmem((2, 2 * block, width // 2), BF16), vmem((2, 2 * block, width // 2), BF16),
            vmem((2, block, width // 2), BF16), vmem((2, block, width // 2), BF16),
            vmem((steps, size), F32),
            vmem((half_d, LANE), F32), vmem((half_d, LANE), F32), vmem((half_d, LANE), F32),
            vmem((2 * block, LANE), F32), vmem((2 * block, LANE), F32), vmem((block, LANE), F32),
            vmem((block, LANE), F32),
            vmem((8, steps), F32), vmem((3, 8, steps), F32),
            *[
                vmem((*lead, *dims), F32)
                for dims in (packed, (16, LANE))
                for lead in ((), (), (), (n,), (), (4,))
            ],
            dma((8,)), dma((3,)), dma((3,)), dma((2, 6)), dma((2, 6)), dma((4,)), dma((4,)),
            dma((2,)), dma((2,)), dma((6,)), dma((6,)), dma((3,)), dma((3,)),
            *[dma, dma, dma((n - 1,)), dma((n - 1,)), dma((3,)), dma((3,))] * 2,
        ],
        compiler_params=pltpu.CompilerParams(
            dimension_semantics=("arbitrary",), vmem_limit_bytes=56 * 1024 * 1024,
            collective_id=5, has_side_effects=True,
        ),
        cost_estimate=estimate(50),
        name="tail",
    )(
        grad_b, grad_v, normed, weight, tok, back, late, w_group,
        raw_t, fixed, gate_grad, gate_grad, tok, tok, inv, gain, sel_bc, sel_raw,
        late_rows, late_gain, *small,
    )


def pad_rows(x, rows=8):
    return jnp.concatenate([x, jnp.zeros((rows - x.shape[0], x.shape[1]), x.dtype)], axis=0)


def pad_cols(x, cols=LANE):
    return jnp.concatenate([x, jnp.zeros((x.shape[0], cols - x.shape[1]), x.dtype)], axis=1)


def on_device(
    tokens, cotangent, doc_lengths, zx_weight, bcdt_weight, out_weight, input_gain, chan_params,
    bc_params, head_params, zx_first, bcdt_first, out_first, gain_first, chan_first, bc_first,
    head_first, zx_second, bcdt_second, out_second, gain_second, chan_second, bc_second, head_second,
):
    n_tensor = lax.axis_size("tensor")
    t_index = lax.axis_index("tensor")
    c_index = lax.axis_index("context")
    tok = tokens[0]
    resid = tok.astype(F32)
    back = cotangent[0]
    steps = resid.shape[0]
    inner_loc = INNER // n_tensor
    heads_loc = H // n_tensor
    share = D // n_tensor
    count = steps // L
    rows_loc = zx_weight.shape[0]
    cols_loc = bcdt_weight.shape[1]

    gain8 = jnp.broadcast_to(input_gain[None], (8, D))
    proj_w, cols_z, normed, inv_rms, info, marks_rows, edge_mask = line_gather(
        zx_weight, bcdt_weight.T, tok, gain8, doc_lengths
    )
    down_block, _ = lax.optimization_barrier((out_weight.astype(BF16).T, proj_w))
    down_t = lax.all_gather(down_block, ("shard", "context"), axis=0, tiled=True)
    chan_loc = lax.dynamic_slice_in_dim(chan_params, t_index * inner_loc, inner_loc, 1)
    head_loc = lax.dynamic_slice_in_dim(head_params, t_index * heads_loc, heads_loc, 1)
    chan8, bc8 = chan_loc, bc_params
    head8 = pad_rows(pad_cols(head_loc))
    spread_at = np.arange(2 * LANE)[:, None] % LANE == np.arange(inner_loc)[None, :] // P_SIZE
    expand = spread_at.astype(ml_dtypes.bfloat16)
    (
        projected, cols, act, delta, cum, sloc, pfx, final, halo_v, halo_b,
    ) = run_project(
        normed, proj_w, cols_z, chan8, bc8, head8, expand, info, heads_loc, cols_loc
    )
    entry, back_scaled = run_entry(final, back, down_t)
    ssd, sums = run_ahead(
        act, delta, cum, info, marks_rows, sloc, pfx, entry, projected, back_scaled, chan8, head8,
        expand, heads_loc,
    )
    scaled, *out_fan = run_out(ssd, projected, sums, chan8, down_t)
    gate_grad, mixed_grad, aloc, sfx, first_adj, norm_gain_grad = run_norm(
        ssd, projected, back_scaled, sums, act, cum, info, chan8, expand, heads_loc
    )
    later, out_own, out_next, *z_arrays = run_middle(
        first_adj, out_fan, normed, gate_grad, back, scaled
    )
    in_line = lax.axis_size("context") == 4
    total_width = inner_loc + 2 * N

    (
        grad_v, grad_b, raw_t, last_rows, _, taps_grad, bias_grad, skip_grad, head_grad,
        ng_late, late_rows, late_gain, out_last, *z_sum,
    ) = run_grand(
        projected, cols, halo_v, halo_b, info, marks_rows, delta, cum, ssd, mixed_grad,
        sloc, pfx, entry, aloc, sfx, later, chan8, bc8, head8, expand, heads_loc,
        gate_grad, proj_w, tok, inv_rms, gain8, edge_mask, out_next, z_arrays if in_line else [],
    )
    if in_line:
        pair_g = z_sum[0]
    else:
        pair_g = jnp.stack(
            [lax.psum_scatter(z_arrays[0][k], "context", scatter_dimension=0, tiled=True) for k in (0, 1)]
        )
    column = np.arange(4 * LANE)
    column = np.where(column % LANE < cols_loc, column // LANE * cols_loc + column % LANE, -1)[None, :]
    sel_bc = (np.arange(2 * N)[:, None] == column).astype(ml_dtypes.bfloat16)
    slot = np.arange(4 * 16)[:, None]
    of_slot = np.where(slot % 16 < heads_loc, 2 * N + slot // 16 * heads_loc + slot % 16, -2)
    sel_raw = (of_slot == column).astype(ml_dtypes.bfloat16)
    tokens_grad, value_g, cols_g, packed, packed_gain = run_tail(
        grad_b, grad_v, normed, proj_w, tok, back, ng_late, cols_z, raw_t, last_rows, gate_grad,
        inv_rms, gain8, sel_bc, sel_raw, late_rows, late_gain,
        taps_grad, bias_grad, norm_gain_grad, skip_grad, head_grad,
    )
    tokens_grad = tokens_grad[None]
    if not in_line:
        value_g = lax.psum_scatter(value_g, "context", scatter_dimension=0, tiled=True)
        cols_g = lax.psum_scatter(cols_g[:, :cols_loc], "context", scatter_dimension=0, tiled=True)
        cols_g = pad_cols(cols_g)
    flip = lambda *arrays: tuple(a.T for a in arrays)
    lift = lambda *arrays: tuple(a.reshape(D // LANE, LANE) for a in arrays)
    news = run_adam(
        pair_g, value_g, cols_g, packed, packed_gain, tok, out_own, out_last, t_index,
        (
            (zx_weight, zx_first, zx_second), flip(out_weight, out_first, out_second),
            flip(bcdt_weight, bcdt_first, bcdt_second), lift(input_gain, gain_first, gain_second),
            (chan_params, chan_first, chan_second), (bc_params, bc_first, bc_second),
            (head_params, head_first, head_second),
        ),
        heads_loc, cols_loc,
    )
    zx_new, out_new, bcdt_new, gain_new = news[:3], flip(*news[3:6]), flip(*news[6:9]), news[9:12]
    block_out = news[21][None]
    return (
        block_out, tokens_grad, *zx_new, *bcdt_new, *out_new, *[g.reshape(D) for g in gain_new], *news[12:21]
    )


def solution(mesh):
    big = P(("shard", "context"), None, "tensor")
    cols = P(("shard", "context"), "tensor")
    down = P("tensor", ("shard", "context"))
    rows = P("shard", "context", None)
    out_rows = P("shard", "context", "tensor")
    return jax.shard_map(
        on_device,
        mesh=mesh,
        in_specs=(
            rows, rows, P("shard", None), big, cols, down, P(), P(), P(), P(),
            big, cols, down, P(), P(), P(), P(),
            big, cols, down, P(), P(), P(), P(),
        ),
        out_specs=(
            out_rows, out_rows, big, big, big, cols, cols, cols, down, down, down,
            *([P()] * 12),
        ),
        check_vma=False,
    )
```

```python
import functools

import jax
import jax.numpy as jnp
import ml_dtypes
import numpy as np
from jax import lax
from jax.experimental import pallas as pl
from jax.experimental.pallas import tpu as pltpu
from jax.sharding import PartitionSpec as P

D = 1536
INNER = 3072
H = 48
P_SIZE = 64
N = 128
KERNEL = 4
STEP = 10

EPS = 1e-05
BETA_ONE = 0.9
BETA_TWO = 0.999
ADAM_EPS = 1e-08
DECAY = 0.1
RATE_MATRIX = 0.05
RATE_SMALL = 0.2

L = 128
LANE = 128
GROUP = 4 * L
PART = 2 * L
END = 32
LOG2E = 1.4426950408889634
F32 = jnp.float32
BF16 = jnp.bfloat16
VMEM_LIMIT = 58 * 1024 * 1024


def from_behind(block, axis, distance):
    devices = range(lax.axis_size(axis))
    route = [(i - distance, i) for i in devices if i - distance in devices]
    return lax.ppermute(block, axis, route)


def adamw(weight, grad, first, second, rate, decay):
    first_new = BETA_ONE * first + (1.0 - BETA_ONE) * grad
    second_new = BETA_TWO * second + (1.0 - BETA_TWO) * grad * grad
    scale_one = 1.0 - BETA_ONE**STEP
    scale_two = 1.0 - BETA_TWO**STEP
    update = first_new / scale_one / (jnp.sqrt(second_new / scale_two) + ADAM_EPS)
    return (weight - rate * (update + decay * weight), first_new, second_new)


def two(x):
    hi = x.astype(BF16)
    return hi, (x - hi.astype(F32)).astype(BF16)


def dot(a, b, ca=1, cb=0):
    return lax.dot_general(a, b, (((ca,), (cb,)), ((), ())), preferred_element_type=F32)


def dot3(a, b, ca=1, cb=0):
    ah, al = two(a)
    bh, bl = two(b)
    return dot(
        jnp.concatenate([ah, al, ah], axis=ca), jnp.concatenate([bh, bh, bl], axis=cb), ca, cb
    )


def over_rows(left, lanes, right):
    total = None
    for at in range(0, left.shape[0], GROUP):
        rows = slice(at, at + GROUP)
        part = dot(left[rows, lanes], right(rows), 0, 0)
        total = part if total is None else total + part
    return total


def tri_sum(tri, x):
    hi = x.astype(BF16)
    rest = x - hi.astype(F32)
    mid = rest.astype(BF16)
    low = (rest - mid.astype(F32)).astype(BF16)
    out = dot(tri, jnp.concatenate([hi, mid, low], axis=1))
    w = x.shape[1]
    return out[:, :w] + out[:, w : 2 * w] + out[:, 2 * w :]


def spread(x, e_ref):
    hi, lo = two(x)
    return dot(jnp.concatenate([hi, lo], axis=1), e_ref[...])


def per_head(x, e_ref):
    hi, lo = two(x)
    e = e_ref[:LANE, :]
    return dot(hi, e, 1, 1) + dot(lo, e, 1, 1)


def sigmoid(x):
    return 1.0 / (1.0 + jnp.exp(-x))


def softplus(x):
    return jnp.maximum(x, 0.0) + jnp.log1p(jnp.exp(-jnp.abs(x)))


def tiles(width):
    return [slice(k, k + LANE) for k in range(0, width, LANE)]


def fold(x):
    return jnp.sum(x.reshape(x.shape[0] // 8, 8, x.shape[1]), axis=0)


def lower_mask():
    row = lax.broadcasted_iota(jnp.int32, (L, L), 0)
    col = lax.broadcasted_iota(jnp.int32, (L, L), 1)
    return row >= col


def keep_mask(info, marks_row):
    return jnp.logical_and(lower_mask(), info[:, 5:6] == marks_row[0:1, :])


def decay_of(keep, cum, cum_t, h):
    return jnp.exp2(jnp.where(keep, cum[:, h : h + 1] - cum_t[h : h + 1, :], -1e30))


def load_ext(ext_ref, cur_ref, prev_ref, halo_ref, j, first):
    if j > 0:
        ext_ref[0:8, :] = cur_ref[j * L - 8 : j * L, :]
    else:

        @pl.when(first)
        def _():
            ext_ref[0:8, :] = halo_ref[...]

        @pl.when(jnp.logical_not(first))
        def _():
            ext_ref[0:8, :] = prev_ref[...]

    ext_ref[8 : 8 + L, :] = cur_ref[j * L : (j + 1) * L, :]


def rows_of_chunk(ref, j):
    return ref.at[pl.ds(pl.multiple_of(j * L, L), L), :]


def lead_of_chunk(ref, j):
    return ref.at[pl.ds(j, 1)]


def load_ext_of(ext_ref, cur_ref, prev_ref, halo_ref, j, first):
    @pl.when(first)
    def _():
        ext_ref[0:8, :] = halo_ref[...]

    @pl.when(jnp.logical_and(j == 0, jnp.logical_not(first)))
    def _():
        ext_ref[0:8, :] = prev_ref[...]

    @pl.when(j > 0)
    def _():
        ext_ref[0:8, :] = cur_ref[pl.ds(pl.multiple_of(jnp.maximum(j * L - 8, 0), 8), 8), :]

    ext_ref[8 : 8 + L, :] = cur_ref[pl.ds(pl.multiple_of(j * L, L), L), :]


def rows_at(ref, j):
    return ref.at[j * L : (j + 1) * L, :]


def lead_at(ref, j):
    return ref.at[j : j + 1]


def conv_tile(ext_ref, info, taps, sl):
    shifted = []
    total = jnp.broadcast_to(taps[KERNEL : KERNEL + 1, :], (L, LANE))
    for k in range(KERNEL):
        val = ext_ref[pl.ds(8 - KERNEL + 1 + k, L), sl]
        if k < KERNEL - 1:
            val = val * info[:, k : k + 1]
        shifted.append(val)
        total = total + taps[k : k + 1, :] * val
    return shifted, total


def prep_chunk(
    bc, info_ref, chan, bcpar, head, e_ref, act, delta_ref, cum_ref, sloc, pfx, ext_v, ext_b, state, prod
):
    info = info_ref[...]
    width = ext_v.shape[1]
    for sl in tiles(width):
        _, total = conv_tile(ext_v, info, chan[:, sl], sl)
        act[:, sl] = total * sigmoid(total)
    for sl in tiles(2 * N):
        _, total = conv_tile(ext_b, info, bcpar[:, sl], sl)
        act[:, slice(width + sl.start, width + sl.stop)] = total * sigmoid(total)
    raw = bc[:, 2 * N : 3 * N]
    delta = softplus(raw + head[0:1, :])
    dlog = -delta * (jnp.exp(head[1:2, :]) * LOG2E)
    tri = jnp.where(lower_mask(), 1.0, 0.0).astype(BF16)
    cum = tri_sum(tri, dlog)
    delta_ref[...] = delta
    cum_ref[...] = cum
    sloc[0] = state[...]
    pfx[0] = prod[...]
    last = cum[L - 1 : L, :]
    tail = info[:, 4:5] * jnp.exp2(last - cum) * delta
    through = spread(
        jnp.broadcast_to(info[L - 1 : L, 3:4] * jnp.exp2(last), (8, LANE)), e_ref
    )
    weights = spread(tail, e_ref)
    tail_u = act[:, :width] * weights
    fresh = dot3(act[:, width : width + N], tail_u, 0, 0)
    state[...] = state[...] * through[0:1, :] + fresh
    prod[...] = prod[...] * through


def row_block(width, col=0, rows=GROUP):
    return pl.BlockSpec((rows, width), lambda i: (i, col))


def prev_block(width, col=0, rows=GROUP):
    return pl.BlockSpec((8, width), lambda i: (jnp.maximum(i * (rows // 8) - 1, 0), col))


def lead_block(*dims, rows=GROUP):
    return pl.BlockSpec((rows // L, *dims), lambda i: (i, 0, 0))


def whole(*shape):
    return pl.BlockSpec(shape, lambda i: (0,) * len(shape))


def once(*shape):
    return pl.BlockSpec(shape, lambda i: (0,) * len(shape), pipeline_mode=pl.Buffered(1))


def estimate(us):
    return pl.CostEstimate(flops=int(us * 1.1e9), bytes_accessed=int(us * 1e6), transcendentals=0)


def params(**kw):
    return pltpu.CompilerParams(
        dimension_semantics=("arbitrary",), vmem_limit_bytes=VMEM_LIMIT, **kw
    )


def shape(*dims, dtype=F32):
    return jax.ShapeDtypeStruct(dims, dtype)


def ahead_kernel(
    heads, act, delta, cum, info, marks, sloc, pfx, entry, gate, back, chan, head, e_ref, ssd, sums,
    mine, held, send, recv,
):
    i = pl.program_id(0)
    s, c, t = lax.axis_index("shard"), lax.axis_index("context"), lax.axis_index("tensor")
    group = [(s, c, lax.rem(t + k, 4)) for k in (1, 2, 3)]

    @pl.when(i == 0)
    def _():
        pl.semaphore_wait(greet(group), 3)

    chunks = act.shape[0] // L
    for j in range(act.shape[0] // L):
        ahead_chunk(
            rows_at(act, j), rows_at(delta, j), rows_at(cum, j), rows_at(info, j), lead_at(marks, j),
            lead_at(sloc, j), lead_at(pfx, j), entry, rows_at(gate, j), rows_at(back, j), chan, head,
            e_ref, rows_at(ssd, j), mine.at[pl.ds(i * chunks + j, 1)],
        )

    @pl.when(i == pl.num_programs(0) - 1)
    def _():
        copies = [
            remote(mine, held.at[k], send.at[k], recv.at[k], target) for k, target in enumerate(group)
        ]
        for copy in copies:
            copy.start()
        total = mine[...]
        for k, copy in enumerate(copies):
            copy.wait()
            total = total + held[k]
        sums[...] = total


def ahead_chunk(
    act, delta_ref, cum_ref, info_ref, marks_ref, sloc, pfx, entry, gate, back, chan, head, e_ref, ssd, sums
):
    width = act.shape[1] - 2 * N
    info = info_ref[...]
    cum = cum_ref[...]
    cum_t = cum.T
    keep = keep_mask(info, marks_ref[0])
    bmat = act[:, width : width + N]
    cmat = act[:, width + N :]
    scores = dot3(cmat, bmat, 1, 1)
    xs = act[:, :width]
    u_hi, u_lo = two(xs * spread(delta_ref[...], e_ref))
    state = sloc[0] + entry[...] * pfx[0, 0:1, :]
    entering = dot3(cmat, state)
    eexp = spread(info[:, 3:4] * jnp.exp2(cum), e_ref)
    skip = spread(jnp.broadcast_to(head[2:3, :], (8, LANE)), e_ref)
    lane = lax.broadcasted_iota(jnp.int32, (1, LANE), 1)
    left = jnp.where(lane < P_SIZE, 1.0, 0.0).astype(BF16)
    right = jnp.where(lane < P_SIZE, 0.0, 1.0).astype(BF16)
    square = jnp.zeros((L, LANE), F32)
    cross = jnp.zeros((L, LANE), F32)
    for q, sl in enumerate(tiles(width)):
        mix = jnp.concatenate(
            [(scores * decay_of(keep, cum, cum_t, 2 * q + r)).astype(BF16) for r in (0, 1)], axis=1
        )
        both = jnp.concatenate([u_hi[:, sl], u_lo[:, sl]], axis=1)
        rhs = jnp.concatenate(
            [both * jnp.concatenate([m, m], axis=1) for m in (left, right)], axis=0
        )
        out = dot(mix, rhs)
        y = out[:, :LANE] + out[:, LANE:] + entering[:, sl] * eexp[:, sl]
        y = y + skip[0:1, sl] * xs[:, sl]
        ssd[:, sl] = y
        g = gate[:, sl]
        gated = y * g * sigmoid(g)
        square = square + gated * gated
        cross = cross + gated * (back[:, sl] * chan[KERNEL + 1 : KERNEL + 2, sl])
    ones = jnp.ones((8, LANE), BF16)
    rows = []
    for part in (square, cross):
        hi, lo = two(part)
        rows.append(dot(ones, hi, 1, 1) + dot(ones, lo, 1, 1))
    pick = lax.broadcasted_iota(jnp.int32, (8, LANE), 0)
    sums[0] = jnp.where(pick == 0, rows[0], jnp.where(pick == 1, rows[1], 0.0))


def run_ahead(act, delta, cum, info, marks, sloc, pfx, entry, projected, back, chan, head, expand, heads):
    steps, width = projected.shape[0], projected.shape[1] // 2
    count = steps // L
    return pl.pallas_call(
        functools.partial(ahead_kernel, heads),
        grid=(steps // GROUP,),
        in_specs=[
            row_block(width + 2 * N), row_block(LANE), row_block(LANE), row_block(LANE),
            lead_block(8, L), lead_block(N, width), lead_block(8, width),
            once(N, width), row_block(width, 0), row_block(width),
            once(KERNEL + 2, width), once(8, LANE), once(2 * LANE, width),
        ],
        out_specs=[row_block(width), once(count, 8, L)],
        out_shape=[shape(steps, width), shape(count, 8, L)],
        scratch_shapes=[
            pltpu.VMEM((count, 8, L), F32), pltpu.VMEM((3, count, 8, L), F32),
            pltpu.SemaphoreType.DMA((3,)), pltpu.SemaphoreType.DMA((3,)),
        ],
        compiler_params=params(collective_id=1, has_side_effects=True),
        cost_estimate=estimate(20),
        name="ahead",
    )(act, delta, cum, info, marks, sloc, pfx, entry, projected, back, chan, head, expand)


def norm_kernel(
    heads, ssd, gate, back, sums, cmat, cum, info, chan, e_ref,
    gate_grad, mixed_grad, aloc, sfx, fin, gain_grad, state, prod,
):
    i = pl.program_id(0)

    @pl.when(i == 0)
    def _():
        state[...] = jnp.zeros_like(state)
        prod[...] = jnp.ones_like(prod)
        gain_grad[...] = jnp.zeros_like(gain_grad)

    chunks = ssd.shape[0] // L

    for j in reversed(range(chunks)):
        norm_chunk(
            rows_at(ssd, j), rows_at(gate, j), rows_at(back, j), lead_at(sums, j), rows_at(cmat, j),
            rows_at(cum, j), rows_at(info, j), chan, e_ref, rows_at(gate_grad, j),
            rows_at(mixed_grad, j), lead_at(aloc, j), lead_at(sfx, j), gain_grad, state, prod,
        )

    @pl.when(i == pl.num_programs(0) - 1)
    def _():
        fin[:N, :] = state[...]
        fin[N:, :] = prod[...]


def norm_chunk(
    ssd, gate, back, sums, cmat_ref, cum_ref, info_ref, chan, e_ref,
    gate_grad, mixed_grad, aloc, sfx, gain_grad, state, prod,
):
    width = ssd.shape[1]
    rows = sums[0]
    inv_row = lax.rsqrt(rows[0:1, :] / INNER + EPS)
    cross_row = inv_row * inv_row * inv_row * (rows[1:2, :] / INNER)
    inv = jnp.broadcast_to(inv_row, (LANE, L)).T
    cross = jnp.broadcast_to(cross_row, (LANE, L)).T
    info = info_ref[...]
    cum = cum_ref[...]
    eexp = spread(info[:, 3:4] * jnp.exp2(cum), e_ref)
    e_mixed = []
    for sl in tiles(width):
        g = gate[:, sl]
        sig = sigmoid(g)
        soft = g * sig
        y = ssd[:, sl]
        gated = y * soft
        bs = back[:, sl]
        gain = chan[KERNEL + 1 : KERNEL + 2, sl]
        normed = gated * inv
        gain_grad[:, sl] += fold(bs * normed)
        gg = inv * (bs * gain) - gated * cross
        mg = gg * soft
        mixed_grad[:, sl] = mg
        gate_grad[:, sl] = (gg * y * sig * (1.0 + g * (1.0 - sig))).astype(BF16)
        e_mixed.append(mg * eexp[:, sl])
    aloc[0] = state[...]
    sfx[0] = prod[...]
    through = spread(
        jnp.broadcast_to(info[L - 1 : L, 3:4] * jnp.exp2(cum[L - 1 : L, :]), (8, LANE)), e_ref
    )
    fresh = dot3(cmat_ref[...], jnp.concatenate(e_mixed, axis=1), 0, 0)
    state[...] = state[...] * through[0:1, :] + fresh
    prod[...] = prod[...] * through


def run_norm(ssd, projected, back, sums, act, cum, info, chan, expand, heads):
    steps, width = ssd.shape
    count = steps // L
    blocks = steps // GROUP
    turn = lambda spec: pl.BlockSpec(
        spec.block_shape, lambda i, m=spec.index_map: m(blocks - 1 - i)
    )
    c_col = width // N + 1
    return pl.pallas_call(
        functools.partial(norm_kernel, heads),
        grid=(blocks,),
        in_specs=[
            turn(row_block(width)), turn(row_block(width, 0)), turn(row_block(width)),
            turn(lead_block(8, L)),
            turn(row_block(N, c_col)), turn(row_block(LANE)), turn(row_block(LANE)),
            once(KERNEL + 2, width), once(2 * LANE, width),
        ],
        out_specs=[
            turn(row_block(width)), turn(row_block(width)),
            turn(lead_block(N, width)),
            turn(lead_block(8, width)),
            whole(N + 8, width), whole(8, width),
        ],
        out_shape=[
            shape(steps, width, dtype=BF16), shape(steps, width),
            shape(count, N, width), shape(count, 8, width), shape(N + 8, width), shape(8, width),
        ],
        scratch_shapes=[pltpu.VMEM((N, width), F32), pltpu.VMEM((8, width), F32)],
        compiler_params=params(),
        cost_estimate=estimate(21),
        name="norm_back",
    )(ssd, projected, back, sums, act, cum, info, chan, expand)


def behind_chunk(
    heads, j, start, first, val, valp, bc, bcp, halo_v, halo_b, info_ref, marks_ref, delta_ref, cum_ref,
    ssd, mixed_grad, sloc, pfx, entry, aloc, sfx, later, chan, bcpar, head, e_ref,
    grad_v, grad_b, raw_grad, tail_rows, head_rows, taps_grad, bias_grad, skip_grad, head_grad,
    ext_v, ext_b, slope, d_tot,
):
    width = val.shape[1]
    total_width = width + 2 * N

    @pl.when(start)
    def _():
        d_tot[0:8, :] = jnp.zeros((8, total_width), F32)
        taps_grad[...] = jnp.zeros_like(taps_grad)
        bias_grad[...] = jnp.zeros_like(bias_grad)
        skip_grad[...] = jnp.zeros_like(skip_grad)
        head_grad[...] = jnp.zeros_like(head_grad)

    d_tot[L:, :] = d_tot[0:8, :]
    load_ext_of(ext_v, val, valp, halo_v, j, first)
    load_ext_of(ext_b, bc, bcp, halo_b, j, first)
    raw = bc[pl.ds(pl.multiple_of(j * L, L), L), 2 * N : 3 * N]
    info_ref, marks_ref = rows_of_chunk(info_ref, j), lead_of_chunk(marks_ref, j)
    delta_ref, cum_ref = rows_of_chunk(delta_ref, j), rows_of_chunk(cum_ref, j)
    ssd, mixed_grad = rows_of_chunk(ssd, j), rows_of_chunk(mixed_grad, j)
    sloc, pfx = lead_of_chunk(sloc, j), lead_of_chunk(pfx, j)
    aloc, sfx = lead_of_chunk(aloc, j), lead_of_chunk(sfx, j)
    grad_v, grad_b = rows_of_chunk(grad_v, j), rows_of_chunk(grad_b, j)
    raw_grad = raw_grad.at[:, pl.ds(pl.multiple_of(j * L, L), L)]
    info = info_ref[...]

    def activate(ext_ref, taps, sl, at):
        _, total = conv_tile(ext_ref, info, taps[:, sl], sl)
        sig = sigmoid(total)
        slope[:, slice(at, at + LANE)] = sig * (1.0 + total * (1.0 - sig))
        return total * sig

    xs = jnp.concatenate([activate(ext_v, chan, sl, sl.start) for sl in tiles(width)], axis=1)
    bmat = activate(ext_b, bcpar, slice(0, N), width)
    cmat = activate(ext_b, bcpar, slice(N, 2 * N), width + N)

    delta = delta_ref[...]
    cum = cum_ref[...]
    cum_t = cum.T
    keep = keep_mask(info, marks_ref[0])
    last = cum[L - 1 : L, :]
    scores = dot3(cmat, bmat, 1, 1)
    dexp = spread(delta, e_ref)
    eexp = spread(info[:, 3:4] * jnp.exp2(cum), e_ref)
    texp = spread(info[:, 4:5] * jnp.exp2(last - cum), e_ref)
    u = xs * dexp
    u_hi, u_lo = two(u)
    dy = mixed_grad[...]
    dy_hi, dy_lo = two(dy)
    skip = spread(jnp.broadcast_to(head[2:3, :], (8, LANE)), e_ref)
    state = sloc[0] + entry[...] * pfx[0, 0:1, :]
    adj = aloc[0] + later[...] * sfx[0, 0:1, :]
    tail_du = dot3(bmat, adj) * texp
    lane = lax.broadcasted_iota(jnp.int32, (1, LANE), 1)
    left = jnp.where(lane < P_SIZE, 1.0, 0.0).astype(BF16)
    right = jnp.where(lane < P_SIZE, 0.0, 1.0).astype(BF16)
    two_left = jnp.concatenate([left, left], axis=1)
    two_right = jnp.concatenate([right, right], axis=1)
    d_scores = jnp.zeros((L, L), F32)
    inner_du = []
    for q, sl in enumerate(tiles(width)):
        decays = [decay_of(keep, cum, cum_t, 2 * q + r) for r in (0, 1)]
        mix = jnp.concatenate([(scores * d).astype(BF16) for d in decays], axis=0)
        dy_both = jnp.concatenate([dy_hi[:, sl], dy_lo[:, sl]], axis=1)
        rhs = jnp.concatenate([dy_both * two_left, dy_both * two_right], axis=0)
        out = dot(mix, rhs, 0, 0)
        inner_du.append(out[:, :LANE] + out[:, LANE:])
        u_twice = jnp.concatenate([u_hi[:, sl], u_hi[:, sl]], axis=1)
        u_rows = jnp.concatenate([u_twice * two_left, u_twice * two_right], axis=0)
        d_mix = dot(dy_both, u_rows, 1, 1)
        d_scores = d_scores + d_mix[:, :L] * decays[0] + d_mix[:, L:] * decays[1]
    du = jnp.concatenate(inner_du, axis=1) + tail_du
    d_xs = dexp * du + skip[0:1, :] * dy
    d_b = dot3(d_scores, cmat, 0, 0) + dot3(u * texp, adj, 1, 1)
    d_c = dot3(d_scores, bmat) + dot3(dy * eexp, state, 1, 1)
    skip_grad[...] += fold(dy * xs)

    direct = per_head(xs * du, e_ref)
    mixed = ssd[...] - skip[0:1, :] * xs
    d_cum = per_head(dy * mixed, e_ref) - delta * direct
    at_last = jnp.sum(per_head(u * tail_du, e_ref), axis=0, keepdims=True)
    through = info[L - 1 : L, 3:4] * jnp.exp2(last)
    pair = per_head(fold(adj * state), e_ref)
    at_last = at_last + through * jnp.sum(pair, axis=0, keepdims=True)
    upper = jnp.where(lower_mask(), 1.0, 0.0).astype(BF16).T
    d_log = tri_sum(upper, d_cum) + at_last
    rate = jnp.exp(head[1:2, :])
    valid = lane < heads
    d_raw = (direct - d_log * rate) * sigmoid(raw + head[0:1, :])
    d_raw = jnp.where(valid, d_raw, 0.0)
    raw_grad[...] = d_raw.T[:16, :].astype(BF16)
    head_grad[0:8, :] += fold(d_raw)
    head_grad[8:16, :] += fold(jnp.where(valid, -d_log * delta * rate, 0.0))

    d_act = [d_xs[:, sl] for sl in tiles(width)] + [d_b, d_c]
    for q in range(total_width // LANE):
        sl = slice(q * LANE, (q + 1) * LANE)
        if q < width // LANE:
            ext_ref, taps, part = ext_v, chan[:, sl], sl
        else:
            part = slice(sl.start - width, sl.stop - width)
            ext_ref, taps = ext_b, bcpar[:, part]
        dt = d_act[q] * slope[:, sl]
        d_tot[0:L, sl] = dt
        bias_grad[:, sl] += fold(dt)
        for k in range(KERNEL):
            moved = ext_ref[pl.ds(8 - KERNEL + 1 + k, L), part]
            if k < KERNEL - 1:
                moved = moved * info[:, k : k + 1]
            taps_grad[8 * k : 8 * k + 8, sl] += fold(dt * moved)
        total = dt * taps[KERNEL - 1 : KERNEL, :]
        for s in range(1, KERNEL):
            total = total + taps[KERNEL - 1 - s : KERNEL - s, :] * (
                d_tot[pl.ds(s, L), sl] * info[:, 7 + s : 8 + s]
            )
        if q < width // LANE:
            grad_v[:, sl] = total.astype(BF16)
        else:
            grad_b[:, part] = total

        @pl.when(start)
        def _():
            tail_rows[:, sl] = total[L - 8 :, :]

    @pl.when(first)
    def _():
        head_rows[...] = d_tot[0:8, :]


def remote(src, dst, send, recv, target):
    return pltpu.make_async_remote_copy(
        src_ref=src, dst_ref=dst, send_sem=send, recv_sem=recv, device_id=target,
        device_id_type=pl.DeviceIdType.MESH,
    )


def greet(targets):
    barrier = pltpu.get_barrier_semaphore()
    for target in targets:
        pl.semaphore_signal(
            barrier, inc=1, device_id=target, device_id_type=pl.DeviceIdType.MESH
        )
    return barrier


def count_rows(parts, z, gain, at, gain_grad):
    rows = jnp.zeros((parts[0].shape[0], LANE), F32)
    size = parts[0].shape[1]
    for part, k in zip(parts, at):
        lanes = pl.ds(pl.multiple_of(k * size, size), size)
        part = part * z(lanes)
        gain_grad[:, lanes] += fold(part)
        part = part * gain[0:1, lanes]
        for sl in tiles(size):
            rows = rows + part[:, sl]
    return rows


def row_dots(rows):
    ones = jnp.ones((8, LANE), BF16)
    hi, lo = two(rows)
    return dot(ones, hi, 1, 1) + dot(ones, lo, 1, 1)


def grand_kernel(heads, n, *refs):
    behind, refs = refs[:22], refs[22:]
    gate_grad, w_ref, tok, inv, gain, edge_mask, out_next = refs[:7]
    refs = refs[7:]
    in_line = n == 4
    if in_line:
        z_out, z_mid, z_mine = refs[:3]
        refs = refs[3:]
    outs, refs = refs[:9], refs[9:]
    ng_own, row_sums, gain_grad, out_last = refs[:4]
    refs = refs[4:]
    if in_line:
        z_sum, refs = refs[0], refs[1:]
    scratch, refs = refs[:4], refs[4:]
    mid, send, got, nxt, last, edge, s1, r1, s2, r2, edge_s, edge_r, o_s, o_r = refs[:14]
    if in_line:
        z_got, z_on, z_last, z_s, z_r = refs[14:]
    chan, bcpar = behind[18], behind[19]
    grad_v, tail_rows = outs[0], outs[3]
    d_tot = scratch[3]
    i, n_steps = pl.program_id(0), pl.num_programs(0)
    s, c, t = lax.axis_index("shard"), lax.axis_index("context"), lax.axis_index("tensor")
    near = peers(t)
    to = [(s, c, near[0]), (s, c, near[1])]
    width = grad_v.shape[1]
    size = w_ref.shape[0] // 4
    inside = mid.shape[0]
    chunks = grad_v.shape[0] // L

    @pl.when(i == 0)
    def _():
        pl.semaphore_wait(greet(to + beside_of(n)), 4)
        gain_grad[...] = jnp.zeros_like(gain_grad)

    def out_hop(side):
        return remote(
            out_next.at[side], out_last.at[side], o_s.at[side], o_r.at[side], to[1 - side]
        )

    @pl.when(i == 0)
    def _():
        for side in (0, 1):
            out_hop(side).start()

    if in_line:
        line = [(s, c + 1 - 2 * lax.rem(c, 2), t), (s, 3 - c, t)]
        block = z_mid.shape[1]

        def z_first(k):
            return remote(z_out.at[k], z_got.at[k], z_s.at[k], z_r.at[k], line[k])

        def z_second(k):
            return remote(z_on.at[k], z_last.at[k], z_s.at[2 + k], z_r.at[2 + k], line[1 - k])

        @pl.when(i == 0)
        def _():
            for k in (0, 1):
                z_first(k).start()

        @pl.when(i == n_steps // 2)
        def _():
            for k in (0, 1):
                z_first(k).wait()
                z_on[k] = (z_mid[k] + z_got[k, block:, :].astype(F32)).astype(BF16)
                z_second(k).start()
                z_sum[k] = z_mine[k] + z_got[k, :block, :].astype(F32)

        @pl.when(i == n_steps - 1)
        def _():
            for k in (0, 1):
                z_second(k).wait()
                z_sum[k] += z_last[k].astype(F32)

    def first_hop(k, side):
        return remote(send.at[k], got.at[k], s1.at[k], r1.at[k], to[side])

    def second_hop(k, side):
        return remote(nxt.at[k], last.at[k], s2.at[k], r2.at[k], to[1 - side])

    def place(k):
        return pl.ds(pl.multiple_of((inside - 1 - k) * PART, PART), PART)

    def turn_over(k, side):
        first_hop(k, side).wait()
        nxt[k] = (mid[k] + got[k, :, size:].astype(F32)).astype(BF16)
        second_hop(k, side).start()
        ng_own[place(k), :] += got[k, :, :size].astype(F32)

    def one(step, carry):
        j = chunks - 1 - step
        behind_chunk(
            heads, j, jnp.logical_and(i == 0, step == 0),
            jnp.logical_and(i == n_steps - 1, j == 0), *behind, *outs, *scratch,
        )
        for side in (0, 1):
            ready = jnp.logical_and(step == 0, lax.rem(i, 2) == 1 - side)

            @pl.when(jnp.logical_and(ready, jnp.logical_and(i >= 2, i < inside + 2)))
            def _():
                turn_over(i - 2, side)

        return carry

    lax.fori_loop(0, chunks, one, 0)

    def fan(side):
        counted = jnp.where(i == 0, PART - END, PART)
        x = jnp.concatenate([gate_grad[...], grad_v[...]], axis=1)
        keep, go = shares_of(side, t)
        gone = dot(x, pick(w_ref, *go), 1, 1)
        send[i] = gone.astype(BF16)
        first_hop(i, side).start()
        kept = dot(x, pick(w_ref, *keep), 1, 1)
        ng_own[place(i), :] = kept[:, :size]
        mid[i] = kept[:, size:]
        row = lax.broadcasted_iota(jnp.int32, (PART, 1), 0)
        scale = jnp.where(row < counted, inv[...], 0.0)
        parts = [kept[:, :size], kept[:, size:], gone[:, :size], gone[:, size:]]
        sums = count_rows(
            parts, lambda lanes: tok[:, lanes].astype(F32) * scale, gain, keep + go, gain_grad
        )
        row_sums[0] = row_dots(sums)

    for side in (0, 1):
        parity = lax.rem(i, 2) == 1 - side

        @pl.when(jnp.logical_and(parity, i < inside))
        def _():
            fan(side)

    @pl.when(i == n_steps - 1)
    def _():
        before = (s, jnp.maximum(c - 1, 0), t)
        copy = remote(d_tot.at[pl.ds(0, 8), :], edge, edge_s, edge_r, before)

        @pl.when(c > 0)
        def _():
            copy.start()

        for k in range(inside):
            second_hop(k, 1 - k % 2).wait()
            ng_own[place(k), :] += last[k].astype(F32)
        for side in (0, 1):
            out_hop(side).wait()

        @pl.when(c < n - 1)
        def _():
            copy.wait_recv()
            for shift in range(1, KERNEL):
                moved = pltpu.roll(edge[...], 8 - shift, 0) * edge_mask[
                    8 * shift - 8 : 8 * shift, 0:1
                ]
                tap = slice(KERNEL - 1 - shift, KERNEL - shift)
                tail_rows[:, :width] += chan[tap, :] * moved[:, :width]
                tail_rows[:, width:] += bcpar[tap, :] * moved[:, width:]

        @pl.when(c > 0)
        def _():
            copy.wait_send()


def run_grand(
    projected, cols, halo_v, halo_b, info, marks, delta, cum, ssd, mixed_grad, sloc, pfx, entry,
    aloc, sfx, later, chan, bcpar, head, expand, heads, gate_grad, weight, tok, inv, gain, edge_mask,
    out_next, z_arrays,
):
    steps, width = ssd.shape
    parts = steps // PART
    inside = (steps - GROUP) // PART
    size = D // 4
    turn = lambda spec: pl.BlockSpec(
        spec.block_shape, lambda i, m=spec.index_map: m(parts - 1 - i)
    )
    in_part = lambda w: pl.BlockSpec((PART, w), lambda i: (parts - 1 - i, 0))
    chunk = lead_block(N, width, rows=PART)
    few = lead_block(8, width, rows=PART)
    total = width + 2 * N
    dma = pltpu.SemaphoreType.DMA
    return pl.pallas_call(
        functools.partial(grand_kernel, heads, lax.axis_size("context")),
        grid=(parts,),
        in_specs=[
            turn(row_block(width, 1, rows=PART)), turn(prev_block(width, 1, rows=PART)),
            turn(row_block(3 * N, rows=PART)), turn(prev_block(3 * N, rows=PART)),
            once(8, width), once(8, 3 * N), turn(row_block(LANE, rows=PART)),
            turn(lead_block(8, L, rows=PART)),
            turn(row_block(LANE, rows=PART)), turn(row_block(LANE, rows=PART)), turn(row_block(width, rows=PART)), turn(row_block(width, rows=PART)),
            turn(chunk), turn(few), once(N, width), turn(chunk), turn(few), once(N, width),
            once(KERNEL + 2, width), once(KERNEL + 1, 2 * N), once(8, LANE), once(2 * LANE, width),
            turn(row_block(width, rows=PART)), once(*weight.shape), in_part(D), in_part(1), once(8, D),
            once(24, LANE), pl.BlockSpec(memory_space=pl.ANY),
        ]
        + ([pl.BlockSpec(memory_space=pl.ANY)] + [once(*z.shape) for z in z_arrays[1:]] if z_arrays else []),
        out_specs=[
            turn(row_block(width, rows=PART)), turn(row_block(2 * N, rows=PART)),
            pl.BlockSpec((16, PART), lambda i: (0, parts - 1 - i)),
            whole(8, total), whole(8, total), whole(8 * KERNEL, total), whole(8, total),
            whole(8, width), whole(16, LANE),
            once(inside * PART, size),
            pl.BlockSpec((1, 8, PART), lambda i: (parts - 1 - i, 0, 0)),
            whole(8, D), pl.BlockSpec(memory_space=pl.ANY),
        ]
        + [once(*z.shape) for z in z_arrays[1:2]],
        out_shape=[
            shape(steps, width, dtype=BF16), shape(steps, 2 * N), shape(16, steps, dtype=BF16),
            shape(8, total), shape(8, total), shape(8 * KERNEL, total), shape(8, total),
            shape(8, width), shape(16, LANE),
            shape(inside * PART, size), shape(parts, 8, PART), shape(8, D),
            shape(*out_next.shape, dtype=BF16),
        ]
        + [shape(*z.shape) for z in z_arrays[1:2]],
        scratch_shapes=[
            pltpu.VMEM((8 + L, width), F32), pltpu.VMEM((8 + L, 3 * N), F32),
            pltpu.VMEM((L, total), F32), pltpu.VMEM((L + 8, total), F32),
            pltpu.VMEM((inside, PART, size), F32),
            pltpu.VMEM((inside, PART, 2 * size), BF16), pltpu.VMEM((inside, PART, 2 * size), BF16),
            pltpu.VMEM((inside, PART, size), BF16), pltpu.VMEM((inside, PART, size), BF16),
            pltpu.VMEM((8, total), F32),
            dma((inside,)), dma((inside,)), dma((inside,)), dma((inside,)), dma, dma,
            dma((2,)), dma((2,)),
        ]
        + (
            [
                pltpu.VMEM(z_arrays[0].shape, BF16), pltpu.VMEM(z_arrays[1].shape, BF16),
                pltpu.VMEM(z_arrays[1].shape, BF16), dma((4,)), dma((4,)),
            ]
            if z_arrays
            else []
        ),
        compiler_params=pltpu.CompilerParams(
            dimension_semantics=("arbitrary",), vmem_limit_bytes=52 * 1024 * 1024,
            collective_id=4, has_side_effects=True,
        ),
        cost_estimate=estimate(90),
        name="behind",
    )(
        projected, projected, cols, cols, halo_v, halo_b, info, marks, delta, cum, ssd, mixed_grad,
        sloc, pfx, entry, aloc, sfx, later, chan, bcpar, head, expand,
        gate_grad, weight, tok, inv, gain, edge_mask, out_next, *z_arrays,
    )


def peers(t):
    return t + 1 - 2 * lax.rem(t, 2), lax.rem(t + 2, 4)


def pick(w_ref, one, other):
    size = w_ref.shape[0] // 4
    at = lambda k: pl.ds(pl.multiple_of(k * size, size), size)
    return jnp.concatenate([w_ref[at(one), :], w_ref[at(other), :]], axis=0)


def shares_of(side, t):
    near = peers(t)
    return (t, near[1 - side]), (near[side], 3 - t)


def out_kernel(
    ssd, gate, sums, chan, w_ref, scaled, own, mid, send_a, send_b,
):
    i, half = pl.program_id(0), pl.num_programs(0) // 2
    t = lax.axis_index("tensor")
    width = ssd.shape[1]
    for k in range(ssd.shape[0] // L):
        rows = slice(k * L, (k + 1) * L)
        inv = jnp.broadcast_to(lax.rsqrt(sums[k, 0:1, :] / INNER + EPS), (LANE, L)).T
        for sl in tiles(width):
            g = gate[rows, sl]
            gated = ssd[rows, sl] * g * sigmoid(g)
            scaled[rows, sl] = (gated * inv * chan[KERNEL + 1 : KERNEL + 2, sl]).astype(BF16)
    x = scaled[...]
    size = own.shape[1]

    def part(side, send):
        keep, go = shares_of(side, t)
        send[...] = dot(x, pick(w_ref, *go), 1, 1).astype(BF16)
        kept = dot(x, pick(w_ref, *keep), 1, 1)
        own[...] = kept[:, :size]
        mid[...] = kept[:, size:]

    @pl.when(i < half)
    def _():
        part(0, send_a)

    @pl.when(i >= half)
    def _():
        part(1, send_b)


def run_out(ssd, projected, sums, chan, weight):
    steps, width = ssd.shape
    block = 512
    count = steps // block
    half = count // 2
    size = D // 4
    in_block = lambda w, col=0: pl.BlockSpec((block, w), lambda i: (i, col))
    return pl.pallas_call(
        out_kernel,
        grid=(count,),
        in_specs=[
            in_block(width), in_block(width, 0),
            pl.BlockSpec((block // L, 8, L), lambda i: (i, 0, 0)),
            once(KERNEL + 2, width), once(*weight.shape),
        ],
        out_specs=[
            in_block(width), in_block(size), in_block(size),
            pl.BlockSpec((block, 2 * size), lambda i: (jnp.minimum(i, half - 1), 0)),
            pl.BlockSpec((block, 2 * size), lambda i: (jnp.maximum(i - half, 0), 0)),
        ],
        out_shape=[
            shape(steps, width, dtype=BF16), shape(steps, size), shape(steps, size),
            shape(steps // 2, 2 * size, dtype=BF16), shape(steps // 2, 2 * size, dtype=BF16),
        ],
        compiler_params=params(),
        cost_estimate=estimate(12),
        name="out",
    )(ssd, projected, sums, chan, weight)


def line_kernel(
    n, n_tensor, piece, zx_raw, cols_raw, tok_hbm, gain, lengths,
    zx_out, cols_out, normed_out, inv_out, info_out, marks_out, edge_out,
    zx_ref, cols_ref, tok, normed, inv, info, marks, edge, work_s,
    local, zx_s, zx_r, core_s, core_r, col_s, col_r, group_s, group_r, bulk_s, bulk_r,
):
    load_tok = pltpu.make_async_copy(tok_hbm, tok, work_s.at[0])
    load_tok.start()
    s, c, t = lax.axis_index("shard"), lax.axis_index("context"), lax.axis_index("tensor")
    on = (c < n - 1, c > 0)
    to = ((s, jnp.minimum(c + 1, n - 1), t), (s, jnp.maximum(c - 1, 0), t))
    to_core = (1 - s, c, t)
    to_group = [(s, c, lax.rem(t + k, n_tensor)) for k in range(1, n_tensor)]
    beside = [(s, lax.rem(c + k, n), t) for k in (1, n - 1)]
    barrier = greet([to_core] + to_group + beside)
    width = zx_raw.shape[2]
    for k in (0, 1):
        zx_ref[:, k * width : (k + 1) * width] = zx_raw[:, k, :].astype(BF16)
    gap = jnp.zeros((LANE - cols_raw.shape[0], cols_raw.shape[1]), F32)
    cols_ref[...] = jnp.concatenate([cols_raw[...], gap], axis=0).T.astype(BF16)
    pl.semaphore_wait(barrier, n_tensor + 2)
    rows, width = zx_ref.shape[0], cols_ref.shape[1]
    spans = [(at, min(piece, rows - at)) for at in range(0, rows, piece)]

    def block_of(way, hop):
        return jnp.maximum(c - hop, 0) if way == 0 else jnp.minimum(c + hop, n - 1)

    def has(way, hop):
        return c - hop >= 0 if way == 0 else c + hop <= n - 1

    def place(ref, block, at=0, size=rows):
        return ref.at[pl.ds(pl.multiple_of((s * n + block) * rows + at, 16), size), :]

    lanes = pl.ds(pl.multiple_of(t * width, LANE), width)

    def place_cols(block):
        return cols_out.at[pl.ds(pl.multiple_of((s * n + block) * rows, 16), rows), lanes]

    def zx_copy(way, step, p):
        at, size = spans[p]
        where = place(zx_out, block_of(way, step), at, size)
        src = zx_ref.at[pl.ds(at, size), :] if step == 0 else where
        return remote(src, where, zx_s.at[way, step, p], zx_r.at[way, step, p], to[way])

    def col_copy(way, step):
        where = place_cols(block_of(way, step))
        src = cols_ref if step == 0 else where
        return remote(src, where, col_s.at[way, step], col_r.at[way, step], to[way])

    def group_copies(way, hop):
        where = place_cols(block_of(way, hop))
        src = cols_ref if hop == 0 else where
        return [
            remote(src, where, group_s.at[k, way, hop], group_r.at[k, way, hop], target)
            for k, target in enumerate(to_group)
        ]

    def core_copy(way, hop, p):
        at, size = spans[p]
        where = place(zx_out, block_of(way, hop), at, size)
        src = zx_ref.at[pl.ds(at, size), :] if hop == 0 else where
        return remote(src, where, core_s.at[way, hop, p], core_r.at[way, hop, p], to_core)

    pieces = range(len(spans))
    for way in (0, 1):

        @pl.when(on[way])
        def _():
            col_copy(way, 0).start()
            for p in pieces:
                zx_copy(way, 0, p).start()

    for copy in group_copies(0, 0):
        copy.start()
    own_cols = pltpu.make_async_copy(cols_ref, place_cols(c), local.at[0])
    own_zx = pltpu.make_async_copy(zx_ref, place(zx_out, c), local.at[1])
    own_cols.start()
    own_zx.start()
    for p in pieces:
        core_copy(0, 0, p).start()
    load_tok.wait()
    steps = tok.shape[0]
    begin = c * steps

    def work(j, carry):
        x, scale = norm_rows(rows_of_chunk(tok, j)[...], gain)
        rows_of_chunk(normed, j)[...] = x
        rows_of_chunk(inv, j)[...] = scale
        mark_chunk(
            lengths, begin + j * L, begin + steps, rows_of_chunk(info, j), lead_of_chunk(marks, j)
        )
        return carry

    lax.fori_loop(0, steps // L, work, 0)
    row = lax.broadcasted_iota(jnp.int32, (24, LANE), 0)
    shift, at_row = row // 8 + 1, row % 8
    there = at_row - 8 + shift + begin + steps
    agree = doc_of(lengths, there) == doc_of(lengths, there - shift)
    edge[...] = jnp.where(jnp.logical_and(at_row >= 8 - shift, agree), 1.0, 0.0)
    stores = [
        pltpu.make_async_copy(src, dst, work_s.at[k + 1])
        for k, (src, dst) in enumerate(
            [
                (normed, normed_out), (inv, inv_out), (info, info_out), (marks, marks_out),
                (edge, edge_out),
            ]
        )
    ]
    for store in stores:
        store.start()

    start = pl.ds(pl.multiple_of(s * n * rows, 16), n * rows)
    bulk = remote(cols_out.at[start, :], cols_out.at[start, :], bulk_s, bulk_r, to_core)
    for step in range(n - 1):
        further = step < n - 2
        for way in (0, 1):

            @pl.when(has(way, step + 1))
            def _():
                col_copy(way, step).wait_recv()
                for copy in group_copies(way, step + 1):
                    copy.start()
                if further:

                    @pl.when(on[way])
                    def _():
                        col_copy(way, step + 1).start()

        if not further:
            own_cols.wait()
            for copy in group_copies(0, 0):
                copy.wait()
            for hop in range(1, n):
                for way in (0, 1):

                    @pl.when(has(way, hop))
                    def _():
                        for copy in group_copies(way, hop):
                            copy.wait()

            bulk.start()
        for p in pieces:
            for way in (0, 1):

                @pl.when(has(way, step + 1))
                def _():
                    zx_copy(way, step, p).wait_recv()
                    core_copy(way, step + 1, p).start()
                    if further:

                        @pl.when(on[way])
                        def _():
                            zx_copy(way, step + 1, p).start()

    for step in range(n - 1):
        for way in (0, 1):

            @pl.when(jnp.logical_and(on[way], has(way, step)))
            def _():
                col_copy(way, step).wait_send()
                for p in pieces:
                    zx_copy(way, step, p).wait_send()

            @pl.when(has(way, step + 1))
            def _():
                for p in pieces:
                    core_copy(way, step + 1, p).wait()

    for p in pieces:
        core_copy(0, 0, p).wait()
    bulk.wait()
    own_zx.wait()
    for store in stores:
        store.wait()


PIECE = 64


def line_gather(zx, cols, tok, gain, lengths):
    n, n_tensor = lax.axis_size("context"), lax.axis_size("tensor")
    rows, width = zx.shape[0], 2 * zx.shape[2]
    pieces = -(-rows // PIECE)
    dma = pltpu.SemaphoreType.DMA
    steps = tok.shape[0]
    made = [
        shape(steps, D, dtype=BF16), shape(steps, 1), shape(steps, LANE), shape(steps // L, 8, L),
        shape(24, LANE),
    ]
    return pl.pallas_call(
        functools.partial(line_kernel, n, n_tensor, PIECE),
        in_specs=[pl.BlockSpec(memory_space=pltpu.VMEM)] * 2
        + [
            pl.BlockSpec(memory_space=pl.ANY), pl.BlockSpec(memory_space=pltpu.VMEM),
            pl.BlockSpec(memory_space=pltpu.SMEM),
        ],
        out_specs=[pl.BlockSpec(memory_space=pl.ANY)] * (2 + len(made)),
        out_shape=[
            shape(2 * n * rows, width, dtype=BF16),
            shape(2 * n * rows, n_tensor * LANE, dtype=BF16),
            *made,
        ],
        scratch_shapes=[
            pltpu.VMEM((rows, width), BF16), pltpu.VMEM((rows, LANE), BF16),
            pltpu.VMEM(tok.shape, BF16), *[pltpu.VMEM(m.shape, m.dtype) for m in made], dma((6,)),
            dma((2,)), dma((2, n - 1, pieces)), dma((2, n - 1, pieces)),
            dma((2, n, pieces)), dma((2, n, pieces)), dma((2, n - 1)), dma((2, n - 1)),
            dma((n_tensor - 1, 2, n)), dma((n_tensor - 1, 2, n)), dma, dma,
        ],
        compiler_params=pltpu.CompilerParams(
            vmem_limit_bytes=60 * 1024 * 1024, collective_id=0, has_side_effects=True
        ),
        name="line_gather",
    )(zx, cols, tok, gain, lengths)


SLICES = 8


class Chain:
    def __init__(self, n, backward, packed, entering, got, sent, send_sem, recv_sem):
        s, c, t = lax.axis_index("shard"), lax.axis_index("context"), lax.axis_index("tensor")
        self.from_other = c < n - 1 if backward else c > 0
        self.to_other = c > 0 if backward else c < n - 1
        ahead = jnp.maximum(c - 1, 0) if backward else jnp.minimum(c + 1, n - 1)
        self.target = (s, ahead, t)
        self.refs = packed, entering, got, sent, send_sem, recv_sem

    def copy(self, j):
        _, _, got, sent, send_sem, recv_sem = self.refs
        rows = pl.ds(j * (N // SLICES), N // SLICES)
        return remote(sent.at[rows, :], got.at[rows, :], send_sem.at[j], recv_sem.at[j], self.target)

    def begin(self):
        packed, entering, _, sent, _, _ = self.refs

        @pl.when(jnp.logical_not(self.from_other))
        def _():
            entering[...] = jnp.zeros_like(entering)

            @pl.when(self.to_other)
            def _():
                sent[...] = packed[:N, :]
                for j in range(SLICES):
                    self.copy(j).start()

    def step(self, j):
        packed, entering, got, sent, _, _ = self.refs
        rows = slice(j * (N // SLICES), (j + 1) * (N // SLICES))

        @pl.when(self.from_other)
        def _():
            self.copy(j).wait_recv()
            entering[rows, :] = got[rows, :]

            @pl.when(self.to_other)
            def _():
                sent[rows, :] = packed[rows, :] + packed[N : N + 1, :] * entering[rows, :]
                self.copy(j).start()

    def finish(self):
        @pl.when(self.to_other)
        def _():
            for j in range(SLICES):
                self.copy(j).wait_send()


def beside_of(n):
    s, c, t = lax.axis_index("shard"), lax.axis_index("context"), lax.axis_index("tensor")
    return [(s, lax.rem(c + k, n), t) for k in (1, n - 1)]


def entry_kernel(
    n, packed, back, w_hbm, entry, out, bk, w_ref, buf, got, sent, load_sem, out_sem, chain_s, chain_r
):
    block = buf.shape[1]
    count = back.shape[0] // block
    load_w = pltpu.make_async_copy(w_hbm, w_ref, load_sem.at[count])
    load_w.start()

    def load(k):
        rows = pl.ds(k * block, block)
        return pltpu.make_async_copy(back.at[rows, :], bk.at[rows, :], load_sem.at[k])

    def store(k):
        return pltpu.make_async_copy(
            buf.at[k % 2], out.at[pl.ds(k * block, block), :], out_sem.at[k % 2]
        )

    for k in range(count):
        load(k).start()
    pl.semaphore_wait(greet(beside_of(n)), 2)
    chain = Chain(n, False, packed, entry, got, sent, chain_s, chain_r)
    chain.begin()
    load_w.wait()
    for k in range(count):
        load(k).wait()
        if k >= 2:
            store(k - 2).wait()
        buf[k % 2] = dot(bk[k * block : (k + 1) * block, :], w_ref[...])
        store(k).start()
        if k < SLICES:
            chain.step(k)
    for k in range(count, SLICES):
        chain.step(k)
    chain.finish()
    for k in range(max(count - 2, 0), count):
        store(k).wait()


def run_entry(packed, back, weight):
    n = lax.axis_size("context")
    steps, width = back.shape[0], weight.shape[1]
    block = 256
    dma = pltpu.SemaphoreType.DMA
    vmem = pltpu.VMEM
    inside = pl.BlockSpec(memory_space=pltpu.VMEM)
    hbm = pl.BlockSpec(memory_space=pl.ANY)
    return pl.pallas_call(
        functools.partial(entry_kernel, n),
        in_specs=[inside, hbm, hbm],
        out_specs=[inside, hbm],
        out_shape=[shape(N, width), shape(steps, width)],
        scratch_shapes=[
            vmem(back.shape, BF16), vmem(weight.shape, BF16), vmem((2, block, width), F32),
            vmem((N, width), F32), vmem((N, width), F32),
            dma((steps // block + 1,)), dma((2,)), dma((SLICES,)), dma((SLICES,)),
        ],
        compiler_params=pltpu.CompilerParams(
            vmem_limit_bytes=58 * 1024 * 1024, collective_id=6, has_side_effects=True
        ),
        cost_estimate=estimate(15),
        name="entry",
    )(packed, back, weight)


def middle_kernel(
    n, packed, send_a, send_b, mid_hbm, own_hbm, normed_hbm, gate_hbm, back_hbm, scaled_hbm, *refs
):
    if n == 4:
        later, own, next_out, z_out, z_mid, z_mine = refs[:6]
        refs = refs[6:]
    else:
        later, own, next_out, both_out = refs[:4]
        refs = refs[4:]
    (
        mid, nm, gg, bk, sc, peer_part, core_part, own_part, got, chain_got, chain_sent,
        local, core_s, core_r, f_s, f_r, chain_s, chain_r,
    ) = refs
    s, c, t = lax.axis_index("shard"), lax.axis_index("context"), lax.axis_index("tensor")
    near = peers(t)
    to = [(s, c, near[0]), (s, c, near[1])]
    to_core = (1 - s, c, t)
    loads = [
        pltpu.make_async_copy(src, dst, local.at[k])
        for k, (src, dst) in enumerate(
            [
                (normed_hbm, nm), (gate_hbm, gg), (back_hbm, bk), (scaled_hbm, sc),
                (mid_hbm, mid), (own_hbm, own),
            ]
        )
    ]
    for load in loads:
        load.start()
    pl.semaphore_wait(greet(to + [to_core] + beside_of(n)), 5)
    hops = [
        remote(src, got.at[side], f_s.at[side], f_r.at[side], to[side])
        for side, src in enumerate((send_a, send_b))
    ]
    for hop in hops:
        hop.start()
    chain = Chain(n, True, packed, later, chain_got, chain_sent, chain_s, chain_r)
    half_d = nm.shape[1] // 2
    steps = nm.shape[0]
    step = 256
    pairs = ((nm, gg), (bk, sc))

    def product(which, shard, into, m):
        left, right = pairs[which]
        lanes = pl.ds(pl.multiple_of(shard * half_d + m * step, step), step)
        into[which, m * step : (m + 1) * step, :] = over_rows(left, lanes, lambda rows: right[rows, :])

    cores = [
        remote(peer_part.at[k], core_part.at[k], core_s.at[k], core_r.at[k], to_core) for k in (0, 1)
    ]
    chain.begin()
    chain.step(0)
    done = 1
    for which in (0, 1):
        loads[2 * which].wait()
        loads[2 * which + 1].wait()
        for m in range(half_d // step):
            product(which, 1 - s, peer_part, m)
            if done < SLICES:
                chain.step(done)
                done += 1
        cores[which].start()
    for which in (0, 1):
        for m in range(half_d // step):
            product(which, s, own_part, m)
            if done < SLICES:
                chain.step(done)
                done += 1
    chain.finish()
    block = half_d // n

    for which in (0, 1):
        cores[which].wait()
        if n == 4:
            first = c + 1 - 2 * lax.rem(c, 2) if which == 0 else 3 - c
            third = 3 - c if which == 0 else c + 1 - 2 * lax.rem(c, 2)

            def total(k):
                rows = pl.ds(pl.multiple_of(k * block, 8), block)
                return own_part[which, rows, :] + core_part[which, rows, :]

            z_out[which, :block, :] = total(first).astype(BF16)
            z_out[which, block:, :] = total(lax.rem(c + 2, 4)).astype(BF16)
            z_mid[which] = total(third)
            z_mine[which] = total(c)
        else:
            both_out[which] = own_part[which] + core_part[which]
    loads[4].wait()
    loads[5].wait()
    size = mid.shape[1]
    half = steps // 2
    for side in (0, 1):
        hops[side].wait()
        for k in range(half // step):
            rows = slice(k * step, (k + 1) * step)
            at = slice(side * half + k * step, side * half + (k + 1) * step)
            next_out[side, rows, :] = (mid[at, :] + got[side, rows, size:].astype(F32)).astype(BF16)
            own[at, :] += got[side, rows, :size].astype(F32)


def run_middle(packed, fan, normed, gate_grad, back, scaled):
    n = lax.axis_size("context")
    own, mid, send_a, send_b = fan
    steps, width = gate_grad.shape
    size = own.shape[1]
    half_d = D // 2
    block = half_d // n
    dma = pltpu.SemaphoreType.DMA
    vmem = pltpu.VMEM
    inside = pl.BlockSpec(memory_space=pltpu.VMEM)
    hbm = pl.BlockSpec(memory_space=pl.ANY)
    if n == 4:
        more = [
            shape(2, 2 * block, width, dtype=BF16), shape(2, block, width), shape(2, block, width)
        ]
    else:
        more = [shape(2, half_d, width)]
    pair = (2, half_d, width)
    return pl.pallas_call(
        functools.partial(middle_kernel, n),
        in_specs=[inside] + [hbm] * 8,
        out_specs=[inside] * (3 + len(more)),
        out_shape=[shape(N, width), shape(steps, size), shape(2, steps // 2, size, dtype=BF16)] + more,
        scratch_shapes=[
            vmem((steps, size), F32), vmem(normed.shape, BF16), vmem(gate_grad.shape, BF16),
            vmem(back.shape, BF16), vmem(scaled.shape, BF16),
            vmem(pair, F32), vmem(pair, F32), vmem(pair, F32), vmem((2, steps // 2, 2 * size), BF16),
            vmem((N, width), F32), vmem((N, width), F32),
            dma((6,)), dma((2,)), dma((2,)), dma((2,)), dma((2,)), dma((SLICES,)), dma((SLICES,)),
        ],
        compiler_params=pltpu.CompilerParams(
            vmem_limit_bytes=54 * 1024 * 1024, collective_id=7, has_side_effects=True
        ),
        cost_estimate=estimate(35),
        name="middle",
    )(packed, send_a, send_b, mid, own, normed, gate_grad, back, scaled)


def adam_kernel(
    heads, cols_loc, table, gate_g, value_g, down_g, cols_g, packed, packed_gain, resid, own, last, *refs
):
    zx, out, bcdt, gain, chan, bc, head = [refs[3 * k : 3 * k + 3] for k in range(7)]
    refs = refs[21:]
    zx_new, out_new, bcdt_new, gain_new, chan_new, bc_new, head_new = [
        refs[3 * k : 3 * k + 3] for k in range(7)
    ]
    width = value_g.shape[1]
    refs[21][...] = (resid[...].astype(F32) + own[...] + last[0].astype(F32)).astype(BF16)

    def put(news, olds, grad, rate, decay, at=(Ellipsis,)):
        for ref, val in zip(news, adamw(olds[0][at], grad, olds[1][at], olds[2][at], rate, decay)):
            ref[at] = val

    for k, grad in enumerate((gate_g[0], value_g[...])):
        put(zx_new, zx, grad, RATE_MATRIX, DECAY, (slice(None), k, slice(None)))
    put(out_new, out, down_g[0], RATE_MATRIX, DECAY)

    @pl.when(pl.program_id(0) == 0)
    def _():
        put(bcdt_new, bcdt, cols_g[...].T[:cols_loc, :], RATE_MATRIX, DECAY)
        adam_small(
            heads, width, packed, packed_gain, put, gain, chan, bc, head, gain_new, chan_new, bc_new, head_new
        )


def adam_small(
    heads, width, packed, packed_gain, put, gain, chan, bc, head, gain_new, chan_new, bc_new, head_new
):
    over = packed[0] + packed[1] + packed[2] + packed[3]
    gains = packed_gain[0] + packed_gain[1] + packed_gain[2] + packed_gain[3]
    put(gain_new, gain, gains[: D // LANE, :], RATE_SMALL, 0.0)
    put(bc_new, bc, over[: KERNEL + 1, width : width + 2 * N], RATE_SMALL, 0.0)
    grad = jnp.concatenate([packed[k, : KERNEL + 2, :width] for k in range(4)], axis=1)
    put(chan_new, chan, grad, RATE_SMALL, 0.0)
    lane = lax.broadcasted_iota(jnp.int32, (LANE, 4 * heads), 0)
    slot = lax.broadcasted_iota(jnp.int32, (LANE, 4 * heads), 1)
    channel = lax.broadcasted_iota(jnp.int32, (width, 4 * heads), 0)
    wide_slot = lax.broadcasted_iota(jnp.int32, (width, 4 * heads), 1)
    rows = jnp.zeros((8, 4 * heads), F32)
    for k in range(4):
        here = jnp.where(lane + k * heads == slot, 1.0, 0.0)
        here = jnp.where(lane < heads, here, 0.0).astype(BF16)
        wide = jnp.where(channel // P_SIZE + k * heads == wide_slot, 1.0, 0.0).astype(BF16)
        hi, lo = two(packed[k, KERNEL + 3 : KERNEL + 11, :LANE])
        at = lax.broadcasted_iota(jnp.int32, rows.shape, 0)
        rows = rows + jnp.where(at < 2, dot(hi, here) + dot(lo, here), 0.0)
        hi, lo = two(packed[k, KERNEL + 2 : KERNEL + 10, :width])
        skip = dot(hi, wide) + dot(lo, wide)
        rows = rows + jnp.where(at == 2, jnp.broadcast_to(skip[0:1, :], rows.shape), 0.0)
    put(head_new, head, rows[:3, :], RATE_SMALL, 0.0)


def run_adam(pair, value_g, cols_g, packed, packed_gain, tok, own, last, t_index, olds, heads, cols_loc):
    rows, width = value_g.shape
    steps, size = own.shape
    count = 4 if rows % 32 == 0 else 2
    block, span = rows // count, steps // count
    half = count // 2
    one = lambda k: pl.BlockSpec((1, block, width), lambda i, t: (k, i, 0))
    some = pl.BlockSpec((block, width), lambda i, t: (i, 0))
    large = pl.BlockSpec((block, 2, width), lambda i, t: (i, 0, 0))
    tokens = pl.BlockSpec((span, size), lambda i, t: (i, 0))
    every = lambda x: pl.BlockSpec(x.shape, lambda i, t: (0,) * x.ndim, pipeline_mode=pl.Buffered(1))
    flat = [x for group in olds for x in group]
    specs = [large] * 3 + [some] * 3 + [every(x) for x in flat[6:]]
    return pl.pallas_call(
        functools.partial(adam_kernel, heads, cols_loc),
        grid_spec=pltpu.PrefetchScalarGridSpec(
            num_scalar_prefetch=1,
            grid=(count,),
            in_specs=[
                one(0), some, one(1), every(cols_g), every(packed), every(packed_gain),
                pl.BlockSpec((span, size), lambda i, t: (i, t[0])), tokens,
                pl.BlockSpec((1, span, size), lambda i, t: (i // half, i % half, 0)),
            ]
            + specs,
            out_specs=specs + [tokens],
        ),
        out_shape=[shape(*x.shape) for x in flat] + [shape(steps, size, dtype=BF16)],
        compiler_params=params(),
        cost_estimate=estimate(8),
        name="optimizer",
    )(
        jnp.full((1,), t_index, jnp.int32), pair, value_g, pair, cols_g, packed, packed_gain, tok, own,
        last, *flat,
    )


def doc_of(lengths, position):
    found = jnp.zeros(position.shape, F32)
    end = 0
    for k in range(lengths.shape[1] - 1):
        end = end + lengths[0, k]
        found = found + jnp.where(position >= end, 1.0, 0.0)
    return jnp.where(position < 0, -1.0, found)


def mark_chunk(lengths, begin, limit, info_ref, marks_ref):
    row = lax.broadcasted_iota(jnp.int32, (L, LANE), 0)
    lane = lax.broadcasted_iota(jnp.int32, (L, LANE), 1)
    offset = jnp.where(lane < KERNEL - 1, lane - KERNEL + 1, jnp.where(lane >= 8, lane - 7, 0))
    other = jnp.where(lane == 3, -1, jnp.where(lane == 4, L - 1, row + offset)) + begin
    mark = doc_of(lengths, row + begin)
    same = jnp.logical_and(doc_of(lengths, other) == mark, other < limit)
    info = jnp.where(same, 1.0, 0.0)
    info_ref[...] = jnp.where(lane == 5, mark, jnp.where(lane < 7 + KERNEL, info, 0.0))
    marks_ref[0] = doc_of(lengths, begin + lax.broadcasted_iota(jnp.int32, (8, L), 1))


def norm_rows(tok, gain):
    x = tok.astype(F32)
    square = x * x
    total = square[:, :LANE]
    for sl in tiles(D)[1:]:
        total = total + square[:, sl]
    inv = lax.rsqrt(jnp.sum(total, axis=1, keepdims=True) / D + EPS)
    return (x * inv * gain[0:1, :]).astype(BF16), inv


def project_kernel(
    heads, n, cols_loc, normed, ends, w_ref, wg_ref, chan, bcpar, head, e_ref, info,
    projected, cols, act, delta, cum, sloc, pfx, fin,
    halo_v, halo_b, ext_v, ext_b, state, prod, w_cols, prev_v, prev_b, halo_out, halo_got, h_s, h_r,
):
    i = pl.program_id(0)
    s, c, t = lax.axis_index("shard"), lax.axis_index("context"), lax.axis_index("tensor")
    width = w_ref.shape[1] // 2
    block = normed.shape[0]
    after = (s, jnp.minimum(c + 1, n - 1), t)
    halo = remote(halo_out, halo_got, h_s, h_r, after)

    @pl.when(i == 0)
    def _():
        pl.semaphore_wait(greet(beside_of(n)), 2)
        state[...] = jnp.zeros_like(state)
        prod[...] = jnp.ones_like(prod)
        lane = lax.broadcasted_iota(jnp.int32, (4 * LANE, 3 * N), 0)
        want = lax.broadcasted_iota(jnp.int32, (4 * LANE, 3 * N), 1)
        have = lane // LANE * cols_loc + lane % LANE
        want = jnp.where(want < 2 * N, want, jnp.where(want < 2 * N + heads, want + heads * t, -1))
        chosen = jnp.logical_and(have == want, lane % LANE < cols_loc)
        select = jnp.where(chosen, 1.0, 0.0).astype(BF16)
        for k in range(0, D, block):
            w_cols[k : k + block, :] = dot(wg_ref[k : k + block, :], select).astype(BF16)
        halo_out[:, :width] = dot(ends[...], w_ref[:, width:])[8:, :]
        halo_out[:, width:] = dot(ends[...], w_cols[...])[8:, :]

        @pl.when(c < n - 1)
        def _():
            halo.start()

    for k in range(0, 2 * width, 512):
        projected[:, k : k + 512] = dot(normed[...], w_ref[:, k : k + 512])
    cols[...] = dot(normed[...], w_cols[...])

    @pl.when(i == 0)
    def _():
        @pl.when(c > 0)
        def _():
            halo.wait_recv()
            halo_v[...] = halo_got[:, :width]
            halo_b[...] = halo_got[:, width:]

        @pl.when(c == 0)
        def _():
            halo_v[...] = jnp.zeros_like(halo_v)
            halo_b[...] = jnp.zeros_like(halo_b)

        @pl.when(c < n - 1)
        def _():
            halo.wait_send()

    val = projected.at[:, pl.ds(width, width)]

    for j in range(block // L):
        first = i == 0
        load_ext(ext_v, val, prev_v, halo_v, j, first)
        load_ext(ext_b, cols, prev_b, halo_b, j, first)
        prep_chunk(
            rows_at(cols, j), rows_at(info, j), chan, bcpar, head, e_ref, rows_at(act, j),
            rows_at(delta, j), rows_at(cum, j), lead_at(sloc, j), lead_at(pfx, j),
            ext_v, ext_b, state, prod,
        )
    prev_v[...] = projected[block - 8 :, width:]
    prev_b[...] = cols[block - 8 :, :]

    @pl.when(i == pl.num_programs(0) - 1)
    def _():
        fin[:N, :] = state[...]
        fin[N:, :] = prod[...]


def run_project(normed, weight, w_group, chan, bcpar, head, expand, info, heads, cols_loc):
    steps, width = normed.shape[0], weight.shape[1] // 2
    count = steps // L
    dma = pltpu.SemaphoreType.DMA
    return pl.pallas_call(
        functools.partial(project_kernel, heads, lax.axis_size("context"), cols_loc),
        grid=(steps // GROUP,),
        in_specs=[
            row_block(D),
            pl.BlockSpec((16, D), lambda i: (steps // 16 - 1, 0), pipeline_mode=pl.Buffered(1)),
            once(*weight.shape), once(*w_group.shape),
            once(KERNEL + 2, width), once(KERNEL + 1, 2 * N), once(8, LANE), once(2 * LANE, width),
            row_block(LANE),
        ],
        out_specs=[
            row_block(2 * width), row_block(3 * N),
            row_block(width + 2 * N), row_block(LANE), row_block(LANE), lead_block(N, width),
            lead_block(8, width), once(N + 8, width), once(8, width), once(8, 3 * N),
        ],
        out_shape=[
            shape(steps, 2 * width), shape(steps, 3 * N),
            shape(steps, width + 2 * N), shape(steps, LANE), shape(steps, LANE),
            shape(count, N, width), shape(count, 8, width), shape(N + 8, width), shape(8, width),
            shape(8, 3 * N),
        ],
        scratch_shapes=[
            pltpu.VMEM((8 + L, width), F32), pltpu.VMEM((8 + L, 3 * N), F32),
            pltpu.VMEM((N, width), F32), pltpu.VMEM((8, width), F32),
            pltpu.VMEM((D, 3 * N), BF16), pltpu.VMEM((8, width), F32), pltpu.VMEM((8, 3 * N), F32),
            pltpu.VMEM((8, width + 3 * N), F32), pltpu.VMEM((8, width + 3 * N), F32), dma, dma,
        ],
        compiler_params=pltpu.CompilerParams(
            dimension_semantics=("arbitrary",), vmem_limit_bytes=58 * 1024 * 1024,
            collective_id=8, has_side_effects=True,
        ),
        cost_estimate=estimate(45),
        name="project",
    )(normed, normed, weight, w_group, chan, bcpar, head, expand, info)


class AllSum:
    def __init__(self, n, refs, sems):
        s, c, t = lax.axis_index("shard"), lax.axis_index("context"), lax.axis_index("tensor")
        self.n, self.c, self.t = n, c, t
        self.mine, self.other, self.pair, self.pieces, self.total, self.every = refs
        core_s, core_r, piece_s, piece_r, group_s, group_r = sems
        self.core = remote(self.mine, self.other, core_s, core_r, (1 - s, c, t))
        self.along = [
            remote(self.pair, self.pieces.at[c], piece_s.at[k], piece_r.at[k], (s, lax.rem(c + k + 1, n), t))
            for k in range(n - 1)
        ]
        self.across = [
            remote(self.total, self.every.at[t], group_s.at[k], group_r.at[k], (s, c, lax.rem(t + k + 1, 4)))
            for k in range(3)
        ]

    def start(self):
        self.core.start()

    def after_core(self):
        self.core.wait()
        self.pair[...] = self.mine[...] + self.other[...]
        self.pieces[self.c] = self.pair[...]
        for copy in self.along:
            copy.start()

    def after_pieces(self):
        for copy in self.along:
            copy.wait()
        self.total[...] = sum(self.pieces[k] for k in range(1, self.n)) + self.pieces[0]
        self.every[self.t] = self.total[...]
        for copy in self.across:
            copy.start()

    def finish(self):
        for copy in self.across:
            copy.wait()


PACK = 16


def tail_kernel(
    n, grad_b, grad_v, normed_hbm, w_hbm, tok_hbm, back_hbm, late_hbm, wg_hbm,
    raw_t, fixed, gate_top, gate_end, tok_top, tok_end, inv, gain, sel_bc, sel_raw,
    late_rows, late_gain, taps_grad, bias_grad, norm_gain_grad, skip_grad, head_grad,
    tokens_out, value_out, cols_out, pack_out, gain_out,
    gb, gv, nm, w_ref, tok, back, w_cols, col_grad,
    peer_part, own_part, core_part, b_got, b_next, b_last, b_full, raw_full,
    early, mid, send, got, nxt, last, gain_grad, z_out, z_got, z_on, z_last,
    ng, col_peer, col_own, col_core, col_out, col_got, col_on, col_last,
    row_buf, row_held, *refs,
):
    tail_body(
        n, grad_b, grad_v, normed_hbm, w_hbm, tok_hbm, back_hbm, late_hbm, wg_hbm,
        raw_t, fixed, gate_top, gate_end, tok_top, tok_end, inv, gain, sel_bc, sel_raw,
        late_rows, late_gain, taps_grad, bias_grad, norm_gain_grad, skip_grad, head_grad,
        tokens_out, value_out, cols_out, pack_out, gain_out,
        gb, gv, nm, w_ref, tok, back, w_cols, col_grad,
        peer_part, own_part, core_part, b_got, b_next, b_last, b_full, raw_full,
        early, mid, send, got, nxt, last, gain_grad, z_out, z_got, z_on, z_last,
        ng, col_peer, col_own, col_core, col_out, col_got, col_on, col_last,
        row_buf, row_held, refs[:6], refs[6:12], *refs[12:25], refs[25:31], refs[31:37],
    )


def tail_body(
    n, grad_b, grad_v, normed_hbm, w_hbm, tok_hbm, back_hbm, late_hbm, wg_hbm,
    raw_t, fixed, gate_top, gate_end, tok_top, tok_end, inv, gain, sel_bc, sel_raw,
    late_rows, late_gain, taps_grad, bias_grad, norm_gain_grad, skip_grad, head_grad,
    tokens_out, value_out, cols_out, pack_out, gain_out,
    gb, gv, nm, w_ref, tok, back, w_cols, col_grad,
    peer_part, own_part, core_part, b_got, b_next, b_last, b_full, raw_full,
    early, mid, send, got, nxt, last, gain_grad, z_out, z_got, z_on, z_last,
    ng, col_peer, col_own, col_core, col_out, col_got, col_on, col_last,
    row_buf, row_held, pack_refs, gain_refs,
    local, raw_s, raw_r, b_s, b_r, f_s, f_r, core_s, core_r, z_s, z_r, row_s, row_r,
    pack_sems, gain_sems,
):
    s, c, t = lax.axis_index("shard"), lax.axis_index("context"), lax.axis_index("tensor")
    near = peers(t)
    to = [(s, c, near[0]), (s, c, near[1])]
    group = [(s, c, lax.rem(t + k, 4)) for k in (1, 2, 3)]
    to_core = (1 - s, c, t)
    to_piece = [(s, lax.rem(c + k, n), t) for k in range(1, n)]
    in_line = n == 4
    line = [(s, c + 1 - 2 * lax.rem(c, 2), t), (s, 3 - c, t)] if in_line else []
    steps, width = grad_v.shape
    size = w_ref.shape[0] // 4
    share = steps // 4
    mine_lanes = pl.ds(pl.multiple_of(t * size, size), size)
    loads = [
        pltpu.make_async_copy(src, dst, local.at[k])
        for k, (src, dst) in enumerate(
            [
                (grad_b, gb), (grad_v, gv), (normed_hbm, nm), (w_hbm, w_ref),
                (tok_hbm.at[:, mine_lanes], tok), (back_hbm.at[:, mine_lanes], back),
                (late_hbm, ng.at[pl.ds(GROUP, steps - GROUP), :]),
                (wg_hbm.at[mine_lanes, :], w_cols),
            ]
        )
    ]
    for load in loads[:2]:
        load.start()
    pl.semaphore_wait(greet(group + [to_core] + to_piece), n + 3)

    raw_full[t] = raw_t[...]
    raws = [
        remote(raw_t, raw_full.at[t], raw_s.at[k], raw_r.at[k], target)
        for k, target in enumerate(group)
    ]
    for copy in raws:
        copy.start()

    def rows_of(k):
        return pl.ds(pl.multiple_of(k * share, share), share)

    def lanes_of(side):
        return pl.ds(side * N, N)

    loads[0].wait()
    for load in loads[2:]:
        load.start()
    gb[steps - 8 :, :] = fixed[:, width:]

    def b_first(side, part):
        k = near[side] if part == 0 else 3 - t
        return remote(
            gb.at[rows_of(k), lanes_of(side)], b_got.at[side, part], b_s.at[side, part],
            b_r.at[side, part], to[side],
        )

    def b_second(side):
        return remote(
            b_next.at[side], b_last.at[side], b_s.at[side, 2], b_r.at[side, 2], to[1 - side]
        )

    def b_back(side, part):
        k = near[1 - side] if part == 2 else t
        where = b_full.at[rows_of(k), lanes_of(side)]
        return remote(
            where, where, b_s.at[side, 3 + part], b_r.at[side, 3 + part],
            to[1 - side] if part == 0 else to[side],
        )

    for side in (0, 1):
        for part in (0, 1):
            b_first(side, part).start()

    pack = pack_refs[0]
    pack[...] = jnp.zeros_like(pack)
    gain_refs[0][...] = jnp.zeros_like(gain_refs[0])
    total = width + 2 * N
    add_up = lambda x: jnp.sum(x, axis=0, keepdims=True)
    for k in range(KERNEL):
        pack[k : k + 1, :total] = add_up(taps_grad[8 * k : 8 * k + 8, :])
    pack[KERNEL : KERNEL + 1, :total] = add_up(bias_grad[...])
    pack[KERNEL + 1 : KERNEL + 2, :width] = add_up(norm_gain_grad[...])
    pack[KERNEL + 2 : KERNEL + 3, :width] = add_up(skip_grad[...])
    pack[KERNEL + 3 : KERNEL + 4, :LANE] = add_up(head_grad[:8, :])
    pack[KERNEL + 4 : KERNEL + 5, :LANE] = add_up(head_grad[8:, :])
    pack_sum = AllSum(n, pack_refs, pack_sems)
    gain_sum = AllSum(n, gain_refs, gain_sems)
    pack_sum.start()

    loads[1].wait()
    tail = gv[steps - 16 :, :].astype(F32)
    gv[steps - 16 :, :] = jnp.concatenate([tail[:8], fixed[:, :width]], axis=0).astype(BF16)
    loads[2].wait()
    half_d = nm.shape[1] // 2
    step = 256

    def product(shard, right, into):
        for m in range(half_d // step):
            lanes = pl.ds(pl.multiple_of(shard * half_d + m * step, step), step)
            into[m * step : (m + 1) * step, :] = over_rows(nm, lanes, right)

    product(1 - s, lambda rows: gv[rows, :], peer_part)
    core = remote(peer_part, core_part, core_s.at[0], core_r.at[0], to_core)
    core.start()

    for side in (0, 1):
        for part in (0, 1):
            b_first(side, part).wait()
        b_next[side] = gb[rows_of(near[1 - side]), lanes_of(side)] + b_got[side, 1]
        b_second(side).start()
    pack_sum.after_core()

    product(s, lambda rows: gv[rows, :], own_part)

    for side in (0, 1):
        b_second(side).wait()
        mine = gb[rows_of(t), lanes_of(side)] + b_got[side, 0] + b_last[side]
        b_full[rows_of(t), lanes_of(side)] = mine.astype(BF16)
        b_back(side, 0).start()

    block = half_d // n
    side_w = width // 2
    both = own_part
    if in_line:
        first = [c + 1 - 2 * lax.rem(c, 2), 3 - c]
        across = lax.rem(c + 2, 4)

    def block_rows(k):
        return pl.ds(pl.multiple_of(k * block, 8), block)

    def z_block(k, side):
        return both[block_rows(k), side * side_w : (side + 1) * side_w]

    def z_first(side):
        return remote(z_out.at[side], z_got.at[side], z_s.at[side], z_r.at[side], line[side])

    def z_second(side):
        return remote(z_on.at[side], z_last.at[side], z_s.at[2 + side], z_r.at[2 + side], line[1 - side])

    def col_first():
        return remote(col_out, col_got, z_s.at[4], z_r.at[4], line[0])

    def col_second():
        return remote(col_on, col_last, z_s.at[5], z_r.at[5], line[1])

    core.wait()
    both[...] = both[...] + core_part[...]
    if in_line:
        for side in (0, 1):
            z_out[side, :block, :] = z_block(first[side], side).astype(BF16)
            z_out[side, block:, :] = z_block(across, side).astype(BF16)
            z_first(side).start()
    for side in (0, 1):
        b_back(side, 0).wait()
        for part in (1, 2):
            b_back(side, part).start()

    loads[3].wait()
    pack_sum.after_pieces()
    half = GROUP // 2
    tail_half = END // 2

    def f_first(side):
        return remote(send.at[side], got.at[side], f_s.at[side], f_r.at[side], to[side])

    def f_second(side):
        return remote(
            nxt.at[side], last.at[side], f_s.at[2 + side], f_r.at[2 + side], to[1 - side]
        )

    gain_grad[...] = late_gain[...]
    for g in range(GROUP // PART, steps // PART):
        row_buf[:, g * PART : (g + 1) * PART] = late_rows[g]
    ends = [jnp.zeros((LANE - END, LANE), F32)]
    for side in (0, 1):
        rows = slice(side * half, (side + 1) * half)
        tail_rows = slice(side * tail_half, (side + 1) * tail_half)
        end_rows = slice(steps - END + side * tail_half, steps - END + (side + 1) * tail_half)
        x = jnp.concatenate(
            [
                jnp.concatenate([gate_top[rows, :], gv[rows, :]], axis=1),
                jnp.concatenate([gate_end[tail_rows, :], gv[end_rows, :]], axis=1),
            ],
            axis=0,
        )
        keep, go = shares_of(side, t)
        gone = dot(x, pick(w_ref, *go), 1, 1)
        send[side] = gone.astype(BF16)
        f_first(side).start()
        kept = dot(x, pick(w_ref, *keep), 1, 1)
        early[side] = kept[:, :size]
        mid[side] = kept[:, size:]
        scale = jnp.concatenate([inv[rows, :], inv[end_rows, :]], axis=0)
        parts = [kept[:, :size], kept[:, size:], gone[:, :size], gone[:, size:]]

        def z(lanes):
            values = jnp.concatenate([tok_top[rows, lanes], tok_end[tail_rows, lanes]], axis=0)
            return values.astype(F32) * scale

        sums = count_rows(parts, z, gain, keep + go, gain_grad)
        row_buf[:, rows] = row_dots(sums[:half])
        ends.append(sums[half:])
    row_buf[:, steps - LANE :] += row_dots(jnp.concatenate(ends, axis=0))

    for copy in raws:
        copy.wait()
    for side in (0, 1):
        for part in (1, 2):
            b_back(side, part).wait()
    raw_all = jnp.concatenate([raw_full[k] for k in range(4)], axis=0)

    for k in range(steps // GROUP):
        rows = slice(k * GROUP, (k + 1) * GROUP)
        chosen = dot(b_full[rows, :], sel_bc[...]) + dot(raw_all[:, rows], sel_raw[...], 0, 0)
        col_grad[rows, :] = chosen.astype(BF16)
    own_lanes = pl.ds(pl.multiple_of(t * LANE, LANE), LANE)
    product(1 - s, lambda rows: col_grad[rows, own_lanes], col_peer)
    col_core_copy = remote(col_peer, col_core, core_s.at[1], core_r.at[1], to_core)
    col_core_copy.start()
    gain_mine = gain[0:1, mine_lanes]
    loads[4].wait()
    loads[6].wait()
    loads[7].wait()
    ng[steps - END :, :] = jnp.zeros((END, size), F32)
    for k in range(steps // GROUP):
        rows = slice(k * GROUP, (k + 1) * GROUP)
        part = dot(col_grad[rows, :], w_cols[...], 1, 1)
        ng[rows, :] = part if k == 0 else ng[rows, :] + part
        part = part * (tok[rows, :].astype(F32) * inv[rows, :])
        gain_grad[:, mine_lanes] += fold(part)
        part = part * gain_mine
        sums = part[:, :LANE]
        for sl in tiles(size)[1:]:
            sums = sums + part[:, sl]
        row_buf[:, rows] += row_dots(sums)
    row_copies = [
        remote(row_buf, row_held.at[k], row_s.at[k], row_r.at[k], target)
        for k, target in enumerate(group)
    ]
    for copy in row_copies:
        copy.start()

    for k in range(D // LANE):
        gain_refs[0][k : k + 1, :] = add_up(gain_grad[:, k * LANE : (k + 1) * LANE])
    gain_sum.start()

    for side in (0, 1):
        f_first(side).wait()
        nxt[side] = (mid[side] + got[side, :, size:].astype(F32)).astype(BF16)
        f_second(side).start()
        early[side] += got[side, :, :size].astype(F32)

    product(s, lambda rows: col_grad[rows, own_lanes], col_own)

    gain_sum.after_core()
    if in_line:
        for side in (0, 1):
            z_first(side).wait()
            z_on[side] = (
                z_block(first[1 - side], side) + z_got[side, block:, :].astype(F32)
            ).astype(BF16)
            z_second(side).start()
    col_core_copy.wait()
    col_own[...] = col_own[...] + col_core[...]
    if in_line:
        col_out[:block, :] = col_own[block_rows(first[0]), :]
        col_out[block:, :] = col_own[block_rows(across), :]
        col_first().start()

    gain_sum.after_pieces()
    if in_line:
        col_first().wait()
        col_on[...] = col_own[block_rows(first[1]), :] + col_got[block:, :]
        col_second().start()

    loads[5].wait()
    for copy in row_copies:
        copy.wait()
    for side in (0, 1):
        f_second(side).wait()
        early[side] += last[side].astype(F32)
        at = steps - END + side * tail_half
        ng[at : at + tail_half, :] += early[side, half:, :]
        ng[side * half : (side + 1) * half, :] += early[side, :half, :]
    row_total = row_buf[...] + row_held[0] + row_held[1] + row_held[2]
    for k in range(steps // LANE):
        rows = slice(k * LANE, (k + 1) * LANE)
        row_dot = jnp.broadcast_to(row_total[0:1, rows] * (1.0 / D), (LANE, LANE)).T
        scale = inv[rows, :]
        for sl in tiles(size):
            z_tile = tok[rows, sl].astype(F32) * scale
            change = scale * (ng[rows, sl] * gain_mine[:, sl] - z_tile * row_dot)
            tokens_out[rows, sl] = (back[rows, sl].astype(F32) + change).astype(BF16)

    if in_line:
        for side in (0, 1):
            z_second(side).wait()
            value_out[:, side * side_w : (side + 1) * side_w] = (
                z_block(c, side) + z_got[side, :block, :].astype(F32) + z_last[side].astype(F32)
            )
        col_second().wait()
        cols_out[...] = col_own[block_rows(c), :] + col_got[:block, :] + col_last[...]
    else:
        value_out[...] = both[...]
        cols_out[...] = col_own[...]
    pack_sum.finish()
    pack_out[...] = pack_refs[5][...]
    gain_sum.finish()
    gain_out[...] = gain_refs[5][...]


def run_tail(
    grad_b, grad_v, normed, weight, tok, back, late, w_group, raw_t, fixed, gate_grad, inv, gain,
    sel_bc, sel_raw, late_rows, late_gain, *small,
):
    n = lax.axis_size("context")
    steps, width = grad_v.shape
    size = D // 4
    half_d = D // 2
    block = half_d // n
    side_rows = (GROUP + END) // 2
    share = steps // 4
    top = lambda w: pl.BlockSpec((GROUP, w), lambda i: (0, 0), pipeline_mode=pl.Buffered(1))
    end = lambda w: pl.BlockSpec(
        (END, w), lambda i: (steps // END - 1, 0), pipeline_mode=pl.Buffered(1)
    )
    full = lambda x: once(*x.shape)
    hbm = pl.BlockSpec(memory_space=pl.ANY)
    dma = pltpu.SemaphoreType.DMA
    vmem = pltpu.VMEM
    value_rows = block if n == 4 else half_d
    pair = (2, side_rows, size)
    packed = (PACK, width + 2 * N)
    return pl.pallas_call(
        functools.partial(tail_kernel, n),
        grid=(1,),
        in_specs=[hbm] * 8
        + [full(raw_t), full(fixed), top(width), end(width), top(D), end(D)]
        + [full(x) for x in (inv, gain, sel_bc, sel_raw)]
        + [full(x) for x in (late_rows, late_gain, *small)],
        out_specs=[
            once(steps, size), once(value_rows, width), once(value_rows, LANE), once(4, *packed),
            once(4, 16, LANE),
        ],
        out_shape=[
            shape(steps, size, dtype=BF16), shape(value_rows, width), shape(value_rows, LANE),
            shape(4, *packed), shape(4, 16, LANE),
        ],
        scratch_shapes=[
            vmem((steps, 2 * N), F32), vmem((steps, width), BF16), vmem(normed.shape, BF16),
            vmem(weight.shape, BF16), vmem((steps, size), BF16), vmem((steps, size), BF16),
            vmem((size, w_group.shape[1]), BF16),
            vmem((steps, w_group.shape[1]), BF16),
            vmem((half_d, width), F32), vmem((half_d, width), F32), vmem((half_d, width), F32),
            vmem((2, 2, share, N), F32), vmem((2, share, N), F32), vmem((2, share, N), F32),
            vmem((steps, 2 * N), BF16), vmem((4, 16, steps), BF16),
            vmem(pair, F32), vmem(pair, F32), vmem((2, side_rows, 2 * size), BF16),
            vmem((2, side_rows, 2 * size), BF16), vmem(pair, BF16), vmem(pair, BF16), vmem((8, D), F32),
            vmem((2, 2 * block, width // 2), BF16), vmem((2, 2 * block, width // 2), BF16),
            vmem((2, block, width // 2), BF16), vmem((2, block, width // 2), BF16),
            vmem((steps, size), F32),
            vmem((half_d, LANE), F32), vmem((half_d, LANE), F32), vmem((half_d, LANE), F32),
            vmem((2 * block, LANE), F32), vmem((2 * block, LANE), F32), vmem((block, LANE), F32),
            vmem((block, LANE), F32),
            vmem((8, steps), F32), vmem((3, 8, steps), F32),
            *[
                vmem((*lead, *dims), F32)
                for dims in (packed, (16, LANE))
                for lead in ((), (), (), (n,), (), (4,))
            ],
            dma((8,)), dma((3,)), dma((3,)), dma((2, 6)), dma((2, 6)), dma((4,)), dma((4,)),
            dma((2,)), dma((2,)), dma((6,)), dma((6,)), dma((3,)), dma((3,)),
            *[dma, dma, dma((n - 1,)), dma((n - 1,)), dma((3,)), dma((3,))] * 2,
        ],
        compiler_params=pltpu.CompilerParams(
            dimension_semantics=("arbitrary",), vmem_limit_bytes=56 * 1024 * 1024,
            collective_id=5, has_side_effects=True,
        ),
        cost_estimate=estimate(50),
        name="tail",
    )(
        grad_b, grad_v, normed, weight, tok, back, late, w_group,
        raw_t, fixed, gate_grad, gate_grad, tok, tok, inv, gain, sel_bc, sel_raw,
        late_rows, late_gain, *small,
    )


def pad_rows(x, rows=8):
    return jnp.concatenate([x, jnp.zeros((rows - x.shape[0], x.shape[1]), x.dtype)], axis=0)


def pad_cols(x, cols=LANE):
    return jnp.concatenate([x, jnp.zeros((x.shape[0], cols - x.shape[1]), x.dtype)], axis=1)


def on_device(
    tokens, cotangent, doc_lengths, zx_weight, bcdt_weight, out_weight, input_gain, chan_params,
    bc_params, head_params, zx_first, bcdt_first, out_first, gain_first, chan_first, bc_first,
    head_first, zx_second, bcdt_second, out_second, gain_second, chan_second, bc_second, head_second,
):
    n_tensor = lax.axis_size("tensor")
    t_index = lax.axis_index("tensor")
    c_index = lax.axis_index("context")
    tok = tokens[0]
    resid = tok.astype(F32)
    back = cotangent[0]
    steps = resid.shape[0]
    inner_loc = INNER // n_tensor
    heads_loc = H // n_tensor
    share = D // n_tensor
    count = steps // L
    rows_loc = zx_weight.shape[0]
    cols_loc = bcdt_weight.shape[1]

    gain8 = jnp.broadcast_to(input_gain[None], (8, D))
    proj_w, cols_z, normed, inv_rms, info, marks_rows, edge_mask = line_gather(
        zx_weight, bcdt_weight.T, tok, gain8, doc_lengths
    )
    down_block, _ = lax.optimization_barrier((out_weight.astype(BF16).T, proj_w))
    down_t = lax.all_gather(down_block, ("shard", "context"), axis=0, tiled=True)
    chan_loc = lax.dynamic_slice_in_dim(chan_params, t_index * inner_loc, inner_loc, 1)
    head_loc = lax.dynamic_slice_in_dim(head_params, t_index * heads_loc, heads_loc, 1)
    chan8, bc8 = chan_loc, bc_params
    head8 = pad_rows(pad_cols(head_loc))
    spread_at = np.arange(2 * LANE)[:, None] % LANE == np.arange(inner_loc)[None, :] // P_SIZE
    expand = spread_at.astype(ml_dtypes.bfloat16)
    (
        projected, cols, act, delta, cum, sloc, pfx, final, halo_v, halo_b,
    ) = run_project(
        normed, proj_w, cols_z, chan8, bc8, head8, expand, info, heads_loc, cols_loc
    )
    entry, back_scaled = run_entry(final, back, down_t)
    ssd, sums = run_ahead(
        act, delta, cum, info, marks_rows, sloc, pfx, entry, projected, back_scaled, chan8, head8,
        expand, heads_loc,
    )
    scaled, *out_fan = run_out(ssd, projected, sums, chan8, down_t)
    gate_grad, mixed_grad, aloc, sfx, first_adj, norm_gain_grad = run_norm(
        ssd, projected, back_scaled, sums, act, cum, info, chan8, expand, heads_loc
    )
    later, out_own, out_next, *z_arrays = run_middle(
        first_adj, out_fan, normed, gate_grad, back, scaled
    )
    in_line = lax.axis_size("context") == 4
    total_width = inner_loc + 2 * N

    (
        grad_v, grad_b, raw_t, last_rows, _, taps_grad, bias_grad, skip_grad, head_grad,
        ng_late, late_rows, late_gain, out_last, *z_sum,
    ) = run_grand(
        projected, cols, halo_v, halo_b, info, marks_rows, delta, cum, ssd, mixed_grad,
        sloc, pfx, entry, aloc, sfx, later, chan8, bc8, head8, expand, heads_loc,
        gate_grad, proj_w, tok, inv_rms, gain8, edge_mask, out_next, z_arrays if in_line else [],
    )
    if in_line:
        pair_g = z_sum[0]
    else:
        pair_g = jnp.stack(
            [lax.psum_scatter(z_arrays[0][k], "context", scatter_dimension=0, tiled=True) for k in (0, 1)]
        )
    column = np.arange(4 * LANE)
    column = np.where(column % LANE < cols_loc, column // LANE * cols_loc + column % LANE, -1)[None, :]
    sel_bc = (np.arange(2 * N)[:, None] == column).astype(ml_dtypes.bfloat16)
    slot = np.arange(4 * 16)[:, None]
    of_slot = np.where(slot % 16 < heads_loc, 2 * N + slot // 16 * heads_loc + slot % 16, -2)
    sel_raw = (of_slot == column).astype(ml_dtypes.bfloat16)
    tokens_grad, value_g, cols_g, packed, packed_gain = run_tail(
        grad_b, grad_v, normed, proj_w, tok, back, ng_late, cols_z, raw_t, last_rows, gate_grad,
        inv_rms, gain8, sel_bc, sel_raw, late_rows, late_gain,
        taps_grad, bias_grad, norm_gain_grad, skip_grad, head_grad,
    )
    tokens_grad = tokens_grad[None]
    if not in_line:
        value_g = lax.psum_scatter(value_g, "context", scatter_dimension=0, tiled=True)
        cols_g = lax.psum_scatter(cols_g[:, :cols_loc], "context", scatter_dimension=0, tiled=True)
        cols_g = pad_cols(cols_g)
    flip = lambda *arrays: tuple(a.T for a in arrays)
    lift = lambda *arrays: tuple(a.reshape(D // LANE, LANE) for a in arrays)
    news = run_adam(
        pair_g, value_g, cols_g, packed, packed_gain, tok, out_own, out_last, t_index,
        (
            (zx_weight, zx_first, zx_second), flip(out_weight, out_first, out_second),
            flip(bcdt_weight, bcdt_first, bcdt_second), lift(input_gain, gain_first, gain_second),
            (chan_params, chan_first, chan_second), (bc_params, bc_first, bc_second),
            (head_params, head_first, head_second),
        ),
        heads_loc, cols_loc,
    )
    zx_new, out_new, bcdt_new, gain_new = news[:3], flip(*news[3:6]), flip(*news[6:9]), news[9:12]
    block_out = news[21][None]
    return (
        block_out, tokens_grad, *zx_new, *bcdt_new, *out_new, *[g.reshape(D) for g in gain_new], *news[12:21]
    )


def solution(mesh):
    big = P(("shard", "context"), None, "tensor")
    cols = P(("shard", "context"), "tensor")
    down = P("tensor", ("shard", "context"))
    rows = P("shard", "context", None)
    out_rows = P("shard", "context", "tensor")
    return jax.shard_map(
        on_device,
        mesh=mesh,
        in_specs=(
            rows, rows, P("shard", None), big, cols, down, P(), P(), P(), P(),
            big, cols, down, P(), P(), P(), P(),
            big, cols, down, P(), P(), P(), P(),
        ),
        out_specs=(
            out_rows, out_rows, big, big, big, cols, cols, cols, down, down, down,
            *([P()] * 12),
        ),
        check_vma=False,
    )
```
